32 devices in a mesh: gx: 8 (over z, core), gy: 4 (over y, x).
Axes of the slice: x: 2, y: 2, z: 4, core: 2. Of those that a mesh axis runs over, the one named last changes fastest.
Arguments:
- temp_fluid: float32 [128, 256, 1024], P('gx', 'gy'), may hold values from -6 to 6
- velocity: bfloat16 [3, 128, 256, 1024], P(None, 'gx', 'gy'), may hold values from -1 to 1
- wall_old: float32 [128, 256, 128], P('gx', 'gy'), may hold values from -6 to 6
- wall_mask: int32 [128, 256, 128], P('gx', 'gy'), may hold values 0 or 1
- owner_map: int32 [32, 1024, 1], P(('gx', 'gy')), may hold values from 0 to 31; in each aligned block of 1024 rows (0 to 1023, 1024 to 2047, ..., all dimensions but the last counted through in order) at most 96 rows name the same one
- slot_map: int32 [32, 1024], P(('gx', 'gy')), may hold values from 0 to 511
- temp_solid: float32 [128, 128, 128], P('gx', 'gy'), may hold values from -6 to 6
- material: int32 [128, 128, 128], P('gx', 'gy'), may hold values from 0 to 3
Outputs:
- fluid_next: float32 [128, 256, 1024], P('gx', 'gy')
- wall_next: float32 [128, 256, 128], P('gx', 'gy')
- solid_next: float32 [128, 128, 128], P('gx', 'gy')
- stress_force: float32 [3, 128, 128, 128], P(None, 'gx', 'gy')
The draws below stay inside these ranges and needn't reach their ends.
Inputs may be any that keep to these rules, and one draw needn't show every extreme that they name: `owner_map`: among the rows of one device, no owner is named by more than 96 rows, a bound that some block reaches.
All inputs are finite; a program needn't handle non-finite values. No bound on the sum of `wall_mask` on one device may be relied on, other than what follows from the above.
Results may differ from the reference program's by a relative error of at most 0.0003.
Values sent between devices are 32-bit elements; how exact they have to be, the bound alone decides.
No kernel may reach another device: no remote copies, remote signals or barrier semaphores. Data moves between devices by JAX's collectives and lax.ppermute only.
A program may use at most 128 MiB of HBM per device.

```python
import math
import jax
import jax.numpy as jnp
import numpy as np

CX = 16
CY = 64
NZ = 1024
ROW = 128
SX = 16
SY = 32
FSTEPS = 2
SSTEPS = 4
NMAT = 4
SZ = 128
NX = 128
NY = 256
SXG = 128
SYG = 128
ROWS = 1024
SLOTS = 512
CAP = 96
N_GX = 8
N_GY = 4
DEVICES = 32


def place_ends(array, own_key, low, largest):
    longest = array.shape.index(max(array.shape))
    spots = []
    for shift in (0, 1):
        where = [jax.random.randint(jax.random.fold_in(own_key, axis), (), 0, length) for axis, length in enumerate(array.shape)]
        where[longest] = (where[longest] + shift) % array.shape[longest]
        spots.append(tuple(where))
    return array.at[spots[0]].set(low).at[spots[1]].set(largest)


def level_of(stream_key, dims, pieces, smallest, top_value):
    loudness, own = 1.0, jax.random.fold_in(stream_key, 6)
    for position, parts in pieces:
        heights = jnp.exp(jax.random.uniform(jax.random.fold_in(own, position), (parts,), jnp.float32, smallest / len(pieces), top_value / len(pieces)))
        loudness = loudness * jnp.repeat(heights, dims[position] // parts).reshape([-1 if axis == position else 1 for axis in range(len(dims))])
    return loudness


def deal_out(own_key, own, number, rows, amount, top, most, skew):
    order = jax.random.permutation(own_key, amount)
    packed, ordinary = load_shares(amount, rows * top, most, skew, True), load_shares(amount, rows * top, most, skew, False)
    places = jnp.arange(amount)

    def named(sizes, turn):
        used = int((sizes > 0).sum())
        fixed = max(1, used // 4)
        shifted = fixed + (places - fixed + turn * (used - fixed)) % max(1, amount - fixed)
        return jnp.zeros((amount,), jnp.int32).at[order[jnp.where(places < fixed, places, shifted)]].set(jnp.asarray(sizes, jnp.int32))

    sizes = jnp.where(number % 4 == 0, named(packed, number // 4), named(ordinary, number - number // 4 - 1))
    mixed = jax.random.permutation(jax.random.fold_in(own, 3), amount)
    source_of, receiver = mixed[0:amount // 2 * 2:2], mixed[1:amount // 2 * 2:2]
    margin = jnp.minimum(sizes[source_of] - 1, most - sizes[receiver]) // 2
    margin = jnp.where((source_of == order[0]) | (receiver == order[0]) | (sizes[receiver] == 0), 0, jnp.maximum(margin, 0))
    shifted = jax.random.randint(jax.random.fold_in(own, 4), (amount // 2,), 0, 1 << 20) % (margin + 1)
    sizes = sizes.at[source_of].add(-shifted).at[receiver].add(shifted)
    labels = jnp.searchsorted(jnp.cumsum(sizes), jnp.arange(rows * top), side="right").astype(jnp.int32)
    listing = labels.reshape(top, rows).T
    listing = listing[jax.random.permutation(jax.random.fold_in(own, 1), rows)]
    turn = jax.random.randint(jax.random.fold_in(own, 2), (rows, 1), 0, top)
    return jnp.take_along_axis(listing, (jnp.arange(top)[None, :] + turn) % top, axis=1)


def load_shares(number_of, total, limit, lean, full):
    weights = [(1 << 20) // math.isqrt(standing ** lean) + 1 for standing in range(1, number_of + 1)]
    largest = limit if full else min(limit, max(-(-total // number_of), total * weights[0] // sum(weights)))
    least = 1 if total - largest >= number_of - 1 else 0
    holding, surplus = [largest] + [least] * (number_of - 1), total - largest - least * (number_of - 1)
    while surplus > 0:
        free = [i for i in range(1, number_of) if holding[i] < largest] or [i for i in range(1, number_of) if holding[i] < limit]
        mass, left = sum([weights[i] for i in free]), surplus
        for i in free:
            extra = min(limit - holding[i], max(1, left * weights[i] // mass), surplus)
            holding[i] = holding[i] + extra
            surplus = surplus - extra
    return np.array(holding)


def centred(stream_key, extent, width, most, cuts=(), dtype=jnp.bfloat16):
    entries = jax.random.normal(stream_key, extent, jnp.float32) * width
    if len(cuts) > 0:
        entries = level_of(stream_key, extent, cuts, -0.22, 0.18) * entries
    return jnp.clip(entries, min=-most, max=most).astype(dtype)


def setup_inputs(seed: int = 0) -> dict:
    keys = jax.random.split(jax.random.key(seed), 9)
    temp_fluid = centred(keys[0], (NX, NY, NZ), 1.0, 6.0, ((0, 8), (1, 4)), jnp.float32)
    velocity = jnp.clip(jax.random.uniform(keys[1], (3, NX, NY, NZ), jnp.float32, -1.0, 1.0) * level_of(keys[1], (3, NX, NY, NZ), ((1, 8), (2, 4)), -0.4, 0.0), -1.0, 1.0).astype(jnp.bfloat16)
    wall_old = centred(keys[2], (NX, NY, ROW), 1.0, 6.0, ((0, 8), (1, 4)), jnp.float32)
    wall_mask = place_ends((jax.random.randint(keys[3], (NX, NY, ROW), 0, 4) < 3).astype(jnp.int32), jax.random.fold_in(keys[3], 1), 0, 1)
    owner_map_keys = jax.random.split(jax.random.fold_in(keys[4], 1), DEVICES * ROWS // ROWS)
    owner_map_turns = jax.random.permutation(jax.random.fold_in(keys[4], 3), DEVICES * ROWS // ROWS)
    owner_map = jax.vmap(lambda own, number: deal_out(jax.random.fold_in(keys[4], 2), own, number, ROWS, DEVICES, 1, CAP, 2))(owner_map_keys, owner_map_turns).reshape((DEVICES, ROWS, 1))
    slot_map = place_ends(jax.random.randint(keys[5], (DEVICES, ROWS), 0, SLOTS), jax.random.fold_in(keys[5], 1), 0, SLOTS - 1).astype(jnp.int32)
    temp_solid = centred(keys[6], (SXG, SYG, SZ), 1.0, 6.0, ((0, 8), (1, 4)), jnp.float32)
    material = place_ends(jax.random.randint(keys[7], (SXG, SYG, SZ), 0, NMAT), jax.random.fold_in(keys[7], 1), 0, NMAT - 1).astype(jnp.int32)
    return dict(temp_fluid=temp_fluid, velocity=velocity, wall_old=wall_old, wall_mask=wall_mask, owner_map=owner_map, slot_map=slot_map, temp_solid=temp_solid, material=material)


time_step = 0.1
diffusivity = 0.5
film_coef = 2.0
solid_step = 0.05
source_gain = 4.0
conduct_table = (0.4, 0.9, 1.5, 2.2)
modulus_table = (0.5, 1.0, 1.6, 2.4)


def laplace(padded):
    center = padded[1:-1, 1:-1, 1:-1]
    beside = padded[2:, 1:-1, 1:-1] + padded[:-2, 1:-1, 1:-1]
    beside = beside + padded[1:-1, 2:, 1:-1] + padded[1:-1, :-2, 1:-1]
    beside = beside + padded[1:-1, 1:-1, 2:] + padded[1:-1, 1:-1, :-2]
    return beside - 6.0 * center


def advect(padded, velocity):
    center = padded[1:-1, 1:-1, 1:-1]
    uppers = (padded[2:, 1:-1, 1:-1], padded[1:-1, 2:, 1:-1], padded[1:-1, 1:-1, 2:])
    lowers = (padded[:-2, 1:-1, 1:-1], padded[1:-1, :-2, 1:-1], padded[1:-1, 1:-1, :-2])
    total = jnp.zeros_like(center)
    for comp in range(3):
        speed = velocity[comp].astype(jnp.float32)
        total = total + jnp.maximum(speed, 0.0) * (center - lowers[comp]) + jnp.minimum(speed, 0.0) * (uppers[comp] - center)
    return total


def fluid_update(padded, velocity, sink):
    center = padded[1:-1, 1:-1, 1:-1]
    return center + time_step * (diffusivity * laplace(padded) - advect(padded, velocity)) - time_step * sink


def table_lookup(material, table):
    out = jnp.zeros(material.shape, jnp.float32)
    for index in range(NMAT):
        out = out + jnp.where(material == index, table[index], 0.0).astype(jnp.float32)
    return out


def solid_update(padded, cond, heat):
    center = padded[1:-1, 1:-1, 1:-1]
    return center + solid_step * (cond * laplace(padded) + source_gain * heat)


def gradient(padded):
    first = 0.5 * (padded[2:, 1:-1, 1:-1] - padded[:-2, 1:-1, 1:-1])
    second = 0.5 * (padded[1:-1, 2:, 1:-1] - padded[1:-1, :-2, 1:-1])
    third = 0.5 * (padded[1:-1, 1:-1, 2:] - padded[1:-1, 1:-1, :-2])
    return jnp.stack([first, second, third])


def reference(temp_fluid, velocity, wall_old, wall_mask, owner_map, slot_map, temp_solid, material):
    flux = wall_mask.astype(jnp.float32) * film_coef * (temp_fluid[:, :, :ROW] - wall_old)
    flux_rows = flux.reshape(N_GX, CX, N_GY, CY, ROW).transpose(0, 2, 1, 3, 4).reshape(DEVICES, ROWS, ROW)
    owner = owner_map[:, :, 0]
    solid_x = (owner // N_GY) * SX + slot_map // SY
    solid_y = (owner % N_GY) * SY + slot_map % SY
    heat = jnp.zeros((SXG, SYG, SZ), jnp.float32).at[solid_x, solid_y].add(flux_rows)
    sink = jnp.concatenate([flux, jnp.zeros((NX, NY, NZ - ROW), jnp.float32)], axis=2)
    fluid = temp_fluid
    for step in range(FSTEPS):
        fluid = fluid_update(jnp.pad(fluid, 1), velocity, sink)
    cond = table_lookup(material, conduct_table)
    modulus = table_lookup(material, modulus_table)
    solid = temp_solid
    for step in range(SSTEPS):
        solid = solid_update(jnp.pad(solid, 1), cond, heat)
    stress_force = gradient(jnp.pad(modulus * solid, 1))
    returned = solid[solid_x, solid_y]
    wall_next = returned.reshape(N_GX, N_GY, CX, CY, ROW).transpose(0, 2, 1, 3, 4).reshape(NX, NY, ROW)
    return fluid, wall_next, solid, stress_force
```

```python
import functools
import jax
import jax.numpy as jnp
from jax import lax
from jax.experimental import pallas as pl
from jax.experimental.pallas import tpu as pltpu
from jax.sharding import PartitionSpec as P

FSTEPS = 2
SSTEPS = 4
time_step = 0.1
diffusivity = 0.5
film_coef = 2.0
solid_step = 0.05
source_gain = 4.0
conduct_table = (0.4, 0.9, 1.5, 2.2)
modulus_table = (0.5, 1.0, 1.6, 2.4)
F32 = jnp.float32
BF16 = jnp.bfloat16
VMEM_LIMIT = 40 * 1024 * 1024
AXES = ("gx", "gy")


def params():
    return pltpu.CompilerParams(vmem_limit_bytes=VMEM_LIMIT)


def cost(flops, bytes_accessed):
    return pl.CostEstimate(flops=flops, bytes_accessed=bytes_accessed, transcendentals=0)


def halves(value):
    high = value.astype(BF16)
    low = (value - high.astype(F32)).astype(BF16)
    return high, low


def ones_where(test):
    return jnp.where(test, 1.0, 0.0).astype(BF16)


def neighbours(before, after, axis):
    size = lax.axis_size(axis)
    up = [(i, i + 1) for i in range(size - 1)]
    down = [(j, i) for i, j in up]
    return lax.ppermute(before, axis, up), lax.ppermute(after, axis, down)


def pack_kernel(ndev, cap, owner_ref, slot_ref, temp_ref, old_ref, mask_ref,
                out_ref, meta_ref, flux_ref, dest_ref, rhs_ref):
    rows = owner_ref.shape[1]
    row_len = temp_ref.shape[2]
    flux = mask_ref[...].astype(F32) * film_coef * (temp_ref[...] - old_ref[...])
    flux_ref[...] = flux
    high, low = halves(flux.reshape(rows, row_len))
    rhs_ref[:, :row_len] = high
    rhs_ref[:, row_len:] = low
    lane = 128
    tri = ones_where(
        lax.broadcasted_iota(jnp.int32, (lane, lane), 0)
        <= lax.broadcasted_iota(jnp.int32, (lane, lane), 1)
    )
    names = lax.broadcasted_iota(jnp.int32, (ndev, lane), 0)
    carry = jnp.zeros((ndev, 1), F32)
    for chunk in range(rows // lane):
        cols = slice(chunk * lane, (chunk + 1) * lane)
        own = owner_ref[:, cols]
        hit = jnp.where(names == own, 1.0, 0.0)
        ranks = jnp.dot(hit.astype(BF16), tri, preferred_element_type=F32) + carry
        carry = ranks[:, lane - 1:]
        place = jnp.sum(hit * ranks, axis=0, keepdims=True) - 1.0
        dest_ref[:, cols] = own * cap + place.astype(jnp.int32)
    dest = dest_ref[...]
    code = slot_ref[...] + 1
    pieces = jnp.concatenate(
        [(code // 32).astype(F32), (code % 32).astype(F32), jnp.zeros((6, rows), F32)], axis=0
    ).astype(BF16)
    block = 256

    def step(index, none):
        base = pl.multiple_of(index * block, block)
        pick = ones_where(
            lax.broadcasted_iota(jnp.int32, (block, rows), 0) + base == dest
        )
        both = jnp.dot(pick, rhs_ref[...], preferred_element_type=F32)
        out_ref[pl.ds(base, block), :] = both[:, :row_len] + both[:, row_len:]
        names2 = lax.dot_general(
            pieces, pick, (((1,), (1,)), ((), ())), preferred_element_type=F32
        )
        meta_ref[:, pl.ds(base, block)] = names2[0:1] * 32.0 + names2[1:2]
        return none

    lax.fori_loop(0, ndev * cap // block, step, 0)


def pack(owner, slot, temp, old, mask, ndev, cap):
    cx, cy, _ = temp.shape
    row_len = old.shape[2]
    rows = cx * cy
    total = ndev * cap
    whole = lambda shape: pl.BlockSpec(shape, lambda i: (0,) * len(shape))
    return pl.pallas_call(
        functools.partial(pack_kernel, ndev, cap),
        grid=(1,),
        in_specs=[
            whole((1, rows)),
            whole((1, rows)),
            whole((cx, cy, row_len)),
            whole((cx, cy, row_len)),
            whole((cx, cy, row_len)),
        ],
        out_specs=[
            whole((total, row_len)),
            whole((1, total)),
            whole((cx, cy, row_len)),
            whole((1, rows)),
        ],
        out_shape=[
            jax.ShapeDtypeStruct((total, row_len), F32),
            jax.ShapeDtypeStruct((1, total), F32),
            jax.ShapeDtypeStruct((cx, cy, row_len), F32),
            jax.ShapeDtypeStruct((1, rows), jnp.int32),
        ],
        scratch_shapes=[pltpu.VMEM((rows, 2 * row_len), BF16)],
        compiler_params=params(),
        cost_estimate=cost(4 * total * rows * row_len, 5 * rows * row_len * 4),
        name="pack",
    )(owner, slot, temp, old, mask)


def heat_kernel(rows_ref, code_ref, heat_ref):
    slots, row_len = heat_ref.shape
    total = rows_ref.shape[0]
    block = 512
    heat_ref[...] = jnp.zeros_like(heat_ref)

    def step(index, none):
        base = pl.multiple_of(index * block, block)
        high, low = halves(rows_ref[pl.ds(base, block), :])
        code = code_ref[:, pl.ds(base, block)].astype(jnp.int32) - 1
        pick = ones_where(lax.broadcasted_iota(jnp.int32, (slots, block), 0) == code)
        both = jnp.dot(
            pick, jnp.concatenate([high, low], axis=1), preferred_element_type=F32
        )
        heat_ref[...] += both[:, :row_len] + both[:, row_len:]
        return none

    lax.fori_loop(0, total // block, step, 0)


def heat_sum(incoming, code, slots):
    total, row_len = incoming.shape
    return pl.pallas_call(
        heat_kernel,
        in_specs=[pl.BlockSpec(memory_space=pltpu.VMEM)] * 2,
        out_specs=pl.BlockSpec(memory_space=pltpu.VMEM),
        out_shape=jax.ShapeDtypeStruct((slots, row_len), F32),
        compiler_params=params(),
        cost_estimate=cost(4 * total * slots * row_len, 4 * total * row_len),
        name="heat_sum",
    )(incoming, code)


def table(kind, values):
    out = jnp.zeros(kind.shape, F32)
    for index, value in enumerate(values):
        out = jnp.where(kind == index + 1.0, value, out)
    return out


OFF = 8


def solid_kernel(rim, state_ref, xlo_ref, xhi_ref, ylo_ref, yhi_ref,
                 heat_ref, hxlo_ref, hxhi_ref, hylo_ref, hyhi_ref, code_ref,
                 next_ref, sigma_ref, reply_ref, temp_ref, work_ref, cond_ref, src_ref, rhs_ref):
    _, sx, sy, sz = state_ref.shape
    wide = sx + 2 * rim
    thin = rim - 1
    temp_ref[...] = jnp.zeros_like(temp_ref)
    work_ref[...] = jnp.zeros_like(work_ref)
    cond_ref[...] = jnp.zeros_like(cond_ref)
    src_ref[...] = jnp.zeros_like(src_ref)
    for which, ref in ((0, temp_ref), (1, cond_ref)):
        ref[rim:rim + sx, OFF:OFF + sy, :] = state_ref[which]
        ref[0:rim, OFF:OFF + sy, :] = xlo_ref[which]
        ref[rim + sx:wide, OFF:OFF + sy, :] = xhi_ref[which]
        ref[:, OFF - rim:OFF, :] = ylo_ref[which]
        ref[:, OFF + sy:OFF + sy + rim, :] = yhi_ref[which]
    src_ref[rim:rim + sx, OFF:OFF + sy, :] = heat_ref[...]
    src_ref[1:rim, OFF:OFF + sy, :] = hxlo_ref[...]
    src_ref[rim + sx:wide - 1, OFF:OFF + sy, :] = hxhi_ref[...]
    src_ref[1:wide - 1, OFF - thin:OFF, :] = hylo_ref[...]
    src_ref[1:wide - 1, OFF + sy:OFF + sy + thin, :] = hyhi_ref[...]
    kind = cond_ref[...]
    sigma_ref[...] = table(kind[rim - 1:rim + sx + 1], modulus_table)
    cond_ref[...] = solid_step * table(kind, conduct_table)
    src_ref[...] = (solid_step * source_gain) * src_ref[...]
    height = temp_ref.shape[1]
    first = lax.broadcasted_iota(jnp.int32, (height, sz), 1) == 0
    last = lax.broadcasted_iota(jnp.int32, (height, sz), 1) == sz - 1
    pair = (temp_ref, work_ref)
    for turn in range(rim - 1):
        now, later = pair[turn % 2], pair[(turn + 1) % 2]

        def plane(x, none):
            centre = now[x]
            beside = now[x - 1] + now[x + 1]
            beside += pltpu.roll(centre, 1, 0) + pltpu.roll(centre, height - 1, 0)
            beside += jnp.where(first, 0.0, pltpu.roll(centre, 1, 1))
            beside += jnp.where(last, 0.0, pltpu.roll(centre, sz - 1, 1))
            later[x] = centre + (cond_ref[x] * (beside - 6.0 * centre) + src_ref[x])
            return none

        lax.fori_loop(1 + turn, wide - 1 - turn, plane, 0)
    final = pair[(rim - 1) % 2]
    solid = final[rim:rim + sx, OFF:OFF + sy, :]
    next_ref[...] = solid
    sigma_ref[...] = sigma_ref[...] * final[rim - 1:rim + sx + 1]
    high, low = halves(solid.reshape(sx * sy, sz))
    rhs_ref[:, :sz] = high
    rhs_ref[:, sz:] = low
    block = 256

    def answer(index, none):
        base = pl.multiple_of(index * block, block)
        code = code_ref[pl.ds(base, block), :].astype(jnp.int32) - 1
        pick = ones_where(lax.broadcasted_iota(jnp.int32, (block, sx * sy), 1) == code)
        both = jnp.dot(pick, rhs_ref[...], preferred_element_type=F32)
        reply_ref[pl.ds(base, block), :] = both[:, :sz] + both[:, sz:]
        return none

    lax.fori_loop(0, reply_ref.shape[0] // block, answer, 0)


def solid_steps(rim, state, state_rim, heat, heat_rim, code):
    _, sx, sy, sz = state.shape
    total = code.shape[0]
    wide, height = sx + 2 * rim, sy + 2 * OFF
    vmem = pl.BlockSpec(memory_space=pltpu.VMEM)
    return pl.pallas_call(
        functools.partial(solid_kernel, rim),
        in_specs=[vmem] * 11,
        out_specs=[vmem] * 3,
        out_shape=[
            jax.ShapeDtypeStruct((sx, sy, sz), F32),
            jax.ShapeDtypeStruct((sx + 2, height, sz), F32),
            jax.ShapeDtypeStruct((total, sz), F32),
        ],
        scratch_shapes=[pltpu.VMEM((wide, height, sz), F32)] * 4
        + [pltpu.VMEM((sx * sy, 2 * sz), BF16)],
        compiler_params=params(),
        cost_estimate=cost(4 * total * sx * sy * sz, 4 * total * sz),
        name="solid_steps",
    )(state, *state_rim, heat, *heat_rim, code)


def stress_kernel(sigma_ref, out_ref):
    _, sx, sy, sz = out_ref.shape
    height = sigma_ref.shape[1]
    first = lax.broadcasted_iota(jnp.int32, (height, sz), 1) == 0
    last = lax.broadcasted_iota(jnp.int32, (height, sz), 1) == sz - 1

    def plane(x, none):
        centre = sigma_ref[x + 1]
        out_ref[0, x] = 0.5 * (sigma_ref[x + 2] - sigma_ref[x])[OFF:OFF + sy]
        along = pltpu.roll(centre, height - 1, 0) - pltpu.roll(centre, 1, 0)
        out_ref[1, x] = 0.5 * along[OFF:OFF + sy]
        along = jnp.where(last, 0.0, pltpu.roll(centre, sz - 1, 1)) - jnp.where(
            first, 0.0, pltpu.roll(centre, 1, 1)
        )
        out_ref[2, x] = 0.5 * along[OFF:OFF + sy]
        return none

    lax.fori_loop(0, sx, plane, 0)


def stress(sigma, sx, sy):
    sz = sigma.shape[2]
    vmem = pl.BlockSpec(memory_space=pltpu.VMEM)
    return pl.pallas_call(
        stress_kernel,
        in_specs=[vmem],
        out_specs=vmem,
        out_shape=jax.ShapeDtypeStruct((3, sx, sy, sz), F32),
        compiler_params=params(),
        cost_estimate=cost(10 * sx * sy * sz, 16 * sx * sy * sz),
        name="stress",
    )(sigma)


def unpack_kernel(dest_ref, back_ref, out_ref):
    rows = out_ref.shape[0]

    def step(index, none):
        base = pl.multiple_of(index * 8, 8)
        lines = [back_ref[pl.ds(dest_ref[0, base + i], 1), :] for i in range(8)]
        out_ref[pl.ds(base, 8), :] = jnp.concatenate(lines, axis=0)
        return none

    lax.fori_loop(0, rows // 8, step, 0, unroll=2)


def unpack(dest, back):
    rows = dest.shape[1]
    vmem = pl.BlockSpec(memory_space=pltpu.VMEM)
    return pl.pallas_call(
        unpack_kernel,
        in_specs=[pl.BlockSpec(memory_space=pltpu.SMEM), vmem],
        out_specs=vmem,
        out_shape=jax.ShapeDtypeStruct((rows, back.shape[1]), F32),
        compiler_params=params(),
        cost_estimate=cost(rows * 128, 8 * rows * back.shape[1]),
        name="unpack",
    )(dest, back)


def fluid_kernel(before_ref, here_ref, after_ref, xlo_ref, xhi_ref, ylo_ref, yhi_ref,
                 speed_ref, flux_ref, out_ref, ext_ref):
    index, count = pl.program_id(0), pl.num_programs(0)
    _, cy, depth = here_ref.shape
    row_len = flux_ref.shape[2]
    ext_ref[OFF:OFF + cy, :] = here_ref[0]
    ext_ref[OFF - 1:OFF, :] = ylo_ref[0]
    ext_ref[OFF + cy:OFF + cy + 1, :] = yhi_ref[0]
    lanes = lax.broadcasted_iota(jnp.int32, (8, depth), 1)
    first, last = lanes == 0, lanes == depth - 1
    at_first, at_last = index == 0, index == count - 1
    rate = time_step * diffusivity

    def push(total, centre, lower, upper, speed):
        scaled = time_step * speed
        total = total + (rate + jnp.maximum(scaled, 0.0)) * (lower - centre)
        return total + (rate - jnp.minimum(scaled, 0.0)) * (upper - centre)

    for tile in range(cy // 16):
        speeds = [speed_ref[k, 0, tile * 16:tile * 16 + 16, :].astype(F32) for k in range(3)]
        for part in range(2):
            y = tile * 16 + part * 8
            u, v, w = [s[part * 8:part * 8 + 8] for s in speeds]
            centre = here_ref[0, y:y + 8, :]
            lower = jnp.where(at_first, xlo_ref[0, y:y + 8, :], before_ref[0, y:y + 8, :])
            upper = jnp.where(at_last, xhi_ref[0, y:y + 8, :], after_ref[0, y:y + 8, :])
            total = push(centre, centre, lower, upper, u)
            lower = ext_ref[OFF + y - 1:OFF + y + 7, :]
            upper = ext_ref[OFF + y + 1:OFF + y + 9, :]
            total = push(total, centre, lower, upper, v)
            lower = jnp.where(first, 0.0, pltpu.roll(centre, 1, 1))
            upper = jnp.where(last, 0.0, pltpu.roll(centre, depth - 1, 1))
            total = push(total, centre, lower, upper, w)
            out_ref[0, y:y + 8, row_len:] = total[:, row_len:]
            out_ref[0, y:y + 8, :row_len] = (
                total[:, :row_len] - time_step * flux_ref[0, y:y + 8, :]
            )


def fluid_step(temp, rims, velocity, flux):
    cx, cy, depth = temp.shape
    row_len = flux.shape[2]
    plane = (1, cy, depth)
    fixed = pl.BlockSpec(plane, lambda i: (0, 0, 0))
    line = pl.BlockSpec((1, 1, depth), lambda i: (i, 0, 0))
    return pl.pallas_call(
        fluid_kernel,
        grid=(cx,),
        in_specs=[
            pl.BlockSpec(plane, lambda i: (jnp.maximum(i - 1, 0), 0, 0)),
            pl.BlockSpec(plane, lambda i: (i, 0, 0)),
            pl.BlockSpec(plane, lambda i: (jnp.minimum(i + 1, cx - 1), 0, 0)),
            fixed,
            fixed,
            line,
            line,
            pl.BlockSpec((3, 1, cy, depth), lambda i: (0, i, 0, 0)),
            pl.BlockSpec((1, cy, row_len), lambda i: (i, 0, 0)),
        ],
        out_specs=pl.BlockSpec(plane, lambda i: (i, 0, 0)),
        out_shape=jax.ShapeDtypeStruct(temp.shape, F32),
        scratch_shapes=[pltpu.VMEM((cy + 2 * OFF, depth), F32)],
        compiler_params=params(),
        cost_estimate=cost(40 * cx * cy * depth, 22 * cx * cy * depth),
        name="fluid_step",
    )(temp, temp, temp, *rims, velocity, flux)


def fluid_rims(temp):
    xlo, xhi = neighbours(temp[-1:], temp[:1], "gx")
    ylo, yhi = neighbours(temp[:, -1:], temp[:, :1], "gy")
    return xlo, xhi, ylo, yhi


def body(temp_fluid, velocity, wall_old, wall_mask, owner_map, slot_map, temp_solid, material):
    cx, cy, depth = temp_fluid.shape
    row_len = wall_old.shape[2]
    sx, sy, sz = temp_solid.shape
    ndev = lax.axis_size("gx") * lax.axis_size("gy")
    rows = cx * cy
    cap = (3 * rows + ndev - 1) // ndev
    cap = -(-cap // 8) * 8
    total = ndev * cap
    rim = SSTEPS + 1

    outgoing, meta, flux, dest = pack(
        owner_map.reshape(1, rows), slot_map, temp_fluid, wall_old, wall_mask, ndev, cap
    )
    incoming = lax.all_to_all(
        outgoing.reshape(ndev, cap, row_len), AXES, split_axis=0, concat_axis=0, tiled=True
    )
    code = lax.all_to_all(meta.reshape(ndev, cap), AXES, split_axis=0, concat_axis=0, tiled=True)
    code_row = code.reshape(1, total)
    code_col = code.reshape(total, 1)

    state = jnp.stack([temp_solid, material.astype(F32) + 1.0])
    xlo, xhi = neighbours(state[:, sx - rim:], state[:, :rim], "gx")
    tall = lambda cut: jnp.concatenate([xlo[:, :, cut], state[:, :, cut], xhi[:, :, cut]], axis=1)
    ylo, yhi = neighbours(tall(slice(sy - rim, sy)), tall(slice(0, rim)), "gy")

    fluid = fluid_step(temp_fluid, fluid_rims(temp_fluid), velocity, flux)

    heat = heat_sum(incoming.reshape(total, row_len), code_row, sx * sy).reshape(sx, sy, sz)
    thin = rim - 1
    hxlo, hxhi = neighbours(heat[sx - thin:], heat[:thin], "gx")
    tall2 = lambda cut: jnp.concatenate([hxlo[:, cut], heat[:, cut], hxhi[:, cut]], axis=0)
    hylo, hyhi = neighbours(tall2(slice(sy - thin, sy)), tall2(slice(0, thin)), "gy")
    solid, sigma, replies = solid_steps(
        rim, state, (xlo, xhi, ylo, yhi), heat, (hxlo, hxhi, hylo, hyhi), code_col
    )
    returned = lax.all_to_all(
        replies.reshape(ndev, cap, sz), AXES, split_axis=0, concat_axis=0, tiled=True
    )
    fluid = fluid_step(fluid, fluid_rims(fluid), velocity, flux)
    force = stress(sigma, sx, sy)
    wall_next = unpack(dest, returned.reshape(total, sz)).reshape(cx, cy, row_len)
    return fluid, wall_next, solid, force


def solution(mesh):
    placed = (
        P("gx", "gy", None),
        P(None, "gx", "gy", None),
        P("gx", "gy", None),
        P("gx", "gy", None),
        P(("gx", "gy"), None, None),
        P(("gx", "gy"), None),
        P("gx", "gy", None),
        P("gx", "gy", None),
    )
    return jax.shard_map(
        body,
        mesh=mesh,
        in_specs=placed,
        out_specs=(
            P("gx", "gy", None),
            P("gx", "gy", None),
            P("gx", "gy", None),
            P(None, "gx", "gy", None),
        ),
        check_vma=False,
    )
```

```python
import functools
import jax
import jax.numpy as jnp
from jax import lax
from jax.experimental import pallas as pl
from jax.experimental.pallas import tpu as pltpu
from jax.sharding import PartitionSpec as P

FSTEPS = 2
SSTEPS = 4
time_step = 0.1
diffusivity = 0.5
film_coef = 2.0
solid_step = 0.05
source_gain = 4.0
conduct_table = (0.4, 0.9, 1.5, 2.2)
modulus_table = (0.5, 1.0, 1.6, 2.4)
F32 = jnp.float32
BF16 = jnp.bfloat16
VMEM_LIMIT = 60 * 1024 * 1024
AXES = ("gx", "gy")


def params():
    return pltpu.CompilerParams(vmem_limit_bytes=VMEM_LIMIT)


def cost(flops, bytes_accessed):
    return pl.CostEstimate(flops=flops, bytes_accessed=bytes_accessed, transcendentals=0)


def halves(value):
    high = value.astype(BF16)
    low = (value - high.astype(F32)).astype(BF16)
    return high, low


def ones_where(test):
    return jnp.where(test, 1.0, 0.0).astype(BF16)


def neighbours(before, after, axis):
    size = lax.axis_size(axis)
    up = [(i, i + 1) for i in range(size - 1)]
    down = [(j, i) for i, j in up]
    return lax.ppermute(before, axis, up), lax.ppermute(after, axis, down)


def whole(shape):
    return pl.BlockSpec(shape, lambda i: (0,) * len(shape))


anywhere = pl.BlockSpec(memory_space=pl.ANY)


def pack_kernel(cap, owner_ref, slot_ref, temp_ref, old_ref, mask_ref,
                out_ref, flux_ref, dest_ref, rhs_ref, where_ref):
    rows = owner_ref.shape[1]
    ndev, tall, row_len = out_ref.shape
    flux = mask_ref[...].astype(F32) * film_coef * (temp_ref[...] - old_ref[...])
    flux_ref[...] = flux
    high, low = halves(flux.reshape(rows, row_len))
    rhs_ref[:, :row_len] = high
    rhs_ref[:, row_len:] = low
    lane = 128
    tri = ones_where(
        lax.broadcasted_iota(jnp.int32, (lane, lane), 0)
        <= lax.broadcasted_iota(jnp.int32, (lane, lane), 1)
    )
    names = lax.broadcasted_iota(jnp.int32, (ndev, lane), 0)
    steps = lax.broadcasted_iota(jnp.int32, (lane, lane), 0)
    carry = jnp.zeros((ndev, 1), F32)
    codes = jnp.zeros((2 * ndev, lane), F32)
    for chunk in range(rows // lane):
        cols = slice(chunk * lane, (chunk + 1) * lane)
        own = owner_ref[:, cols]
        hit = jnp.where(names == own, 1.0, 0.0)
        ranks = jnp.dot(hit.astype(BF16), tri, preferred_element_type=F32) + carry
        carry = ranks[:, lane - 1:]
        place = jnp.sum(hit * ranks, axis=0, keepdims=True).astype(jnp.int32) - 1
        dest_ref[:, cols] = own * cap + place
        where_ref[:, cols] = own * tall + place
        code = slot_ref[:, cols] + 1
        pieces = jnp.concatenate(
            [hit * (code // 32).astype(F32), hit * (code % 32).astype(F32)], axis=0
        ).astype(BF16)
        codes = codes + lax.dot_general(
            pieces, ones_where(steps == place), (((1,), (1,)), ((), ())),
            preferred_element_type=F32,
        )
    where = where_ref[...]
    group = max(1, 256 // tall)
    block = group * tall

    def step(index, none):
        base = index * block
        pick = ones_where(
            lax.broadcasted_iota(jnp.int32, (block, rows), 0) + base == where
        )
        both = jnp.dot(pick, rhs_ref[...], preferred_element_type=F32)
        lines = both[:, :row_len] + both[:, row_len:]
        out_ref[pl.ds(index * group, group)] = lines.reshape(group, tall, row_len)
        return none

    lax.fori_loop(0, ndev // group, step, 0)
    out_ref[:, cap, :] = codes[:ndev] * 32.0 + codes[ndev:]


def pack(owner, slot, temp, old, mask, ndev, cap):
    cx, cy, _ = temp.shape
    row_len = old.shape[2]
    rows = cx * cy
    tall = cap + 8
    return pl.pallas_call(
        functools.partial(pack_kernel, cap),
        grid=(1,),
        in_specs=[
            whole((1, rows)),
            whole((1, rows)),
            whole((cx, cy, row_len)),
            whole((cx, cy, row_len)),
            whole((cx, cy, row_len)),
        ],
        out_specs=[
            whole((ndev, tall, row_len)),
            whole((cx, cy, row_len)),
            whole((1, rows)),
        ],
        out_shape=[
            jax.ShapeDtypeStruct((ndev, tall, row_len), F32),
            jax.ShapeDtypeStruct((cx, cy, row_len), F32),
            jax.ShapeDtypeStruct((1, rows), jnp.int32),
        ],
        scratch_shapes=[
            pltpu.VMEM((rows, 2 * row_len), BF16),
            pltpu.VMEM((1, rows), jnp.int32),
        ],
        compiler_params=params(),
        cost_estimate=cost(4 * ndev * tall * rows * row_len, 5 * rows * row_len * 4),
        name="pack",
    )(owner, slot, temp, old, mask)


def heat_kernel(cap, rows_ref, *refs):
    heat_ref, code_ref = refs[-2:]
    ndev, tall, row_len = rows_ref.shape
    slots = heat_ref.shape[0]
    codes = rows_ref[:, cap, :].astype(jnp.int32) - 1
    turned = jnp.transpose(codes)
    for source in range(ndev):
        code_ref[source * cap:(source + 1) * cap, :] = jnp.broadcast_to(
            turned[:cap, source:source + 1], (cap, row_len)
        )
    group = max(1, 256 // tall)
    names = lax.broadcasted_iota(jnp.int32, (slots, tall), 0)
    total = jnp.zeros((slots, 2 * row_len), F32)
    for index in range(0, ndev, group):
        lines = rows_ref[index:index + group].reshape(group * tall, row_len)
        high, low = halves(lines)
        pick = jnp.concatenate(
            [
                jnp.where(names == codes[index + i:index + i + 1, :tall], 1.0, 0.0)
                for i in range(group)
            ],
            axis=1,
        ).astype(BF16)
        total = total + jnp.dot(
            pick, jnp.concatenate([high, low], axis=1), preferred_element_type=F32
        )
    heat_ref[...] = total[:, :row_len] + total[:, row_len:]


def heat_sum(incoming, cap, slots, after):
    ndev, tall, row_len = incoming.shape
    return pl.pallas_call(
        functools.partial(heat_kernel, cap),
        grid=(1,),
        in_specs=[whole(incoming.shape)] + [anywhere] * len(after),
        out_specs=[whole((slots, row_len)), whole((ndev * cap, row_len))],
        out_shape=[
            jax.ShapeDtypeStruct((slots, row_len), F32),
            jax.ShapeDtypeStruct((ndev * cap, row_len), jnp.int32),
        ],
        compiler_params=params(),
        cost_estimate=cost(4 * ndev * tall * slots * row_len, 4 * ndev * tall * row_len),
        name="heat_sum",
    )(incoming, *after)


def table(kind, values):
    out = jnp.zeros(kind.shape, F32)
    for index, value in enumerate(values):
        out = jnp.where(kind == index + 1.0, value, out)
    return out


OFF = 8


def solid_kernel(rim, state_ref, xlo_ref, xhi_ref, ylo_ref, yhi_ref,
                 heat_ref, hxlo_ref, hxhi_ref, hylo_ref, hyhi_ref, code_ref,
                 next_ref, sigma_ref, reply_ref, temp_ref, work_ref, cond_ref, src_ref, rhs_ref):
    _, sx, sy, sz = state_ref.shape
    wide = sx + 2 * rim
    thin = rim - 1
    for which, ref in ((0, temp_ref), (1, cond_ref)):
        ref[rim:rim + sx, OFF:OFF + sy, :] = state_ref[which]
        ref[0:rim, OFF:OFF + sy, :] = xlo_ref[which]
        ref[rim + sx:wide, OFF:OFF + sy, :] = xhi_ref[which]
        ref[:, OFF - rim:OFF, :] = ylo_ref[which]
        ref[:, OFF + sy:OFF + sy + rim, :] = yhi_ref[which]
    src_ref[rim:rim + sx, OFF:OFF + sy, :] = heat_ref[...]
    src_ref[1:rim, OFF:OFF + sy, :] = hxlo_ref[...]
    src_ref[rim + sx:wide - 1, OFF:OFF + sy, :] = hxhi_ref[...]
    src_ref[1:wide - 1, OFF - thin:OFF, :] = hylo_ref[...]
    src_ref[1:wide - 1, OFF + sy:OFF + sy + thin, :] = hyhi_ref[...]
    kind = cond_ref[...]
    sigma_ref[...] = table(kind[rim - 1:rim + sx + 1], modulus_table)
    cond_ref[...] = solid_step * table(kind, conduct_table)
    src_ref[...] = (solid_step * source_gain) * src_ref[...]
    height = temp_ref.shape[1]
    first = lax.broadcasted_iota(jnp.int32, (height, sz), 1) == 0
    last = lax.broadcasted_iota(jnp.int32, (height, sz), 1) == sz - 1
    pair = (temp_ref, work_ref)
    for turn in range(rim - 1):
        now, later = pair[turn % 2], pair[(turn + 1) % 2]
        for x in range(1 + turn, wide - 1 - turn):
            centre = now[x]
            beside = now[x - 1] + now[x + 1]
            beside += pltpu.roll(centre, 1, 0) + pltpu.roll(centre, height - 1, 0)
            beside += jnp.where(first, 0.0, pltpu.roll(centre, 1, 1))
            beside += jnp.where(last, 0.0, pltpu.roll(centre, sz - 1, 1))
            later[x] = centre + (cond_ref[x] * (beside - 6.0 * centre) + src_ref[x])
    final = pair[(rim - 1) % 2]
    solid = final[rim:rim + sx, OFF:OFF + sy, :]
    next_ref[...] = solid
    sigma_ref[...] = sigma_ref[...] * final[rim - 1:rim + sx + 1]
    high, low = halves(solid.reshape(sx * sy, sz))
    rhs_ref[:, :sz] = high
    rhs_ref[:, sz:] = low
    block = 512
    slots = sx * sy
    names = lax.broadcasted_iota(jnp.int32, (block, sz), 1)

    def answer(index, none):
        base = pl.multiple_of(index * block, block)
        code = code_ref[pl.ds(base, block), :]
        pick = jnp.concatenate(
            [jnp.where(names + at == code, 1.0, 0.0) for at in range(0, slots, sz)], axis=1
        ).astype(BF16)
        both = jnp.dot(pick, rhs_ref[...], preferred_element_type=F32)
        reply_ref[pl.ds(base, block), :] = both[:, :sz] + both[:, sz:]
        return none

    lax.fori_loop(0, reply_ref.shape[0] // block, answer, 0)


def solid_steps(rim, state, state_rim, heat, heat_rim, code):
    _, sx, sy, sz = state.shape
    total = code.shape[0]
    wide, height = sx + 2 * rim, sy + 2 * OFF
    args = (state, *state_rim, heat, *heat_rim, code)
    return pl.pallas_call(
        functools.partial(solid_kernel, rim),
        grid=(1,),
        in_specs=[whole(x.shape) for x in args],
        out_specs=[whole((sx, sy, sz)), whole((sx + 2, height, sz)), whole((total, sz))],
        out_shape=[
            jax.ShapeDtypeStruct((sx, sy, sz), F32),
            jax.ShapeDtypeStruct((sx + 2, height, sz), F32),
            jax.ShapeDtypeStruct((total, sz), F32),
        ],
        scratch_shapes=[pltpu.VMEM((wide, height, sz), F32)] * 4
        + [pltpu.VMEM((sx * sy, 2 * sz), BF16)],
        compiler_params=params(),
        cost_estimate=cost(4 * total * sx * sy * sz, 4 * total * sz),
        name="solid_steps",
    )(*args)


def stress_kernel(sigma_ref, out_ref):
    _, sx, sy, sz = out_ref.shape
    height = sigma_ref.shape[1]
    first = lax.broadcasted_iota(jnp.int32, (height, sz), 1) == 0
    last = lax.broadcasted_iota(jnp.int32, (height, sz), 1) == sz - 1

    def plane(x, none):
        centre = sigma_ref[x + 1]
        out_ref[0, x] = 0.5 * (sigma_ref[x + 2] - sigma_ref[x])[OFF:OFF + sy]
        along = pltpu.roll(centre, height - 1, 0) - pltpu.roll(centre, 1, 0)
        out_ref[1, x] = 0.5 * along[OFF:OFF + sy]
        along = jnp.where(last, 0.0, pltpu.roll(centre, sz - 1, 1)) - jnp.where(
            first, 0.0, pltpu.roll(centre, 1, 1)
        )
        out_ref[2, x] = 0.5 * along[OFF:OFF + sy]
        return none

    lax.fori_loop(0, sx, plane, 0)


def stress(sigma, sx, sy):
    sz = sigma.shape[2]
    return pl.pallas_call(
        stress_kernel,
        grid=(1,),
        in_specs=[whole(sigma.shape)],
        out_specs=whole((3, sx, sy, sz)),
        out_shape=jax.ShapeDtypeStruct((3, sx, sy, sz), F32),
        compiler_params=params(),
        cost_estimate=cost(10 * sx * sy * sz, 16 * sx * sy * sz),
        name="stress",
    )(sigma)


def unpack_kernel(dest_ref, back_ref, *refs):
    out_ref = refs[-1]
    rows = out_ref.shape[0]

    def step(index, none):
        base = pl.multiple_of(index * 8, 8)
        lines = [back_ref[pl.ds(dest_ref[0, base + i], 1), :] for i in range(8)]
        out_ref[pl.ds(base, 8), :] = jnp.concatenate(lines, axis=0)
        return none

    lax.fori_loop(0, rows // 8, step, 0, unroll=4)


def unpack(dest, back, after):
    rows = dest.shape[1]
    row_len = back.shape[1]
    return pl.pallas_call(
        unpack_kernel,
        grid=(1,),
        in_specs=[pl.BlockSpec(memory_space=pltpu.SMEM), whole(back.shape)]
        + [anywhere] * len(after),
        out_specs=whole((rows, row_len)),
        out_shape=jax.ShapeDtypeStruct((rows, row_len), F32),
        compiler_params=params(),
        cost_estimate=cost(rows * 128, 8 * rows * row_len),
        name="unpack",
    )(dest, back, *after)


def fluid_kernel(before_ref, here_ref, after_ref, xlo_ref, xhi_ref, ylo_ref, yhi_ref,
                 speed_ref, flux_ref, out_ref, ext_ref):
    index, count = pl.program_id(0), pl.num_programs(0)
    _, cy, depth = here_ref.shape
    row_len = flux_ref.shape[2]
    ext_ref[OFF:OFF + cy, :] = here_ref[0]
    ext_ref[OFF - 1:OFF, :] = ylo_ref[0]
    ext_ref[OFF + cy:OFF + cy + 1, :] = yhi_ref[0]
    lanes = lax.broadcasted_iota(jnp.int32, (8, depth), 1)
    first, last = lanes == 0, lanes == depth - 1
    at_first, at_last = index == 0, index == count - 1
    rate = time_step * diffusivity

    def push(total, centre, lower, upper, speed):
        scaled = time_step * speed
        total = total + (rate + jnp.maximum(scaled, 0.0)) * (lower - centre)
        return total + (rate - jnp.minimum(scaled, 0.0)) * (upper - centre)

    for tile in range(cy // 16):
        speeds = [speed_ref[k, 0, tile * 16:tile * 16 + 16, :].astype(F32) for k in range(3)]
        for part in range(2):
            y = tile * 16 + part * 8
            u, v, w = [s[part * 8:part * 8 + 8] for s in speeds]
            centre = here_ref[0, y:y + 8, :]
            lower = jnp.where(at_first, xlo_ref[0, y:y + 8, :], before_ref[0, y:y + 8, :])
            upper = jnp.where(at_last, xhi_ref[0, y:y + 8, :], after_ref[0, y:y + 8, :])
            total = push(centre, centre, lower, upper, u)
            lower = ext_ref[OFF + y - 1:OFF + y + 7, :]
            upper = ext_ref[OFF + y + 1:OFF + y + 9, :]
            total = push(total, centre, lower, upper, v)
            lower = jnp.where(first, 0.0, pltpu.roll(centre, 1, 1))
            upper = jnp.where(last, 0.0, pltpu.roll(centre, depth - 1, 1))
            total = push(total, centre, lower, upper, w)
            out_ref[0, y:y + 8, row_len:] = total[:, row_len:]
            out_ref[0, y:y + 8, :row_len] = (
                total[:, :row_len] - time_step * flux_ref[0, y:y + 8, :]
            )


def fluid_step(temp, rims, velocity, flux):
    cx, cy, depth = temp.shape
    row_len = flux.shape[2]
    plane = (1, cy, depth)
    fixed = pl.BlockSpec(plane, lambda i: (0, 0, 0))
    line = pl.BlockSpec((1, 1, depth), lambda i: (i, 0, 0))
    return pl.pallas_call(
        fluid_kernel,
        grid=(cx,),
        in_specs=[
            pl.BlockSpec(plane, lambda i: (jnp.maximum(i - 1, 0), 0, 0)),
            pl.BlockSpec(plane, lambda i: (i, 0, 0)),
            pl.BlockSpec(plane, lambda i: (jnp.minimum(i + 1, cx - 1), 0, 0)),
            fixed,
            fixed,
            line,
            line,
            pl.BlockSpec((3, 1, cy, depth), lambda i: (0, i, 0, 0)),
            pl.BlockSpec((1, cy, row_len), lambda i: (i, 0, 0)),
        ],
        out_specs=pl.BlockSpec(plane, lambda i: (i, 0, 0)),
        out_shape=jax.ShapeDtypeStruct(temp.shape, F32),
        scratch_shapes=[pltpu.VMEM((cy + 2 * OFF, depth), F32)],
        compiler_params=params(),
        cost_estimate=cost(40 * cx * cy * depth, 22 * cx * cy * depth),
        name="fluid_step",
    )(temp, temp, temp, *rims, velocity, flux)


def fluid_rims(temp):
    xlo, xhi = neighbours(temp[-1:], temp[:1], "gx")
    ylo, yhi = neighbours(temp[:, -1:], temp[:, :1], "gy")
    return xlo, xhi, ylo, yhi


def body(temp_fluid, velocity, wall_old, wall_mask, owner_map, slot_map, temp_solid, material):
    cx, cy, depth = temp_fluid.shape
    row_len = wall_old.shape[2]
    sx, sy, sz = temp_solid.shape
    ndev = lax.axis_size("gx") * lax.axis_size("gy")
    rows = cx * cy
    cap = (3 * rows + ndev - 1) // ndev
    cap = -(-cap // 8) * 8
    total = ndev * cap
    rim = SSTEPS + 1

    outgoing, flux, dest = pack(
        owner_map.reshape(1, rows), slot_map, temp_fluid, wall_old, wall_mask, ndev, cap
    )
    incoming = lax.all_to_all(outgoing, AXES, split_axis=0, concat_axis=0, tiled=True)

    state = jnp.stack([temp_solid, material.astype(F32) + 1.0])
    xlo, xhi = neighbours(state[:, sx - rim:], state[:, :rim], "gx")
    tall = lambda cut: jnp.concatenate([xlo[:, :, cut], state[:, :, cut], xhi[:, :, cut]], axis=1)
    ylo, yhi = neighbours(tall(slice(sy - rim, sy)), tall(slice(0, rim)), "gy")

    fluid = fluid_step(temp_fluid, fluid_rims(temp_fluid), velocity, flux)

    heat, code = heat_sum(incoming, cap, sx * sy, (fluid, xlo, xhi, ylo, yhi))
    heat = heat.reshape(sx, sy, sz)
    thin = rim - 1
    hxlo, hxhi = neighbours(heat[sx - thin:], heat[:thin], "gx")
    tall2 = lambda cut: jnp.concatenate([hxlo[:, cut], heat[:, cut], hxhi[:, cut]], axis=0)
    hylo, hyhi = neighbours(tall2(slice(sy - thin, sy)), tall2(slice(0, thin)), "gy")
    solid, sigma, replies = solid_steps(
        rim, state, (xlo, xhi, ylo, yhi), heat, (hxlo, hxhi, hylo, hyhi), code
    )
    returned = lax.all_to_all(
        replies.reshape(ndev, cap, sz), AXES, split_axis=0, concat_axis=0, tiled=True
    )
    fluid = fluid_step(fluid, fluid_rims(fluid), velocity, flux)
    force = stress(sigma, sx, sy)
    wall_next = unpack(dest, returned.reshape(total, sz), (fluid, force))
    return fluid, wall_next.reshape(cx, cy, row_len), solid, force


def solution(mesh):
    placed = (
        P("gx", "gy", None),
        P(None, "gx", "gy", None),
        P("gx", "gy", None),
        P("gx", "gy", None),
        P(("gx", "gy"), None, None),
        P(("gx", "gy"), None),
        P("gx", "gy", None),
        P("gx", "gy", None),
    )
    return jax.shard_map(
        body,
        mesh=mesh,
        in_specs=placed,
        out_specs=(
            P("gx", "gy", None),
            P("gx", "gy", None),
            P("gx", "gy", None),
            P(None, "gx", "gy", None),
        ),
        check_vma=False,
    )
```

```python
import functools
import jax
import jax.numpy as jnp
from jax import lax
from jax.experimental import pallas as pl
from jax.experimental.pallas import tpu as pltpu
from jax.sharding import PartitionSpec as P

FSTEPS = 2
SSTEPS = 4
time_step = 0.1
diffusivity = 0.5
film_coef = 2.0
solid_step = 0.05
source_gain = 4.0
conduct_table = (0.4, 0.9, 1.5, 2.2)
modulus_table = (0.5, 1.0, 1.6, 2.4)
F32 = jnp.float32
BF16 = jnp.bfloat16
AXES = ("gx", "gy")
LANE = 128
PART = 16
OFF = 8


def params(mib):
    return pltpu.CompilerParams(vmem_limit_bytes=mib * 1024 * 1024)


def cost(flops, bytes_accessed):
    return pl.CostEstimate(flops=flops, bytes_accessed=bytes_accessed, transcendentals=0)


def halves(value):
    high = value.astype(BF16)
    low = (value - high.astype(F32)).astype(BF16)
    return high, low


def ones_where(test):
    return jnp.where(test, 1.0, 0.0).astype(BF16)


def neighbours(before, after, axis):
    size = lax.axis_size(axis)
    up = [(i, i + 1) for i in range(size - 1)]
    down = [(j, i) for i, j in up]
    return lax.ppermute(before, axis, up), lax.ppermute(after, axis, down)


def whole(shape):
    return pl.BlockSpec(shape, lambda i: (0,) * len(shape))


anywhere = pl.BlockSpec(memory_space=pl.ANY)


def pack_kernel(cap, owner_ref, slot_ref, temp_ref, old_ref, mask_ref,
                out_ref, flux_ref, dest_ref, rhs_ref, where_ref):
    rows = owner_ref.shape[1]
    ndev, tall, row_len = out_ref.shape
    flux = mask_ref[...].astype(F32) * film_coef * (temp_ref[...] - old_ref[...])
    flux_ref[...] = flux
    high, low = halves(flux.reshape(rows, row_len))
    rhs_ref[:, :row_len] = high
    rhs_ref[:, row_len:] = low
    lane = 128
    tri = ones_where(
        lax.broadcasted_iota(jnp.int32, (lane, lane), 0)
        <= lax.broadcasted_iota(jnp.int32, (lane, lane), 1)
    )
    names = lax.broadcasted_iota(jnp.int32, (ndev, lane), 0)
    steps = lax.broadcasted_iota(jnp.int32, (lane, lane), 0)
    carry = jnp.zeros((ndev, 1), F32)
    codes = jnp.zeros((2 * ndev, lane), F32)
    for chunk in range(rows // lane):
        cols = slice(chunk * lane, (chunk + 1) * lane)
        own = owner_ref[:, cols]
        hit = jnp.where(names == own, 1.0, 0.0)
        ranks = jnp.dot(hit.astype(BF16), tri, preferred_element_type=F32) + carry
        carry = ranks[:, lane - 1:]
        place = jnp.sum(hit * ranks, axis=0, keepdims=True).astype(jnp.int32) - 1
        dest_ref[:, cols] = own * cap + place
        where_ref[:, cols] = own * tall + place
        code = slot_ref[:, cols] + 1
        pieces = jnp.concatenate(
            [hit * (code // 32).astype(F32), hit * (code % 32).astype(F32)], axis=0
        ).astype(BF16)
        codes = codes + lax.dot_general(
            pieces, ones_where(steps == place), (((1,), (1,)), ((), ())),
            preferred_element_type=F32,
        )
    where = where_ref[...]
    group = ndev // 4
    block = group * tall

    def step(index, none):
        base = index * block
        pick = ones_where(
            lax.broadcasted_iota(jnp.int32, (block, rows), 0) + base == where
        )
        both = jnp.dot(pick, rhs_ref[...], preferred_element_type=F32)
        lines = both[:, :row_len] + both[:, row_len:]
        out_ref[pl.ds(index * group, group)] = lines.reshape(group, tall, row_len)
        return none

    lax.fori_loop(0, ndev // group, step, 0)
    out_ref[:, cap, :] = codes[:ndev] * 32.0 + codes[ndev:]


def pack(owner, slot, temp, old, mask, ndev, cap):
    cx, cy, _ = temp.shape
    row_len = old.shape[2]
    rows = cx * cy
    tall = cap + 8
    return pl.pallas_call(
        functools.partial(pack_kernel, cap),
        grid=(1,),
        in_specs=[
            whole((1, rows)),
            whole((1, rows)),
            whole((cx, cy, row_len)),
            whole((cx, cy, row_len)),
            whole((cx, cy, row_len)),
        ],
        out_specs=[
            whole((ndev, tall, row_len)),
            whole((cx, cy, row_len)),
            whole((1, rows)),
        ],
        out_shape=[
            jax.ShapeDtypeStruct((ndev, tall, row_len), F32),
            jax.ShapeDtypeStruct((cx, cy, row_len), F32),
            jax.ShapeDtypeStruct((1, rows), jnp.int32),
        ],
        scratch_shapes=[
            pltpu.VMEM((rows, 2 * row_len), BF16),
            pltpu.VMEM((1, rows), jnp.int32),
        ],
        compiler_params=params(60),
        cost_estimate=cost(4 * ndev * tall * rows * row_len, 5 * rows * row_len * 4),
        name="pack",
    )(owner, slot, temp, old, mask)


def heat_kernel(cap, thin, rows_ref, *refs):
    heat_ref, first_ref, last_ref, code_ref = refs[-4:]
    ndev, tall, row_len = rows_ref.shape
    sx, sy, _ = heat_ref.shape
    slots = sx * sy
    codes = rows_ref[:, cap, :].astype(jnp.int32) - 1
    code_ref[...] = codes
    group = ndev // 4
    names = lax.broadcasted_iota(jnp.int32, (slots, tall), 0)
    total = jnp.zeros((slots, 2 * row_len), F32)
    for index in range(0, ndev, group):
        lines = rows_ref[index:index + group].reshape(group * tall, row_len)
        high, low = halves(lines)
        pick = jnp.concatenate(
            [
                jnp.where(names == codes[index + i:index + i + 1, :tall], 1.0, 0.0)
                for i in range(group)
            ],
            axis=1,
        ).astype(BF16)
        total = total + jnp.dot(
            pick, jnp.concatenate([high, low], axis=1), preferred_element_type=F32
        )
    heat = (total[:, :row_len] + total[:, row_len:]).reshape(sx, sy, row_len)
    heat_ref[...] = heat
    first_ref[...] = heat[:thin]
    last_ref[...] = heat[sx - thin:]


def heat_sum(incoming, cap, block, thin, after):
    ndev, tall, row_len = incoming.shape
    sx, sy, _ = block
    edge = (thin, sy, row_len)
    return pl.pallas_call(
        functools.partial(heat_kernel, cap, thin),
        grid=(1,),
        in_specs=[whole(incoming.shape)] + [anywhere] * len(after),
        out_specs=[whole(block), whole(edge), whole(edge), whole((ndev, row_len))],
        out_shape=[
            jax.ShapeDtypeStruct(block, F32),
            jax.ShapeDtypeStruct(edge, F32),
            jax.ShapeDtypeStruct(edge, F32),
            jax.ShapeDtypeStruct((ndev, row_len), jnp.int32),
        ],
        compiler_params=params(20),
        cost_estimate=cost(4 * ndev * tall * sx * sy * row_len, 4 * ndev * tall * row_len),
        name="heat_sum",
    )(incoming, *after)


def put_rim(ref, base, slabs):
    across = ref.shape[1] // LANE
    for n, slab in enumerate(slabs):
        row = base + n // across * PART
        ref[row:row + PART, n % across * LANE:(n % across + 1) * LANE] = slab


def get_rim(ref, n):
    across = ref.shape[1] // LANE
    row = n // across * PART
    return ref[row:row + PART, n % across * LANE:(n % across + 1) * LANE]


def rim_rows(count, depth):
    across = depth // LANE
    return -(-count // across) * PART


def x_faces_kernel(rim, bottom_ref, top_ref, temp_ref, kind_ref, low_ref, high_ref):
    _, cy, _ = bottom_ref.shape
    sx, sy, _ = temp_ref.shape
    low_ref[:cy, :] = bottom_ref[0]
    high_ref[:cy, :] = top_ref[0]
    for ref, start in ((low_ref, 0), (high_ref, sx - rim)):
        slabs = [
            get(start + k, slice(h, h + PART))
            for get in (
                lambda x, cut: temp_ref[x, cut, :],
                lambda x, cut: kind_ref[x, cut, :].astype(F32) + 1.0,
            )
            for k in range(rim)
            for h in range(0, sy, PART)
        ]
        put_rim(ref, cy, slabs)


def x_faces(rim, fluid, temp, kind):
    cx, cy, depth = fluid.shape
    sx, sy, sz = temp.shape
    height = cy + rim_rows(2 * rim * (sy // PART), depth)
    plane = (1, cy, depth)
    return pl.pallas_call(
        functools.partial(x_faces_kernel, rim),
        grid=(1,),
        in_specs=[
            pl.BlockSpec(plane, lambda i: (0, 0, 0)),
            pl.BlockSpec(plane, lambda i: (cx - 1, 0, 0)),
            whole(temp.shape),
            whole(temp.shape),
        ],
        out_specs=[whole((height, depth))] * 2,
        out_shape=[jax.ShapeDtypeStruct((height, depth), F32)] * 2,
        compiler_params=params(12),
        cost_estimate=cost(1000, 4 * 4 * height * depth),
        name="x_faces",
    )(fluid, fluid, temp, kind)


def fill_x(rim, ref, which, own, lo_ref, hi_ref):
    sx, sy, _ = own.shape
    pieces = sy // PART
    ref[rim:rim + sx, OFF:OFF + sy, :] = own
    for k in range(rim):
        for h in range(pieces):
            n = (which * rim + k) * pieces + h
            cut = slice(OFF + h * PART, OFF + (h + 1) * PART)
            ref[k, cut, :] = get_rim(lo_ref, n)
            ref[rim + sx + k, cut, :] = get_rim(hi_ref, n)


def y_faces_kernel(rim, near_ref, far_ref, temp_ref, kind_ref, lo_ref, hi_ref,
                   left_ref, right_ref, work_ref):
    cx, near, _ = near_ref.shape
    sx, sy, _ = temp_ref.shape
    left_ref[:cx, :] = near_ref[:, 0, :]
    right_ref[:cx, :] = far_ref[:, near - 1, :]
    slabs = ([], [])
    long = work_ref.shape[1]
    work_ref[...] = jnp.zeros_like(work_ref)
    for which, own in enumerate((temp_ref[...], kind_ref[...].astype(F32) + 1.0)):
        fill_x(rim, work_ref.at[which], which, own, lo_ref, hi_ref)
        for into, start in zip(slabs, (OFF, OFF + sy - rim)):
            for k in range(rim):
                for h in range(0, long, PART):
                    into.append(work_ref[which, h:h + PART, start + k, :])
    put_rim(left_ref, cx, slabs[0])
    put_rim(right_ref, cx, slabs[1])


def y_faces(rim, fluid, temp, kind, lo, hi):
    cx, cy, depth = fluid.shape
    sx, sy, sz = temp.shape
    long = -(-(sx + 2 * rim) // PART) * PART
    height = cx + rim_rows(2 * rim * (long // PART), depth)
    edge = (cx, 8, depth)
    return pl.pallas_call(
        functools.partial(y_faces_kernel, rim),
        grid=(1,),
        in_specs=[
            pl.BlockSpec(edge, lambda i: (0, 0, 0)),
            pl.BlockSpec(edge, lambda i: (0, cy // 8 - 1, 0)),
            whole(temp.shape),
            whole(temp.shape),
            whole(lo.shape),
            whole(hi.shape),
        ],
        out_specs=[whole((height, depth))] * 2,
        out_shape=[jax.ShapeDtypeStruct((height, depth), F32)] * 2,
        scratch_shapes=[pltpu.VMEM((2, long, sy + 2 * OFF, sz), F32)],
        compiler_params=params(16),
        cost_estimate=cost(1000, 4 * 4 * height * depth),
        name="y_faces",
    )(fluid, fluid, temp, kind, lo, hi)


def table(kind, values):
    out = jnp.zeros(kind.shape, F32)
    for index, value in enumerate(values):
        out = jnp.where(kind == index + 1.0, value, out)
    return out


def solid_kernel(rim, cap, own_ref, kind_ref, xlo_ref, xhi_ref, ylo_ref, yhi_ref,
                 heat_ref, hxlo_ref, hxhi_ref, hylo_ref, hyhi_ref, code_ref,
                 next_ref, sigma_ref, reply_ref, temp_ref, work_ref, cond_ref, src_ref, rhs_ref):
    sx, sy, sz = own_ref.shape
    wide = sx + 2 * rim
    thin = rim - 1
    pieces = -(-wide // PART)
    for which, (own, ref) in enumerate(
        ((own_ref[...], temp_ref), (kind_ref[...].astype(F32) + 1.0, cond_ref))
    ):
        fill_x(rim, ref, which, own, xlo_ref, xhi_ref)
        for k in range(rim):
            for h in range(pieces):
                n = (which * rim + k) * pieces + h
                count = min(PART, wide - h * PART)
                cut = slice(h * PART, h * PART + count)
                ref[cut, OFF - rim + k, :] = get_rim(ylo_ref, n)[:count]
                ref[cut, OFF + sy + k, :] = get_rim(yhi_ref, n)[:count]
    src_ref[rim:rim + sx, OFF:OFF + sy, :] = heat_ref[...]
    src_ref[1:rim, OFF:OFF + sy, :] = hxlo_ref[...]
    src_ref[rim + sx:wide - 1, OFF:OFF + sy, :] = hxhi_ref[...]
    src_ref[1:wide - 1, OFF - thin:OFF, :] = hylo_ref[...]
    src_ref[1:wide - 1, OFF + sy:OFF + sy + thin, :] = hyhi_ref[...]
    kind = cond_ref[...]
    sigma_ref[...] = table(kind[rim - 1:rim + sx + 1], modulus_table)
    cond_ref[...] = solid_step * table(kind, conduct_table)
    src_ref[...] = (solid_step * source_gain) * src_ref[...]
    height = temp_ref.shape[1]
    first = lax.broadcasted_iota(jnp.int32, (height, sz), 1) == 0
    last = lax.broadcasted_iota(jnp.int32, (height, sz), 1) == sz - 1
    pair = (temp_ref, work_ref)
    for turn in range(rim - 1):
        now, later = pair[turn % 2], pair[(turn + 1) % 2]
        for x in range(1 + turn, wide - 1 - turn):
            centre = now[x]
            beside = now[x - 1] + now[x + 1]
            beside += pltpu.roll(centre, 1, 0) + pltpu.roll(centre, height - 1, 0)
            beside += jnp.where(first, 0.0, pltpu.roll(centre, 1, 1))
            beside += jnp.where(last, 0.0, pltpu.roll(centre, sz - 1, 1))
            later[x] = centre + (cond_ref[x] * (beside - 6.0 * centre) + src_ref[x])
    final = pair[(rim - 1) % 2]
    solid = final[rim:rim + sx, OFF:OFF + sy, :]
    next_ref[...] = solid
    sigma_ref[...] = sigma_ref[...] * final[rim - 1:rim + sx + 1]
    high, low = halves(solid.reshape(sx * sy, sz))
    rhs_ref[:, :sz] = high
    rhs_ref[:, sz:] = low
    slots = sx * sy
    ndev = code_ref.shape[0]
    turned = jnp.transpose(code_ref[...])
    names = lax.broadcasted_iota(jnp.int32, (cap, slots), 1)
    group = ndev // 4
    for index in range(0, ndev, group):
        pick = jnp.concatenate(
            [
                ones_where(names == turned[:cap, index + i:index + i + 1])
                for i in range(group)
            ],
            axis=0,
        )
        both = jnp.dot(pick, rhs_ref[...], preferred_element_type=F32)
        reply_ref[index * cap:(index + group) * cap, :] = both[:, :sz] + both[:, sz:]


def solid_steps(rim, cap, temp, kind, state_rim, heat, heat_rim, code):
    sx, sy, sz = temp.shape
    total = code.shape[0] * cap
    wide, height = sx + 2 * rim, sy + 2 * OFF
    args = (temp, kind, *state_rim, heat, *heat_rim, code)
    return pl.pallas_call(
        functools.partial(solid_kernel, rim, cap),
        grid=(1,),
        in_specs=[whole(x.shape) for x in args],
        out_specs=[whole((sx, sy, sz)), whole((sx + 2, height, sz)), whole((total, sz))],
        out_shape=[
            jax.ShapeDtypeStruct((sx, sy, sz), F32),
            jax.ShapeDtypeStruct((sx + 2, height, sz), F32),
            jax.ShapeDtypeStruct((total, sz), F32),
        ],
        scratch_shapes=[pltpu.VMEM((wide, height, sz), F32)] * 4
        + [pltpu.VMEM((sx * sy, 2 * sz), BF16)],
        compiler_params=params(24),
        cost_estimate=cost(4 * total * sx * sy * sz, 4 * total * sz),
        name="solid_steps",
    )(*args)


def stress_kernel(sigma_ref, out_ref):
    _, sx, sy, sz = out_ref.shape
    height = sigma_ref.shape[1]
    first = lax.broadcasted_iota(jnp.int32, (height, sz), 1) == 0
    last = lax.broadcasted_iota(jnp.int32, (height, sz), 1) == sz - 1

    def plane(x, none):
        centre = sigma_ref[x + 1]
        out_ref[0, x] = 0.5 * (sigma_ref[x + 2] - sigma_ref[x])[OFF:OFF + sy]
        along = pltpu.roll(centre, height - 1, 0) - pltpu.roll(centre, 1, 0)
        out_ref[1, x] = 0.5 * along[OFF:OFF + sy]
        along = jnp.where(last, 0.0, pltpu.roll(centre, sz - 1, 1)) - jnp.where(
            first, 0.0, pltpu.roll(centre, 1, 1)
        )
        out_ref[2, x] = 0.5 * along[OFF:OFF + sy]
        return none

    lax.fori_loop(0, sx, plane, 0)


def stress(sigma, sx, sy):
    sz = sigma.shape[2]
    return pl.pallas_call(
        stress_kernel,
        grid=(1,),
        in_specs=[whole(sigma.shape)],
        out_specs=whole((3, sx, sy, sz)),
        out_shape=jax.ShapeDtypeStruct((3, sx, sy, sz), F32),
        compiler_params=params(8),
        cost_estimate=cost(10 * sx * sy * sz, 16 * sx * sy * sz),
        name="stress",
    )(sigma)


def unpack_kernel(dest_ref, back_ref, *refs):
    out_ref = refs[-1]
    rows = out_ref.shape[0]

    def step(index, none):
        base = pl.multiple_of(index * 8, 8)
        lines = [back_ref[pl.ds(dest_ref[0, base + i], 1), :] for i in range(8)]
        out_ref[pl.ds(base, 8), :] = jnp.concatenate(lines, axis=0)
        return none

    lax.fori_loop(0, rows // 8, step, 0, unroll=4)


def unpack(dest, back, after):
    rows = dest.shape[1]
    row_len = back.shape[1]
    return pl.pallas_call(
        unpack_kernel,
        grid=(1,),
        in_specs=[pl.BlockSpec(memory_space=pltpu.SMEM), whole(back.shape)]
        + [anywhere] * len(after),
        out_specs=whole((rows, row_len)),
        out_shape=jax.ShapeDtypeStruct((rows, row_len), F32),
        compiler_params=params(10),
        cost_estimate=cost(rows * 128, 8 * rows * row_len),
        name="unpack",
    )(dest, back, *after)


def fluid_kernel(here_ref, xlo_ref, xhi_ref, ylo_ref, yhi_ref, speed_ref, flux_ref,
                 out_ref, ring_ref):
    index, count = pl.program_id(0), pl.num_programs(0)
    cx = count - 1
    _, cy, depth = here_ref.shape
    row_len = flux_ref.shape[2]
    rows = slice(OFF, OFF + cy)

    @pl.when(index == 0)
    def _():
        ring_ref[2, rows, :] = xlo_ref[...]

    new = lax.rem(index, 3)

    @pl.when(index < cx)
    def _():
        ring_ref[new, rows, :] = here_ref[0]
        ring_ref[new, OFF - 1:OFF, :] = ylo_ref[pl.ds(index, 1), :]
        ring_ref[new, OFF + cy:OFF + cy + 1, :] = yhi_ref[pl.ds(index, 1), :]

    @pl.when(index == cx)
    def _():
        ring_ref[new, rows, :] = xhi_ref[...]

    rate = time_step * diffusivity

    def push(total, centre, lower, upper, speed):
        scaled = time_step * speed
        total = total + (rate + jnp.maximum(scaled, 0.0)) * (lower - centre)
        return total + (rate - jnp.minimum(scaled, 0.0)) * (upper - centre)

    @pl.when(index > 0)
    def _():
        lanes = lax.broadcasted_iota(jnp.int32, (8, depth), 1)
        first, last = lanes == 0, lanes == depth - 1
        mid, old = lax.rem(index + 2, 3), lax.rem(index + 1, 3)
        for tile in range(cy // 16):
            speeds = [speed_ref[k, 0, tile * 16:tile * 16 + 16, :].astype(F32) for k in range(3)]
            for part in range(2):
                y = tile * 16 + part * 8
                at = OFF + y
                u, v, w = [s[part * 8:part * 8 + 8] for s in speeds]
                centre = ring_ref[mid, at:at + 8, :]
                total = push(
                    centre, centre, ring_ref[old, at:at + 8, :], ring_ref[new, at:at + 8, :], u
                )
                total = push(
                    total, centre, ring_ref[mid, at - 1:at + 7, :],
                    ring_ref[mid, at + 1:at + 9, :], v,
                )
                lower = jnp.where(first, 0.0, pltpu.roll(centre, 1, 1))
                upper = jnp.where(last, 0.0, pltpu.roll(centre, depth - 1, 1))
                total = push(total, centre, lower, upper, w)
                out_ref[0, y:y + 8, row_len:] = total[:, row_len:]
                out_ref[0, y:y + 8, :row_len] = (
                    total[:, :row_len] - time_step * flux_ref[0, y:y + 8, :]
                )


def fluid_step(temp, rims, velocity, flux):
    cx, cy, depth = temp.shape
    row_len = flux.shape[2]
    plane = (1, cy, depth)
    face = pl.BlockSpec((cy, depth), lambda i: (0, 0))
    line = pl.BlockSpec((cx, depth), lambda i: (0, 0))
    back = lambda i: (jnp.maximum(i - 1, 0), 0, 0)
    return pl.pallas_call(
        fluid_kernel,
        grid=(cx + 1,),
        in_specs=[
            pl.BlockSpec(plane, lambda i: (jnp.minimum(i, cx - 1), 0, 0)),
            face,
            face,
            line,
            line,
            pl.BlockSpec((3, 1, cy, depth), lambda i: (0, jnp.maximum(i - 1, 0), 0, 0)),
            pl.BlockSpec((1, cy, row_len), back),
        ],
        out_specs=pl.BlockSpec(plane, back),
        out_shape=jax.ShapeDtypeStruct(temp.shape, F32),
        scratch_shapes=[pltpu.VMEM((3, cy + 2 * OFF, depth), F32)],
        compiler_params=params(16),
        cost_estimate=cost(40 * cx * cy * depth, 14 * cx * cy * depth),
        name="fluid_step",
    )(temp, *rims, velocity, flux)


def fluid_rims(temp):
    xlo, xhi = neighbours(temp[-1], temp[0], "gx")
    ylo, yhi = neighbours(temp[:, -1], temp[:, 0], "gy")
    return xlo, xhi, ylo, yhi


def body(temp_fluid, velocity, wall_old, wall_mask, owner_map, slot_map, temp_solid, material):
    cx, cy, depth = temp_fluid.shape
    row_len = wall_old.shape[2]
    sx, sy, sz = temp_solid.shape
    ndev = lax.axis_size("gx") * lax.axis_size("gy")
    rows = cx * cy
    cap = (3 * rows + ndev - 1) // ndev
    cap = -(-cap // 8) * 8
    total = ndev * cap
    rim = SSTEPS + 1

    outgoing, flux, dest = pack(
        owner_map.reshape(1, rows), slot_map, temp_fluid, wall_old, wall_mask, ndev, cap
    )
    incoming = lax.all_to_all(outgoing, AXES, split_axis=0, concat_axis=0, tiled=True)

    first, last = x_faces(rim, temp_fluid, temp_solid, material)
    xlo, xhi = neighbours(last, first, "gx")
    first, last = y_faces(rim, temp_fluid, temp_solid, material, xlo[cy:], xhi[cy:])
    ylo, yhi = neighbours(last, first, "gy")
    rims = (xlo[cy:], xhi[cy:], ylo[cx:], yhi[cx:])

    fluid = fluid_step(temp_fluid, (xlo, xhi, ylo, yhi), velocity, flux)

    thin = rim - 1
    heat, first, last, code = heat_sum(incoming, cap, temp_solid.shape, thin, (fluid, *rims))
    hxlo, hxhi = neighbours(last, first, "gx")
    tall = lambda cut: jnp.concatenate([hxlo[:, cut], heat[:, cut], hxhi[:, cut]], axis=0)
    hylo, hyhi = neighbours(tall(slice(sy - thin, sy)), tall(slice(0, thin)), "gy")
    solid, sigma, replies = solid_steps(
        rim, cap, temp_solid, material, rims, heat, (hxlo, hxhi, hylo, hyhi), code
    )
    returned = lax.all_to_all(
        replies.reshape(ndev, cap, sz), AXES, split_axis=0, concat_axis=0, tiled=True
    )
    fluid = fluid_step(fluid, fluid_rims(fluid), velocity, flux)
    force = stress(sigma, sx, sy)
    wall_next = unpack(dest, returned.reshape(total, sz), (fluid, force))
    return fluid, wall_next.reshape(cx, cy, row_len), solid, force


def solution(mesh):
    placed = (
        P("gx", "gy", None),
        P(None, "gx", "gy", None),
        P("gx", "gy", None),
        P("gx", "gy", None),
        P(("gx", "gy"), None, None),
        P(("gx", "gy"), None),
        P("gx", "gy", None),
        P("gx", "gy", None),
    )
    return jax.shard_map(
        body,
        mesh=mesh,
        in_specs=placed,
        out_specs=(
            P("gx", "gy", None),
            P("gx", "gy", None),
            P("gx", "gy", None),
            P(None, "gx", "gy", None),
        ),
        check_vma=False,
    )
```

```python
import functools
import jax
import jax.numpy as jnp
from jax import lax
from jax.experimental import pallas as pl
from jax.experimental.pallas import tpu as pltpu
from jax.sharding import PartitionSpec as P

FSTEPS = 2
SSTEPS = 4
time_step = 0.1
diffusivity = 0.5
film_coef = 2.0
solid_step = 0.05
source_gain = 4.0
conduct_table = (0.4, 0.9, 1.5, 2.2)
modulus_table = (0.5, 1.0, 1.6, 2.4)
F32 = jnp.float32
BF16 = jnp.bfloat16
AXES = ("gx", "gy")
LANE = 128
PART = 16
OFF = 8


def params(mib):
    return pltpu.CompilerParams(vmem_limit_bytes=mib * 1024 * 1024)


def cost(flops, bytes_accessed):
    return pl.CostEstimate(flops=flops, bytes_accessed=bytes_accessed, transcendentals=0)


def halves(value):
    high = value.astype(BF16)
    low = (value - high.astype(F32)).astype(BF16)
    return high, low


def ones_where(test):
    return jnp.where(test, 1.0, 0.0).astype(BF16)


def neighbours(before, after, axis):
    size = lax.axis_size(axis)
    up = [(i, i + 1) for i in range(size - 1)]
    down = [(j, i) for i, j in up]
    return lax.ppermute(before, axis, up), lax.ppermute(after, axis, down)


def whole(shape):
    return pl.BlockSpec(shape, lambda i: (0,) * len(shape))


anywhere = pl.BlockSpec(memory_space=pl.ANY)


def rank_kernel(cap, owner_ref, slot_ref, dest_ref, where_ref, code_ref):
    rows = owner_ref.shape[1]
    ndev = code_ref.shape[0]
    tall = cap + 8
    tri = ones_where(
        lax.broadcasted_iota(jnp.int32, (LANE, LANE), 0)
        <= lax.broadcasted_iota(jnp.int32, (LANE, LANE), 1)
    )
    names = lax.broadcasted_iota(jnp.int32, (ndev, LANE), 0)
    steps = lax.broadcasted_iota(jnp.int32, (LANE, LANE), 0)
    carry = jnp.zeros((ndev, 1), F32)
    codes = jnp.zeros((2 * ndev, LANE), F32)
    for chunk in range(rows // LANE):
        cols = slice(chunk * LANE, (chunk + 1) * LANE)
        own = owner_ref[:, cols]
        hit = jnp.where(names == own, 1.0, 0.0)
        ranks = jnp.dot(hit.astype(BF16), tri, preferred_element_type=F32) + carry
        carry = ranks[:, LANE - 1:]
        place = jnp.sum(hit * ranks, axis=0, keepdims=True).astype(jnp.int32) - 1
        dest_ref[:, cols] = own * cap + place
        where_ref[:, cols] = own * tall + place
        code = slot_ref[:, cols] + 1
        pieces = jnp.concatenate(
            [hit * (code // 32).astype(F32), hit * (code % 32).astype(F32)], axis=0
        ).astype(BF16)
        codes = codes + lax.dot_general(
            pieces, ones_where(steps == place), (((1,), (1,)), ((), ())),
            preferred_element_type=F32,
        )
    code_ref[...] = codes[:ndev] * 32.0 + codes[ndev:]


def rank(owner, slot, ndev, cap):
    rows = owner.shape[1]
    line = jax.ShapeDtypeStruct((1, rows), jnp.int32)
    return pl.pallas_call(
        functools.partial(rank_kernel, cap),
        grid=(1,),
        in_specs=[whole((1, rows))] * 2,
        out_specs=[whole((1, rows))] * 2 + [whole((ndev, LANE))],
        out_shape=[line, line, jax.ShapeDtypeStruct((ndev, LANE), F32)],
        compiler_params=params(8),
        cost_estimate=cost(8 * ndev * LANE * rows, 20 * rows),
        name="rank",
    )(owner, slot)


def pack_kernel(cap, where_ref, code_ref, temp_ref, old_ref, mask_ref, *refs):
    out_ref, flux_ref, rhs_ref = refs[-3:]
    rows = where_ref.shape[1]
    ndev, tall, row_len = out_ref.shape
    flux = mask_ref[...].astype(F32) * film_coef * (temp_ref[...] - old_ref[...])
    flux_ref[...] = flux
    high, low = halves(flux.reshape(rows, row_len))
    rhs_ref[:, :row_len] = high
    rhs_ref[:, row_len:] = low
    where = where_ref[...]
    group = ndev // 4
    block = group * tall

    def step(index, none):
        base = index * block
        pick = ones_where(
            lax.broadcasted_iota(jnp.int32, (block, rows), 0) + base == where
        )
        both = jnp.dot(pick, rhs_ref[...], preferred_element_type=F32)
        lines = both[:, :row_len] + both[:, row_len:]
        out_ref[pl.ds(index * group, group)] = lines.reshape(group, tall, row_len)
        return none

    lax.fori_loop(0, ndev // group, step, 0)
    out_ref[:, cap, :] = code_ref[...]


def pack(where, code, temp, old, mask, cap, after):
    cx, cy, _ = temp.shape
    row_len = old.shape[2]
    rows = cx * cy
    ndev = code.shape[0]
    tall = cap + 8
    return pl.pallas_call(
        functools.partial(pack_kernel, cap),
        grid=(1,),
        in_specs=[whole((1, rows)), whole(code.shape)]
        + [whole((cx, cy, row_len))] * 3
        + [anywhere] * len(after),
        out_specs=[whole((ndev, tall, row_len)), whole((cx, cy, row_len))],
        out_shape=[
            jax.ShapeDtypeStruct((ndev, tall, row_len), F32),
            jax.ShapeDtypeStruct((cx, cy, row_len), F32),
        ],
        scratch_shapes=[pltpu.VMEM((rows, 2 * row_len), BF16)],
        compiler_params=params(61),
        cost_estimate=cost(4 * ndev * tall * rows * row_len, 5 * rows * row_len * 4),
        name="pack",
    )(where, code, temp, old, mask, *after)


def heat_kernel(cap, thin, rows_ref, *refs):
    heat_ref, first_ref, last_ref, code_ref = refs[-4:]
    ndev, tall, row_len = rows_ref.shape
    sx, sy, _ = heat_ref.shape
    slots = sx * sy
    codes = rows_ref[:, cap, :].astype(jnp.int32) - 1
    code_ref[...] = codes
    group = ndev // 4
    names = lax.broadcasted_iota(jnp.int32, (slots, tall), 0)
    total = jnp.zeros((slots, 2 * row_len), F32)
    for index in range(0, ndev, group):
        lines = rows_ref[index:index + group].reshape(group * tall, row_len)
        high, low = halves(lines)
        pick = jnp.concatenate(
            [
                jnp.where(names == codes[index + i:index + i + 1, :tall], 1.0, 0.0)
                for i in range(group)
            ],
            axis=1,
        ).astype(BF16)
        total = total + jnp.dot(
            pick, jnp.concatenate([high, low], axis=1), preferred_element_type=F32
        )
    heat = (total[:, :row_len] + total[:, row_len:]).reshape(sx, sy, row_len)
    heat_ref[...] = heat
    first_ref[...] = heat[:thin]
    last_ref[...] = heat[sx - thin:]


def heat_sum(incoming, cap, block, thin, after):
    ndev, tall, row_len = incoming.shape
    sx, sy, _ = block
    edge = (thin, sy, row_len)
    return pl.pallas_call(
        functools.partial(heat_kernel, cap, thin),
        grid=(1,),
        in_specs=[whole(incoming.shape)] + [anywhere] * len(after),
        out_specs=[whole(block), whole(edge), whole(edge), whole((ndev, row_len))],
        out_shape=[
            jax.ShapeDtypeStruct(block, F32),
            jax.ShapeDtypeStruct(edge, F32),
            jax.ShapeDtypeStruct(edge, F32),
            jax.ShapeDtypeStruct((ndev, row_len), jnp.int32),
        ],
        compiler_params=params(20),
        cost_estimate=cost(4 * ndev * tall * sx * sy * row_len, 4 * ndev * tall * row_len),
        name="heat_sum",
    )(incoming, *after)


def put_rim(ref, base, slabs):
    across = ref.shape[1] // LANE
    for n, slab in enumerate(slabs):
        row = base + n // across * PART
        ref[row:row + PART, n % across * LANE:(n % across + 1) * LANE] = slab


def get_rim(ref, n):
    across = ref.shape[1] // LANE
    row = n // across * PART
    return ref[row:row + PART, n % across * LANE:(n % across + 1) * LANE]


def rim_rows(count, depth):
    across = depth // LANE
    return -(-count // across) * PART


def x_faces_kernel(rim, bottom_ref, top_ref, temp_ref, kind_ref, low_ref, high_ref):
    _, cy, _ = bottom_ref.shape
    sx, sy, _ = temp_ref.shape
    low_ref[:cy, :] = bottom_ref[0]
    high_ref[:cy, :] = top_ref[0]
    for ref, start in ((low_ref, 0), (high_ref, sx - rim)):
        slabs = [
            get(start + k, slice(h, h + PART))
            for get in (
                lambda x, cut: temp_ref[x, cut, :],
                lambda x, cut: kind_ref[x, cut, :].astype(F32) + 1.0,
            )
            for k in range(rim)
            for h in range(0, sy, PART)
        ]
        put_rim(ref, cy, slabs)


def x_faces(rim, fluid, temp, kind):
    cx, cy, depth = fluid.shape
    sx, sy, sz = temp.shape
    height = cy + rim_rows(2 * rim * (sy // PART), depth)
    plane = (1, cy, depth)
    return pl.pallas_call(
        functools.partial(x_faces_kernel, rim),
        grid=(1,),
        in_specs=[
            pl.BlockSpec(plane, lambda i: (0, 0, 0)),
            pl.BlockSpec(plane, lambda i: (cx - 1, 0, 0)),
            whole(temp.shape),
            whole(temp.shape),
        ],
        out_specs=[whole((height, depth))] * 2,
        out_shape=[jax.ShapeDtypeStruct((height, depth), F32)] * 2,
        compiler_params=params(61),
        cost_estimate=cost(1000, 4 * 4 * height * depth),
        name="x_faces",
    )(fluid, fluid, temp, kind)


def fill_x(rim, ref, which, own, lo_ref, hi_ref):
    sx, sy, _ = own.shape
    pieces = sy // PART
    ref[rim:rim + sx, OFF:OFF + sy, :] = own
    for k in range(rim):
        for h in range(pieces):
            n = (which * rim + k) * pieces + h
            cut = slice(OFF + h * PART, OFF + (h + 1) * PART)
            ref[k, cut, :] = get_rim(lo_ref, n)
            ref[rim + sx + k, cut, :] = get_rim(hi_ref, n)


def y_faces_kernel(rim, near_ref, far_ref, temp_ref, kind_ref, lo_ref, hi_ref, *refs):
    left_ref, right_ref, work_ref = refs[-3:]
    cx, near, _ = near_ref.shape
    sx, sy, _ = temp_ref.shape
    left_ref[:cx, :] = near_ref[:, 0, :]
    right_ref[:cx, :] = far_ref[:, near - 1, :]
    slabs = ([], [])
    long = work_ref.shape[1]
    work_ref[...] = jnp.zeros_like(work_ref)
    for which, own in enumerate((temp_ref[...], kind_ref[...].astype(F32) + 1.0)):
        fill_x(rim, work_ref.at[which], which, own, lo_ref, hi_ref)
        for into, start in zip(slabs, (OFF, OFF + sy - rim)):
            for k in range(rim):
                for h in range(0, long, PART):
                    into.append(work_ref[which, h:h + PART, start + k, :])
    put_rim(left_ref, cx, slabs[0])
    put_rim(right_ref, cx, slabs[1])


def y_faces(rim, fluid, temp, kind, lo, hi, after):
    cx, cy, depth = fluid.shape
    sx, sy, sz = temp.shape
    long = -(-(sx + 2 * rim) // PART) * PART
    height = cx + rim_rows(2 * rim * (long // PART), depth)
    edge = (cx, 8, depth)
    return pl.pallas_call(
        functools.partial(y_faces_kernel, rim),
        grid=(1,),
        in_specs=[
            pl.BlockSpec(edge, lambda i: (0, 0, 0)),
            pl.BlockSpec(edge, lambda i: (0, cy // 8 - 1, 0)),
            whole(temp.shape),
            whole(temp.shape),
            whole(lo.shape),
            whole(hi.shape),
        ]
        + [anywhere] * len(after),
        out_specs=[whole((height, depth))] * 2,
        out_shape=[jax.ShapeDtypeStruct((height, depth), F32)] * 2,
        scratch_shapes=[pltpu.VMEM((2, long, sy + 2 * OFF, sz), F32)],
        compiler_params=params(16),
        cost_estimate=cost(1000, 4 * 4 * height * depth),
        name="y_faces",
    )(fluid, fluid, temp, kind, lo, hi, *after)


def table(kind, values):
    out = jnp.zeros(kind.shape, F32)
    for index, value in enumerate(values):
        out = jnp.where(kind == index + 1.0, value, out)
    return out


def solid_kernel(rim, cap, own_ref, kind_ref, xlo_ref, xhi_ref, ylo_ref, yhi_ref,
                 heat_ref, hxlo_ref, hxhi_ref, hylo_ref, hyhi_ref, code_ref,
                 next_ref, sigma_ref, reply_ref, temp_ref, work_ref, cond_ref, src_ref, rhs_ref,
                 stage_ref, sems):
    sx, sy, sz = own_ref.shape
    wide = sx + 2 * rim
    thin = rim - 1
    pieces = -(-wide // PART)
    for which, (own, ref) in enumerate(
        ((own_ref[...], temp_ref), (kind_ref[...].astype(F32) + 1.0, cond_ref))
    ):
        fill_x(rim, ref, which, own, xlo_ref, xhi_ref)
        for k in range(rim):
            for h in range(pieces):
                n = (which * rim + k) * pieces + h
                count = min(PART, wide - h * PART)
                cut = slice(h * PART, h * PART + count)
                ref[cut, OFF - rim + k, :] = get_rim(ylo_ref, n)[:count]
                ref[cut, OFF + sy + k, :] = get_rim(yhi_ref, n)[:count]
    src_ref[rim:rim + sx, OFF:OFF + sy, :] = heat_ref[...]
    src_ref[1:rim, OFF:OFF + sy, :] = hxlo_ref[...]
    src_ref[rim + sx:wide - 1, OFF:OFF + sy, :] = hxhi_ref[...]
    src_ref[1:wide - 1, OFF - thin:OFF, :] = hylo_ref[...]
    src_ref[1:wide - 1, OFF + sy:OFF + sy + thin, :] = hyhi_ref[...]
    kind = cond_ref[...]
    sigma_ref[...] = table(kind[rim - 1:rim + sx + 1], modulus_table)
    cond_ref[...] = solid_step * table(kind, conduct_table)
    src_ref[...] = (solid_step * source_gain) * src_ref[...]
    height = temp_ref.shape[1]
    first = lax.broadcasted_iota(jnp.int32, (height, sz), 1) == 0
    last = lax.broadcasted_iota(jnp.int32, (height, sz), 1) == sz - 1
    pair = (temp_ref, work_ref)
    for turn in range(rim - 1):
        now, later = pair[turn % 2], pair[(turn + 1) % 2]
        for x in range(1 + turn, wide - 1 - turn):
            centre = now[x]
            beside = now[x - 1] + now[x + 1]
            beside += pltpu.roll(centre, 1, 0) + pltpu.roll(centre, height - 1, 0)
            beside += jnp.where(first, 0.0, pltpu.roll(centre, 1, 1))
            beside += jnp.where(last, 0.0, pltpu.roll(centre, sz - 1, 1))
            later[x] = centre + (cond_ref[x] * (beside - 6.0 * centre) + src_ref[x])
    final = pair[(rim - 1) % 2]
    solid = final[rim:rim + sx, OFF:OFF + sy, :]
    next_ref[...] = solid
    sigma_ref[...] = sigma_ref[...] * final[rim - 1:rim + sx + 1]
    high, low = halves(solid.reshape(sx * sy, sz))
    rhs_ref[:, :sz] = high
    rhs_ref[:, sz:] = low
    slots = sx * sy
    ndev = code_ref.shape[0]
    turned = jnp.transpose(code_ref[...])
    names = lax.broadcasted_iota(jnp.int32, (cap, slots), 1)
    group = ndev // 4
    for index in range(0, ndev, group):
        pick = jnp.concatenate(
            [
                ones_where(names == turned[:cap, index + i:index + i + 1])
                for i in range(group)
            ],
            axis=0,
        )
        both = jnp.dot(pick, rhs_ref[...], preferred_element_type=F32)
        lines = slice(index * cap, (index + group) * cap)
        stage_ref[lines, :] = both[:, :sz] + both[:, sz:]
        pltpu.make_async_copy(
            stage_ref.at[lines], reply_ref.at[lines], sems.at[index // group]
        ).start()
    for index in range(0, ndev, group):
        lines = slice(index * cap, (index + group) * cap)
        pltpu.make_async_copy(
            stage_ref.at[lines], reply_ref.at[lines], sems.at[index // group]
        ).wait()


def solid_steps(rim, cap, temp, kind, state_rim, heat, heat_rim, code):
    sx, sy, sz = temp.shape
    total = code.shape[0] * cap
    wide, height = sx + 2 * rim, sy + 2 * OFF
    args = (temp, kind, *state_rim, heat, *heat_rim, code)
    return pl.pallas_call(
        functools.partial(solid_kernel, rim, cap),
        grid=(1,),
        in_specs=[whole(x.shape) for x in args],
        out_specs=[
            whole((sx, sy, sz)),
            whole((sx + 2, height, sz)),
            pl.BlockSpec(memory_space=pltpu.HBM),
        ],
        out_shape=[
            jax.ShapeDtypeStruct((sx, sy, sz), F32),
            jax.ShapeDtypeStruct((sx + 2, height, sz), F32),
            jax.ShapeDtypeStruct((total, sz), F32),
        ],
        scratch_shapes=[pltpu.VMEM((wide, height, sz), F32)] * 4
        + [
            pltpu.VMEM((sx * sy, 2 * sz), BF16),
            pltpu.VMEM((total, sz), F32),
            pltpu.SemaphoreType.DMA((4,)),
        ],
        compiler_params=params(24),
        cost_estimate=cost(4 * total * sx * sy * sz, 4 * total * sz),
        name="solid_steps",
    )(*args)


def stress_kernel(sigma_ref, out_ref):
    _, sx, sy, sz = out_ref.shape
    height = sigma_ref.shape[1]
    first = lax.broadcasted_iota(jnp.int32, (height, sz), 1) == 0
    last = lax.broadcasted_iota(jnp.int32, (height, sz), 1) == sz - 1

    def plane(x, none):
        centre = sigma_ref[x + 1]
        out_ref[0, x] = 0.5 * (sigma_ref[x + 2] - sigma_ref[x])[OFF:OFF + sy]
        along = pltpu.roll(centre, height - 1, 0) - pltpu.roll(centre, 1, 0)
        out_ref[1, x] = 0.5 * along[OFF:OFF + sy]
        along = jnp.where(last, 0.0, pltpu.roll(centre, sz - 1, 1)) - jnp.where(
            first, 0.0, pltpu.roll(centre, 1, 1)
        )
        out_ref[2, x] = 0.5 * along[OFF:OFF + sy]
        return none

    lax.fori_loop(0, sx, plane, 0)


def stress(sigma, sx, sy):
    sz = sigma.shape[2]
    return pl.pallas_call(
        stress_kernel,
        grid=(1,),
        in_specs=[whole(sigma.shape)],
        out_specs=whole((3, sx, sy, sz)),
        out_shape=jax.ShapeDtypeStruct((3, sx, sy, sz), F32),
        compiler_params=params(8),
        cost_estimate=cost(10 * sx * sy * sz, 16 * sx * sy * sz),
        name="stress",
    )(sigma)


def unpack_kernel(dest_ref, back_ref, *refs):
    out_ref = refs[-1]
    rows = out_ref.shape[0]

    def step(index, none):
        base = pl.multiple_of(index * 8, 8)
        lines = [back_ref[pl.ds(dest_ref[0, base + i], 1), :] for i in range(8)]
        out_ref[pl.ds(base, 8), :] = jnp.concatenate(lines, axis=0)
        return none

    lax.fori_loop(0, rows // 8, step, 0, unroll=4)


def unpack(dest, back, after):
    rows = dest.shape[1]
    row_len = back.shape[1]
    return pl.pallas_call(
        unpack_kernel,
        grid=(1,),
        in_specs=[pl.BlockSpec(memory_space=pltpu.SMEM), whole(back.shape)]
        + [anywhere] * len(after),
        out_specs=whole((rows, row_len)),
        out_shape=jax.ShapeDtypeStruct((rows, row_len), F32),
        compiler_params=params(61),
        cost_estimate=cost(rows * 128, 8 * rows * row_len),
        name="unpack",
    )(dest, back, *after)


def fluid_kernel(here_ref, xlo_ref, xhi_ref, ylo_ref, yhi_ref, speed_ref, flux_ref, *refs):
    out_ref, xfirst_ref, xlast_ref, yfirst_ref, ylast_ref, ring_ref = refs[-6:]
    index, count = pl.program_id(0), pl.num_programs(0)
    cx = count - 1
    _, cy, depth = here_ref.shape
    row_len = flux_ref.shape[2]
    rows = slice(OFF, OFF + cy)

    @pl.when(index == 0)
    def _():
        ring_ref[2, rows, :] = xlo_ref[...]

    new = lax.rem(index, 3)

    @pl.when(index < cx)
    def _():
        ring_ref[new, rows, :] = here_ref[0]
        ring_ref[new, OFF - 1:OFF, :] = ylo_ref[pl.ds(index, 1), :]
        ring_ref[new, OFF + cy:OFF + cy + 1, :] = yhi_ref[pl.ds(index, 1), :]

    @pl.when(index == cx)
    def _():
        ring_ref[new, rows, :] = xhi_ref[...]

    rate = time_step * diffusivity

    def push(total, centre, lower, upper, speed):
        scaled = time_step * speed
        total = total + (rate + jnp.maximum(scaled, 0.0)) * (lower - centre)
        return total + (rate - jnp.minimum(scaled, 0.0)) * (upper - centre)

    @pl.when(index > 0)
    def _():
        lanes = lax.broadcasted_iota(jnp.int32, (8, depth), 1)
        first, last = lanes == 0, lanes == depth - 1
        mid, old = lax.rem(index + 2, 3), lax.rem(index + 1, 3)
        for tile in range(cy // 16):
            speeds = [speed_ref[k, 0, tile * 16:tile * 16 + 16, :].astype(F32) for k in range(3)]
            for part in range(2):
                y = tile * 16 + part * 8
                at = OFF + y
                u, v, w = [s[part * 8:part * 8 + 8] for s in speeds]
                centre = ring_ref[mid, at:at + 8, :]
                total = push(
                    centre, centre, ring_ref[old, at:at + 8, :], ring_ref[new, at:at + 8, :], u
                )
                total = push(
                    total, centre, ring_ref[mid, at - 1:at + 7, :],
                    ring_ref[mid, at + 1:at + 9, :], v,
                )
                lower = jnp.where(first, 0.0, pltpu.roll(centre, 1, 1))
                upper = jnp.where(last, 0.0, pltpu.roll(centre, depth - 1, 1))
                total = push(total, centre, lower, upper, w)
                out_ref[0, y:y + 8, row_len:] = total[:, row_len:]
                out_ref[0, y:y + 8, :row_len] = (
                    total[:, :row_len] - time_step * flux_ref[0, y:y + 8, :]
                )
        yfirst_ref[pl.ds(index - 1, 1), :] = out_ref[0, 0:1, :]
        ylast_ref[pl.ds(index - 1, 1), :] = out_ref[0, cy - 1:cy, :]

    @pl.when(index == 1)
    def _():
        xfirst_ref[...] = out_ref[0]

    @pl.when(index == cx)
    def _():
        xlast_ref[...] = out_ref[0]


def fluid_step(temp, rims, velocity, flux, after):
    cx, cy, depth = temp.shape
    row_len = flux.shape[2]
    plane = (1, cy, depth)
    face = pl.BlockSpec((cy, depth), lambda i: (0, 0))
    line = pl.BlockSpec((cx, depth), lambda i: (0, 0))
    back = lambda i: (jnp.maximum(i - 1, 0), 0, 0)
    return pl.pallas_call(
        fluid_kernel,
        grid=(cx + 1,),
        in_specs=[
            pl.BlockSpec(plane, lambda i: (jnp.minimum(i, cx - 1), 0, 0)),
            face,
            face,
            line,
            line,
            pl.BlockSpec((3, 1, cy, depth), lambda i: (0, jnp.maximum(i - 1, 0), 0, 0)),
            pl.BlockSpec((1, cy, row_len), back),
        ]
        + [anywhere] * len(after),
        out_specs=[pl.BlockSpec(plane, back), face, face, line, line],
        out_shape=[
            jax.ShapeDtypeStruct(temp.shape, F32),
            jax.ShapeDtypeStruct((cy, depth), F32),
            jax.ShapeDtypeStruct((cy, depth), F32),
            jax.ShapeDtypeStruct((cx, depth), F32),
            jax.ShapeDtypeStruct((cx, depth), F32),
        ],
        scratch_shapes=[pltpu.VMEM((3, cy + 2 * OFF, depth), F32)],
        compiler_params=params(61),
        cost_estimate=cost(40 * cx * cy * depth, 14 * cx * cy * depth),
        name="fluid_step",
    )(temp, *rims, velocity, flux, *after)


def body(temp_fluid, velocity, wall_old, wall_mask, owner_map, slot_map, temp_solid, material):
    cx, cy, depth = temp_fluid.shape
    row_len = wall_old.shape[2]
    sx, sy, sz = temp_solid.shape
    ndev = lax.axis_size("gx") * lax.axis_size("gy")
    rows = cx * cy
    cap = (3 * rows + ndev - 1) // ndev
    cap = -(-cap // 8) * 8
    total = ndev * cap
    rim = SSTEPS + 1

    first, last = x_faces(rim, temp_fluid, temp_solid, material)
    xlo, xhi = neighbours(last, first, "gx")
    dest, where, codes = rank(owner_map.reshape(1, rows), slot_map, ndev, cap)
    outgoing, flux = pack(where, codes, temp_fluid, wall_old, wall_mask, cap, (xlo, xhi))
    incoming = lax.all_to_all(outgoing, AXES, split_axis=0, concat_axis=0, tiled=True)

    first, last = y_faces(rim, temp_fluid, temp_solid, material, xlo[cy:], xhi[cy:], (flux,))
    ylo, yhi = neighbours(last, first, "gy")
    rims = (xlo[cy:], xhi[cy:], ylo[cx:], yhi[cx:])
    faces = (xlo, xhi, ylo, yhi)
    for turn in range(FSTEPS - 1):
        fluid, xfirst, xlast, yfirst, ylast = fluid_step(
            fluid if turn else temp_fluid, faces, velocity, flux, ()
        )
        faces = (*neighbours(xlast, xfirst, "gx"), *neighbours(ylast, yfirst, "gy"))

    thin = rim - 1
    heat, first, last, code = heat_sum(incoming, cap, temp_solid.shape, thin, (*faces, *rims))
    hxlo, hxhi = neighbours(last, first, "gx")
    tall = lambda cut: jnp.concatenate([hxlo[:, cut], heat[:, cut], hxhi[:, cut]], axis=0)
    hylo, hyhi = neighbours(tall(slice(sy - thin, sy)), tall(slice(0, thin)), "gy")
    solid, sigma, replies = solid_steps(
        rim, cap, temp_solid, material, rims, heat, (hxlo, hxhi, hylo, hyhi), code
    )
    returned = lax.all_to_all(
        replies.reshape(ndev, cap, sz), AXES, split_axis=0, concat_axis=0, tiled=True
    )
    fluid = fluid_step(fluid, faces, velocity, flux, (sigma,))[0]
    force = stress(sigma, sx, sy)
    wall_next = unpack(dest, returned.reshape(total, sz), (fluid, force))
    return fluid, wall_next.reshape(cx, cy, row_len), solid, force


def solution(mesh):
    placed = (
        P("gx", "gy", None),
        P(None, "gx", "gy", None),
        P("gx", "gy", None),
        P("gx", "gy", None),
        P(("gx", "gy"), None, None),
        P(("gx", "gy"), None),
        P("gx", "gy", None),
        P("gx", "gy", None),
    )
    return jax.shard_map(
        body,
        mesh=mesh,
        in_specs=placed,
        out_specs=(
            P("gx", "gy", None),
            P("gx", "gy", None),
            P("gx", "gy", None),
            P(None, "gx", "gy", None),
        ),
        check_vma=False,
    )
```

```python
import functools
import jax
import jax.numpy as jnp
from jax import lax
from jax.experimental import pallas as pl
from jax.experimental.pallas import tpu as pltpu
from jax.sharding import PartitionSpec as P

FSTEPS = 2
SSTEPS = 4
time_step = 0.1
diffusivity = 0.5
film_coef = 2.0
solid_step = 0.05
source_gain = 4.0
conduct_table = (0.4, 0.9, 1.5, 2.2)
modulus_table = (0.5, 1.0, 1.6, 2.4)
F32 = jnp.float32
BF16 = jnp.bfloat16
AXES = ("gx", "gy")
LANE = 128
PART = 16
OFF = 8


def params(mib):
    return pltpu.CompilerParams(vmem_limit_bytes=mib * 1024 * 1024)


def cost(flops, bytes_accessed):
    return pl.CostEstimate(flops=flops, bytes_accessed=bytes_accessed, transcendentals=0)


def halves(value):
    high = value.astype(BF16)
    low = (value - high.astype(F32)).astype(BF16)
    return high, low


def ones_where(test):
    return jnp.where(test, 1.0, 0.0).astype(BF16)


def neighbours(before, after, axis):
    size = lax.axis_size(axis)
    up = [(i, i + 1) for i in range(size - 1)]
    down = [(j, i) for i, j in up]
    return lax.ppermute(before, axis, up), lax.ppermute(after, axis, down)


def whole(shape):
    return pl.BlockSpec(shape, lambda i: (0,) * len(shape))


anywhere = pl.BlockSpec(memory_space=pl.ANY)


def rank_kernel(cap, owner_ref, slot_ref, dest_ref, where_ref, code_ref):
    rows = owner_ref.shape[1]
    ndev = code_ref.shape[0]
    tall = cap + 8
    tri = ones_where(
        lax.broadcasted_iota(jnp.int32, (LANE, LANE), 0)
        <= lax.broadcasted_iota(jnp.int32, (LANE, LANE), 1)
    )
    names = lax.broadcasted_iota(jnp.int32, (ndev, LANE), 0)
    steps = lax.broadcasted_iota(jnp.int32, (LANE, LANE), 0)
    carry = jnp.zeros((ndev, 1), F32)
    codes = jnp.zeros((2 * ndev, LANE), F32)
    for chunk in range(rows // LANE):
        cols = slice(chunk * LANE, (chunk + 1) * LANE)
        own = owner_ref[:, cols]
        hit = jnp.where(names == own, 1.0, 0.0)
        ranks = jnp.dot(hit.astype(BF16), tri, preferred_element_type=F32) + carry
        carry = ranks[:, LANE - 1:]
        place = jnp.sum(hit * ranks, axis=0, keepdims=True).astype(jnp.int32) - 1
        dest_ref[:, cols] = own * cap + place
        where_ref[:, cols] = own * tall + place
        code = slot_ref[:, cols] + 1
        pieces = jnp.concatenate(
            [hit * (code // 32).astype(F32), hit * (code % 32).astype(F32)], axis=0
        ).astype(BF16)
        codes = codes + lax.dot_general(
            pieces, ones_where(steps == place), (((1,), (1,)), ((), ())),
            preferred_element_type=F32,
        )
    code_ref[...] = codes[:ndev] * 32.0 + codes[ndev:]


def rank(owner, slot, ndev, cap):
    rows = owner.shape[1]
    line = jax.ShapeDtypeStruct((1, rows), jnp.int32)
    return pl.pallas_call(
        functools.partial(rank_kernel, cap),
        grid=(1,),
        in_specs=[whole((1, rows))] * 2,
        out_specs=[whole((1, rows))] * 2 + [whole((ndev, LANE))],
        out_shape=[line, line, jax.ShapeDtypeStruct((ndev, LANE), F32)],
        compiler_params=params(8),
        cost_estimate=cost(8 * ndev * LANE * rows, 20 * rows),
        name="rank",
    )(owner, slot)


def pack_kernel(cap, where_ref, code_ref, temp_ref, old_ref, mask_ref, *refs):
    out_ref, flux_ref, rhs_ref = refs[-3:]
    rows = where_ref.shape[1]
    ndev, tall, row_len = out_ref.shape
    flux = mask_ref[...].astype(F32) * film_coef * (temp_ref[...] - old_ref[...])
    flux_ref[...] = flux
    high, low = halves(flux.reshape(rows, row_len))
    rhs_ref[:, :row_len] = high
    rhs_ref[:, row_len:] = low
    where = where_ref[...]
    group = ndev // 4
    block = group * tall

    def step(index, none):
        base = index * block
        pick = ones_where(
            lax.broadcasted_iota(jnp.int32, (block, rows), 0) + base == where
        )
        both = jnp.dot(pick, rhs_ref[...], preferred_element_type=F32)
        lines = both[:, :row_len] + both[:, row_len:]
        out_ref[pl.ds(index * group, group)] = lines.reshape(group, tall, row_len)
        return none

    lax.fori_loop(0, ndev // group, step, 0)
    out_ref[:, cap, :] = code_ref[...]


def pack(where, code, temp, old, mask, cap, after):
    cx, cy, _ = temp.shape
    row_len = old.shape[2]
    rows = cx * cy
    ndev = code.shape[0]
    tall = cap + 8
    return pl.pallas_call(
        functools.partial(pack_kernel, cap),
        grid=(1,),
        in_specs=[whole((1, rows)), whole(code.shape)]
        + [whole((cx, cy, row_len))] * 3
        + [anywhere] * len(after),
        out_specs=[whole((ndev, tall, row_len)), whole((cx, cy, row_len))],
        out_shape=[
            jax.ShapeDtypeStruct((ndev, tall, row_len), F32),
            jax.ShapeDtypeStruct((cx, cy, row_len), F32),
        ],
        scratch_shapes=[pltpu.VMEM((rows, 2 * row_len), BF16)],
        compiler_params=params(40),
        cost_estimate=cost(4 * ndev * tall * rows * row_len, 5 * rows * row_len * 4),
        name="pack",
    )(where, code, temp, old, mask, *after)


def heat_kernel(cap, thin, rows_ref, *refs):
    heat_ref, first_ref, last_ref, code_ref = refs[-4:]
    ndev, tall, row_len = rows_ref.shape
    sx, sy, _ = heat_ref.shape
    slots = sx * sy
    codes = rows_ref[:, cap, :].astype(jnp.int32) - 1
    code_ref[...] = codes
    group = ndev // 4
    names = lax.broadcasted_iota(jnp.int32, (slots, tall), 0)
    total = jnp.zeros((slots, 2 * row_len), F32)
    for index in range(0, ndev, group):
        lines = rows_ref[index:index + group].reshape(group * tall, row_len)
        high, low = halves(lines)
        pick = jnp.concatenate(
            [
                jnp.where(names == codes[index + i:index + i + 1, :tall], 1.0, 0.0)
                for i in range(group)
            ],
            axis=1,
        ).astype(BF16)
        total = total + jnp.dot(
            pick, jnp.concatenate([high, low], axis=1), preferred_element_type=F32
        )
    heat = (total[:, :row_len] + total[:, row_len:]).reshape(sx, sy, row_len)
    heat_ref[...] = heat
    first_ref[...] = heat[:thin]
    last_ref[...] = heat[sx - thin:]


def heat_sum(incoming, cap, block, thin, after):
    ndev, tall, row_len = incoming.shape
    sx, sy, _ = block
    edge = (thin, sy, row_len)
    return pl.pallas_call(
        functools.partial(heat_kernel, cap, thin),
        grid=(1,),
        in_specs=[whole(incoming.shape)] + [anywhere] * len(after),
        out_specs=[whole(block), whole(edge), whole(edge), whole((ndev, row_len))],
        out_shape=[
            jax.ShapeDtypeStruct(block, F32),
            jax.ShapeDtypeStruct(edge, F32),
            jax.ShapeDtypeStruct(edge, F32),
            jax.ShapeDtypeStruct((ndev, row_len), jnp.int32),
        ],
        compiler_params=params(20),
        cost_estimate=cost(4 * ndev * tall * sx * sy * row_len, 4 * ndev * tall * row_len),
        name="heat_sum",
    )(incoming, *after)


def put_rim(ref, base, slabs):
    across = ref.shape[1] // LANE
    for n, slab in enumerate(slabs):
        row = base + n // across * PART
        ref[row:row + PART, n % across * LANE:(n % across + 1) * LANE] = slab


def get_rim(ref, base, n):
    across = ref.shape[1] // LANE
    row = base + n // across * PART
    return ref[row:row + PART, n % across * LANE:(n % across + 1) * LANE]


def rim_rows(count, depth):
    across = depth // LANE
    return -(-count // across) * PART


def x_faces_kernel(rim, bottom_ref, top_ref, near_ref, far_ref, temp_ref, kind_ref,
                   low_ref, high_ref, left_ref, right_ref):
    _, cy, _ = bottom_ref.shape
    left_ref[...] = near_ref[:, 0, :]
    right_ref[...] = far_ref[:, near_ref.shape[1] - 1, :]
    sx, sy, _ = temp_ref.shape
    low_ref[:cy, :] = bottom_ref[0]
    high_ref[:cy, :] = top_ref[0]
    for ref, start in ((low_ref, 0), (high_ref, sx - rim)):
        slabs = [
            get(start + k, slice(h, h + PART))
            for get in (
                lambda x, cut: temp_ref[x, cut, :],
                lambda x, cut: kind_ref[x, cut, :].astype(F32) + 1.0,
            )
            for k in range(rim)
            for h in range(0, sy, PART)
        ]
        put_rim(ref, cy, slabs)


def x_faces(rim, fluid, temp, kind):
    cx, cy, depth = fluid.shape
    sx, sy, sz = temp.shape
    height = cy + rim_rows(2 * rim * (sy // PART), depth)
    plane = (1, cy, depth)
    return pl.pallas_call(
        functools.partial(x_faces_kernel, rim),
        grid=(1,),
        in_specs=[
            pl.BlockSpec(plane, lambda i: (0, 0, 0)),
            pl.BlockSpec(plane, lambda i: (cx - 1, 0, 0)),
            pl.BlockSpec((cx, 8, depth), lambda i: (0, 0, 0)),
            pl.BlockSpec((cx, 8, depth), lambda i: (0, cy // 8 - 1, 0)),
            whole(temp.shape),
            whole(temp.shape),
        ],
        out_specs=[whole((height, depth))] * 2 + [whole((cx, depth))] * 2,
        out_shape=[jax.ShapeDtypeStruct((height, depth), F32)] * 2
        + [jax.ShapeDtypeStruct((cx, depth), F32)] * 2,
        compiler_params=params(61),
        cost_estimate=cost(1000, 4 * 4 * height * depth),
        name="x_faces",
    )(fluid, fluid, fluid, fluid, temp, kind)


def fill_x(rim, ref, which, own, lo_ref, hi_ref):
    sx, sy, _ = own.shape
    pieces = sy // PART
    base = lo_ref.shape[0] - rim_rows(2 * rim * pieces, lo_ref.shape[1])
    ref[rim:rim + sx, OFF:OFF + sy, :] = own
    for k in range(rim):
        for h in range(pieces):
            n = (which * rim + k) * pieces + h
            cut = slice(OFF + h * PART, OFF + (h + 1) * PART)
            ref[k, cut, :] = get_rim(lo_ref, base, n)
            ref[rim + sx + k, cut, :] = get_rim(hi_ref, base, n)


def y_faces_kernel(rim, temp_ref, kind_ref, lo_ref, hi_ref, *refs):
    left_ref, right_ref, work_ref = refs[-3:]
    sx, sy, _ = temp_ref.shape
    slabs = ([], [])
    long = work_ref.shape[1]
    work_ref[...] = jnp.zeros_like(work_ref)
    for which, own in enumerate((temp_ref[...], kind_ref[...].astype(F32) + 1.0)):
        fill_x(rim, work_ref.at[which], which, own, lo_ref, hi_ref)
        for into, start in zip(slabs, (OFF, OFF + sy - rim)):
            for k in range(rim):
                for h in range(0, long, PART):
                    into.append(work_ref[which, h:h + PART, start + k, :])
    put_rim(left_ref, 0, slabs[0])
    put_rim(right_ref, 0, slabs[1])


def y_faces(rim, temp, kind, lo, hi, after):
    sx, sy, sz = temp.shape
    depth = lo.shape[1]
    long = -(-(sx + 2 * rim) // PART) * PART
    height = rim_rows(2 * rim * (long // PART), depth)
    return pl.pallas_call(
        functools.partial(y_faces_kernel, rim),
        grid=(1,),
        in_specs=[whole(temp.shape)] * 2 + [whole(lo.shape)] * 2 + [anywhere] * len(after),
        out_specs=[whole((height, depth))] * 2,
        out_shape=[jax.ShapeDtypeStruct((height, depth), F32)] * 2,
        scratch_shapes=[pltpu.VMEM((2, long, sy + 2 * OFF, sz), F32)],
        compiler_params=params(16),
        cost_estimate=cost(1000, 4 * 4 * height * depth),
        name="y_faces",
    )(temp, kind, lo, hi, *after)


def table(kind, values):
    out = jnp.zeros(kind.shape, F32)
    for index, value in enumerate(values):
        out = jnp.where(kind == index + 1.0, value, out)
    return out


def solid_kernel(rim, cap, own_ref, kind_ref, xlo_ref, xhi_ref, ylo_ref, yhi_ref,
                 heat_ref, hxlo_ref, hxhi_ref, hylo_ref, hyhi_ref, code_ref,
                 next_ref, sigma_ref, reply_ref, temp_ref, work_ref, cond_ref, src_ref, rhs_ref,
                 stage_ref, sems):
    sx, sy, sz = own_ref.shape
    wide = sx + 2 * rim
    thin = rim - 1
    pieces = -(-wide // PART)
    for which, (own, ref) in enumerate(
        ((own_ref[...], temp_ref), (kind_ref[...].astype(F32) + 1.0, cond_ref))
    ):
        fill_x(rim, ref, which, own, xlo_ref, xhi_ref)
        for k in range(rim):
            for h in range(pieces):
                n = (which * rim + k) * pieces + h
                count = min(PART, wide - h * PART)
                cut = slice(h * PART, h * PART + count)
                ref[cut, OFF - rim + k, :] = get_rim(ylo_ref, 0, n)[:count]
                ref[cut, OFF + sy + k, :] = get_rim(yhi_ref, 0, n)[:count]
    src_ref[rim:rim + sx, OFF:OFF + sy, :] = heat_ref[...]
    src_ref[1:rim, OFF:OFF + sy, :] = hxlo_ref[...]
    src_ref[rim + sx:wide - 1, OFF:OFF + sy, :] = hxhi_ref[...]
    src_ref[1:wide - 1, OFF - thin:OFF, :] = hylo_ref[...]
    src_ref[1:wide - 1, OFF + sy:OFF + sy + thin, :] = hyhi_ref[...]
    kind = cond_ref[...]
    sigma_ref[...] = table(kind[rim - 1:rim + sx + 1], modulus_table)
    cond_ref[...] = solid_step * table(kind, conduct_table)
    src_ref[...] = (solid_step * source_gain) * src_ref[...]
    height = temp_ref.shape[1]
    first = lax.broadcasted_iota(jnp.int32, (height, sz), 1) == 0
    last = lax.broadcasted_iota(jnp.int32, (height, sz), 1) == sz - 1
    pair = (temp_ref, work_ref)
    for turn in range(rim - 1):
        now, later = pair[turn % 2], pair[(turn + 1) % 2]
        for x in range(1 + turn, wide - 1 - turn):
            centre = now[x]
            beside = now[x - 1] + now[x + 1]
            beside += pltpu.roll(centre, 1, 0) + pltpu.roll(centre, height - 1, 0)
            beside += jnp.where(first, 0.0, pltpu.roll(centre, 1, 1))
            beside += jnp.where(last, 0.0, pltpu.roll(centre, sz - 1, 1))
            later[x] = centre + (cond_ref[x] * (beside - 6.0 * centre) + src_ref[x])
    final = pair[(rim - 1) % 2]
    solid = final[rim:rim + sx, OFF:OFF + sy, :]
    next_ref[...] = solid
    sigma_ref[...] = sigma_ref[...] * final[rim - 1:rim + sx + 1]
    high, low = halves(solid.reshape(sx * sy, sz))
    rhs_ref[:, :sz] = high
    rhs_ref[:, sz:] = low
    slots = sx * sy
    ndev = code_ref.shape[0]
    turned = jnp.transpose(code_ref[...])
    names = lax.broadcasted_iota(jnp.int32, (cap, slots), 1)
    group = ndev // 4
    for index in range(0, ndev, group):
        pick = jnp.concatenate(
            [
                ones_where(names == turned[:cap, index + i:index + i + 1])
                for i in range(group)
            ],
            axis=0,
        )
        both = jnp.dot(pick, rhs_ref[...], preferred_element_type=F32)
        lines = slice(index * cap, (index + group) * cap)
        stage_ref[lines, :] = both[:, :sz] + both[:, sz:]
        pltpu.make_async_copy(
            stage_ref.at[lines], reply_ref.at[lines], sems.at[index // group]
        ).start()
    for index in range(0, ndev, group):
        lines = slice(index * cap, (index + group) * cap)
        pltpu.make_async_copy(
            stage_ref.at[lines], reply_ref.at[lines], sems.at[index // group]
        ).wait()


def solid_steps(rim, cap, temp, kind, state_rim, heat, heat_rim, code):
    sx, sy, sz = temp.shape
    total = code.shape[0] * cap
    wide, height = sx + 2 * rim, sy + 2 * OFF
    args = (temp, kind, *state_rim, heat, *heat_rim, code)
    return pl.pallas_call(
        functools.partial(solid_kernel, rim, cap),
        grid=(1,),
        in_specs=[whole(x.shape) for x in args],
        out_specs=[
            whole((sx, sy, sz)),
            whole((sx + 2, height, sz)),
            pl.BlockSpec(memory_space=pltpu.HBM),
        ],
        out_shape=[
            jax.ShapeDtypeStruct((sx, sy, sz), F32),
            jax.ShapeDtypeStruct((sx + 2, height, sz), F32),
            jax.ShapeDtypeStruct((total, sz), F32),
        ],
        scratch_shapes=[pltpu.VMEM((wide, height, sz), F32)] * 4
        + [
            pltpu.VMEM((sx * sy, 2 * sz), BF16),
            pltpu.VMEM((total, sz), F32),
            pltpu.SemaphoreType.DMA((4,)),
        ],
        compiler_params=params(24),
        cost_estimate=cost(4 * total * sx * sy * sz, 4 * total * sz),
        name="solid_steps",
    )(*args)


def stress_kernel(sigma_ref, out_ref):
    _, sx, sy, sz = out_ref.shape
    height = sigma_ref.shape[1]
    first = lax.broadcasted_iota(jnp.int32, (height, sz), 1) == 0
    last = lax.broadcasted_iota(jnp.int32, (height, sz), 1) == sz - 1

    def plane(x, none):
        centre = sigma_ref[x + 1]
        out_ref[0, x] = 0.5 * (sigma_ref[x + 2] - sigma_ref[x])[OFF:OFF + sy]
        along = pltpu.roll(centre, height - 1, 0) - pltpu.roll(centre, 1, 0)
        out_ref[1, x] = 0.5 * along[OFF:OFF + sy]
        along = jnp.where(last, 0.0, pltpu.roll(centre, sz - 1, 1)) - jnp.where(
            first, 0.0, pltpu.roll(centre, 1, 1)
        )
        out_ref[2, x] = 0.5 * along[OFF:OFF + sy]
        return none

    lax.fori_loop(0, sx, plane, 0)


def stress(sigma, sx, sy):
    sz = sigma.shape[2]
    return pl.pallas_call(
        stress_kernel,
        grid=(1,),
        in_specs=[whole(sigma.shape)],
        out_specs=whole((3, sx, sy, sz)),
        out_shape=jax.ShapeDtypeStruct((3, sx, sy, sz), F32),
        compiler_params=params(8),
        cost_estimate=cost(10 * sx * sy * sz, 16 * sx * sy * sz),
        name="stress",
    )(sigma)


def unpack_kernel(dest_ref, back_ref, *refs):
    out_ref = refs[-1]
    rows = out_ref.shape[0]

    def step(index, none):
        base = pl.multiple_of(index * 8, 8)
        lines = [back_ref[pl.ds(dest_ref[0, base + i], 1), :] for i in range(8)]
        out_ref[pl.ds(base, 8), :] = jnp.concatenate(lines, axis=0)
        return none

    lax.fori_loop(0, rows // 8, step, 0, unroll=4)


def unpack(dest, back, after):
    rows = dest.shape[1]
    row_len = back.shape[1]
    return pl.pallas_call(
        unpack_kernel,
        grid=(1,),
        in_specs=[pl.BlockSpec(memory_space=pltpu.SMEM), whole(back.shape)]
        + [anywhere] * len(after),
        out_specs=whole((rows, row_len)),
        out_shape=jax.ShapeDtypeStruct((rows, row_len), F32),
        compiler_params=params(10),
        cost_estimate=cost(rows * 128, 8 * rows * row_len),
        name="unpack",
    )(dest, back, *after)


PLANES = 2
RING = 3 * PLANES


def fluid_kernel(here_ref, xlo_ref, xhi_ref, ylo_ref, yhi_ref, speed_ref, flux_ref, *refs):
    out_ref, xfirst_ref, xlast_ref, yfirst_ref, ylast_ref, ring_ref = refs[-6:]
    index, count = pl.program_id(0), pl.num_programs(0)
    cx = (count - 1) * PLANES
    _, cy, depth = here_ref.shape
    row_len = flux_ref.shape[2]
    rows = slice(OFF, OFF + cy)

    @pl.when(index == 0)
    def _():
        ring_ref[RING - 1, rows, :] = xlo_ref[...]

    @pl.when(index < count - 1)
    def _():
        for p in range(PLANES):
            plane = index * PLANES + p
            slot = lax.rem(plane, RING)
            ring_ref[slot, rows, :] = here_ref[p]
            ring_ref[slot, OFF - 1:OFF, :] = ylo_ref[pl.ds(plane, 1), :]
            ring_ref[slot, OFF + cy:OFF + cy + 1, :] = yhi_ref[pl.ds(plane, 1), :]

    @pl.when(index == count - 1)
    def _():
        ring_ref[lax.rem(cx, RING), rows, :] = xhi_ref[...]

    rate = time_step * diffusivity

    def push(total, centre, lower, upper, speed):
        scaled = time_step * speed
        total = total + (rate + jnp.maximum(scaled, 0.0)) * (lower - centre)
        return total + (rate - jnp.minimum(scaled, 0.0)) * (upper - centre)

    def advance(p, none):
        lanes = lax.broadcasted_iota(jnp.int32, (8, depth), 1)
        first, last = lanes == 0, lanes == depth - 1
        plane = (index - 1) * PLANES + p
        mid = lax.rem(plane, RING)
        old, new = lax.rem(plane + RING - 1, RING), lax.rem(plane + 1, RING)
        for tile in range(cy // 16):
            speeds = [
                speed_ref[k, p, tile * 16:tile * 16 + 16, :].astype(F32) for k in range(3)
            ]
            for part in range(2):
                y = tile * 16 + part * 8
                at = OFF + y
                u, v, w = [s[part * 8:part * 8 + 8] for s in speeds]
                centre = ring_ref[mid, at:at + 8, :]
                total = push(
                    centre, centre, ring_ref[old, at:at + 8, :], ring_ref[new, at:at + 8, :], u
                )
                total = push(
                    total, centre, ring_ref[mid, at - 1:at + 7, :],
                    ring_ref[mid, at + 1:at + 9, :], v,
                )
                lower = jnp.where(first, 0.0, pltpu.roll(centre, 1, 1))
                upper = jnp.where(last, 0.0, pltpu.roll(centre, depth - 1, 1))
                total = push(total, centre, lower, upper, w)
                out_ref[p, y:y + 8, row_len:] = total[:, row_len:]
                out_ref[p, y:y + 8, :row_len] = (
                    total[:, :row_len] - time_step * flux_ref[p, y:y + 8, :]
                )
        yfirst_ref[pl.ds(plane, 1), :] = out_ref[p, 0:1, :]
        ylast_ref[pl.ds(plane, 1), :] = out_ref[p, cy - 1:cy, :]
        return none

    @pl.when(index > 0)
    def _():
        lax.fori_loop(0, PLANES, advance, 0)

    @pl.when(index == 1)
    def _():
        xfirst_ref[...] = out_ref[0]

    @pl.when(index == count - 1)
    def _():
        xlast_ref[...] = out_ref[PLANES - 1]


def fluid_step(temp, rims, velocity, flux, after):
    cx, cy, depth = temp.shape
    row_len = flux.shape[2]
    plane = (PLANES, cy, depth)
    steps = cx // PLANES
    face = pl.BlockSpec((cy, depth), lambda i: (0, 0))
    line = pl.BlockSpec((cx, depth), lambda i: (0, 0))
    back = lambda i: (jnp.maximum(i - 1, 0), 0, 0)
    return pl.pallas_call(
        fluid_kernel,
        grid=(steps + 1,),
        in_specs=[
            pl.BlockSpec(plane, lambda i: (jnp.minimum(i, steps - 1), 0, 0)),
            face,
            face,
            line,
            line,
            pl.BlockSpec((3, PLANES, cy, depth), lambda i: (0, jnp.maximum(i - 1, 0), 0, 0)),
            pl.BlockSpec((PLANES, cy, row_len), back),
        ]
        + [anywhere] * len(after),
        out_specs=[pl.BlockSpec(plane, back), face, face, line, line],
        out_shape=[
            jax.ShapeDtypeStruct(temp.shape, F32),
            jax.ShapeDtypeStruct((cy, depth), F32),
            jax.ShapeDtypeStruct((cy, depth), F32),
            jax.ShapeDtypeStruct((cx, depth), F32),
            jax.ShapeDtypeStruct((cx, depth), F32),
        ],
        scratch_shapes=[pltpu.VMEM((RING, cy + 2 * OFF, depth), F32)],
        compiler_params=params(61),
        cost_estimate=cost(40 * cx * cy * depth, 14 * cx * cy * depth),
        name="fluid_step",
    )(temp, *rims, velocity, flux, *after)


def body(temp_fluid, velocity, wall_old, wall_mask, owner_map, slot_map, temp_solid, material):
    cx, cy, depth = temp_fluid.shape
    row_len = wall_old.shape[2]
    sx, sy, sz = temp_solid.shape
    ndev = lax.axis_size("gx") * lax.axis_size("gy")
    rows = cx * cy
    cap = (3 * rows + ndev - 1) // ndev
    cap = -(-cap // 8) * 8
    total = ndev * cap
    rim = SSTEPS + 1

    first, last, left, right = x_faces(rim, temp_fluid, temp_solid, material)
    faces = (*neighbours(last, first, "gx"), *neighbours(right, left, "gy"))
    xlo, xhi = faces[:2]
    dest, where, codes = rank(owner_map.reshape(1, rows), slot_map, ndev, cap)
    outgoing, flux = pack(where, codes, temp_fluid, wall_old, wall_mask, cap, faces)
    incoming = lax.all_to_all(outgoing, AXES, split_axis=0, concat_axis=0, tiled=True)

    first, last = y_faces(rim, temp_solid, material, xlo, xhi, (flux,))
    ylo, yhi = neighbours(last, first, "gy")
    rims = (xlo, xhi, ylo, yhi)
    for turn in range(FSTEPS - 1):
        fluid, xfirst, xlast, yfirst, ylast = fluid_step(
            fluid if turn else temp_fluid, faces, velocity, flux, ()
        )
        faces = (*neighbours(xlast, xfirst, "gx"), *neighbours(ylast, yfirst, "gy"))

    thin = rim - 1
    heat, first, last, code = heat_sum(incoming, cap, temp_solid.shape, thin, (*faces, *rims))
    hxlo, hxhi = neighbours(last, first, "gx")
    tall = lambda cut: jnp.concatenate([hxlo[:, cut], heat[:, cut], hxhi[:, cut]], axis=0)
    hylo, hyhi = neighbours(tall(slice(sy - thin, sy)), tall(slice(0, thin)), "gy")
    solid, sigma, replies = solid_steps(
        rim, cap, temp_solid, material, rims, heat, (hxlo, hxhi, hylo, hyhi), code
    )
    returned = lax.all_to_all(
        replies.reshape(ndev, cap, sz), AXES, split_axis=0, concat_axis=0, tiled=True
    )
    fluid = fluid_step(fluid, faces, velocity, flux, (sigma,))[0]
    force = stress(sigma, sx, sy)
    wall_next = unpack(dest, returned.reshape(total, sz), (fluid, force))
    return fluid, wall_next.reshape(cx, cy, row_len), solid, force


def solution(mesh):
    placed = (
        P("gx", "gy", None),
        P(None, "gx", "gy", None),
        P("gx", "gy", None),
        P("gx", "gy", None),
        P(("gx", "gy"), None, None),
        P(("gx", "gy"), None),
        P("gx", "gy", None),
        P("gx", "gy", None),
    )
    return jax.shard_map(
        body,
        mesh=mesh,
        in_specs=placed,
        out_specs=(
            P("gx", "gy", None),
            P("gx", "gy", None),
            P("gx", "gy", None),
            P(None, "gx", "gy", None),
        ),
        check_vma=False,
    )
```

```python
import functools
import jax
import jax.numpy as jnp
from jax import lax
from jax.experimental import pallas as pl
from jax.experimental.pallas import tpu as pltpu
from jax.sharding import PartitionSpec as P

FSTEPS = 2
SSTEPS = 4
time_step = 0.1
diffusivity = 0.5
film_coef = 2.0
solid_step = 0.05
source_gain = 4.0
conduct_table = (0.4, 0.9, 1.5, 2.2)
modulus_table = (0.5, 1.0, 1.6, 2.4)
F32 = jnp.float32
BF16 = jnp.bfloat16
AXES = ("gx", "gy")
LANE = 128
PART = 16
OFF = 8


def params(mib):
    return pltpu.CompilerParams(vmem_limit_bytes=mib * 1024 * 1024)


def cost(flops, bytes_accessed):
    return pl.CostEstimate(flops=flops, bytes_accessed=bytes_accessed, transcendentals=0)


def halves(value):
    high = value.astype(BF16)
    low = (value - high.astype(F32)).astype(BF16)
    return high, low


def ones_where(test):
    return jnp.where(test, 1.0, 0.0).astype(BF16)


def neighbours(before, after, axis):
    size = lax.axis_size(axis)
    up = [(i, i + 1) for i in range(size - 1)]
    down = [(j, i) for i, j in up]
    return lax.ppermute(before, axis, up), lax.ppermute(after, axis, down)


def whole(shape):
    return pl.BlockSpec(shape, lambda i: (0,) * len(shape))


anywhere = pl.BlockSpec(memory_space=pl.ANY)
in_vmem = pl.BlockSpec(memory_space=pltpu.VMEM)
in_hbm = pl.BlockSpec(memory_space=pltpu.HBM)


def far(value):
    return pltpu.with_memory_space_constraint(value, pltpu.HBM)


def rank_kernel(cap, owner_ref, slot_ref, dest_ref, where_ref, code_ref):
    rows = owner_ref.shape[1]
    ndev = code_ref.shape[0]
    tall = cap + 8
    tri = ones_where(
        lax.broadcasted_iota(jnp.int32, (LANE, LANE), 0)
        <= lax.broadcasted_iota(jnp.int32, (LANE, LANE), 1)
    )
    names = lax.broadcasted_iota(jnp.int32, (ndev, LANE), 0)
    steps = lax.broadcasted_iota(jnp.int32, (LANE, LANE), 0)
    carry = jnp.zeros((ndev, 1), F32)
    codes = jnp.zeros((2 * ndev, LANE), F32)
    for chunk in range(rows // LANE):
        cols = slice(chunk * LANE, (chunk + 1) * LANE)
        own = owner_ref[:, cols]
        hit = jnp.where(names == own, 1.0, 0.0)
        ranks = jnp.dot(hit.astype(BF16), tri, preferred_element_type=F32) + carry
        carry = ranks[:, LANE - 1:]
        place = jnp.sum(hit * ranks, axis=0, keepdims=True).astype(jnp.int32) - 1
        dest_ref[:, cols] = own * cap + place
        where_ref[:, cols] = own * tall + place
        code = slot_ref[:, cols] + 1
        pieces = jnp.concatenate(
            [hit * (code // 32).astype(F32), hit * (code % 32).astype(F32)], axis=0
        ).astype(BF16)
        codes = codes + lax.dot_general(
            pieces, ones_where(steps == place), (((1,), (1,)), ((), ())),
            preferred_element_type=F32,
        )
    code_ref[...] = codes[:ndev] * 32.0 + codes[ndev:]


def rank(owner, slot, ndev, cap):
    rows = owner.shape[1]
    line = jax.ShapeDtypeStruct((1, rows), jnp.int32)
    return pl.pallas_call(
        functools.partial(rank_kernel, cap),
        grid=(1,),
        in_specs=[whole((1, rows))] * 2,
        out_specs=[whole((1, rows))] * 2 + [whole((ndev, LANE))],
        out_shape=[line, line, jax.ShapeDtypeStruct((ndev, LANE), F32)],
        compiler_params=params(8),
        cost_estimate=cost(8 * ndev * LANE * rows, 20 * rows),
        name="rank",
    )(owner, slot)


GROUPS = 4


def pack_kernel(cap, where_ref, code_ref, temp_ref, old_ref, mask_ref, *refs):
    out_ref, flux_ref, rhs_ref, stage_ref, sems = refs[-5:]
    rows = where_ref.shape[1]
    ndev, tall, row_len = stage_ref.shape
    flux = mask_ref[...].astype(F32) * film_coef * (temp_ref[...] - old_ref[...])
    flux_ref[...] = flux
    high, low = halves(flux.reshape(rows, row_len))
    rhs_ref[:, :row_len] = high
    rhs_ref[:, row_len:] = low
    where = where_ref[...]
    group = ndev // GROUPS
    block = group * tall
    lines = lax.broadcasted_iota(jnp.int32, (block, rows), 0)
    copies = []
    for index in range(GROUPS):
        cut = slice(index * group, (index + 1) * group)
        pick = ones_where(lines == where - index * block)
        both = jnp.dot(pick, rhs_ref[...], preferred_element_type=F32)
        both = both[:, :row_len] + both[:, row_len:]
        stage_ref[cut] = both.reshape(group, tall, row_len)
        stage_ref[cut, cap, :] = code_ref[cut, :]
        copies.append(pltpu.make_async_copy(stage_ref.at[cut], out_ref.at[cut], sems.at[index]))
        copies[-1].start()
    for copy in copies:
        copy.wait()


def pack(where, code, temp, old, mask, cap, after):
    cx, cy, _ = temp.shape
    row_len = old.shape[2]
    rows = cx * cy
    ndev = code.shape[0]
    tall = cap + 8
    return pl.pallas_call(
        functools.partial(pack_kernel, cap),
        grid=(1,),
        in_specs=[whole((1, rows)), whole(code.shape)]
        + [whole((cx, cy, row_len))] * 3
        + [anywhere] * len(after),
        out_specs=[in_hbm, whole((cx, cy, row_len))],
        out_shape=[
            pltpu.HBM((ndev, tall, row_len), F32),
            jax.ShapeDtypeStruct((cx, cy, row_len), F32),
        ],
        scratch_shapes=[
            pltpu.VMEM((rows, 2 * row_len), BF16),
            pltpu.VMEM((ndev, tall, row_len), F32),
            pltpu.SemaphoreType.DMA((GROUPS,)),
        ],
        compiler_params=params(24),
        cost_estimate=cost(4 * ndev * tall * rows * row_len, 5 * rows * row_len * 4),
        name="pack",
    )(where, code, far(temp), far(old), far(mask), *after)


def heat_kernel(cap, thin, rows_ref, *refs):
    heat_ref, first_ref, last_ref, code_ref = refs[-4:]
    ndev, tall, row_len = rows_ref.shape
    sx, sy, _ = heat_ref.shape
    slots = sx * sy
    codes = rows_ref[:, cap, :].astype(jnp.int32) - 1
    code_ref[...] = codes
    group = ndev // 4
    names = lax.broadcasted_iota(jnp.int32, (slots, tall), 0)
    total = jnp.zeros((slots, 2 * row_len), F32)
    for index in range(0, ndev, group):
        lines = rows_ref[index:index + group].reshape(group * tall, row_len)
        high, low = halves(lines)
        pick = jnp.concatenate(
            [
                jnp.where(names == codes[index + i:index + i + 1, :tall], 1.0, 0.0)
                for i in range(group)
            ],
            axis=1,
        ).astype(BF16)
        total = total + jnp.dot(
            pick, jnp.concatenate([high, low], axis=1), preferred_element_type=F32
        )
    heat = (total[:, :row_len] + total[:, row_len:]).reshape(sx, sy, row_len)
    heat_ref[...] = heat
    first_ref[...] = heat[:thin]
    last_ref[...] = heat[sx - thin:]


def heat_sum(incoming, cap, block, thin, after):
    ndev, tall, row_len = incoming.shape
    sx, sy, _ = block
    edge = (thin, sy, row_len)
    return pl.pallas_call(
        functools.partial(heat_kernel, cap, thin),
        in_specs=[in_vmem] + [anywhere] * len(after),
        out_specs=[in_vmem] * 4,
        out_shape=[
            jax.ShapeDtypeStruct(block, F32),
            jax.ShapeDtypeStruct(edge, F32),
            jax.ShapeDtypeStruct(edge, F32),
            jax.ShapeDtypeStruct((ndev, row_len), jnp.int32),
        ],
        compiler_params=params(20),
        cost_estimate=cost(4 * ndev * tall * sx * sy * row_len, 4 * ndev * tall * row_len),
        name="heat_sum",
    )(incoming, *after)


def put_rim(ref, base, slabs):
    across = ref.shape[1] // LANE
    for n, slab in enumerate(slabs):
        row = base + n // across * PART
        ref[row:row + PART, n % across * LANE:(n % across + 1) * LANE] = slab


def get_rim(ref, base, n):
    across = ref.shape[1] // LANE
    row = base + n // across * PART
    return ref[row:row + PART, n % across * LANE:(n % across + 1) * LANE]


def rim_rows(count, depth):
    across = depth // LANE
    return -(-count // across) * PART


def x_faces_kernel(rim, bottom_ref, top_ref, near_ref, far_ref, temp_ref, kind_ref,
                   low_ref, high_ref, left_ref, right_ref):
    _, cy, _ = bottom_ref.shape
    left_ref[...] = near_ref[:, 0, :]
    right_ref[...] = far_ref[:, near_ref.shape[1] - 1, :]
    sx, sy, _ = temp_ref.shape
    low_ref[:cy, :] = bottom_ref[0]
    high_ref[:cy, :] = top_ref[0]
    for ref, start in ((low_ref, 0), (high_ref, sx - rim)):
        slabs = [
            get(start + k, slice(h, h + PART))
            for get in (
                lambda x, cut: temp_ref[x, cut, :],
                lambda x, cut: kind_ref[x, cut, :].astype(F32) + 1.0,
            )
            for k in range(rim)
            for h in range(0, sy, PART)
        ]
        put_rim(ref, cy, slabs)


def x_faces(rim, fluid, temp, kind):
    cx, cy, depth = fluid.shape
    sx, sy, sz = temp.shape
    height = cy + rim_rows(2 * rim * (sy // PART), depth)
    plane = (1, cy, depth)
    return pl.pallas_call(
        functools.partial(x_faces_kernel, rim),
        grid=(1,),
        in_specs=[
            pl.BlockSpec(plane, lambda i: (0, 0, 0)),
            pl.BlockSpec(plane, lambda i: (cx - 1, 0, 0)),
            pl.BlockSpec((cx, 8, depth), lambda i: (0, 0, 0)),
            pl.BlockSpec((cx, 8, depth), lambda i: (0, cy // 8 - 1, 0)),
            whole(temp.shape),
            whole(temp.shape),
        ],
        out_specs=[whole((height, depth))] * 2 + [whole((cx, depth))] * 2,
        out_shape=[jax.ShapeDtypeStruct((height, depth), F32)] * 2
        + [jax.ShapeDtypeStruct((cx, depth), F32)] * 2,
        compiler_params=params(16),
        cost_estimate=cost(1000, 4 * 4 * height * depth),
        name="x_faces",
    )(far(fluid), far(fluid), far(fluid), far(fluid), far(temp), far(kind))


def fill_x(rim, ref, which, own, lo_ref, hi_ref):
    sx, sy, _ = own.shape
    pieces = sy // PART
    base = lo_ref.shape[0] - rim_rows(2 * rim * pieces, lo_ref.shape[1])
    ref[rim:rim + sx, OFF:OFF + sy, :] = own
    for k in range(rim):
        for h in range(pieces):
            n = (which * rim + k) * pieces + h
            cut = slice(OFF + h * PART, OFF + (h + 1) * PART)
            ref[k, cut, :] = get_rim(lo_ref, base, n)
            ref[rim + sx + k, cut, :] = get_rim(hi_ref, base, n)


def y_faces_kernel(rim, near_ref, far_ref, temp_ref, kind_ref, lo_ref, hi_ref,
                   left_ref, right_ref, state_ref):
    cx = near_ref.shape[0]
    sx, sy, _ = temp_ref.shape
    left_ref[:cx, :] = near_ref[...]
    right_ref[:cx, :] = far_ref[...]
    slabs = ([], [])
    long = state_ref.shape[1]
    state_ref[...] = jnp.zeros_like(state_ref)
    for which, own in enumerate((temp_ref[...], kind_ref[...].astype(F32) + 1.0)):
        fill_x(rim, state_ref.at[which], which, own, lo_ref, hi_ref)
        for into, start in zip(slabs, (OFF, OFF + sy - rim)):
            for k in range(rim):
                for h in range(0, long, PART):
                    into.append(state_ref[which, h:h + PART, start + k, :])
    put_rim(left_ref, cx, slabs[0])
    put_rim(right_ref, cx, slabs[1])


def y_faces(rim, near, far_side, temp, kind, lo, hi):
    cx, depth = near.shape
    sx, sy, sz = temp.shape
    long = -(-(sx + 2 * rim) // PART) * PART
    height = cx + rim_rows(2 * rim * (long // PART), depth)
    args = (near, far_side, far(temp), far(kind), lo, hi)
    return pl.pallas_call(
        functools.partial(y_faces_kernel, rim),
        grid=(1,),
        in_specs=[whole(x.shape) for x in args],
        out_specs=[whole((height, depth))] * 2 + [in_vmem],
        out_shape=[jax.ShapeDtypeStruct((height, depth), F32)] * 2
        + [jax.ShapeDtypeStruct((2, long, sy + 2 * OFF, sz), F32)],
        compiler_params=params(16),
        cost_estimate=cost(1000, 4 * 4 * height * depth),
        name="y_faces",
    )(*args)


def table(kind, values):
    out = jnp.zeros(kind.shape, F32)
    for index, value in enumerate(values):
        out = jnp.where(kind == index + 1.0, value, out)
    return out


def solid_kernel(rim, cap, state_ref, ylo_ref, yhi_ref,
                 heat_ref, hxlo_ref, hxhi_ref, hylo_ref, hyhi_ref, code_ref,
                 next_ref, sigma_ref, reply_ref, work_ref, src_ref, rhs_ref,
                 stage_ref, sems):
    sx, sy, sz = heat_ref.shape
    wide = sx + 2 * rim
    thin = rim - 1
    long = state_ref.shape[1]
    pieces = long // PART
    base = ylo_ref.shape[0] - rim_rows(2 * rim * pieces, ylo_ref.shape[1])
    temp_ref, cond_ref = work_ref.at[0], work_ref.at[1]
    work_ref, spare_ref = work_ref.at[2], work_ref
    for which in range(2):
        spare_ref[which] = state_ref[which]
        for k in range(rim):
            for h in range(pieces):
                n = (which * rim + k) * pieces + h
                cut = slice(h * PART, (h + 1) * PART)
                spare_ref[which, cut, OFF - rim + k, :] = get_rim(ylo_ref, base, n)
                spare_ref[which, cut, OFF + sy + k, :] = get_rim(yhi_ref, base, n)
    src_ref[rim:rim + sx, OFF:OFF + sy, :] = heat_ref[...]
    src_ref[1:rim, OFF:OFF + sy, :] = hxlo_ref[...]
    src_ref[rim + sx:wide - 1, OFF:OFF + sy, :] = hxhi_ref[...]
    src_ref[1:wide - 1, OFF - thin:OFF, :] = hylo_ref[...]
    src_ref[1:wide - 1, OFF + sy:OFF + sy + thin, :] = hyhi_ref[...]
    kind = cond_ref[:wide]
    sigma_ref[...] = table(kind[rim - 1:rim + sx + 1], modulus_table)
    cond_ref[:wide] = solid_step * table(kind, conduct_table)
    src_ref[...] = (solid_step * source_gain) * src_ref[...]
    height = state_ref.shape[2]
    first = lax.broadcasted_iota(jnp.int32, (height, sz), 1) == 0
    last = lax.broadcasted_iota(jnp.int32, (height, sz), 1) == sz - 1
    pair = (temp_ref, work_ref)
    for turn in range(rim - 1):
        now, later = pair[turn % 2], pair[(turn + 1) % 2]
        for x in range(1 + turn, wide - 1 - turn):
            centre = now[x]
            beside = now[x - 1] + now[x + 1]
            beside += pltpu.roll(centre, 1, 0) + pltpu.roll(centre, height - 1, 0)
            beside += jnp.where(first, 0.0, pltpu.roll(centre, 1, 1))
            beside += jnp.where(last, 0.0, pltpu.roll(centre, sz - 1, 1))
            later[x] = centre + (cond_ref[x] * (beside - 6.0 * centre) + src_ref[x])
    final = pair[(rim - 1) % 2]
    solid = final[rim:rim + sx, OFF:OFF + sy, :]
    next_ref[...] = solid
    sigma_ref[...] = sigma_ref[...] * final[rim - 1:rim + sx + 1]
    high, low = halves(solid.reshape(sx * sy, sz))
    rhs_ref[:, :sz] = high
    rhs_ref[:, sz:] = low
    slots = sx * sy
    ndev = code_ref.shape[0]
    turned = jnp.transpose(code_ref[...])
    names = lax.broadcasted_iota(jnp.int32, (cap, slots), 1)
    group = ndev // GROUPS
    for index in range(0, ndev, group):
        pick = jnp.concatenate(
            [
                ones_where(names == turned[:cap, index + i:index + i + 1])
                for i in range(group)
            ],
            axis=0,
        )
        both = jnp.dot(pick, rhs_ref[...], preferred_element_type=F32)
        lines = slice(index * cap, (index + group) * cap)
        stage_ref[lines, :] = both[:, :sz] + both[:, sz:]
        pltpu.make_async_copy(
            stage_ref.at[lines], reply_ref.at[lines], sems.at[index // group]
        ).start()
    for index in range(0, ndev, group):
        lines = slice(index * cap, (index + group) * cap)
        pltpu.make_async_copy(
            stage_ref.at[lines], reply_ref.at[lines], sems.at[index // group]
        ).wait()


def solid_steps(rim, cap, state, state_rim, heat, heat_rim, code):
    sx, sy, sz = heat.shape
    _, long, height, _ = state.shape
    total = code.shape[0] * cap
    return pl.pallas_call(
        functools.partial(solid_kernel, rim, cap),
        in_specs=[in_vmem] * 9,
        out_specs=[in_vmem, in_vmem, in_hbm],
        out_shape=[
            jax.ShapeDtypeStruct((sx, sy, sz), F32),
            jax.ShapeDtypeStruct((sx + 2, height, sz), F32),
            pltpu.HBM((total, sz), F32),
        ],
        scratch_shapes=[
            pltpu.VMEM((3, long, height, sz), F32),
            pltpu.VMEM((sx + 2 * rim, height, sz), F32),
            pltpu.VMEM((sx * sy, 2 * sz), BF16),
            pltpu.VMEM((total, sz), F32),
            pltpu.SemaphoreType.DMA((GROUPS,)),
        ],
        compiler_params=params(24),
        cost_estimate=cost(4 * total * sx * sy * sz, 4 * total * sz),
        name="solid_steps",
    )(state, *state_rim, heat, *heat_rim, code)


def stress_kernel(sigma_ref, out_ref, tick_ref):
    tick_ref[...] = jnp.zeros_like(tick_ref)
    _, sx, sy, sz = out_ref.shape
    height = sigma_ref.shape[1]
    first = lax.broadcasted_iota(jnp.int32, (height, sz), 1) == 0
    last = lax.broadcasted_iota(jnp.int32, (height, sz), 1) == sz - 1

    def plane(x, none):
        centre = sigma_ref[x + 1]
        out_ref[0, x] = 0.5 * (sigma_ref[x + 2] - sigma_ref[x])[OFF:OFF + sy]
        along = pltpu.roll(centre, height - 1, 0) - pltpu.roll(centre, 1, 0)
        out_ref[1, x] = 0.5 * along[OFF:OFF + sy]
        along = jnp.where(last, 0.0, pltpu.roll(centre, sz - 1, 1)) - jnp.where(
            first, 0.0, pltpu.roll(centre, 1, 1)
        )
        out_ref[2, x] = 0.5 * along[OFF:OFF + sy]
        return none

    lax.fori_loop(0, sx, plane, 0)


def stress(sigma, sx, sy):
    sz = sigma.shape[2]
    return pl.pallas_call(
        stress_kernel,
        grid=(1,),
        in_specs=[whole(sigma.shape)],
        out_specs=[whole((3, sx, sy, sz)), whole((8, LANE))],
        out_shape=[pltpu.HBM((3, sx, sy, sz), F32), jax.ShapeDtypeStruct((8, LANE), F32)],
        compiler_params=params(8),
        cost_estimate=cost(10 * sx * sy * sz, 16 * sx * sy * sz),
        name="stress",
    )(sigma)


def unpack_kernel(dest_ref, back_ref, *refs):
    out_ref = refs[-1]
    rows = out_ref.shape[0]

    def step(index, none):
        base = pl.multiple_of(index * 8, 8)
        lines = [back_ref[pl.ds(dest_ref[0, base + i], 1), :] for i in range(8)]
        out_ref[pl.ds(base, 8), :] = jnp.concatenate(lines, axis=0)
        return none

    lax.fori_loop(0, rows // 8, step, 0, unroll=4)


def unpack(dest, back, after):
    rows = dest.shape[1]
    row_len = back.shape[1]
    return pl.pallas_call(
        unpack_kernel,
        grid=(1,),
        in_specs=[pl.BlockSpec(memory_space=pltpu.SMEM), whole(back.shape)]
        + [anywhere] * len(after),
        out_specs=whole((rows, row_len)),
        out_shape=jax.ShapeDtypeStruct((rows, row_len), F32),
        compiler_params=params(10),
        cost_estimate=cost(rows * 128, 8 * rows * row_len),
        name="unpack",
    )(dest, back, *after)


PLANES = 2
RING = 3 * PLANES


def fluid_kernel(here_ref, xlo_ref, xhi_ref, ylo_ref, yhi_ref, speed_ref, flux_ref, *refs):
    out_ref, xfirst_ref, xlast_ref, yfirst_ref, ylast_ref, ring_ref = refs[-6:]
    index, count = pl.program_id(0), pl.num_programs(0)
    cx = (count - 1) * PLANES
    _, cy, depth = here_ref.shape
    row_len = flux_ref.shape[2]
    rows = slice(OFF, OFF + cy)

    @pl.when(index == 0)
    def _():
        ring_ref[RING - 1, rows, :] = xlo_ref[...]

    @pl.when(index < count - 1)
    def _():
        for p in range(PLANES):
            plane = index * PLANES + p
            slot = lax.rem(plane, RING)
            ring_ref[slot, rows, :] = here_ref[p]
            ring_ref[slot, OFF - 1:OFF, :] = ylo_ref[pl.ds(plane, 1), :]
            ring_ref[slot, OFF + cy:OFF + cy + 1, :] = yhi_ref[pl.ds(plane, 1), :]

    @pl.when(index == count - 1)
    def _():
        ring_ref[lax.rem(cx, RING), rows, :] = xhi_ref[...]

    rate = time_step * diffusivity

    def push(total, centre, lower, upper, speed):
        scaled = time_step * speed
        total = total + (rate + jnp.maximum(scaled, 0.0)) * (lower - centre)
        return total + (rate - jnp.minimum(scaled, 0.0)) * (upper - centre)

    def advance(p, none):
        lanes = lax.broadcasted_iota(jnp.int32, (8, depth), 1)
        first, last = lanes == 0, lanes == depth - 1
        plane = (index - 1) * PLANES + p
        mid = lax.rem(plane, RING)
        old, new = lax.rem(plane + RING - 1, RING), lax.rem(plane + 1, RING)
        for tile in range(cy // 16):
            speeds = [
                speed_ref[k, p, tile * 16:tile * 16 + 16, :].astype(F32) for k in range(3)
            ]
            for part in range(2):
                y = tile * 16 + part * 8
                at = OFF + y
                u, v, w = [s[part * 8:part * 8 + 8] for s in speeds]
                centre = ring_ref[mid, at:at + 8, :]
                total = push(
                    centre, centre, ring_ref[old, at:at + 8, :], ring_ref[new, at:at + 8, :], u
                )
                total = push(
                    total, centre, ring_ref[mid, at - 1:at + 7, :],
                    ring_ref[mid, at + 1:at + 9, :], v,
                )
                lower = jnp.where(first, 0.0, pltpu.roll(centre, 1, 1))
                upper = jnp.where(last, 0.0, pltpu.roll(centre, depth - 1, 1))
                total = push(total, centre, lower, upper, w)
                out_ref[p, y:y + 8, row_len:] = total[:, row_len:]
                out_ref[p, y:y + 8, :row_len] = (
                    total[:, :row_len] - time_step * flux_ref[p, y:y + 8, :]
                )
        yfirst_ref[pl.ds(plane, 1), :] = out_ref[p, 0:1, :]
        ylast_ref[pl.ds(plane, 1), :] = out_ref[p, cy - 1:cy, :]
        return none

    @pl.when(index > 0)
    def _():
        lax.fori_loop(0, PLANES, advance, 0)

    @pl.when(index == 1)
    def _():
        xfirst_ref[...] = out_ref[0]

    @pl.when(index == count - 1)
    def _():
        xlast_ref[...] = out_ref[PLANES - 1]


def fluid_step(temp, rims, velocity, flux, after):
    cx, cy, depth = temp.shape
    row_len = flux.shape[2]
    plane = (PLANES, cy, depth)
    steps = cx // PLANES
    face = pl.BlockSpec((cy, depth), lambda i: (0, 0))
    line = pl.BlockSpec((cx, depth), lambda i: (0, 0))
    back = lambda i: (jnp.maximum(i - 1, 0), 0, 0)
    return pl.pallas_call(
        fluid_kernel,
        grid=(steps + 1,),
        in_specs=[
            pl.BlockSpec(plane, lambda i: (jnp.minimum(i, steps - 1), 0, 0)),
            face,
            face,
            line,
            line,
            pl.BlockSpec((3, PLANES, cy, depth), lambda i: (0, jnp.maximum(i - 1, 0), 0, 0)),
            pl.BlockSpec((PLANES, cy, row_len), back),
        ]
        + [anywhere] * len(after),
        out_specs=[pl.BlockSpec(plane, back), face, face, line, line],
        out_shape=[
            pltpu.HBM(temp.shape, F32),
            jax.ShapeDtypeStruct((cy, depth), F32),
            jax.ShapeDtypeStruct((cy, depth), F32),
            jax.ShapeDtypeStruct((cx, depth), F32),
            jax.ShapeDtypeStruct((cx, depth), F32),
        ],
        scratch_shapes=[pltpu.VMEM((RING, cy + 2 * OFF, depth), F32)],
        compiler_params=params(24),
        cost_estimate=cost(40 * cx * cy * depth, 14 * cx * cy * depth),
        name="fluid_step",
    )(far(temp), *rims, far(velocity), flux, *after)


def body(temp_fluid, velocity, wall_old, wall_mask, owner_map, slot_map, temp_solid, material):
    cx, cy, depth = temp_fluid.shape
    row_len = wall_old.shape[2]
    sx, sy, sz = temp_solid.shape
    ndev = lax.axis_size("gx") * lax.axis_size("gy")
    rows = cx * cy
    cap = (3 * rows + ndev - 1) // ndev
    cap = -(-cap // 8) * 8
    total = ndev * cap
    rim = SSTEPS + 1

    first, last, left, right = x_faces(rim, temp_fluid, temp_solid, material)
    faces = (*neighbours(last, first, "gx"), *neighbours(right, left, "gy"))
    xlo, xhi = faces[:2]
    dest, where, codes = rank(owner_map.reshape(1, rows), slot_map, ndev, cap)
    outgoing, flux = pack(where, codes, temp_fluid, wall_old, wall_mask, cap, faces)
    incoming = lax.all_to_all(outgoing, AXES, split_axis=0, concat_axis=0, tiled=True)

    fluid, *edges = fluid_step(temp_fluid, faces, velocity, flux, ())
    first, last, left, right = edges
    left, right, state = y_faces(rim, left, right, temp_solid, material, xlo, xhi)
    faces = (*neighbours(last, first, "gx"), *neighbours(right, left, "gy"))
    rims = faces[2:]

    thin = rim - 1
    heat, first, last, code = heat_sum(incoming, cap, temp_solid.shape, thin, faces)
    hxlo, hxhi = neighbours(last, first, "gx")
    tall = lambda cut: jnp.concatenate([hxlo[:, cut], heat[:, cut], hxhi[:, cut]], axis=0)
    hylo, hyhi = neighbours(tall(slice(sy - thin, sy)), tall(slice(0, thin)), "gy")
    solid, sigma, replies = solid_steps(
        rim, cap, state, rims, heat, (hxlo, hxhi, hylo, hyhi), code
    )
    returned = lax.all_to_all(
        replies.reshape(ndev, cap, sz), AXES, split_axis=0, concat_axis=0, tiled=True
    )
    force, tick = stress(sigma, sx, sy)
    fluid, *edges = fluid_step(fluid, faces, velocity, flux, (tick,))
    wall_next = unpack(dest, returned.reshape(total, sz), edges[2:])
    return fluid, wall_next.reshape(cx, cy, row_len), solid, force


def solution(mesh):
    placed = (
        P("gx", "gy", None),
        P(None, "gx", "gy", None),
        P("gx", "gy", None),
        P("gx", "gy", None),
        P(("gx", "gy"), None, None),
        P(("gx", "gy"), None),
        P("gx", "gy", None),
        P("gx", "gy", None),
    )
    return jax.shard_map(
        body,
        mesh=mesh,
        in_specs=placed,
        out_specs=(
            P("gx", "gy", None),
            P("gx", "gy", None),
            P("gx", "gy", None),
            P(None, "gx", "gy", None),
        ),
        check_vma=False,
    )
```

```python
import functools
import jax
import jax.numpy as jnp
from jax import lax
from jax.experimental import pallas as pl
from jax.experimental.pallas import tpu as pltpu
from jax.sharding import PartitionSpec as P

FSTEPS = 2
SSTEPS = 4
time_step = 0.1
diffusivity = 0.5
film_coef = 2.0
solid_step = 0.05
source_gain = 4.0
conduct_table = (0.4, 0.9, 1.5, 2.2)
modulus_table = (0.5, 1.0, 1.6, 2.4)
F32 = jnp.float32
BF16 = jnp.bfloat16
AXES = ("gx", "gy")
LANE = 128
PART = 16
OFF = 8


def params(mib):
    return pltpu.CompilerParams(vmem_limit_bytes=mib * 1024 * 1024)


def cost(flops, bytes_accessed):
    return pl.CostEstimate(flops=flops, bytes_accessed=bytes_accessed, transcendentals=0)


def halves(value):
    high = value.astype(BF16)
    low = (value - high.astype(F32)).astype(BF16)
    return high, low


def ones_where(test):
    return jnp.where(test, 1.0, 0.0).astype(BF16)


def neighbours(before, after, axis):
    size = lax.axis_size(axis)
    up = [(i, i + 1) for i in range(size - 1)]
    down = [(j, i) for i, j in up]
    return lax.ppermute(before, axis, up), lax.ppermute(after, axis, down)


def whole(shape):
    return pl.BlockSpec(shape, lambda i: (0,) * len(shape))


anywhere = pl.BlockSpec(memory_space=pl.ANY)
in_vmem = pl.BlockSpec(memory_space=pltpu.VMEM)
in_hbm = pl.BlockSpec(memory_space=pltpu.HBM)


def far(value):
    return pltpu.with_memory_space_constraint(value, pltpu.HBM)


def near(value):
    return pltpu.with_memory_space_constraint(value, pltpu.VMEM)


def rank_kernel(cap, owner_ref, slot_ref, dest_ref, where_ref, code_ref):
    rows = owner_ref.shape[1]
    ndev = code_ref.shape[0]
    tall = cap + 8
    tri = ones_where(
        lax.broadcasted_iota(jnp.int32, (LANE, LANE), 0)
        <= lax.broadcasted_iota(jnp.int32, (LANE, LANE), 1)
    )
    names = lax.broadcasted_iota(jnp.int32, (ndev, LANE), 0)
    steps = lax.broadcasted_iota(jnp.int32, (LANE, LANE), 0)
    carry = jnp.zeros((ndev, 1), F32)
    codes = jnp.zeros((2 * ndev, LANE), F32)
    for chunk in range(rows // LANE):
        cols = slice(chunk * LANE, (chunk + 1) * LANE)
        own = owner_ref[:, cols]
        hit = jnp.where(names == own, 1.0, 0.0)
        ranks = jnp.dot(hit.astype(BF16), tri, preferred_element_type=F32) + carry
        carry = ranks[:, LANE - 1:]
        place = jnp.sum(hit * ranks, axis=0, keepdims=True).astype(jnp.int32) - 1
        dest_ref[:, cols] = own * cap + place
        where_ref[:, cols] = own * tall + place
        code = slot_ref[:, cols] + 1
        pieces = jnp.concatenate(
            [hit * (code // 32).astype(F32), hit * (code % 32).astype(F32)], axis=0
        ).astype(BF16)
        codes = codes + lax.dot_general(
            pieces, ones_where(steps == place), (((1,), (1,)), ((), ())),
            preferred_element_type=F32,
        )
    code_ref[...] = codes[:ndev] * 32.0 + codes[ndev:]


def rank(owner, slot, ndev, cap):
    rows = owner.shape[1]
    line = jax.ShapeDtypeStruct((1, rows), jnp.int32)
    return pl.pallas_call(
        functools.partial(rank_kernel, cap),
        grid=(1,),
        in_specs=[whole((1, rows))] * 2,
        out_specs=[whole((1, rows))] * 2 + [whole((ndev, LANE))],
        out_shape=[line, line, jax.ShapeDtypeStruct((ndev, LANE), F32)],
        compiler_params=params(8),
        cost_estimate=cost(8 * ndev * LANE * rows, 20 * rows),
        name="rank",
    )(owner, slot)


GROUPS = 4


def pack_kernel(cap, where_ref, code_ref, temp_ref, old_ref, mask_ref, *refs):
    out_ref, flux_ref, rhs_ref, stage_ref, sems = refs[-5:]
    rows = where_ref.shape[1]
    ndev, tall, row_len = stage_ref.shape
    flux = mask_ref[...].astype(F32) * film_coef * (temp_ref[...] - old_ref[...])
    flux_ref[...] = flux
    high, low = halves(flux.reshape(rows, row_len))
    rhs_ref[:, :row_len] = high
    rhs_ref[:, row_len:] = low
    where = where_ref[...]
    group = ndev // GROUPS
    block = group * tall
    lines = lax.broadcasted_iota(jnp.int32, (block, rows), 0)
    copies = []
    for index in range(GROUPS):
        cut = slice(index * group, (index + 1) * group)
        pick = ones_where(lines == where - index * block)
        both = jnp.dot(pick, rhs_ref[...], preferred_element_type=F32)
        both = both[:, :row_len] + both[:, row_len:]
        stage_ref[cut] = both.reshape(group, tall, row_len)
        stage_ref[cut, cap, :] = code_ref[cut, :]
        copies.append(pltpu.make_async_copy(stage_ref.at[cut], out_ref.at[cut], sems.at[index]))
        copies[-1].start()
    for copy in copies:
        copy.wait()


def pack(where, code, temp, old, mask, cap, after):
    cx, cy, _ = temp.shape
    row_len = old.shape[2]
    rows = cx * cy
    ndev = code.shape[0]
    tall = cap + 8
    return pl.pallas_call(
        functools.partial(pack_kernel, cap),
        grid=(1,),
        in_specs=[whole((1, rows)), whole(code.shape)]
        + [whole((cx, cy, row_len))] * 3
        + [anywhere] * len(after),
        out_specs=[in_hbm, whole((cx, cy, row_len))],
        out_shape=[
            pltpu.HBM((ndev, tall, row_len), F32),
            jax.ShapeDtypeStruct((cx, cy, row_len), F32),
        ],
        scratch_shapes=[
            pltpu.VMEM((rows, 2 * row_len), BF16),
            pltpu.VMEM((ndev, tall, row_len), F32),
            pltpu.SemaphoreType.DMA((GROUPS,)),
        ],
        compiler_params=params(24),
        cost_estimate=cost(4 * ndev * tall * rows * row_len, 5 * rows * row_len * 4),
        name="pack",
    )(where, code, far(temp), far(old), far(mask), *after)


def heat_kernel(cap, thin, far_ref, *refs):
    heat_ref, first_ref, last_ref, code_ref, rows_ref, sems = refs[-6:]
    ndev, tall, row_len = rows_ref.shape
    group = ndev // GROUPS
    copies = []
    for index in range(GROUPS):
        cut = slice(index * group, (index + 1) * group)
        copies.append(pltpu.make_async_copy(far_ref.at[cut], rows_ref.at[cut], sems.at[index]))
        copies[-1].start()
    sx, sy, _ = heat_ref.shape
    slots = sx * sy
    names = lax.broadcasted_iota(jnp.int32, (slots, tall), 0)
    total = jnp.zeros((slots, 2 * row_len), F32)
    for copy, index in zip(copies, range(0, ndev, group)):
        copy.wait()
        codes = rows_ref[index:index + group, cap, :].astype(jnp.int32) - 1
        code_ref[index:index + group, :] = codes
        lines = rows_ref[index:index + group].reshape(group * tall, row_len)
        high, low = halves(lines)
        pick = jnp.concatenate(
            [
                jnp.where(names == codes[i:i + 1, :tall], 1.0, 0.0)
                for i in range(group)
            ],
            axis=1,
        ).astype(BF16)
        total = total + jnp.dot(
            pick, jnp.concatenate([high, low], axis=1), preferred_element_type=F32
        )
    heat = (total[:, :row_len] + total[:, row_len:]).reshape(sx, sy, row_len)
    heat_ref[...] = heat
    first_ref[...] = heat[:thin]
    last_ref[...] = heat[sx - thin:]


def heat_sum(incoming, cap, block, thin, after):
    ndev, tall, row_len = incoming.shape
    sx, sy, _ = block
    edge = (thin, sy, row_len)
    return pl.pallas_call(
        functools.partial(heat_kernel, cap, thin),
        in_specs=[in_hbm] + [anywhere] * len(after),
        out_specs=[in_vmem] * 4,
        out_shape=[
            jax.ShapeDtypeStruct(block, F32),
            jax.ShapeDtypeStruct(edge, F32),
            jax.ShapeDtypeStruct(edge, F32),
            jax.ShapeDtypeStruct((ndev, row_len), jnp.int32),
        ],
        scratch_shapes=[
            pltpu.VMEM(incoming.shape, F32),
            pltpu.SemaphoreType.DMA((GROUPS,)),
        ],
        compiler_params=params(20),
        cost_estimate=cost(4 * ndev * tall * sx * sy * row_len, 4 * ndev * tall * row_len),
        name="heat_sum",
    )(far(incoming), *after)


def put_rim(ref, base, slabs):
    across = ref.shape[1] // LANE
    for n, slab in enumerate(slabs):
        row = base + n // across * PART
        ref[row:row + PART, n % across * LANE:(n % across + 1) * LANE] = slab


def get_rim(ref, base, n):
    across = ref.shape[1] // LANE
    row = base + n // across * PART
    return ref[row:row + PART, n % across * LANE:(n % across + 1) * LANE]


def rim_rows(count, depth):
    across = depth // LANE
    return -(-count // across) * PART


def x_faces_kernel(rim, bottom_ref, top_ref, near_ref, far_ref, temp_ref, kind_ref,
                   low_ref, high_ref, left_ref, right_ref):
    _, cy, _ = bottom_ref.shape
    left_ref[...] = near_ref[:, 0, :]
    right_ref[...] = far_ref[:, near_ref.shape[1] - 1, :]
    sx, sy, _ = temp_ref.shape
    low_ref[:cy, :] = bottom_ref[0]
    high_ref[:cy, :] = top_ref[0]
    for ref, start in ((low_ref, 0), (high_ref, sx - rim)):
        slabs = [
            get(start + k, slice(h, h + PART))
            for get in (
                lambda x, cut: temp_ref[x, cut, :],
                lambda x, cut: kind_ref[x, cut, :].astype(F32) + 1.0,
            )
            for k in range(rim)
            for h in range(0, sy, PART)
        ]
        put_rim(ref, cy, slabs)


def x_faces(rim, fluid, temp, kind):
    cx, cy, depth = fluid.shape
    sx, sy, sz = temp.shape
    height = cy + rim_rows(2 * rim * (sy // PART), depth)
    plane = (1, cy, depth)
    return pl.pallas_call(
        functools.partial(x_faces_kernel, rim),
        grid=(1,),
        in_specs=[
            pl.BlockSpec(plane, lambda i: (0, 0, 0)),
            pl.BlockSpec(plane, lambda i: (cx - 1, 0, 0)),
            pl.BlockSpec((cx, 8, depth), lambda i: (0, 0, 0)),
            pl.BlockSpec((cx, 8, depth), lambda i: (0, cy // 8 - 1, 0)),
            whole(temp.shape),
            whole(temp.shape),
        ],
        out_specs=[whole((height, depth))] * 2 + [whole((cx, depth))] * 2,
        out_shape=[jax.ShapeDtypeStruct((height, depth), F32)] * 2
        + [jax.ShapeDtypeStruct((cx, depth), F32)] * 2,
        compiler_params=params(16),
        cost_estimate=cost(1000, 4 * 4 * height * depth),
        name="x_faces",
    )(far(fluid), far(fluid), far(fluid), far(fluid), far(temp), far(kind))


def fill_x(rim, ref, which, own, lo_ref, hi_ref):
    sx, sy, _ = own.shape
    pieces = sy // PART
    base = lo_ref.shape[0] - rim_rows(2 * rim * pieces, lo_ref.shape[1])
    ref[rim:rim + sx, OFF:OFF + sy, :] = own
    for k in range(rim):
        for h in range(pieces):
            n = (which * rim + k) * pieces + h
            cut = slice(OFF + h * PART, OFF + (h + 1) * PART)
            ref[k, cut, :] = get_rim(lo_ref, base, n)
            ref[rim + sx + k, cut, :] = get_rim(hi_ref, base, n)


def y_faces_kernel(rim, near_ref, far_ref, temp_ref, kind_ref, lo_ref, hi_ref,
                   left_ref, right_ref, state_ref):
    cx = near_ref.shape[0]
    sx, sy, _ = temp_ref.shape
    left_ref[:cx, :] = near_ref[...]
    right_ref[:cx, :] = far_ref[...]
    slabs = ([], [])
    long = state_ref.shape[1]
    state_ref[...] = jnp.zeros_like(state_ref)
    for which, own in enumerate((temp_ref[...], kind_ref[...].astype(F32) + 1.0)):
        fill_x(rim, state_ref.at[which], which, own, lo_ref, hi_ref)
        for into, start in zip(slabs, (OFF, OFF + sy - rim)):
            for k in range(rim):
                for h in range(0, long, PART):
                    into.append(state_ref[which, h:h + PART, start + k, :])
    put_rim(left_ref, cx, slabs[0])
    put_rim(right_ref, cx, slabs[1])


def y_faces(rim, left, right, temp, kind, lo, hi):
    cx, depth = left.shape
    sx, sy, sz = temp.shape
    long = -(-(sx + 2 * rim) // PART) * PART
    height = cx + rim_rows(2 * rim * (long // PART), depth)
    args = (left, right, far(temp), far(kind), lo, hi)
    return pl.pallas_call(
        functools.partial(y_faces_kernel, rim),
        grid=(1,),
        in_specs=[whole(x.shape) for x in args],
        out_specs=[whole((height, depth))] * 2 + [in_vmem],
        out_shape=[jax.ShapeDtypeStruct((height, depth), F32)] * 2
        + [pltpu.VMEM((2, long, sy + 2 * OFF, sz), F32)],
        compiler_params=params(16),
        cost_estimate=cost(1000, 4 * 4 * height * depth),
        name="y_faces",
    )(*args)


def table(kind, values):
    out = jnp.zeros(kind.shape, F32)
    for index, value in enumerate(values):
        out = jnp.where(kind == index + 1.0, value, out)
    return out


def solid_kernel(rim, cap, state_ref, ylo_ref, yhi_ref,
                 heat_ref, hxlo_ref, hxhi_ref, hylo_ref, hyhi_ref, code_ref,
                 next_ref, sigma_ref, reply_ref, work_ref, src_ref, rhs_ref,
                 stage_ref, sems):
    sx, sy, sz = heat_ref.shape
    wide = sx + 2 * rim
    thin = rim - 1
    long = state_ref.shape[1]
    pieces = long // PART
    base = ylo_ref.shape[0] - rim_rows(2 * rim * pieces, ylo_ref.shape[1])
    temp_ref, cond_ref = work_ref.at[0], work_ref.at[1]
    work_ref, spare_ref = work_ref.at[2], work_ref
    for which in range(2):
        spare_ref[which] = state_ref[which]
        for k in range(rim):
            for h in range(pieces):
                n = (which * rim + k) * pieces + h
                cut = slice(h * PART, (h + 1) * PART)
                spare_ref[which, cut, OFF - rim + k, :] = get_rim(ylo_ref, base, n)
                spare_ref[which, cut, OFF + sy + k, :] = get_rim(yhi_ref, base, n)
    src_ref[rim:rim + sx, OFF:OFF + sy, :] = heat_ref[...]
    src_ref[1:rim, OFF:OFF + sy, :] = hxlo_ref[...]
    src_ref[rim + sx:wide - 1, OFF:OFF + sy, :] = hxhi_ref[...]
    src_ref[1:wide - 1, OFF - thin:OFF, :] = hylo_ref[...]
    src_ref[1:wide - 1, OFF + sy:OFF + sy + thin, :] = hyhi_ref[...]
    kind = cond_ref[:wide]
    sigma_ref[...] = table(kind[rim - 1:rim + sx + 1], modulus_table)
    cond_ref[:wide] = solid_step * table(kind, conduct_table)
    src_ref[...] = (solid_step * source_gain) * src_ref[...]
    height = state_ref.shape[2]
    first = lax.broadcasted_iota(jnp.int32, (height, sz), 1) == 0
    last = lax.broadcasted_iota(jnp.int32, (height, sz), 1) == sz - 1
    pair = (temp_ref, work_ref)
    for turn in range(rim - 1):
        now, later = pair[turn % 2], pair[(turn + 1) % 2]
        for x in range(1 + turn, wide - 1 - turn):
            centre = now[x]
            beside = now[x - 1] + now[x + 1]
            beside += pltpu.roll(centre, 1, 0) + pltpu.roll(centre, height - 1, 0)
            beside += jnp.where(first, 0.0, pltpu.roll(centre, 1, 1))
            beside += jnp.where(last, 0.0, pltpu.roll(centre, sz - 1, 1))
            later[x] = centre + (cond_ref[x] * (beside - 6.0 * centre) + src_ref[x])
    final = pair[(rim - 1) % 2]
    solid = final[rim:rim + sx, OFF:OFF + sy, :]
    next_ref[...] = solid
    sigma_ref[...] = sigma_ref[...] * final[rim - 1:rim + sx + 1]
    high, low = halves(solid.reshape(sx * sy, sz))
    rhs_ref[:, :sz] = high
    rhs_ref[:, sz:] = low
    slots = sx * sy
    ndev = code_ref.shape[0]
    turned = jnp.transpose(code_ref[...])
    names = lax.broadcasted_iota(jnp.int32, (cap, slots), 1)
    group = ndev // GROUPS
    for index in range(0, ndev, group):
        pick = jnp.concatenate(
            [
                ones_where(names == turned[:cap, index + i:index + i + 1])
                for i in range(group)
            ],
            axis=0,
        )
        both = jnp.dot(pick, rhs_ref[...], preferred_element_type=F32)
        lines = slice(index * cap, (index + group) * cap)
        stage_ref[lines, :] = both[:, :sz] + both[:, sz:]
        pltpu.make_async_copy(
            stage_ref.at[lines], reply_ref.at[lines], sems.at[index // group]
        ).start()
    for index in range(0, ndev, group):
        lines = slice(index * cap, (index + group) * cap)
        pltpu.make_async_copy(
            stage_ref.at[lines], reply_ref.at[lines], sems.at[index // group]
        ).wait()


def solid_steps(rim, cap, state, state_rim, heat, heat_rim, code):
    sx, sy, sz = heat.shape
    _, long, height, _ = state.shape
    total = code.shape[0] * cap
    return pl.pallas_call(
        functools.partial(solid_kernel, rim, cap),
        in_specs=[in_vmem] * 9,
        out_specs=[in_vmem, in_vmem, in_hbm],
        out_shape=[
            jax.ShapeDtypeStruct((sx, sy, sz), F32),
            jax.ShapeDtypeStruct((sx + 2, height, sz), F32),
            pltpu.HBM((total, sz), F32),
        ],
        scratch_shapes=[
            pltpu.VMEM((3, long, height, sz), F32),
            pltpu.VMEM((sx + 2 * rim, height, sz), F32),
            pltpu.VMEM((sx * sy, 2 * sz), BF16),
            pltpu.VMEM((total, sz), F32),
            pltpu.SemaphoreType.DMA((GROUPS,)),
        ],
        compiler_params=params(24),
        cost_estimate=cost(4 * total * sx * sy * sz, 4 * total * sz),
        name="solid_steps",
    )(near(state), *state_rim, heat, *heat_rim, code)


def stress_kernel(sigma_ref, out_ref, tick_ref):
    tick_ref[...] = jnp.zeros_like(tick_ref)
    _, sx, sy, sz = out_ref.shape
    height = sigma_ref.shape[1]
    first = lax.broadcasted_iota(jnp.int32, (height, sz), 1) == 0
    last = lax.broadcasted_iota(jnp.int32, (height, sz), 1) == sz - 1

    def plane(x, none):
        centre = sigma_ref[x + 1]
        out_ref[0, x] = 0.5 * (sigma_ref[x + 2] - sigma_ref[x])[OFF:OFF + sy]
        along = pltpu.roll(centre, height - 1, 0) - pltpu.roll(centre, 1, 0)
        out_ref[1, x] = 0.5 * along[OFF:OFF + sy]
        along = jnp.where(last, 0.0, pltpu.roll(centre, sz - 1, 1)) - jnp.where(
            first, 0.0, pltpu.roll(centre, 1, 1)
        )
        out_ref[2, x] = 0.5 * along[OFF:OFF + sy]
        return none

    lax.fori_loop(0, sx, plane, 0)


def stress(sigma, sx, sy):
    sz = sigma.shape[2]
    return pl.pallas_call(
        stress_kernel,
        grid=(1,),
        in_specs=[whole(sigma.shape)],
        out_specs=[whole((3, sx, sy, sz)), whole((8, LANE))],
        out_shape=[pltpu.HBM((3, sx, sy, sz), F32), jax.ShapeDtypeStruct((8, LANE), F32)],
        compiler_params=params(8),
        cost_estimate=cost(10 * sx * sy * sz, 16 * sx * sy * sz),
        name="stress",
    )(sigma)


def unpack_kernel(dest_ref, back_ref, *refs):
    out_ref = refs[-1]
    rows = out_ref.shape[0]

    def step(index, none):
        base = pl.multiple_of(index * 8, 8)
        lines = [back_ref[pl.ds(dest_ref[0, base + i], 1), :] for i in range(8)]
        out_ref[pl.ds(base, 8), :] = jnp.concatenate(lines, axis=0)
        return none

    lax.fori_loop(0, rows // 8, step, 0, unroll=4)


def unpack(dest, back, after):
    rows = dest.shape[1]
    row_len = back.shape[1]
    return pl.pallas_call(
        unpack_kernel,
        grid=(1,),
        in_specs=[pl.BlockSpec(memory_space=pltpu.SMEM), whole(back.shape)]
        + [anywhere] * len(after),
        out_specs=whole((rows, row_len)),
        out_shape=jax.ShapeDtypeStruct((rows, row_len), F32),
        compiler_params=params(10),
        cost_estimate=cost(rows * 128, 8 * rows * row_len),
        name="unpack",
    )(dest, back, *after)


PLANES = 2
RING = 3 * PLANES


def fluid_kernel(here_ref, xlo_ref, xhi_ref, ylo_ref, yhi_ref, speed_ref, flux_ref, *refs):
    out_ref, xfirst_ref, xlast_ref, yfirst_ref, ylast_ref, ring_ref = refs[-6:]
    index, count = pl.program_id(0), pl.num_programs(0)
    cx = (count - 1) * PLANES
    _, cy, depth = here_ref.shape
    row_len = flux_ref.shape[2]
    rows = slice(OFF, OFF + cy)

    @pl.when(index == 0)
    def _():
        ring_ref[RING - 1, rows, :] = xlo_ref[...]

    @pl.when(index < count - 1)
    def _():
        for p in range(PLANES):
            plane = index * PLANES + p
            slot = lax.rem(plane, RING)
            ring_ref[slot, rows, :] = here_ref[p]
            ring_ref[slot, OFF - 1:OFF, :] = ylo_ref[pl.ds(plane, 1), :]
            ring_ref[slot, OFF + cy:OFF + cy + 1, :] = yhi_ref[pl.ds(plane, 1), :]

    @pl.when(index == count - 1)
    def _():
        ring_ref[lax.rem(cx, RING), rows, :] = xhi_ref[...]

    rate = time_step * diffusivity

    def push(total, centre, lower, upper, speed):
        scaled = time_step * speed
        total = total + (rate + jnp.maximum(scaled, 0.0)) * (lower - centre)
        return total + (rate - jnp.minimum(scaled, 0.0)) * (upper - centre)

    def advance(p, none):
        lanes = lax.broadcasted_iota(jnp.int32, (8, depth), 1)
        first, last = lanes == 0, lanes == depth - 1
        plane = (index - 1) * PLANES + p
        mid = lax.rem(plane, RING)
        old, new = lax.rem(plane + RING - 1, RING), lax.rem(plane + 1, RING)
        for tile in range(cy // 16):
            speeds = [
                speed_ref[k, p, tile * 16:tile * 16 + 16, :].astype(F32) for k in range(3)
            ]
            for part in range(2):
                y = tile * 16 + part * 8
                at = OFF + y
                u, v, w = [s[part * 8:part * 8 + 8] for s in speeds]
                centre = ring_ref[mid, at:at + 8, :]
                total = push(
                    centre, centre, ring_ref[old, at:at + 8, :], ring_ref[new, at:at + 8, :], u
                )
                total = push(
                    total, centre, ring_ref[mid, at - 1:at + 7, :],
                    ring_ref[mid, at + 1:at + 9, :], v,
                )
                lower = jnp.where(first, 0.0, pltpu.roll(centre, 1, 1))
                upper = jnp.where(last, 0.0, pltpu.roll(centre, depth - 1, 1))
                total = push(total, centre, lower, upper, w)
                out_ref[p, y:y + 8, row_len:] = total[:, row_len:]
                out_ref[p, y:y + 8, :row_len] = (
                    total[:, :row_len] - time_step * flux_ref[p, y:y + 8, :]
                )
        yfirst_ref[pl.ds(plane, 1), :] = out_ref[p, 0:1, :]
        ylast_ref[pl.ds(plane, 1), :] = out_ref[p, cy - 1:cy, :]
        return none

    @pl.when(index > 0)
    def _():
        lax.fori_loop(0, PLANES, advance, 0)

    @pl.when(index == 1)
    def _():
        xfirst_ref[...] = out_ref[0]

    @pl.when(index == count - 1)
    def _():
        xlast_ref[...] = out_ref[PLANES - 1]


def fluid_step(temp, rims, velocity, flux, after):
    cx, cy, depth = temp.shape
    row_len = flux.shape[2]
    plane = (PLANES, cy, depth)
    steps = cx // PLANES
    face = pl.BlockSpec((cy, depth), lambda i: (0, 0))
    line = pl.BlockSpec((cx, depth), lambda i: (0, 0))
    back = lambda i: (jnp.maximum(i - 1, 0), 0, 0)
    return pl.pallas_call(
        fluid_kernel,
        grid=(steps + 1,),
        in_specs=[
            pl.BlockSpec(plane, lambda i: (jnp.minimum(i, steps - 1), 0, 0)),
            face,
            face,
            line,
            line,
            pl.BlockSpec((3, PLANES, cy, depth), lambda i: (0, jnp.maximum(i - 1, 0), 0, 0)),
            pl.BlockSpec((PLANES, cy, row_len), back),
        ]
        + [anywhere] * len(after),
        out_specs=[pl.BlockSpec(plane, back), face, face, line, line],
        out_shape=[
            pltpu.HBM(temp.shape, F32),
            jax.ShapeDtypeStruct((cy, depth), F32),
            jax.ShapeDtypeStruct((cy, depth), F32),
            jax.ShapeDtypeStruct((cx, depth), F32),
            jax.ShapeDtypeStruct((cx, depth), F32),
        ],
        scratch_shapes=[pltpu.VMEM((RING, cy + 2 * OFF, depth), F32)],
        compiler_params=params(24),
        cost_estimate=cost(40 * cx * cy * depth, 14 * cx * cy * depth),
        name="fluid_step",
    )(far(temp), *rims, far(velocity), flux, *after)


def body(temp_fluid, velocity, wall_old, wall_mask, owner_map, slot_map, temp_solid, material):
    cx, cy, depth = temp_fluid.shape
    row_len = wall_old.shape[2]
    sx, sy, sz = temp_solid.shape
    ndev = lax.axis_size("gx") * lax.axis_size("gy")
    rows = cx * cy
    cap = (3 * rows + ndev - 1) // ndev
    cap = -(-cap // 8) * 8
    total = ndev * cap
    rim = SSTEPS + 1

    first, last, left, right = x_faces(rim, temp_fluid, temp_solid, material)
    faces = (*neighbours(last, first, "gx"), *neighbours(right, left, "gy"))
    dest, where, codes = rank(owner_map.reshape(1, rows), slot_map, ndev, cap)
    outgoing, flux = pack(where, codes, temp_fluid, wall_old, wall_mask, cap, (first, last))
    outgoing, *faces = lax.optimization_barrier((outgoing, *faces))
    xlo, xhi = faces[:2]
    incoming = lax.all_to_all(outgoing, AXES, split_axis=0, concat_axis=0, tiled=True)

    fluid, *edges = fluid_step(temp_fluid, faces, velocity, flux, ())
    first, last, left, right = edges
    left, right, state = y_faces(rim, left, right, temp_solid, material, xlo, xhi)
    faces = (*neighbours(last, first, "gx"), *neighbours(right, left, "gy"))
    rims = faces[2:]

    thin = rim - 1
    heat, first, last, code = heat_sum(incoming, cap, temp_solid.shape, thin, faces)
    hxlo, hxhi = neighbours(last, first, "gx")
    tall = lambda cut: jnp.concatenate([hxlo[:, cut], heat[:, cut], hxhi[:, cut]], axis=0)
    hylo, hyhi = neighbours(tall(slice(sy - thin, sy)), tall(slice(0, thin)), "gy")
    solid, sigma, replies = solid_steps(
        rim, cap, state, rims, heat, (hxlo, hxhi, hylo, hyhi), code
    )
    returned = lax.all_to_all(
        replies.reshape(ndev, cap, sz), AXES, split_axis=0, concat_axis=0, tiled=True
    )
    force, tick = stress(sigma, sx, sy)
    fluid, *edges = fluid_step(fluid, faces, velocity, flux, (tick,))
    wall_next = unpack(dest, returned.reshape(total, sz), edges[2:])
    return fluid, wall_next.reshape(cx, cy, row_len), solid, force


def solution(mesh):
    placed = (
        P("gx", "gy", None),
        P(None, "gx", "gy", None),
        P("gx", "gy", None),
        P("gx", "gy", None),
        P(("gx", "gy"), None, None),
        P(("gx", "gy"), None),
        P("gx", "gy", None),
        P("gx", "gy", None),
    )
    return jax.shard_map(
        body,
        mesh=mesh,
        in_specs=placed,
        out_specs=(
            P("gx", "gy", None),
            P("gx", "gy", None),
            P("gx", "gy", None),
            P(None, "gx", "gy", None),
        ),
        check_vma=False,
    )
```

```python
import functools
import jax
import jax.numpy as jnp
from jax import lax
from jax.experimental import pallas as pl
from jax.experimental.pallas import tpu as pltpu
from jax.sharding import PartitionSpec as P

FSTEPS = 2
SSTEPS = 4
time_step = 0.1
diffusivity = 0.5
film_coef = 2.0
solid_step = 0.05
source_gain = 4.0
conduct_table = (0.4, 0.9, 1.5, 2.2)
modulus_table = (0.5, 1.0, 1.6, 2.4)
F32 = jnp.float32
BF16 = jnp.bfloat16
AXES = ("gx", "gy")
LANE = 128
PART = 16
OFF = 8


def params(mib):
    return pltpu.CompilerParams(vmem_limit_bytes=mib * 1024 * 1024)


def cost(flops, bytes_accessed):
    return pl.CostEstimate(flops=flops, bytes_accessed=bytes_accessed, transcendentals=0)


def halves(value):
    high = value.astype(BF16)
    low = (value - high.astype(F32)).astype(BF16)
    return high, low


def ones_where(test):
    return jnp.where(test, 1.0, 0.0).astype(BF16)


def neighbours(before, after, axis):
    size = lax.axis_size(axis)
    up = [(i, i + 1) for i in range(size - 1)]
    down = [(j, i) for i, j in up]
    return lax.ppermute(before, axis, up), lax.ppermute(after, axis, down)


def whole(shape):
    return pl.BlockSpec(shape, lambda i: (0,) * len(shape))


anywhere = pl.BlockSpec(memory_space=pl.ANY)
in_vmem = pl.BlockSpec(memory_space=pltpu.VMEM)
in_hbm = pl.BlockSpec(memory_space=pltpu.HBM)


def far(value):
    return pltpu.with_memory_space_constraint(value, pltpu.HBM)


def near(value):
    return pltpu.with_memory_space_constraint(value, pltpu.VMEM)


def rank_kernel(cap, owner_ref, slot_ref, dest_ref, where_ref, code_ref):
    rows = owner_ref.shape[1]
    ndev = code_ref.shape[0]
    tall = cap + 8
    tri = ones_where(
        lax.broadcasted_iota(jnp.int32, (LANE, LANE), 0)
        <= lax.broadcasted_iota(jnp.int32, (LANE, LANE), 1)
    )
    names = lax.broadcasted_iota(jnp.int32, (ndev, LANE), 0)
    steps = lax.broadcasted_iota(jnp.int32, (LANE, LANE), 0)
    carry = jnp.zeros((ndev, 1), F32)
    codes = jnp.zeros((2 * ndev, LANE), F32)
    for chunk in range(rows // LANE):
        cols = slice(chunk * LANE, (chunk + 1) * LANE)
        own = owner_ref[:, cols]
        hit = jnp.where(names == own, 1.0, 0.0)
        ranks = jnp.dot(hit.astype(BF16), tri, preferred_element_type=F32) + carry
        carry = ranks[:, LANE - 1:]
        place = jnp.sum(hit * ranks, axis=0, keepdims=True).astype(jnp.int32) - 1
        dest_ref[:, cols] = own * cap + place
        where_ref[:, cols] = own * tall + place
        code = slot_ref[:, cols] + 1
        pieces = jnp.concatenate(
            [hit * (code // 32).astype(F32), hit * (code % 32).astype(F32)], axis=0
        ).astype(BF16)
        codes = codes + lax.dot_general(
            pieces, ones_where(steps == place), (((1,), (1,)), ((), ())),
            preferred_element_type=F32,
        )
    code_ref[...] = codes[:ndev] * 32.0 + codes[ndev:]


def rank(owner, slot, ndev, cap):
    rows = owner.shape[1]
    line = jax.ShapeDtypeStruct((1, rows), jnp.int32)
    return pl.pallas_call(
        functools.partial(rank_kernel, cap),
        grid=(1,),
        in_specs=[whole((1, rows))] * 2,
        out_specs=[whole((1, rows))] * 2 + [whole((ndev, LANE))],
        out_shape=[line, line, jax.ShapeDtypeStruct((ndev, LANE), F32)],
        compiler_params=params(8),
        cost_estimate=cost(8 * ndev * LANE * rows, 20 * rows),
        name="rank",
    )(owner, slot)


GROUPS = 4


def pack_kernel(cap, where_ref, code_ref, temp_ref, old_ref, mask_ref, *refs):
    out_ref, flux_ref, rhs_ref, stage_ref, sems = refs[-5:]
    rows = where_ref.shape[1]
    ndev, tall, row_len = stage_ref.shape
    flux = mask_ref[...].astype(F32) * film_coef * (temp_ref[...] - old_ref[...])
    flux_ref[...] = flux
    high, low = halves(flux.reshape(rows, row_len))
    rhs_ref[:, :row_len] = high
    rhs_ref[:, row_len:] = low
    where = where_ref[...]
    group = ndev // GROUPS
    block = group * tall
    lines = lax.broadcasted_iota(jnp.int32, (block, rows), 0)
    copies = []
    for index in range(GROUPS):
        cut = slice(index * group, (index + 1) * group)
        pick = ones_where(lines == where - index * block)
        both = jnp.dot(pick, rhs_ref[...], preferred_element_type=F32)
        both = both[:, :row_len] + both[:, row_len:]
        stage_ref[cut] = both.reshape(group, tall, row_len)
        stage_ref[cut, cap, :] = code_ref[cut, :]
        copies.append(pltpu.make_async_copy(stage_ref.at[cut], out_ref.at[cut], sems.at[index]))
        copies[-1].start()
    for copy in copies:
        copy.wait()


def pack(where, code, temp, old, mask, cap, after):
    cx, cy, _ = temp.shape
    row_len = old.shape[2]
    rows = cx * cy
    ndev = code.shape[0]
    tall = cap + 8
    return pl.pallas_call(
        functools.partial(pack_kernel, cap),
        grid=(1,),
        in_specs=[whole((1, rows)), whole(code.shape)]
        + [whole((cx, cy, row_len))] * 3
        + [anywhere] * len(after),
        out_specs=[in_hbm, whole((cx, cy, row_len))],
        out_shape=[
            pltpu.HBM((ndev, tall, row_len), F32),
            jax.ShapeDtypeStruct((cx, cy, row_len), F32),
        ],
        scratch_shapes=[
            pltpu.VMEM((rows, 2 * row_len), BF16),
            pltpu.VMEM((ndev, tall, row_len), F32),
            pltpu.SemaphoreType.DMA((GROUPS,)),
        ],
        compiler_params=params(24),
        cost_estimate=cost(4 * ndev * tall * rows * row_len, 5 * rows * row_len * 4),
        name="pack",
    )(where, code, far(temp), far(old), far(mask), *after)


def heat_kernel(cap, thin, rows_ref, xfirst_ref, xlast_ref, ylo_ref, yhi_ref,
                yfirst_ref, ylast_ref, clo_ref, chi_ref,
                heat_ref, low_ref, high_ref, left_ref, right_ref, code_ref):
    ndev, tall, row_len = rows_ref.shape
    cx, depth = yfirst_ref.shape
    sx, sy, _ = heat_ref.shape
    slots = sx * sy
    left = yfirst_ref[...] + clo_ref[...] * ylo_ref[:cx, :]
    right = ylast_ref[...] + chi_ref[...] * yhi_ref[:cx, :]
    left_ref[...] = left
    right_ref[...] = right
    edge = thin * sy
    for ref, x in ((low_ref, 0), (high_ref, cx - 1)):
        for at, line in ((edge, left[x:x + 1]), (edge + depth // LANE, right[x:x + 1])):
            for i in range(depth // LANE):
                ref[at + i:at + i + 1, :] = line[:, i * LANE:(i + 1) * LANE]
    codes = rows_ref[:, cap, :].astype(jnp.int32) - 1
    code_ref[...] = codes
    group = ndev // GROUPS
    names = lax.broadcasted_iota(jnp.int32, (slots, tall), 0)
    total = jnp.zeros((slots, 2 * row_len), F32)
    for index in range(0, ndev, group):
        lines = rows_ref[index:index + group].reshape(group * tall, row_len)
        high, low = halves(lines)
        pick = jnp.concatenate(
            [
                jnp.where(names == codes[index + i:index + i + 1, :tall], 1.0, 0.0)
                for i in range(group)
            ],
            axis=1,
        ).astype(BF16)
        total = total + jnp.dot(
            pick, jnp.concatenate([high, low], axis=1), preferred_element_type=F32
        )
    heat = total[:, :row_len] + total[:, row_len:]
    heat_ref[...] = heat.reshape(sx, sy, row_len)
    low_ref[:edge, :] = heat[:edge]
    high_ref[:edge, :] = heat[slots - edge:]


def heat_sum(incoming, cap, block, thin, faces, edges):
    ndev, tall, row_len = incoming.shape
    sx, sy, _ = block
    line = edges[2].shape
    edge = (thin * sy + 2 * (line[1] // LANE), row_len)
    return pl.pallas_call(
        functools.partial(heat_kernel, cap, thin),
        in_specs=[in_vmem] + [anywhere] * 2 + [in_vmem] * 6,
        out_specs=[in_vmem] * 6,
        out_shape=[
            jax.ShapeDtypeStruct(block, F32),
            jax.ShapeDtypeStruct(edge, F32),
            jax.ShapeDtypeStruct(edge, F32),
            jax.ShapeDtypeStruct(line, F32),
            jax.ShapeDtypeStruct(line, F32),
            jax.ShapeDtypeStruct((ndev, row_len), jnp.int32),
        ],
        compiler_params=params(20),
        cost_estimate=cost(4 * ndev * tall * sx * sy * row_len, 4 * ndev * tall * row_len),
        name="heat_sum",
    )(near(incoming), *faces, *edges)


def put_rim(ref, base, slabs):
    across = ref.shape[1] // LANE
    for n, slab in enumerate(slabs):
        row = base + n // across * PART
        ref[row:row + PART, n % across * LANE:(n % across + 1) * LANE] = slab


def get_rim(ref, base, n):
    across = ref.shape[1] // LANE
    row = base + n // across * PART
    return ref[row:row + PART, n % across * LANE:(n % across + 1) * LANE]


def rim_rows(count, depth):
    across = depth // LANE
    return -(-count // across) * PART


def x_faces_kernel(rim, bottom_ref, top_ref, near_ref, far_ref, temp_ref, kind_ref,
                   low_ref, high_ref, left_ref, right_ref):
    _, cy, _ = bottom_ref.shape
    left_ref[...] = near_ref[:, 0, :]
    right_ref[...] = far_ref[:, near_ref.shape[1] - 1, :]
    sx, sy, _ = temp_ref.shape
    low_ref[:cy, :] = bottom_ref[0]
    high_ref[:cy, :] = top_ref[0]
    for ref, start in ((low_ref, 0), (high_ref, sx - rim)):
        slabs = [
            get(start + k, slice(h, h + PART))
            for get in (
                lambda x, cut: temp_ref[x, cut, :],
                lambda x, cut: kind_ref[x, cut, :].astype(F32) + 1.0,
            )
            for k in range(rim)
            for h in range(0, sy, PART)
        ]
        put_rim(ref, cy, slabs)


def x_faces(rim, fluid, temp, kind):
    cx, cy, depth = fluid.shape
    sx, sy, sz = temp.shape
    height = cy + rim_rows(2 * rim * (sy // PART), depth)
    plane = (1, cy, depth)
    return pl.pallas_call(
        functools.partial(x_faces_kernel, rim),
        grid=(1,),
        in_specs=[
            pl.BlockSpec(plane, lambda i: (0, 0, 0)),
            pl.BlockSpec(plane, lambda i: (cx - 1, 0, 0)),
            pl.BlockSpec((cx, 8, depth), lambda i: (0, 0, 0)),
            pl.BlockSpec((cx, 8, depth), lambda i: (0, cy // 8 - 1, 0)),
            whole(temp.shape),
            whole(temp.shape),
        ],
        out_specs=[whole((height, depth))] * 2 + [whole((cx, depth))] * 2,
        out_shape=[jax.ShapeDtypeStruct((height, depth), F32)] * 2
        + [jax.ShapeDtypeStruct((cx, depth), F32)] * 2,
        compiler_params=params(16),
        cost_estimate=cost(1000, 4 * 4 * height * depth),
        name="x_faces",
    )(far(fluid), far(fluid), far(fluid), far(fluid), far(temp), far(kind))


def fill_x(rim, ref, which, own, lo_ref, hi_ref):
    sx, sy, _ = own.shape
    pieces = sy // PART
    base = lo_ref.shape[0] - rim_rows(2 * rim * pieces, lo_ref.shape[1])
    ref[rim:rim + sx, OFF:OFF + sy, :] = own
    for k in range(rim):
        for h in range(pieces):
            n = (which * rim + k) * pieces + h
            cut = slice(OFF + h * PART, OFF + (h + 1) * PART)
            ref[k, cut, :] = get_rim(lo_ref, base, n)
            ref[rim + sx + k, cut, :] = get_rim(hi_ref, base, n)


def y_faces_kernel(rim, near_ref, far_ref, temp_ref, kind_ref, lo_ref, hi_ref,
                   left_ref, right_ref, state_ref):
    cx = near_ref.shape[0]
    sx, sy, _ = temp_ref.shape
    left_ref[:cx, :] = near_ref[...]
    right_ref[:cx, :] = far_ref[...]
    slabs = ([], [])
    long = state_ref.shape[1]
    state_ref[...] = jnp.zeros_like(state_ref)
    for which, own in enumerate((temp_ref[...], kind_ref[...].astype(F32) + 1.0)):
        fill_x(rim, state_ref.at[which], which, own, lo_ref, hi_ref)
        for into, start in zip(slabs, (OFF, OFF + sy - rim)):
            for k in range(rim):
                for h in range(0, long, PART):
                    into.append(state_ref[which, h:h + PART, start + k, :])
    put_rim(left_ref, cx, slabs[0])
    put_rim(right_ref, cx, slabs[1])


def y_faces(rim, left, right, temp, kind, lo, hi):
    cx, depth = left.shape
    sx, sy, sz = temp.shape
    long = -(-(sx + 2 * rim) // PART) * PART
    height = cx + rim_rows(2 * rim * (long // PART), depth)
    args = (left, right, far(temp), far(kind), lo, hi)
    return pl.pallas_call(
        functools.partial(y_faces_kernel, rim),
        grid=(1,),
        in_specs=[whole(x.shape) for x in args],
        out_specs=[whole((height, depth))] * 2 + [whole((2, long, sy + 2 * OFF, sz))],
        out_shape=[jax.ShapeDtypeStruct((height, depth), F32)] * 2
        + [pltpu.HBM((2, long, sy + 2 * OFF, sz), F32)],
        compiler_params=params(16),
        cost_estimate=cost(1000, 4 * 4 * height * depth),
        name="y_faces",
    )(*args)


def strips_kernel(thin, heat_ref, lo_ref, hi_ref, near_ref, away_ref,
                  left_ref, right_ref, work_ref):
    cx = near_ref.shape[0]
    sx, sy, sz = heat_ref.shape
    edge = thin * sy
    left_ref[:cx, :] = near_ref[...]
    right_ref[:cx, :] = away_ref[...]
    work_ref[...] = jnp.zeros_like(work_ref)
    work_ref[:thin] = lo_ref[:edge, :].reshape(thin, sy, sz)
    work_ref[thin:thin + sx] = heat_ref[...]
    work_ref[thin + sx:2 * thin + sx] = hi_ref[:edge, :].reshape(thin, sy, sz)
    long = work_ref.shape[0]
    for ref, start in ((left_ref, 0), (right_ref, sy - thin)):
        slabs = [
            work_ref[h:h + PART, start + k, :] for k in range(thin) for h in range(0, long, PART)
        ]
        put_rim(ref, cx, slabs)


def strips(thin, heat, lo, hi, left, right):
    cx, depth = left.shape
    sx, sy, sz = heat.shape
    long = -(-(sx + 2 * thin) // PART) * PART
    height = cx + rim_rows(thin * (long // PART), depth)
    return pl.pallas_call(
        functools.partial(strips_kernel, thin),
        in_specs=[in_vmem] * 5,
        out_specs=[in_vmem] * 2,
        out_shape=[jax.ShapeDtypeStruct((height, depth), F32)] * 2,
        scratch_shapes=[pltpu.VMEM((long, sy, sz), F32)],
        compiler_params=params(8),
        cost_estimate=cost(1000, 16 * height * depth),
        name="strips",
    )(heat, lo, hi, left, right)


def table(kind, values):
    out = jnp.zeros(kind.shape, F32)
    for index, value in enumerate(values):
        out = jnp.where(kind == index + 1.0, value, out)
    return out


def solid_kernel(rim, cap, state_ref, ylo_ref, yhi_ref,
                 heat_ref, hxlo_ref, hxhi_ref, hylo_ref, hyhi_ref, code_ref,
                 next_ref, sigma_ref, reply_ref, work_ref, src_ref, rhs_ref,
                 pick_ref, stage_ref, load, sems):
    sx, sy, sz = heat_ref.shape
    ndev = code_ref.shape[0]
    slots = sx * sy
    wide = sx + 2 * rim
    thin = rim - 1
    long = state_ref.shape[1]
    pieces = long // PART
    loading = pltpu.make_async_copy(state_ref, work_ref.at[:2], load)
    loading.start()
    turned = jnp.transpose(code_ref[...])
    names = lax.broadcasted_iota(jnp.int32, (cap, slots), 1)
    for source in range(ndev):
        pick_ref[source * cap:(source + 1) * cap, :] = ones_where(
            names == turned[:cap, source:source + 1]
        )
    edge = thin * sy
    src_ref[rim:rim + sx, OFF:OFF + sy, :] = heat_ref[...]
    src_ref[1:rim, OFF:OFF + sy, :] = hxlo_ref[:edge, :].reshape(thin, sy, sz)
    src_ref[rim + sx:wide - 1, OFF:OFF + sy, :] = hxhi_ref[:edge, :].reshape(thin, sy, sz)
    parts = -(-(sx + 2 * thin) // PART)
    base = hylo_ref.shape[0] - rim_rows(thin * parts, hylo_ref.shape[1])
    for k in range(thin):
        for h in range(parts):
            n = k * parts + h
            count = min(PART, sx + 2 * thin - h * PART)
            cut = slice(1 + h * PART, 1 + h * PART + count)
            src_ref[cut, OFF - thin + k, :] = get_rim(hylo_ref, base, n)[:count]
            src_ref[cut, OFF + sy + k, :] = get_rim(hyhi_ref, base, n)[:count]
    loading.wait()
    base = ylo_ref.shape[0] - rim_rows(2 * rim * pieces, ylo_ref.shape[1])
    for which in range(2):
        for k in range(rim):
            for h in range(pieces):
                n = (which * rim + k) * pieces + h
                cut = slice(h * PART, (h + 1) * PART)
                work_ref[which, cut, OFF - rim + k, :] = get_rim(ylo_ref, base, n)
                work_ref[which, cut, OFF + sy + k, :] = get_rim(yhi_ref, base, n)
    temp_ref, cond_ref, work_ref = work_ref.at[0], work_ref.at[1], work_ref.at[2]
    kind = cond_ref[:wide]
    sigma_ref[...] = table(kind[rim - 1:rim + sx + 1], modulus_table)
    cond_ref[:wide] = solid_step * table(kind, conduct_table)
    src_ref[...] = (solid_step * source_gain) * src_ref[...]
    height = state_ref.shape[2]
    first = lax.broadcasted_iota(jnp.int32, (height, sz), 1) == 0
    last = lax.broadcasted_iota(jnp.int32, (height, sz), 1) == sz - 1
    pair = (temp_ref, work_ref)
    for turn in range(rim - 1):
        now, later = pair[turn % 2], pair[(turn + 1) % 2]
        for x in range(1 + turn, wide - 1 - turn):
            centre = now[x]
            beside = now[x - 1] + now[x + 1]
            beside += pltpu.roll(centre, 1, 0) + pltpu.roll(centre, height - 1, 0)
            beside += jnp.where(first, 0.0, pltpu.roll(centre, 1, 1))
            beside += jnp.where(last, 0.0, pltpu.roll(centre, sz - 1, 1))
            later[x] = centre + (cond_ref[x] * (beside - 6.0 * centre) + src_ref[x])
    final = pair[(rim - 1) % 2]
    solid = final[rim:rim + sx, OFF:OFF + sy, :]
    next_ref[...] = solid
    sigma_ref[...] = sigma_ref[...] * final[rim - 1:rim + sx + 1]
    high, low = halves(solid.reshape(sx * sy, sz))
    rhs_ref[:, :sz] = high
    rhs_ref[:, sz:] = low
    block = ndev // GROUPS * cap
    copies = []
    for index in range(GROUPS):
        cut = slice(index * block, (index + 1) * block)
        both = jnp.dot(pick_ref[cut, :], rhs_ref[...], preferred_element_type=F32)
        stage_ref[cut, :] = both[:, :sz] + both[:, sz:]
        copies.append(pltpu.make_async_copy(stage_ref.at[cut], reply_ref.at[cut], sems.at[index]))
        copies[-1].start()
    for copy in copies:
        copy.wait()


def solid_steps(rim, cap, state, state_rim, heat, heat_rim, code):
    sx, sy, sz = heat.shape
    _, long, height, _ = state.shape
    total = code.shape[0] * cap
    return pl.pallas_call(
        functools.partial(solid_kernel, rim, cap),
        in_specs=[in_hbm] + [in_vmem] * 8,
        out_specs=[in_vmem, in_vmem, in_hbm],
        out_shape=[
            jax.ShapeDtypeStruct((sx, sy, sz), F32),
            jax.ShapeDtypeStruct((sx + 2, height, sz), F32),
            pltpu.HBM((total, sz), F32),
        ],
        scratch_shapes=[
            pltpu.VMEM((3, long, height, sz), F32),
            pltpu.VMEM((sx + 2 * rim, height, sz), F32),
            pltpu.VMEM((sx * sy, 2 * sz), BF16),
            pltpu.VMEM((total, sx * sy), BF16),
            pltpu.VMEM((total, sz), F32),
            pltpu.SemaphoreType.DMA,
            pltpu.SemaphoreType.DMA((GROUPS,)),
        ],
        compiler_params=params(24),
        cost_estimate=cost(4 * total * sx * sy * sz, 4 * total * sz),
        name="solid_steps",
    )(far(state), *state_rim, heat, *heat_rim, code)


def stress_kernel(sigma_ref, out_ref, tick_ref):
    tick_ref[...] = jnp.zeros_like(tick_ref)
    _, sx, sy, sz = out_ref.shape
    height = sigma_ref.shape[1]
    first = lax.broadcasted_iota(jnp.int32, (height, sz), 1) == 0
    last = lax.broadcasted_iota(jnp.int32, (height, sz), 1) == sz - 1

    def plane(x, none):
        centre = sigma_ref[x + 1]
        out_ref[0, x] = 0.5 * (sigma_ref[x + 2] - sigma_ref[x])[OFF:OFF + sy]
        along = pltpu.roll(centre, height - 1, 0) - pltpu.roll(centre, 1, 0)
        out_ref[1, x] = 0.5 * along[OFF:OFF + sy]
        along = jnp.where(last, 0.0, pltpu.roll(centre, sz - 1, 1)) - jnp.where(
            first, 0.0, pltpu.roll(centre, 1, 1)
        )
        out_ref[2, x] = 0.5 * along[OFF:OFF + sy]
        return none

    lax.fori_loop(0, sx, plane, 0)


def stress(sigma, sx, sy):
    sz = sigma.shape[2]
    return pl.pallas_call(
        stress_kernel,
        grid=(1,),
        in_specs=[whole(sigma.shape)],
        out_specs=[whole((3, sx, sy, sz)), whole((8, LANE))],
        out_shape=[pltpu.HBM((3, sx, sy, sz), F32), jax.ShapeDtypeStruct((8, LANE), F32)],
        compiler_params=params(8),
        cost_estimate=cost(10 * sx * sy * sz, 16 * sx * sy * sz),
        name="stress",
    )(sigma)


def unpack_kernel(dest_ref, back_ref, *refs):
    out_ref = refs[-1]
    rows = out_ref.shape[0]

    def step(index, none):
        base = pl.multiple_of(index * 8, 8)
        lines = [back_ref[pl.ds(dest_ref[0, base + i], 1), :] for i in range(8)]
        out_ref[pl.ds(base, 8), :] = jnp.concatenate(lines, axis=0)
        return none

    lax.fori_loop(0, rows // 8, step, 0, unroll=4)


def unpack(dest, back, after):
    rows = dest.shape[1]
    row_len = back.shape[1]
    return pl.pallas_call(
        unpack_kernel,
        grid=(1,),
        in_specs=[pl.BlockSpec(memory_space=pltpu.SMEM), whole(back.shape)]
        + [anywhere] * len(after),
        out_specs=whole((rows, row_len)),
        out_shape=jax.ShapeDtypeStruct((rows, row_len), F32),
        compiler_params=params(10),
        cost_estimate=cost(rows * 128, 8 * rows * row_len),
        name="unpack",
    )(dest, back, *after)


PLANES = 2
RING = 3 * PLANES


def fluid_kernel(opening, here_ref, xlo_ref, xhi_ref, speed_ref, flux_ref, *refs):
    index, count = pl.program_id(0), pl.num_programs(0)
    cx = (count - 1) * PLANES
    _, cy, depth = here_ref.shape
    row_len = flux_ref.shape[2]
    rows = slice(OFF, OFF + cy)
    if opening:
        out_ref, xfirst_ref, xlast_ref, yfirst_ref, ylast_ref, clo_ref, chi_ref, ring_ref = refs
    else:
        lo_ref, hi_ref, left_ref, right_ref, ylo_ref, yhi_ref = refs[:6]
        out_ref, tick_ref, ring_ref = refs[-3:]
        tick_ref[...] = jnp.zeros_like(tick_ref)

    def patch(slot, corner_ref):
        wide = depth // LANE
        base = corner_ref.shape[0] - 2 * wide
        for row, at in ((OFF, base), (OFF + cy - 1, base + wide)):
            for i in range(wide):
                ring_ref[slot, row:row + 1, i * LANE:(i + 1) * LANE] = (
                    corner_ref[at + i:at + i + 1, :]
                )

    @pl.when(index == 0)
    def _():
        ring_ref[RING - 1, rows, :] = xlo_ref[...]
        if opening:
            for slot in range(RING):
                ring_ref[slot, OFF - 8:OFF, :] = jnp.zeros((8, depth), F32)
                ring_ref[slot, OFF + cy:OFF + cy + 8, :] = jnp.zeros((8, depth), F32)
        else:
            patch(RING - 1, lo_ref)

    @pl.when(index < count - 1)
    def _():
        for p in range(PLANES):
            plane = index * PLANES + p
            slot = lax.rem(plane, RING)
            ring_ref[slot, rows, :] = here_ref[p]
            if not opening:
                one = pl.ds(plane, 1)
                ring_ref[slot, OFF:OFF + 1, :] = left_ref[one, :]
                ring_ref[slot, OFF + cy - 1:OFF + cy, :] = right_ref[one, :]
                ring_ref[slot, OFF - 1:OFF, :] = ylo_ref[one, :]
                ring_ref[slot, OFF + cy:OFF + cy + 1, :] = yhi_ref[one, :]

    @pl.when(index == count - 1)
    def _():
        ring_ref[lax.rem(cx, RING), rows, :] = xhi_ref[...]
        if not opening:
            patch(lax.rem(cx, RING), hi_ref)

    rate = time_step * diffusivity

    def push(total, centre, lower, upper, speed):
        scaled = time_step * speed
        total = total + (rate + jnp.maximum(scaled, 0.0)) * (lower - centre)
        return total + (rate - jnp.minimum(scaled, 0.0)) * (upper - centre)

    def advance(p, none):
        lanes = lax.broadcasted_iota(jnp.int32, (8, depth), 1)
        first, last = lanes == 0, lanes == depth - 1
        plane = (index - 1) * PLANES + p
        mid = lax.rem(plane, RING)
        old, new = lax.rem(plane + RING - 1, RING), lax.rem(plane + 1, RING)
        for tile in range(cy // 16):
            speeds = [
                speed_ref[k, p, tile * 16:tile * 16 + 16, :].astype(F32) for k in range(3)
            ]
            for part in range(2):
                y = tile * 16 + part * 8
                at = OFF + y
                u, v, w = [s[part * 8:part * 8 + 8] for s in speeds]
                centre = ring_ref[mid, at:at + 8, :]
                total = push(
                    centre, centre, ring_ref[old, at:at + 8, :], ring_ref[new, at:at + 8, :], u
                )
                total = push(
                    total, centre, ring_ref[mid, at - 1:at + 7, :],
                    ring_ref[mid, at + 1:at + 9, :], v,
                )
                lower = jnp.where(first, 0.0, pltpu.roll(centre, 1, 1))
                upper = jnp.where(last, 0.0, pltpu.roll(centre, depth - 1, 1))
                total = push(total, centre, lower, upper, w)
                out_ref[p, y:y + 8, row_len:] = total[:, row_len:]
                out_ref[p, y:y + 8, :row_len] = (
                    total[:, :row_len] - time_step * flux_ref[p, y:y + 8, :]
                )
        if opening:
            one = pl.ds(plane, 1)
            yfirst_ref[one, :] = out_ref[p, 0:1, :]
            ylast_ref[one, :] = out_ref[p, cy - 1:cy, :]
            edge = time_step * speed_ref[1, p, 0:16, :].astype(F32)
            clo_ref[one, :] = rate + jnp.maximum(edge[0:1], 0.0)
            edge = time_step * speed_ref[1, p, cy - 16:cy, :].astype(F32)
            chi_ref[one, :] = rate - jnp.minimum(edge[15:16], 0.0)
        return none

    @pl.when(index > 0)
    def _():
        lax.fori_loop(0, PLANES, advance, 0)

    if opening:

        @pl.when(index == 1)
        def _():
            xfirst_ref[...] = out_ref[0]

        @pl.when(index == count - 1)
        def _():
            xlast_ref[...] = out_ref[PLANES - 1]


def fluid_step(opening, temp, sides, velocity, flux, lines, after):
    cx, cy, depth = temp.shape
    row_len = flux.shape[2]
    plane = (PLANES, cy, depth)
    steps = cx // PLANES
    face = pl.BlockSpec((cy, depth), lambda i: (0, 0))
    line = pl.BlockSpec((cx, depth), lambda i: (0, 0))
    back = lambda i: (jnp.maximum(i - 1, 0), 0, 0)
    shape = jax.ShapeDtypeStruct
    outs = [pl.BlockSpec(plane, back)]
    outs += [face, face] + [line] * 4 if opening else [whole((8, LANE))]
    shapes = [pltpu.HBM(temp.shape, F32)]
    if opening:
        shapes += [shape((cy, depth), F32)] * 2 + [shape((cx, depth), F32)] * 4
    else:
        shapes += [shape((8, LANE), F32)]
    extra = [whole(x.shape) for x in lines[:2]] + [line] * len(lines[2:])
    return pl.pallas_call(
        functools.partial(fluid_kernel, opening),
        grid=(steps + 1,),
        in_specs=[
            pl.BlockSpec(plane, lambda i: (jnp.minimum(i, steps - 1), 0, 0)),
            face,
            face,
            pl.BlockSpec((3, PLANES, cy, depth), lambda i: (0, jnp.maximum(i - 1, 0), 0, 0)),
            pl.BlockSpec((PLANES, cy, row_len), back),
        ]
        + extra
        + [anywhere] * len(after),
        out_specs=outs,
        out_shape=shapes,
        scratch_shapes=[pltpu.VMEM((RING, cy + 2 * OFF, depth), F32)],
        compiler_params=params(24),
        cost_estimate=cost(40 * cx * cy * depth, 14 * cx * cy * depth),
        name="fluid_step",
    )(far(temp), *sides, far(velocity), flux, *lines, *after)


def body(temp_fluid, velocity, wall_old, wall_mask, owner_map, slot_map, temp_solid, material):
    cx, cy, depth = temp_fluid.shape
    row_len = wall_old.shape[2]
    sx, sy, sz = temp_solid.shape
    ndev = lax.axis_size("gx") * lax.axis_size("gy")
    rows = cx * cy
    cap = (3 * rows + ndev - 1) // ndev
    cap = -(-cap // 8) * 8
    total = ndev * cap
    rim = SSTEPS + 1

    first, last, left, right = x_faces(rim, temp_fluid, temp_solid, material)
    xlo, xhi = neighbours(last, first, "gx")
    dest, where, codes = rank(owner_map.reshape(1, rows), slot_map, ndev, cap)
    outgoing, flux = pack(where, codes, temp_fluid, wall_old, wall_mask, cap, (first, last))
    outgoing, xlo, xhi = lax.optimization_barrier((outgoing, xlo, xhi))
    incoming = lax.all_to_all(outgoing, AXES, split_axis=0, concat_axis=0, tiled=True)

    left, right, state = y_faces(rim, left, right, temp_solid, material, xlo, xhi)
    ylo, yhi = neighbours(right, left, "gy")
    fluid, first, last, *edges = fluid_step(
        True, temp_fluid, (xlo, xhi), velocity, flux, (), ()
    )
    sides = neighbours(last, first, "gx")

    thin = rim - 1
    heat, first, last, left, right, code = heat_sum(
        incoming, cap, temp_solid.shape, thin, sides, (ylo, yhi, *edges)
    )
    hxlo, hxhi = neighbours(last, first, "gx")
    first, last = strips(thin, heat, hxlo, hxhi, left, right)
    hylo, hyhi = neighbours(last, first, "gy")
    solid, sigma, replies = solid_steps(
        rim, cap, state, (ylo, yhi), heat, (hxlo, hxhi, hylo, hyhi), code
    )
    returned = lax.all_to_all(
        replies.reshape(ndev, cap, sz), AXES, split_axis=0, concat_axis=0, tiled=True
    )
    force, tick = stress(sigma, sx, sy)
    fluid, tick = fluid_step(
        False, fluid, sides, velocity, flux, (hxlo, hxhi, left, right, hylo, hyhi), (tick,)
    )
    wall_next = unpack(dest, returned.reshape(total, sz), (tick,))
    return fluid, wall_next.reshape(cx, cy, row_len), solid, force


def solution(mesh):
    placed = (
        P("gx", "gy", None),
        P(None, "gx", "gy", None),
        P("gx", "gy", None),
        P("gx", "gy", None),
        P(("gx", "gy"), None, None),
        P(("gx", "gy"), None),
        P("gx", "gy", None),
        P("gx", "gy", None),
    )
    return jax.shard_map(
        body,
        mesh=mesh,
        in_specs=placed,
        out_specs=(
            P("gx", "gy", None),
            P("gx", "gy", None),
            P("gx", "gy", None),
            P(None, "gx", "gy", None),
        ),
        check_vma=False,
    )
```

```python
import functools
import jax
import jax.numpy as jnp
from jax import lax
from jax.experimental import pallas as pl
from jax.experimental.pallas import tpu as pltpu
from jax.sharding import PartitionSpec as P

FSTEPS = 2
SSTEPS = 4
time_step = 0.1
diffusivity = 0.5
film_coef = 2.0
solid_step = 0.05
source_gain = 4.0
conduct_table = (0.4, 0.9, 1.5, 2.2)
modulus_table = (0.5, 1.0, 1.6, 2.4)
F32 = jnp.float32
BF16 = jnp.bfloat16
AXES = ("gx", "gy")
LANE = 128
PART = 16
OFF = 8


def params(mib):
    return pltpu.CompilerParams(vmem_limit_bytes=mib * 1024 * 1024)


def cost(flops, bytes_accessed):
    return pl.CostEstimate(flops=flops, bytes_accessed=bytes_accessed, transcendentals=0)


def halves(value):
    high = value.astype(BF16)
    low = (value - high.astype(F32)).astype(BF16)
    return high, low


def ones_where(test):
    return jnp.where(test, 1.0, 0.0).astype(BF16)


def neighbours(before, after, axis):
    size = lax.axis_size(axis)
    up = [(i, i + 1) for i in range(size - 1)]
    down = [(j, i) for i, j in up]
    return lax.ppermute(before, axis, up), lax.ppermute(after, axis, down)


def whole(shape):
    return pl.BlockSpec(shape, lambda i: (0,) * len(shape))


anywhere = pl.BlockSpec(memory_space=pl.ANY)
in_vmem = pl.BlockSpec(memory_space=pltpu.VMEM)
in_hbm = pl.BlockSpec(memory_space=pltpu.HBM)


def far(value):
    return pltpu.with_memory_space_constraint(value, pltpu.HBM)


def near(value):
    return pltpu.with_memory_space_constraint(value, pltpu.VMEM)


def triangle():
    return ones_where(
        lax.broadcasted_iota(jnp.int32, (LANE, LANE), 0)
        <= lax.broadcasted_iota(jnp.int32, (LANE, LANE), 1)
    )


def rank_kernel(ndev, cap, owner_ref, dest_ref):
    rows = owner_ref.shape[1]
    tri = triangle()
    names = lax.broadcasted_iota(jnp.int32, (ndev, LANE), 0)
    carry = jnp.zeros((ndev, 1), F32)
    for chunk in range(rows // LANE):
        cols = slice(chunk * LANE, (chunk + 1) * LANE)
        own = owner_ref[:, cols]
        hit = jnp.where(names == own, 1.0, 0.0)
        ranks = jnp.dot(hit.astype(BF16), tri, preferred_element_type=F32) + carry
        carry = ranks[:, LANE - 1:]
        place = jnp.sum(hit * ranks, axis=0, keepdims=True).astype(jnp.int32) - 1
        dest_ref[:, cols] = own * cap + place


def rank(owner, ndev, cap):
    rows = owner.shape[1]
    return pl.pallas_call(
        functools.partial(rank_kernel, ndev, cap),
        grid=(1,),
        in_specs=[whole((1, rows))],
        out_specs=whole((1, rows)),
        out_shape=jax.ShapeDtypeStruct((1, rows), jnp.int32),
        compiler_params=params(8),
        cost_estimate=cost(8 * ndev * LANE * rows, 20 * rows),
        name="rank",
    )(owner)


def columns_kernel(slots, me_ref, maps_ref, *refs):
    code_ref, hit_ref, place_ref = refs[-3:]
    ndev, rows = maps_ref.shape
    tri = triangle()
    base = me_ref[0, 0] * slots
    carry = jnp.zeros((ndev, 1), F32)
    for chunk in range(rows // LANE):
        cols = slice(chunk * LANE, (chunk + 1) * LANE)
        slot = maps_ref[:, cols] - base
        hit = jnp.where((slot >= 0) & (slot < slots), 1.0, 0.0)
        ranks = jnp.dot(hit.astype(BF16), tri, preferred_element_type=F32) + carry
        carry = ranks[:, LANE - 1:]
        hit_ref[:, cols] = jnp.where(hit > 0.0, slot + 1, 0)
        place_ref[:, cols] = jnp.where(hit > 0.0, ranks.astype(jnp.int32) - 1, -1)
    steps = lax.broadcasted_iota(jnp.int32, (LANE, rows), 0)

    def source(index, none):
        one = pl.ds(index, 1)
        code = hit_ref[one, :]
        pieces = jnp.concatenate(
            [(code >> 5).astype(F32), (code & 31).astype(F32), jnp.zeros((6, rows), F32)], axis=0
        ).astype(BF16)
        found = lax.dot_general(
            pieces, ones_where(steps == place_ref[one, :]), (((1,), (1,)), ((), ())),
            preferred_element_type=F32,
        )
        code_ref[one, :] = (found[0:1] * 32.0 + found[1:2]).astype(jnp.int32) - 1
        return none

    lax.fori_loop(0, ndev, source, 0, unroll=2)


def columns(slots, me, maps, after):
    ndev, rows = maps.shape
    return pl.pallas_call(
        functools.partial(columns_kernel, slots),
        grid=(1,),
        in_specs=[pl.BlockSpec(memory_space=pltpu.SMEM), whole(maps.shape)]
        + [anywhere] * len(after),
        out_specs=whole((ndev, LANE)),
        out_shape=jax.ShapeDtypeStruct((ndev, LANE), jnp.int32),
        scratch_shapes=[pltpu.VMEM((ndev, rows), jnp.int32)] * 2,
        compiler_params=params(16),
        cost_estimate=cost(16 * ndev * LANE * rows, 4 * ndev * rows),
        name="columns",
    )(me, maps, *after)


GROUPS = 4


def pack_kernel(where_ref, temp_ref, old_ref, mask_ref, *refs):
    out_ref, flux_ref, rhs_ref, stage_ref, sems = refs[-5:]
    rows = where_ref.shape[1]
    ndev, tall, row_len = stage_ref.shape
    flux = mask_ref[...].astype(F32) * film_coef * (temp_ref[...] - old_ref[...])
    flux_ref[...] = flux
    high, low = halves(flux.reshape(rows, row_len))
    rhs_ref[:, :row_len] = high
    rhs_ref[:, row_len:] = low
    where = where_ref[...]
    group = ndev // GROUPS
    block = group * tall
    lines = lax.broadcasted_iota(jnp.int32, (block, rows), 0)
    copies = []
    for index in range(GROUPS):
        cut = slice(index * group, (index + 1) * group)
        pick = ones_where(lines == where - index * block)
        both = jnp.dot(pick, rhs_ref[...], preferred_element_type=F32)
        both = both[:, :row_len] + both[:, row_len:]
        stage_ref[cut] = both.reshape(group, tall, row_len)
        copies.append(pltpu.make_async_copy(stage_ref.at[cut], out_ref.at[cut], sems.at[index]))
        copies[-1].start()
    for copy in copies:
        copy.wait()


def pack(where, temp, old, mask, ndev, cap, after):
    cx, cy, _ = temp.shape
    row_len = old.shape[2]
    rows = cx * cy
    tall = cap
    return pl.pallas_call(
        pack_kernel,
        grid=(1,),
        in_specs=[whole((1, rows))]
        + [whole((cx, cy, row_len))] * 3
        + [anywhere] * len(after),
        out_specs=[in_hbm, whole((cx, cy, row_len))],
        out_shape=[
            pltpu.HBM((ndev, tall, row_len), F32),
            jax.ShapeDtypeStruct((cx, cy, row_len), F32),
        ],
        scratch_shapes=[
            pltpu.VMEM((rows, 2 * row_len), BF16),
            pltpu.VMEM((ndev, tall, row_len), F32),
            pltpu.SemaphoreType.DMA((GROUPS,)),
        ],
        compiler_params=params(24),
        cost_estimate=cost(4 * ndev * tall * rows * row_len, 5 * rows * row_len * 4),
        name="pack",
    )(where, far(temp), far(old), far(mask), *after)


def heat_kernel(thin, rows_ref, code_ref, xfirst_ref, xlast_ref, ylo_ref, yhi_ref,
                yfirst_ref, ylast_ref, clo_ref, chi_ref,
                heat_ref, low_ref, high_ref, left_ref, right_ref):
    ndev, tall, row_len = rows_ref.shape
    cx, depth = yfirst_ref.shape
    sx, sy, _ = heat_ref.shape
    slots = sx * sy
    left = yfirst_ref[...] + clo_ref[...] * ylo_ref[:cx, :]
    right = ylast_ref[...] + chi_ref[...] * yhi_ref[:cx, :]
    left_ref[...] = left
    right_ref[...] = right
    edge = thin * sy
    for ref, x in ((low_ref, 0), (high_ref, cx - 1)):
        for at, line in ((edge, left[x:x + 1]), (edge + depth // LANE, right[x:x + 1])):
            for i in range(depth // LANE):
                ref[at + i:at + i + 1, :] = line[:, i * LANE:(i + 1) * LANE]
    codes = code_ref[...]
    group = ndev // GROUPS
    names = lax.broadcasted_iota(jnp.int32, (slots, tall), 0)
    total = jnp.zeros((slots, 2 * row_len), F32)
    for index in range(0, ndev, group):
        lines = rows_ref[index:index + group].reshape(group * tall, row_len)
        high, low = halves(lines)
        pick = jnp.concatenate(
            [
                jnp.where(names == codes[index + i:index + i + 1, :tall], 1.0, 0.0)
                for i in range(group)
            ],
            axis=1,
        ).astype(BF16)
        total = total + jnp.dot(
            pick, jnp.concatenate([high, low], axis=1), preferred_element_type=F32
        )
    heat = total[:, :row_len] + total[:, row_len:]
    heat_ref[...] = heat.reshape(sx, sy, row_len)
    low_ref[:edge, :] = heat[:edge]
    high_ref[:edge, :] = heat[slots - edge:]


def heat_sum(incoming, code, block, thin, faces, edges):
    ndev, tall, row_len = incoming.shape
    sx, sy, _ = block
    line = edges[2].shape
    edge = (thin * sy + 2 * (line[1] // LANE), row_len)
    return pl.pallas_call(
        functools.partial(heat_kernel, thin),
        grid=(1,),
        in_specs=[whole(incoming.shape), whole(code.shape)]
        + [anywhere] * 2
        + [whole(x.shape) for x in edges],
        out_specs=[whole(block), whole(edge), whole(edge), whole(line), whole(line)],
        out_shape=[
            jax.ShapeDtypeStruct(block, F32),
            jax.ShapeDtypeStruct(edge, F32),
            jax.ShapeDtypeStruct(edge, F32),
            jax.ShapeDtypeStruct(line, F32),
            jax.ShapeDtypeStruct(line, F32),
        ],
        compiler_params=params(20),
        cost_estimate=cost(4 * ndev * tall * sx * sy * row_len, 4 * ndev * tall * row_len),
        name="heat_sum",
    )(incoming, code, *faces, *edges)


def put_rim(ref, base, slabs):
    across = ref.shape[1] // LANE
    for n, slab in enumerate(slabs):
        row = base + n // across * PART
        ref[row:row + PART, n % across * LANE:(n % across + 1) * LANE] = slab


def get_rim(ref, base, n):
    across = ref.shape[1] // LANE
    row = base + n // across * PART
    return ref[row:row + PART, n % across * LANE:(n % across + 1) * LANE]


def rim_rows(count, depth):
    across = depth // LANE
    return -(-count // across) * PART


def x_faces_kernel(rim, bottom_ref, top_ref, near_ref, far_ref, temp_ref, kind_ref,
                   low_ref, high_ref, left_ref, right_ref):
    _, cy, _ = bottom_ref.shape
    left_ref[...] = near_ref[:, 0, :]
    right_ref[...] = far_ref[:, near_ref.shape[1] - 1, :]
    sx, sy, _ = temp_ref.shape
    low_ref[:cy, :] = bottom_ref[0]
    high_ref[:cy, :] = top_ref[0]
    for ref, start in ((low_ref, 0), (high_ref, sx - rim)):
        slabs = [
            get(start + k, slice(h, h + PART))
            for get in (
                lambda x, cut: temp_ref[x, cut, :],
                lambda x, cut: kind_ref[x, cut, :].astype(F32) + 1.0,
            )
            for k in range(rim)
            for h in range(0, sy, PART)
        ]
        put_rim(ref, cy, slabs)


def x_faces(rim, fluid, temp, kind):
    cx, cy, depth = fluid.shape
    sx, sy, sz = temp.shape
    height = cy + rim_rows(2 * rim * (sy // PART), depth)
    plane = (1, cy, depth)
    return pl.pallas_call(
        functools.partial(x_faces_kernel, rim),
        grid=(1,),
        in_specs=[
            pl.BlockSpec(plane, lambda i: (0, 0, 0)),
            pl.BlockSpec(plane, lambda i: (cx - 1, 0, 0)),
            pl.BlockSpec((cx, 8, depth), lambda i: (0, 0, 0)),
            pl.BlockSpec((cx, 8, depth), lambda i: (0, cy // 8 - 1, 0)),
            whole(temp.shape),
            whole(temp.shape),
        ],
        out_specs=[whole((height, depth))] * 2 + [whole((cx, depth))] * 2,
        out_shape=[jax.ShapeDtypeStruct((height, depth), F32)] * 2
        + [jax.ShapeDtypeStruct((cx, depth), F32)] * 2,
        compiler_params=params(16),
        cost_estimate=cost(1000, 4 * 4 * height * depth),
        name="x_faces",
    )(far(fluid), far(fluid), far(fluid), far(fluid), far(temp), far(kind))


def fill_x(rim, ref, which, own, lo_ref, hi_ref):
    sx, sy, _ = own.shape
    pieces = sy // PART
    base = lo_ref.shape[0] - rim_rows(2 * rim * pieces, lo_ref.shape[1])
    ref[rim:rim + sx, OFF:OFF + sy, :] = own
    for k in range(rim):
        for h in range(pieces):
            n = (which * rim + k) * pieces + h
            cut = slice(OFF + h * PART, OFF + (h + 1) * PART)
            ref[k, cut, :] = get_rim(lo_ref, base, n)
            ref[rim + sx + k, cut, :] = get_rim(hi_ref, base, n)


def y_faces_kernel(rim, near_ref, far_ref, temp_ref, kind_ref, lo_ref, hi_ref,
                   left_ref, right_ref, state_ref):
    cx = near_ref.shape[0]
    sx, sy, _ = temp_ref.shape
    left_ref[:cx, :] = near_ref[...]
    right_ref[:cx, :] = far_ref[...]
    slabs = ([], [])
    long = state_ref.shape[1]
    state_ref[...] = jnp.zeros_like(state_ref)
    for which, own in enumerate((temp_ref[...], kind_ref[...].astype(F32) + 1.0)):
        fill_x(rim, state_ref.at[which], which, own, lo_ref, hi_ref)
        for into, start in zip(slabs, (OFF, OFF + sy - rim)):
            for k in range(rim):
                for h in range(0, long, PART):
                    into.append(state_ref[which, h:h + PART, start + k, :])
    put_rim(left_ref, cx, slabs[0])
    put_rim(right_ref, cx, slabs[1])


def y_faces(rim, left, right, temp, kind, lo, hi):
    cx, depth = left.shape
    sx, sy, sz = temp.shape
    long = -(-(sx + 2 * rim) // PART) * PART
    height = cx + rim_rows(2 * rim * (long // PART), depth)
    args = (left, right, far(temp), far(kind), lo, hi)
    return pl.pallas_call(
        functools.partial(y_faces_kernel, rim),
        grid=(1,),
        in_specs=[whole(x.shape) for x in args],
        out_specs=[whole((height, depth))] * 2 + [whole((2, long, sy + 2 * OFF, sz))],
        out_shape=[jax.ShapeDtypeStruct((height, depth), F32)] * 2
        + [pltpu.HBM((2, long, sy + 2 * OFF, sz), F32)],
        compiler_params=params(16),
        cost_estimate=cost(1000, 4 * 4 * height * depth),
        name="y_faces",
    )(*args)


def strips_kernel(thin, heat_ref, lo_ref, hi_ref, near_ref, away_ref,
                  left_ref, right_ref, work_ref):
    cx = near_ref.shape[0]
    sx, sy, sz = heat_ref.shape
    edge = thin * sy
    left_ref[:cx, :] = near_ref[...]
    right_ref[:cx, :] = away_ref[...]
    work_ref[...] = jnp.zeros_like(work_ref)
    work_ref[:thin] = lo_ref[:edge, :].reshape(thin, sy, sz)
    work_ref[thin:thin + sx] = heat_ref[...]
    work_ref[thin + sx:2 * thin + sx] = hi_ref[:edge, :].reshape(thin, sy, sz)
    long = work_ref.shape[0]
    for ref, start in ((left_ref, 0), (right_ref, sy - thin)):
        slabs = [
            work_ref[h:h + PART, start + k, :] for k in range(thin) for h in range(0, long, PART)
        ]
        put_rim(ref, cx, slabs)


def strips(thin, heat, lo, hi, left, right):
    cx, depth = left.shape
    sx, sy, sz = heat.shape
    long = -(-(sx + 2 * thin) // PART) * PART
    height = cx + rim_rows(thin * (long // PART), depth)
    return pl.pallas_call(
        functools.partial(strips_kernel, thin),
        in_specs=[in_vmem] * 5,
        out_specs=[in_vmem] * 2,
        out_shape=[jax.ShapeDtypeStruct((height, depth), F32)] * 2,
        scratch_shapes=[pltpu.VMEM((long, sy, sz), F32)],
        compiler_params=params(8),
        cost_estimate=cost(1000, 16 * height * depth),
        name="strips",
    )(heat, lo, hi, left, right)


def table(kind, values):
    out = jnp.zeros(kind.shape, F32)
    for index, value in enumerate(values):
        out = jnp.where(kind == index + 1.0, value, out)
    return out


def solid_kernel(rim, cap, state_ref, ylo_ref, yhi_ref,
                 heat_ref, hxlo_ref, hxhi_ref, hylo_ref, hyhi_ref, code_ref,
                 next_ref, sigma_ref, reply_ref, work_ref, src_ref, rhs_ref,
                 pick_ref, stage_ref, load, sems):
    sx, sy, sz = heat_ref.shape
    ndev = code_ref.shape[0]
    slots = sx * sy
    wide = sx + 2 * rim
    thin = rim - 1
    long = state_ref.shape[1]
    pieces = long // PART
    loading = pltpu.make_async_copy(state_ref, work_ref.at[:2], load)
    loading.start()
    turned = jnp.transpose(code_ref[...])
    names = lax.broadcasted_iota(jnp.int32, (cap, slots), 1)
    for source in range(ndev):
        pick_ref[source * cap:(source + 1) * cap, :] = ones_where(
            names == turned[:cap, source:source + 1]
        )
    edge = thin * sy
    src_ref[rim:rim + sx, OFF:OFF + sy, :] = heat_ref[...]
    src_ref[1:rim, OFF:OFF + sy, :] = hxlo_ref[:edge, :].reshape(thin, sy, sz)
    src_ref[rim + sx:wide - 1, OFF:OFF + sy, :] = hxhi_ref[:edge, :].reshape(thin, sy, sz)
    parts = -(-(sx + 2 * thin) // PART)
    base = hylo_ref.shape[0] - rim_rows(thin * parts, hylo_ref.shape[1])
    for k in range(thin):
        for h in range(parts):
            n = k * parts + h
            count = min(PART, sx + 2 * thin - h * PART)
            cut = slice(1 + h * PART, 1 + h * PART + count)
            src_ref[cut, OFF - thin + k, :] = get_rim(hylo_ref, base, n)[:count]
            src_ref[cut, OFF + sy + k, :] = get_rim(hyhi_ref, base, n)[:count]
    loading.wait()
    base = ylo_ref.shape[0] - rim_rows(2 * rim * pieces, ylo_ref.shape[1])
    for which in range(2):
        for k in range(rim):
            for h in range(pieces):
                n = (which * rim + k) * pieces + h
                cut = slice(h * PART, (h + 1) * PART)
                work_ref[which, cut, OFF - rim + k, :] = get_rim(ylo_ref, base, n)
                work_ref[which, cut, OFF + sy + k, :] = get_rim(yhi_ref, base, n)
    temp_ref, cond_ref, work_ref = work_ref.at[0], work_ref.at[1], work_ref.at[2]
    kind = cond_ref[:wide]
    sigma_ref[...] = table(kind[rim - 1:rim + sx + 1], modulus_table)
    cond_ref[:wide] = solid_step * table(kind, conduct_table)
    src_ref[...] = (solid_step * source_gain) * src_ref[...]
    height = state_ref.shape[2]
    first = lax.broadcasted_iota(jnp.int32, (height, sz), 1) == 0
    last = lax.broadcasted_iota(jnp.int32, (height, sz), 1) == sz - 1
    pair = (temp_ref, work_ref)
    for turn in range(rim - 1):
        now, later = pair[turn % 2], pair[(turn + 1) % 2]
        for x in range(1 + turn, wide - 1 - turn):
            centre = now[x]
            beside = now[x - 1] + now[x + 1]
            beside += pltpu.roll(centre, 1, 0) + pltpu.roll(centre, height - 1, 0)
            beside += jnp.where(first, 0.0, pltpu.roll(centre, 1, 1))
            beside += jnp.where(last, 0.0, pltpu.roll(centre, sz - 1, 1))
            later[x] = centre + (cond_ref[x] * (beside - 6.0 * centre) + src_ref[x])
    final = pair[(rim - 1) % 2]
    solid = final[rim:rim + sx, OFF:OFF + sy, :]
    next_ref[...] = solid
    sigma_ref[...] = sigma_ref[...] * final[rim - 1:rim + sx + 1]
    high, low = halves(solid.reshape(sx * sy, sz))
    rhs_ref[:, :sz] = high
    rhs_ref[:, sz:] = low
    block = ndev // GROUPS * cap
    copies = []
    for index in range(GROUPS):
        cut = slice(index * block, (index + 1) * block)
        both = jnp.dot(pick_ref[cut, :], rhs_ref[...], preferred_element_type=F32)
        stage_ref[cut, :] = both[:, :sz] + both[:, sz:]
        copies.append(pltpu.make_async_copy(stage_ref.at[cut], reply_ref.at[cut], sems.at[index]))
        copies[-1].start()
    for copy in copies:
        copy.wait()


def solid_steps(rim, cap, state, state_rim, heat, heat_rim, code):
    sx, sy, sz = heat.shape
    _, long, height, _ = state.shape
    total = code.shape[0] * cap
    return pl.pallas_call(
        functools.partial(solid_kernel, rim, cap),
        in_specs=[in_hbm] + [in_vmem] * 8,
        out_specs=[in_vmem, in_vmem, in_hbm],
        out_shape=[
            jax.ShapeDtypeStruct((sx, sy, sz), F32),
            jax.ShapeDtypeStruct((sx + 2, height, sz), F32),
            pltpu.HBM((total, sz), F32),
        ],
        scratch_shapes=[
            pltpu.VMEM((3, long, height, sz), F32),
            pltpu.VMEM((sx + 2 * rim, height, sz), F32),
            pltpu.VMEM((sx * sy, 2 * sz), BF16),
            pltpu.VMEM((total, sx * sy), BF16),
            pltpu.VMEM((total, sz), F32),
            pltpu.SemaphoreType.DMA,
            pltpu.SemaphoreType.DMA((GROUPS,)),
        ],
        compiler_params=params(24),
        cost_estimate=cost(4 * total * sx * sy * sz, 4 * total * sz),
        name="solid_steps",
    )(far(state), *state_rim, heat, *heat_rim, code)


def stress_kernel(sigma_ref, out_ref, tick_ref):
    tick_ref[...] = jnp.zeros_like(tick_ref)
    _, sx, sy, sz = out_ref.shape
    height = sigma_ref.shape[1]
    first = lax.broadcasted_iota(jnp.int32, (height, sz), 1) == 0
    last = lax.broadcasted_iota(jnp.int32, (height, sz), 1) == sz - 1

    def plane(x, none):
        centre = sigma_ref[x + 1]
        out_ref[0, x] = 0.5 * (sigma_ref[x + 2] - sigma_ref[x])[OFF:OFF + sy]
        along = pltpu.roll(centre, height - 1, 0) - pltpu.roll(centre, 1, 0)
        out_ref[1, x] = 0.5 * along[OFF:OFF + sy]
        along = jnp.where(last, 0.0, pltpu.roll(centre, sz - 1, 1)) - jnp.where(
            first, 0.0, pltpu.roll(centre, 1, 1)
        )
        out_ref[2, x] = 0.5 * along[OFF:OFF + sy]
        return none

    lax.fori_loop(0, sx, plane, 0)


def stress(sigma, sx, sy):
    sz = sigma.shape[2]
    return pl.pallas_call(
        stress_kernel,
        grid=(1,),
        in_specs=[whole(sigma.shape)],
        out_specs=[whole((3, sx, sy, sz)), whole((8, LANE))],
        out_shape=[pltpu.HBM((3, sx, sy, sz), F32), jax.ShapeDtypeStruct((8, LANE), F32)],
        compiler_params=params(8),
        cost_estimate=cost(10 * sx * sy * sz, 16 * sx * sy * sz),
        name="stress",
    )(sigma)


def unpack_kernel(dest_ref, back_ref, *refs):
    out_ref = refs[-1]
    rows = out_ref.shape[0]

    def step(index, none):
        base = pl.multiple_of(index * 8, 8)
        lines = [back_ref[pl.ds(dest_ref[0, base + i], 1), :] for i in range(8)]
        out_ref[pl.ds(base, 8), :] = jnp.concatenate(lines, axis=0)
        return none

    lax.fori_loop(0, rows // 8, step, 0, unroll=4)


def unpack(dest, back, after):
    rows = dest.shape[1]
    row_len = back.shape[1]
    return pl.pallas_call(
        unpack_kernel,
        grid=(1,),
        in_specs=[pl.BlockSpec(memory_space=pltpu.SMEM), whole(back.shape)]
        + [anywhere] * len(after),
        out_specs=whole((rows, row_len)),
        out_shape=jax.ShapeDtypeStruct((rows, row_len), F32),
        compiler_params=params(10),
        cost_estimate=cost(rows * 128, 8 * rows * row_len),
        name="unpack",
    )(dest, back, *after)


PLANES = 2
RING = 3 * PLANES


def fluid_kernel(opening, here_ref, xlo_ref, xhi_ref, speed_ref, flux_ref, *refs):
    index, count = pl.program_id(0), pl.num_programs(0)
    cx = (count - 1) * PLANES
    _, cy, depth = here_ref.shape
    row_len = flux_ref.shape[2]
    rows = slice(OFF, OFF + cy)
    if opening:
        out_ref, xfirst_ref, xlast_ref, yfirst_ref, ylast_ref, clo_ref, chi_ref, ring_ref = refs
    else:
        lo_ref, hi_ref, left_ref, right_ref, ylo_ref, yhi_ref = refs[:6]
        out_ref, tick_ref, ring_ref = refs[-3:]
        tick_ref[...] = jnp.zeros_like(tick_ref)

    def patch(slot, corner_ref):
        wide = depth // LANE
        base = corner_ref.shape[0] - 2 * wide
        for row, at in ((OFF, base), (OFF + cy - 1, base + wide)):
            for i in range(wide):
                ring_ref[slot, row:row + 1, i * LANE:(i + 1) * LANE] = (
                    corner_ref[at + i:at + i + 1, :]
                )

    @pl.when(index == 0)
    def _():
        ring_ref[RING - 1, rows, :] = xlo_ref[...]
        if opening:
            for slot in range(RING):
                ring_ref[slot, OFF - 8:OFF, :] = jnp.zeros((8, depth), F32)
                ring_ref[slot, OFF + cy:OFF + cy + 8, :] = jnp.zeros((8, depth), F32)
        else:
            patch(RING - 1, lo_ref)

    @pl.when(index < count - 1)
    def _():
        for p in range(PLANES):
            plane = index * PLANES + p
            slot = lax.rem(plane, RING)
            ring_ref[slot, rows, :] = here_ref[p]
            if not opening:
                one = pl.ds(plane, 1)
                ring_ref[slot, OFF:OFF + 1, :] = left_ref[one, :]
                ring_ref[slot, OFF + cy - 1:OFF + cy, :] = right_ref[one, :]
                ring_ref[slot, OFF - 1:OFF, :] = ylo_ref[one, :]
                ring_ref[slot, OFF + cy:OFF + cy + 1, :] = yhi_ref[one, :]

    @pl.when(index == count - 1)
    def _():
        ring_ref[lax.rem(cx, RING), rows, :] = xhi_ref[...]
        if not opening:
            patch(lax.rem(cx, RING), hi_ref)

    rate = time_step * diffusivity

    def push(total, centre, lower, upper, speed):
        scaled = time_step * speed
        total = total + (rate + jnp.maximum(scaled, 0.0)) * (lower - centre)
        return total + (rate - jnp.minimum(scaled, 0.0)) * (upper - centre)

    def advance(p, none):
        lanes = lax.broadcasted_iota(jnp.int32, (8, depth), 1)
        first, last = lanes == 0, lanes == depth - 1
        plane = (index - 1) * PLANES + p
        mid = lax.rem(plane, RING)
        old, new = lax.rem(plane + RING - 1, RING), lax.rem(plane + 1, RING)
        for tile in range(cy // 16):
            speeds = [
                speed_ref[k, p, tile * 16:tile * 16 + 16, :].astype(F32) for k in range(3)
            ]
            for part in range(2):
                y = tile * 16 + part * 8
                at = OFF + y
                u, v, w = [s[part * 8:part * 8 + 8] for s in speeds]
                centre = ring_ref[mid, at:at + 8, :]
                total = push(
                    centre, centre, ring_ref[old, at:at + 8, :], ring_ref[new, at:at + 8, :], u
                )
                total = push(
                    total, centre, ring_ref[mid, at - 1:at + 7, :],
                    ring_ref[mid, at + 1:at + 9, :], v,
                )
                lower = jnp.where(first, 0.0, pltpu.roll(centre, 1, 1))
                upper = jnp.where(last, 0.0, pltpu.roll(centre, depth - 1, 1))
                total = push(total, centre, lower, upper, w)
                out_ref[p, y:y + 8, row_len:] = total[:, row_len:]
                out_ref[p, y:y + 8, :row_len] = (
                    total[:, :row_len] - time_step * flux_ref[p, y:y + 8, :]
                )
        if opening:
            one = pl.ds(plane, 1)
            yfirst_ref[one, :] = out_ref[p, 0:1, :]
            ylast_ref[one, :] = out_ref[p, cy - 1:cy, :]
            edge = time_step * speed_ref[1, p, 0:16, :].astype(F32)
            clo_ref[one, :] = rate + jnp.maximum(edge[0:1], 0.0)
            edge = time_step * speed_ref[1, p, cy - 16:cy, :].astype(F32)
            chi_ref[one, :] = rate - jnp.minimum(edge[15:16], 0.0)
        return none

    @pl.when(index > 0)
    def _():
        lax.fori_loop(0, PLANES, advance, 0)

    if opening:

        @pl.when(index == 1)
        def _():
            xfirst_ref[...] = out_ref[0]

        @pl.when(index == count - 1)
        def _():
            xlast_ref[...] = out_ref[PLANES - 1]


def fluid_step(opening, temp, sides, velocity, flux, lines, after):
    cx, cy, depth = temp.shape
    row_len = flux.shape[2]
    plane = (PLANES, cy, depth)
    steps = cx // PLANES
    face = pl.BlockSpec((cy, depth), lambda i: (0, 0))
    line = pl.BlockSpec((cx, depth), lambda i: (0, 0))
    back = lambda i: (jnp.maximum(i - 1, 0), 0, 0)
    shape = jax.ShapeDtypeStruct
    outs = [pl.BlockSpec(plane, back)]
    outs += [face, face] + [line] * 4 if opening else [whole((8, LANE))]
    shapes = [pltpu.HBM(temp.shape, F32)]
    if opening:
        shapes += [shape((cy, depth), F32)] * 2 + [shape((cx, depth), F32)] * 4
    else:
        shapes += [shape((8, LANE), F32)]
    extra = [whole(x.shape) for x in lines[:2]] + [line] * len(lines[2:])
    return pl.pallas_call(
        functools.partial(fluid_kernel, opening),
        grid=(steps + 1,),
        in_specs=[
            pl.BlockSpec(plane, lambda i: (jnp.minimum(i, steps - 1), 0, 0)),
            face,
            face,
            pl.BlockSpec((3, PLANES, cy, depth), lambda i: (0, jnp.maximum(i - 1, 0), 0, 0)),
            pl.BlockSpec((PLANES, cy, row_len), back),
        ]
        + extra
        + [anywhere] * len(after),
        out_specs=outs,
        out_shape=shapes,
        scratch_shapes=[pltpu.VMEM((RING, cy + 2 * OFF, depth), F32)],
        compiler_params=params(24),
        cost_estimate=cost(40 * cx * cy * depth, 14 * cx * cy * depth),
        name="fluid_step",
    )(far(temp), *sides, far(velocity), flux, *lines, *after)


def body(temp_fluid, velocity, wall_old, wall_mask, owner_map, slot_map, temp_solid, material):
    cx, cy, depth = temp_fluid.shape
    row_len = wall_old.shape[2]
    sx, sy, sz = temp_solid.shape
    ndev = lax.axis_size("gx") * lax.axis_size("gy")
    rows = cx * cy
    cap = (3 * rows + ndev - 1) // ndev
    cap = -(-cap // 8) * 8
    total = ndev * cap
    rim = SSTEPS + 1

    first, last, left, right = x_faces(rim, temp_fluid, temp_solid, material)
    xlo, xhi = neighbours(last, first, "gx")
    owner = owner_map.reshape(1, rows)
    maps = lax.all_gather(owner * (sx * sy) + slot_map, AXES, axis=0, tiled=True)
    me = lax.axis_index("gx") * lax.axis_size("gy") + lax.axis_index("gy")
    dest = rank(owner, ndev, cap)
    outgoing, flux = pack(dest, temp_fluid, wall_old, wall_mask, ndev, cap, (first, last))
    outgoing, xlo, xhi = lax.optimization_barrier((outgoing, xlo, xhi))
    incoming = lax.all_to_all(outgoing, AXES, split_axis=0, concat_axis=0, tiled=True)

    left, right, state = y_faces(rim, left, right, temp_solid, material, xlo, xhi)
    ylo, yhi = neighbours(right, left, "gy")
    fluid, first, last, *edges = fluid_step(
        True, temp_fluid, (xlo, xhi), velocity, flux, (), ()
    )
    sides = neighbours(last, first, "gx")
    code = columns(sx * sy, me.reshape(1, 1), maps, (edges[0],))

    thin = rim - 1
    heat, first, last, left, right = heat_sum(
        incoming, code, temp_solid.shape, thin, sides, (ylo, yhi, *edges)
    )
    hxlo, hxhi = neighbours(last, first, "gx")
    first, last = strips(thin, heat, hxlo, hxhi, left, right)
    hylo, hyhi = neighbours(last, first, "gy")
    solid, sigma, replies = solid_steps(
        rim, cap, state, (ylo, yhi), heat, (hxlo, hxhi, hylo, hyhi), code
    )
    returned = lax.all_to_all(
        replies.reshape(ndev, cap, sz), AXES, split_axis=0, concat_axis=0, tiled=True
    )
    force, tick = stress(sigma, sx, sy)
    fluid, tick = fluid_step(
        False, fluid, sides, velocity, flux, (hxlo, hxhi, left, right, hylo, hyhi), (tick,)
    )
    wall_next = unpack(dest, returned.reshape(total, sz), (tick,))
    return fluid, wall_next.reshape(cx, cy, row_len), solid, force


def solution(mesh):
    placed = (
        P("gx", "gy", None),
        P(None, "gx", "gy", None),
        P("gx", "gy", None),
        P("gx", "gy", None),
        P(("gx", "gy"), None, None),
        P(("gx", "gy"), None),
        P("gx", "gy", None),
        P("gx", "gy", None),
    )
    return jax.shard_map(
        body,
        mesh=mesh,
        in_specs=placed,
        out_specs=(
            P("gx", "gy", None),
            P("gx", "gy", None),
            P("gx", "gy", None),
            P(None, "gx", "gy", None),
        ),
        check_vma=False,
    )
```

```python
import functools
import jax
import jax.numpy as jnp
from jax import lax
from jax.experimental import pallas as pl
from jax.experimental.pallas import tpu as pltpu
from jax.sharding import PartitionSpec as P

FSTEPS = 2
SSTEPS = 4
time_step = 0.1
diffusivity = 0.5
film_coef = 2.0
solid_step = 0.05
source_gain = 4.0
conduct_table = (0.4, 0.9, 1.5, 2.2)
modulus_table = (0.5, 1.0, 1.6, 2.4)
F32 = jnp.float32
BF16 = jnp.bfloat16
AXES = ("gx", "gy")
LANE = 128
PART = 16
OFF = 8


def params(mib):
    return pltpu.CompilerParams(vmem_limit_bytes=mib * 1024 * 1024)


def cost(flops, bytes_accessed):
    return pl.CostEstimate(flops=flops, bytes_accessed=bytes_accessed, transcendentals=0)


def halves(value):
    high = value.astype(BF16)
    low = (value - high.astype(F32)).astype(BF16)
    return high, low


def ones_where(test):
    return jnp.where(test, 1.0, 0.0).astype(BF16)


def neighbours(before, after, axis):
    size = lax.axis_size(axis)
    up = [(i, i + 1) for i in range(size - 1)]
    down = [(j, i) for i, j in up]
    return lax.ppermute(before, axis, up), lax.ppermute(after, axis, down)


def whole(shape):
    return pl.BlockSpec(shape, lambda i: (0,) * len(shape))


anywhere = pl.BlockSpec(memory_space=pl.ANY)
in_vmem = pl.BlockSpec(memory_space=pltpu.VMEM)
in_hbm = pl.BlockSpec(memory_space=pltpu.HBM)


def far(value):
    return pltpu.with_memory_space_constraint(value, pltpu.HBM)


def near(value):
    return pltpu.with_memory_space_constraint(value, pltpu.VMEM)


def rank_kernel(cap, owner_ref, slot_ref, dest_ref, where_ref, code_ref):
    rows = owner_ref.shape[1]
    ndev = code_ref.shape[0]
    tall = cap + 8
    tri = ones_where(
        lax.broadcasted_iota(jnp.int32, (LANE, LANE), 0)
        <= lax.broadcasted_iota(jnp.int32, (LANE, LANE), 1)
    )
    names = lax.broadcasted_iota(jnp.int32, (ndev, LANE), 0)
    steps = lax.broadcasted_iota(jnp.int32, (LANE, LANE), 0)
    carry = jnp.zeros((ndev, 1), F32)
    codes = jnp.zeros((2 * ndev, LANE), F32)
    for chunk in range(rows // LANE):
        cols = slice(chunk * LANE, (chunk + 1) * LANE)
        own = owner_ref[:, cols]
        hit = jnp.where(names == own, 1.0, 0.0)
        ranks = jnp.dot(hit.astype(BF16), tri, preferred_element_type=F32) + carry
        carry = ranks[:, LANE - 1:]
        place = jnp.sum(hit * ranks, axis=0, keepdims=True).astype(jnp.int32) - 1
        dest_ref[:, cols] = own * cap + place
        where_ref[:, cols] = own * tall + place
        code = slot_ref[:, cols] + 1
        pieces = jnp.concatenate(
            [hit * (code // 32).astype(F32), hit * (code % 32).astype(F32)], axis=0
        ).astype(BF16)
        codes = codes + lax.dot_general(
            pieces, ones_where(steps == place), (((1,), (1,)), ((), ())),
            preferred_element_type=F32,
        )
    code_ref[...] = codes[:ndev] * 32.0 + codes[ndev:]


def rank(owner, slot, ndev, cap):
    rows = owner.shape[1]
    line = jax.ShapeDtypeStruct((1, rows), jnp.int32)
    return pl.pallas_call(
        functools.partial(rank_kernel, cap),
        grid=(1,),
        in_specs=[whole((1, rows))] * 2,
        out_specs=[whole((1, rows))] * 2 + [whole((ndev, LANE))],
        out_shape=[line, line, jax.ShapeDtypeStruct((ndev, LANE), F32)],
        compiler_params=params(8),
        cost_estimate=cost(8 * ndev * LANE * rows, 20 * rows),
        name="rank",
    )(owner, slot)


GROUPS = 4


def pack_kernel(cap, where_ref, code_ref, temp_ref, old_ref, mask_ref, *refs):
    out_ref, flux_ref, rhs_ref, stage_ref, sems = refs[-5:]
    rows = where_ref.shape[1]
    ndev, tall, row_len = stage_ref.shape
    flux = mask_ref[...].astype(F32) * film_coef * (temp_ref[...] - old_ref[...])
    flux_ref[...] = flux
    high, low = halves(flux.reshape(rows, row_len))
    rhs_ref[:, :row_len] = high
    rhs_ref[:, row_len:] = low
    where = where_ref[...]
    group = ndev // GROUPS
    block = group * tall
    lines = lax.broadcasted_iota(jnp.int32, (block, rows), 0)
    copies = []
    for index in range(GROUPS):
        cut = slice(index * group, (index + 1) * group)
        pick = ones_where(lines == where - index * block)
        both = jnp.dot(pick, rhs_ref[...], preferred_element_type=F32)
        both = both[:, :row_len] + both[:, row_len:]
        stage_ref[cut] = both.reshape(group, tall, row_len)
        stage_ref[cut, cap, :] = code_ref[cut, :]
        copies.append(pltpu.make_async_copy(stage_ref.at[cut], out_ref.at[cut], sems.at[index]))
        copies[-1].start()
    for copy in copies:
        copy.wait()


def pack(where, code, temp, old, mask, cap, after):
    cx, cy, _ = temp.shape
    row_len = old.shape[2]
    rows = cx * cy
    ndev = code.shape[0]
    tall = cap + 8
    return pl.pallas_call(
        functools.partial(pack_kernel, cap),
        grid=(1,),
        in_specs=[whole((1, rows)), whole(code.shape)]
        + [whole((cx, cy, row_len))] * 3
        + [anywhere] * len(after),
        out_specs=[in_hbm, whole((cx, cy, row_len))],
        out_shape=[
            pltpu.HBM((ndev, tall, row_len), F32),
            jax.ShapeDtypeStruct((cx, cy, row_len), F32),
        ],
        scratch_shapes=[
            pltpu.VMEM((rows, 2 * row_len), BF16),
            pltpu.VMEM((ndev, tall, row_len), F32),
            pltpu.SemaphoreType.DMA((GROUPS,)),
        ],
        compiler_params=params(18),
        cost_estimate=cost(4 * ndev * tall * rows * row_len, 5 * rows * row_len * 4),
        name="pack",
    )(where, code, far(temp), far(old), far(mask), *after)


def heat_kernel(cap, thin, rows_ref, xfirst_ref, xlast_ref, ylo_ref, yhi_ref,
                yfirst_ref, ylast_ref, clo_ref, chi_ref,
                heat_ref, low_ref, high_ref, left_ref, right_ref, code_ref):
    ndev, tall, row_len = rows_ref.shape
    cx, depth = yfirst_ref.shape
    sx, sy, _ = heat_ref.shape
    slots = sx * sy
    left = yfirst_ref[...] + clo_ref[...] * ylo_ref[:cx, :]
    right = ylast_ref[...] + chi_ref[...] * yhi_ref[:cx, :]
    left_ref[...] = left
    right_ref[...] = right
    edge = thin * sy
    for ref, x in ((low_ref, 0), (high_ref, cx - 1)):
        for at, line in ((edge, left[x:x + 1]), (edge + depth // LANE, right[x:x + 1])):
            for i in range(depth // LANE):
                ref[at + i:at + i + 1, :] = line[:, i * LANE:(i + 1) * LANE]
    codes = rows_ref[:, cap, :].astype(jnp.int32) - 1
    code_ref[...] = codes
    group = ndev // GROUPS
    names = lax.broadcasted_iota(jnp.int32, (slots, tall), 0)
    total = jnp.zeros((slots, 2 * row_len), F32)
    for index in range(0, ndev, group):
        lines = rows_ref[index:index + group].reshape(group * tall, row_len)
        high, low = halves(lines)
        pick = jnp.concatenate(
            [
                jnp.where(names == codes[index + i:index + i + 1, :tall], 1.0, 0.0)
                for i in range(group)
            ],
            axis=1,
        ).astype(BF16)
        total = total + jnp.dot(
            pick, jnp.concatenate([high, low], axis=1), preferred_element_type=F32
        )
    heat = total[:, :row_len] + total[:, row_len:]
    heat_ref[...] = heat.reshape(sx, sy, row_len)
    low_ref[:edge, :] = heat[:edge]
    high_ref[:edge, :] = heat[slots - edge:]


def heat_sum(incoming, cap, block, thin, faces, edges):
    ndev, tall, row_len = incoming.shape
    sx, sy, _ = block
    line = edges[2].shape
    edge = (thin * sy + 2 * (line[1] // LANE), row_len)
    return pl.pallas_call(
        functools.partial(heat_kernel, cap, thin),
        grid=(1,),
        in_specs=[whole(incoming.shape)] + [anywhere] * 2 + [whole(x.shape) for x in edges],
        out_specs=[whole(block), whole(edge), whole(edge), whole(line), whole(line)]
        + [whole((ndev, row_len))],
        out_shape=[
            jax.ShapeDtypeStruct(block, F32),
            jax.ShapeDtypeStruct(edge, F32),
            jax.ShapeDtypeStruct(edge, F32),
            jax.ShapeDtypeStruct(line, F32),
            jax.ShapeDtypeStruct(line, F32),
            jax.ShapeDtypeStruct((ndev, row_len), jnp.int32),
        ],
        compiler_params=params(14),
        cost_estimate=cost(4 * ndev * tall * sx * sy * row_len, 4 * ndev * tall * row_len),
        name="heat_sum",
    )(incoming, *faces, *edges)


def put_rim(ref, base, slabs):
    across = ref.shape[1] // LANE
    for n, slab in enumerate(slabs):
        row = base + n // across * PART
        ref[row:row + PART, n % across * LANE:(n % across + 1) * LANE] = slab


def get_rim(ref, base, n):
    across = ref.shape[1] // LANE
    row = base + n // across * PART
    return ref[row:row + PART, n % across * LANE:(n % across + 1) * LANE]


def rim_rows(count, depth):
    across = depth // LANE
    return -(-count // across) * PART


def x_faces_kernel(rim, bottom_ref, top_ref, near_ref, far_ref, temp_ref, kind_ref,
                   low_ref, high_ref, left_ref, right_ref):
    _, cy, _ = bottom_ref.shape
    left_ref[...] = near_ref[:, 0, :]
    right_ref[...] = far_ref[:, near_ref.shape[1] - 1, :]
    sx, sy, _ = temp_ref.shape
    low_ref[:cy, :] = bottom_ref[0]
    high_ref[:cy, :] = top_ref[0]
    for ref, start in ((low_ref, 0), (high_ref, sx - rim)):
        slabs = [
            get(start + k, slice(h, h + PART))
            for get in (
                lambda x, cut: temp_ref[x, cut, :],
                lambda x, cut: kind_ref[x, cut, :].astype(F32) + 1.0,
            )
            for k in range(rim)
            for h in range(0, sy, PART)
        ]
        put_rim(ref, cy, slabs)


def x_faces(rim, fluid, temp, kind):
    cx, cy, depth = fluid.shape
    sx, sy, sz = temp.shape
    height = cy + rim_rows(2 * rim * (sy // PART), depth)
    plane = (1, cy, depth)
    return pl.pallas_call(
        functools.partial(x_faces_kernel, rim),
        grid=(1,),
        in_specs=[
            pl.BlockSpec(plane, lambda i: (0, 0, 0)),
            pl.BlockSpec(plane, lambda i: (cx - 1, 0, 0)),
            pl.BlockSpec((cx, 8, depth), lambda i: (0, 0, 0)),
            pl.BlockSpec((cx, 8, depth), lambda i: (0, cy // 8 - 1, 0)),
            whole(temp.shape),
            whole(temp.shape),
        ],
        out_specs=[whole((height, depth))] * 2 + [whole((cx, depth))] * 2,
        out_shape=[jax.ShapeDtypeStruct((height, depth), F32)] * 2
        + [jax.ShapeDtypeStruct((cx, depth), F32)] * 2,
        compiler_params=params(16),
        cost_estimate=cost(1000, 4 * 4 * height * depth),
        name="x_faces",
    )(far(fluid), far(fluid), far(fluid), far(fluid), far(temp), far(kind))


def fill_x(rim, ref, which, own, lo_ref, hi_ref):
    sx, sy, _ = own.shape
    pieces = sy // PART
    base = lo_ref.shape[0] - rim_rows(2 * rim * pieces, lo_ref.shape[1])
    ref[rim:rim + sx, OFF:OFF + sy, :] = own
    for k in range(rim):
        for h in range(pieces):
            n = (which * rim + k) * pieces + h
            cut = slice(OFF + h * PART, OFF + (h + 1) * PART)
            ref[k, cut, :] = get_rim(lo_ref, base, n)
            ref[rim + sx + k, cut, :] = get_rim(hi_ref, base, n)


def y_faces_kernel(rim, near_ref, far_ref, temp_ref, kind_ref, lo_ref, hi_ref,
                   left_ref, right_ref, state_ref):
    cx = near_ref.shape[0]
    sx, sy, _ = temp_ref.shape
    left_ref[:cx, :] = near_ref[...]
    right_ref[:cx, :] = far_ref[...]
    slabs = ([], [])
    long = state_ref.shape[1]
    state_ref[...] = jnp.zeros_like(state_ref)
    for which, own in enumerate((temp_ref[...], kind_ref[...].astype(F32) + 1.0)):
        fill_x(rim, state_ref.at[which], which, own, lo_ref, hi_ref)
        for into, start in zip(slabs, (OFF, OFF + sy - rim)):
            for k in range(rim):
                for h in range(0, long, PART):
                    into.append(state_ref[which, h:h + PART, start + k, :])
    put_rim(left_ref, cx, slabs[0])
    put_rim(right_ref, cx, slabs[1])


def y_faces(rim, left, right, temp, kind, lo, hi):
    cx, depth = left.shape
    sx, sy, sz = temp.shape
    long = -(-(sx + 2 * rim) // PART) * PART
    height = cx + rim_rows(2 * rim * (long // PART), depth)
    args = (left, right, far(temp), far(kind), lo, hi)
    return pl.pallas_call(
        functools.partial(y_faces_kernel, rim),
        grid=(1,),
        in_specs=[whole(x.shape) for x in args],
        out_specs=[whole((height, depth))] * 2 + [whole((2, long, sy + 2 * OFF, sz))],
        out_shape=[jax.ShapeDtypeStruct((height, depth), F32)] * 2
        + [pltpu.HBM((2, long, sy + 2 * OFF, sz), F32)],
        compiler_params=params(10),
        cost_estimate=cost(1000, 4 * 4 * height * depth),
        name="y_faces",
    )(*args)


def strips_kernel(thin, heat_ref, lo_ref, hi_ref, near_ref, away_ref,
                  left_ref, right_ref, work_ref):
    cx = near_ref.shape[0]
    sx, sy, sz = heat_ref.shape
    edge = thin * sy
    left_ref[:cx, :] = near_ref[...]
    right_ref[:cx, :] = away_ref[...]
    work_ref[...] = jnp.zeros_like(work_ref)
    work_ref[:thin] = lo_ref[:edge, :].reshape(thin, sy, sz)
    work_ref[thin:thin + sx] = heat_ref[...]
    work_ref[thin + sx:2 * thin + sx] = hi_ref[:edge, :].reshape(thin, sy, sz)
    long = work_ref.shape[0]
    for ref, start in ((left_ref, 0), (right_ref, sy - thin)):
        slabs = [
            work_ref[h:h + PART, start + k, :] for k in range(thin) for h in range(0, long, PART)
        ]
        put_rim(ref, cx, slabs)


def strips(thin, heat, lo, hi, left, right):
    cx, depth = left.shape
    sx, sy, sz = heat.shape
    long = -(-(sx + 2 * thin) // PART) * PART
    height = cx + rim_rows(thin * (long // PART), depth)
    return pl.pallas_call(
        functools.partial(strips_kernel, thin),
        in_specs=[in_vmem] * 5,
        out_specs=[in_vmem] * 2,
        out_shape=[jax.ShapeDtypeStruct((height, depth), F32)] * 2,
        scratch_shapes=[pltpu.VMEM((long, sy, sz), F32)],
        compiler_params=params(8),
        cost_estimate=cost(1000, 16 * height * depth),
        name="strips",
    )(heat, lo, hi, left, right)


def table(kind, values):
    out = jnp.zeros(kind.shape, F32)
    for index, value in enumerate(values):
        out = jnp.where(kind == index + 1.0, value, out)
    return out


def ready_kernel(rim, cap, state_ref, ylo_ref, yhi_ref, code_ref,
                 temp_ref, cond_ref, sigma_ref, pick_ref):
    _, long, height, sz = state_ref.shape
    ndev = code_ref.shape[0]
    slots = pick_ref.shape[1]
    sx = sigma_ref.shape[0] - 2
    sy = height - 2 * OFF
    pieces = long // PART
    turned = jnp.transpose(code_ref[...])
    names = lax.broadcasted_iota(jnp.int32, (cap, slots), 1)
    for source in range(0, ndev, 2):
        pick_ref[source * cap:(source + 2) * cap, :] = jnp.concatenate(
            [
                jnp.where(names == turned[:cap, one:one + 1], 1.0, 0.0)
                for one in (source, source + 1)
            ],
            axis=0,
        ).astype(BF16)
    base = ylo_ref.shape[0] - rim_rows(2 * rim * pieces, ylo_ref.shape[1])
    for which, ref in enumerate((temp_ref, cond_ref)):
        ref[...] = state_ref[which]
        for k in range(rim):
            for h in range(pieces):
                n = (which * rim + k) * pieces + h
                cut = slice(h * PART, (h + 1) * PART)
                ref[cut, OFF - rim + k, :] = get_rim(ylo_ref, base, n)
                ref[cut, OFF + sy + k, :] = get_rim(yhi_ref, base, n)
    kind = cond_ref[...]
    sigma_ref[...] = table(kind[rim - 1:rim + sx + 1], modulus_table)
    cond_ref[...] = solid_step * table(kind, conduct_table)


def ready(rim, cap, state, ylo, yhi, code, block):
    sx, sy, sz = block
    _, long, height, _ = state.shape
    ndev = code.shape[0]
    args = (far(state), ylo, yhi, code)
    return pl.pallas_call(
        functools.partial(ready_kernel, rim, cap),
        grid=(1,),
        in_specs=[whole(x.shape) for x in args],
        out_specs=[in_vmem] * 4,
        out_shape=[
            pltpu.VMEM((long, height, sz), F32),
            pltpu.VMEM((long, height, sz), F32),
            pltpu.VMEM((sx + 2, height, sz), F32),
            pltpu.VMEM((ndev * cap, sx * sy), BF16),
        ],
        compiler_params=params(14),
        cost_estimate=cost(4 * ndev * cap * sx * sy, 4 * ndev * cap * sx * sy),
        name="ready",
    )(*args)


def solid_kernel(rim, start_ref, cond_ref, modulus_ref, pick_ref,
                 heat_ref, hxlo_ref, hxhi_ref, hylo_ref, hyhi_ref,
                 next_ref, sigma_ref, reply_ref, even_ref, odd_ref, src_ref, rhs_ref,
                 stage_ref, sems):
    sx, sy, sz = heat_ref.shape
    wide = sx + 2 * rim
    thin = rim - 1
    edge = thin * sy
    src_ref[rim:rim + sx, OFF:OFF + sy, :] = heat_ref[...]
    src_ref[1:rim, OFF:OFF + sy, :] = hxlo_ref[:edge, :].reshape(thin, sy, sz)
    src_ref[rim + sx:wide - 1, OFF:OFF + sy, :] = hxhi_ref[:edge, :].reshape(thin, sy, sz)
    parts = -(-(sx + 2 * thin) // PART)
    base = hylo_ref.shape[0] - rim_rows(thin * parts, hylo_ref.shape[1])
    for k in range(thin):
        for h in range(parts):
            n = k * parts + h
            count = min(PART, sx + 2 * thin - h * PART)
            cut = slice(1 + h * PART, 1 + h * PART + count)
            src_ref[cut, OFF - thin + k, :] = get_rim(hylo_ref, base, n)[:count]
            src_ref[cut, OFF + sy + k, :] = get_rim(hyhi_ref, base, n)[:count]
    src_ref[...] = (solid_step * source_gain) * src_ref[...]
    height = start_ref.shape[1]
    first = lax.broadcasted_iota(jnp.int32, (height, sz), 1) == 0
    last = lax.broadcasted_iota(jnp.int32, (height, sz), 1) == sz - 1
    now = start_ref
    for turn in range(rim - 1):
        later = (odd_ref, even_ref)[turn % 2]
        for x in range(1 + turn, wide - 1 - turn):
            centre = now[x]
            beside = now[x - 1] + now[x + 1]
            beside += pltpu.roll(centre, 1, 0) + pltpu.roll(centre, height - 1, 0)
            beside += jnp.where(first, 0.0, pltpu.roll(centre, 1, 1))
            beside += jnp.where(last, 0.0, pltpu.roll(centre, sz - 1, 1))
            later[x] = centre + (cond_ref[x] * (beside - 6.0 * centre) + src_ref[x])
        now = later
    solid = now[rim:rim + sx, OFF:OFF + sy, :]
    next_ref[...] = solid
    sigma_ref[...] = modulus_ref[...] * now[rim - 1:rim + sx + 1]
    high, low = halves(solid.reshape(sx * sy, sz))
    rhs_ref[:, :sz] = high
    rhs_ref[:, sz:] = low
    block = pick_ref.shape[0] // GROUPS
    copies = []
    for index in range(GROUPS):
        cut = slice(index * block, (index + 1) * block)
        both = jnp.dot(pick_ref[cut, :], rhs_ref[...], preferred_element_type=F32)
        stage_ref[cut, :] = both[:, :sz] + both[:, sz:]
        copies.append(pltpu.make_async_copy(stage_ref.at[cut], reply_ref.at[cut], sems.at[index]))
        copies[-1].start()
    for copy in copies:
        copy.wait()


def solid_steps(rim, prepared, heat, heat_rim):
    sx, sy, sz = heat.shape
    long, height, _ = prepared[0].shape
    total = prepared[3].shape[0]
    return pl.pallas_call(
        functools.partial(solid_kernel, rim),
        in_specs=[in_vmem] * 9,
        out_specs=[in_vmem, in_vmem, in_hbm],
        out_shape=[
            jax.ShapeDtypeStruct((sx, sy, sz), F32),
            jax.ShapeDtypeStruct((sx + 2, height, sz), F32),
            pltpu.HBM((total, sz), F32),
        ],
        scratch_shapes=[pltpu.VMEM((long, height, sz), F32)] * 2
        + [
            pltpu.VMEM((sx + 2 * rim, height, sz), F32),
            pltpu.VMEM((sx * sy, 2 * sz), BF16),
            pltpu.VMEM((total, sz), F32),
            pltpu.SemaphoreType.DMA((GROUPS,)),
        ],
        compiler_params=params(14),
        cost_estimate=cost(4 * total * sx * sy * sz, 4 * total * sz),
        name="solid_steps",
    )(*[near(x) for x in prepared], heat, *heat_rim)


def stress_kernel(sigma_ref, out_ref, tick_ref):
    tick_ref[...] = jnp.zeros_like(tick_ref)
    _, sx, sy, sz = out_ref.shape
    height = sigma_ref.shape[1]
    first = lax.broadcasted_iota(jnp.int32, (height, sz), 1) == 0
    last = lax.broadcasted_iota(jnp.int32, (height, sz), 1) == sz - 1

    def plane(x, none):
        centre = sigma_ref[x + 1]
        out_ref[0, x] = 0.5 * (sigma_ref[x + 2] - sigma_ref[x])[OFF:OFF + sy]
        along = pltpu.roll(centre, height - 1, 0) - pltpu.roll(centre, 1, 0)
        out_ref[1, x] = 0.5 * along[OFF:OFF + sy]
        along = jnp.where(last, 0.0, pltpu.roll(centre, sz - 1, 1)) - jnp.where(
            first, 0.0, pltpu.roll(centre, 1, 1)
        )
        out_ref[2, x] = 0.5 * along[OFF:OFF + sy]
        return none

    lax.fori_loop(0, sx, plane, 0)


def stress(sigma, sx, sy):
    sz = sigma.shape[2]
    return pl.pallas_call(
        stress_kernel,
        grid=(1,),
        in_specs=[whole(sigma.shape)],
        out_specs=[whole((3, sx, sy, sz)), whole((8, LANE))],
        out_shape=[pltpu.HBM((3, sx, sy, sz), F32), jax.ShapeDtypeStruct((8, LANE), F32)],
        compiler_params=params(8),
        cost_estimate=cost(10 * sx * sy * sz, 16 * sx * sy * sz),
        name="stress",
    )(sigma)


def unpack_kernel(dest_ref, back_ref, *refs):
    out_ref = refs[-1]
    rows = out_ref.shape[0]

    def step(index, none):
        base = pl.multiple_of(index * 8, 8)
        lines = [back_ref[pl.ds(dest_ref[0, base + i], 1), :] for i in range(8)]
        out_ref[pl.ds(base, 8), :] = jnp.concatenate(lines, axis=0)
        return none

    lax.fori_loop(0, rows // 8, step, 0, unroll=4)


def unpack(dest, back, after):
    rows = dest.shape[1]
    row_len = back.shape[1]
    return pl.pallas_call(
        unpack_kernel,
        grid=(1,),
        in_specs=[pl.BlockSpec(memory_space=pltpu.SMEM), whole(back.shape)]
        + [anywhere] * len(after),
        out_specs=whole((rows, row_len)),
        out_shape=jax.ShapeDtypeStruct((rows, row_len), F32),
        compiler_params=params(10),
        cost_estimate=cost(rows * 128, 8 * rows * row_len),
        name="unpack",
    )(dest, back, *after)


PLANES = 2
RING = 3 * PLANES


def fluid_kernel(opening, here_ref, xlo_ref, xhi_ref, speed_ref, flux_ref, *refs):
    index, count = pl.program_id(0), pl.num_programs(0)
    cx = (count - 1) * PLANES
    _, cy, depth = here_ref.shape
    row_len = flux_ref.shape[2]
    rows = slice(OFF, OFF + cy)
    if opening:
        out_ref, xfirst_ref, xlast_ref, yfirst_ref, ylast_ref, clo_ref, chi_ref, ring_ref = refs
    else:
        lo_ref, hi_ref, left_ref, right_ref, ylo_ref, yhi_ref = refs[:6]
        out_ref, tick_ref, ring_ref = refs[-3:]
        tick_ref[...] = jnp.zeros_like(tick_ref)

    def patch(slot, corner_ref):
        wide = depth // LANE
        base = corner_ref.shape[0] - 2 * wide
        for row, at in ((OFF, base), (OFF + cy - 1, base + wide)):
            for i in range(wide):
                ring_ref[slot, row:row + 1, i * LANE:(i + 1) * LANE] = (
                    corner_ref[at + i:at + i + 1, :]
                )

    @pl.when(index == 0)
    def _():
        ring_ref[RING - 1, rows, :] = xlo_ref[...]
        if opening:
            for slot in range(RING):
                ring_ref[slot, OFF - 8:OFF, :] = jnp.zeros((8, depth), F32)
                ring_ref[slot, OFF + cy:OFF + cy + 8, :] = jnp.zeros((8, depth), F32)
        else:
            patch(RING - 1, lo_ref)

    @pl.when(index < count - 1)
    def _():
        for p in range(PLANES):
            plane = index * PLANES + p
            slot = lax.rem(plane, RING)
            ring_ref[slot, rows, :] = here_ref[p]
            if not opening:
                one = pl.ds(plane, 1)
                ring_ref[slot, OFF:OFF + 1, :] = left_ref[one, :]
                ring_ref[slot, OFF + cy - 1:OFF + cy, :] = right_ref[one, :]
                ring_ref[slot, OFF - 1:OFF, :] = ylo_ref[one, :]
                ring_ref[slot, OFF + cy:OFF + cy + 1, :] = yhi_ref[one, :]

    @pl.when(index == count - 1)
    def _():
        ring_ref[lax.rem(cx, RING), rows, :] = xhi_ref[...]
        if not opening:
            patch(lax.rem(cx, RING), hi_ref)

    rate = time_step * diffusivity

    def push(total, centre, lower, upper, speed):
        scaled = time_step * speed
        total = total + (rate + jnp.maximum(scaled, 0.0)) * (lower - centre)
        return total + (rate - jnp.minimum(scaled, 0.0)) * (upper - centre)

    def advance(p, none):
        lanes = lax.broadcasted_iota(jnp.int32, (8, depth), 1)
        first, last = lanes == 0, lanes == depth - 1
        plane = (index - 1) * PLANES + p
        mid = lax.rem(plane, RING)
        old, new = lax.rem(plane + RING - 1, RING), lax.rem(plane + 1, RING)
        for tile in range(cy // 16):
            speeds = [
                speed_ref[k, p, tile * 16:tile * 16 + 16, :].astype(F32) for k in range(3)
            ]
            for part in range(2):
                y = tile * 16 + part * 8
                at = OFF + y
                u, v, w = [s[part * 8:part * 8 + 8] for s in speeds]
                centre = ring_ref[mid, at:at + 8, :]
                total = push(
                    centre, centre, ring_ref[old, at:at + 8, :], ring_ref[new, at:at + 8, :], u
                )
                total = push(
                    total, centre, ring_ref[mid, at - 1:at + 7, :],
                    ring_ref[mid, at + 1:at + 9, :], v,
                )
                lower = jnp.where(first, 0.0, pltpu.roll(centre, 1, 1))
                upper = jnp.where(last, 0.0, pltpu.roll(centre, depth - 1, 1))
                total = push(total, centre, lower, upper, w)
                out_ref[p, y:y + 8, row_len:] = total[:, row_len:]
                out_ref[p, y:y + 8, :row_len] = (
                    total[:, :row_len] - time_step * flux_ref[p, y:y + 8, :]
                )
        if opening:
            one = pl.ds(plane, 1)
            yfirst_ref[one, :] = out_ref[p, 0:1, :]
            ylast_ref[one, :] = out_ref[p, cy - 1:cy, :]
            edge = time_step * speed_ref[1, p, 0:16, :].astype(F32)
            clo_ref[one, :] = rate + jnp.maximum(edge[0:1], 0.0)
            edge = time_step * speed_ref[1, p, cy - 16:cy, :].astype(F32)
            chi_ref[one, :] = rate - jnp.minimum(edge[15:16], 0.0)
        return none

    @pl.when(index > 0)
    def _():
        lax.fori_loop(0, PLANES, advance, 0)

    if opening:

        @pl.when(index == 1)
        def _():
            xfirst_ref[...] = out_ref[0]

        @pl.when(index == count - 1)
        def _():
            xlast_ref[...] = out_ref[PLANES - 1]


def fluid_step(opening, temp, sides, velocity, flux, lines, after):
    cx, cy, depth = temp.shape
    row_len = flux.shape[2]
    plane = (PLANES, cy, depth)
    steps = cx // PLANES
    face = pl.BlockSpec((cy, depth), lambda i: (0, 0))
    line = pl.BlockSpec((cx, depth), lambda i: (0, 0))
    back = lambda i: (jnp.maximum(i - 1, 0), 0, 0)
    shape = jax.ShapeDtypeStruct
    outs = [pl.BlockSpec(plane, back)]
    outs += [face, face] + [line] * 4 if opening else [whole((8, LANE))]
    shapes = [pltpu.HBM(temp.shape, F32)]
    if opening:
        shapes += [shape((cy, depth), F32)] * 2 + [shape((cx, depth), F32)] * 4
    else:
        shapes += [shape((8, LANE), F32)]
    extra = [whole(x.shape) for x in lines[:2]] + [line] * len(lines[2:])
    return pl.pallas_call(
        functools.partial(fluid_kernel, opening),
        grid=(steps + 1,),
        in_specs=[
            pl.BlockSpec(plane, lambda i: (jnp.minimum(i, steps - 1), 0, 0)),
            face,
            face,
            pl.BlockSpec((3, PLANES, cy, depth), lambda i: (0, jnp.maximum(i - 1, 0), 0, 0)),
            pl.BlockSpec((PLANES, cy, row_len), back),
        ]
        + extra
        + [anywhere] * len(after),
        out_specs=outs,
        out_shape=shapes,
        scratch_shapes=[pltpu.VMEM((RING, cy + 2 * OFF, depth), F32)],
        compiler_params=params(16),
        cost_estimate=cost(40 * cx * cy * depth, 14 * cx * cy * depth),
        name="fluid_step",
    )(far(temp), *sides, far(velocity), flux, *lines, *after)


def body(temp_fluid, velocity, wall_old, wall_mask, owner_map, slot_map, temp_solid, material):
    cx, cy, depth = temp_fluid.shape
    row_len = wall_old.shape[2]
    sx, sy, sz = temp_solid.shape
    ndev = lax.axis_size("gx") * lax.axis_size("gy")
    rows = cx * cy
    cap = (3 * rows + ndev - 1) // ndev
    cap = -(-cap // 8) * 8
    total = ndev * cap
    rim = SSTEPS + 1

    first, last, left, right = x_faces(rim, temp_fluid, temp_solid, material)
    xlo, xhi = neighbours(last, first, "gx")
    dest, where, codes = rank(owner_map.reshape(1, rows), slot_map, ndev, cap)
    outgoing, flux = pack(where, codes, temp_fluid, wall_old, wall_mask, cap, (first, last))
    outgoing, xlo, xhi = lax.optimization_barrier((outgoing, xlo, xhi))
    incoming = lax.all_to_all(outgoing, AXES, split_axis=0, concat_axis=0, tiled=True)

    left, right, state = y_faces(rim, left, right, temp_solid, material, xlo, xhi)
    ylo, yhi = neighbours(right, left, "gy")
    fluid, first, last, *edges = fluid_step(
        True, temp_fluid, (xlo, xhi), velocity, flux, (), ()
    )
    sides = neighbours(last, first, "gx")

    thin = rim - 1
    heat, first, last, left, right, code = heat_sum(
        incoming, cap, temp_solid.shape, thin, sides, (ylo, yhi, *edges)
    )
    hxlo, hxhi = neighbours(last, first, "gx")
    first, last = strips(thin, heat, hxlo, hxhi, left, right)
    hylo, hyhi = neighbours(last, first, "gy")
    prepared = ready(rim, cap, state, ylo, yhi, code, heat.shape)
    solid, sigma, replies = solid_steps(rim, prepared, heat, (hxlo, hxhi, hylo, hyhi))
    returned = lax.all_to_all(
        replies.reshape(ndev, cap, sz), AXES, split_axis=0, concat_axis=0, tiled=True
    )
    force, tick = stress(sigma, sx, sy)
    fluid, tick = fluid_step(
        False, fluid, sides, velocity, flux, (hxlo, hxhi, left, right, hylo, hyhi), (tick,)
    )
    wall_next = unpack(dest, returned.reshape(total, sz), (tick,))
    return fluid, wall_next.reshape(cx, cy, row_len), solid, force


def solution(mesh):
    placed = (
        P("gx", "gy", None),
        P(None, "gx", "gy", None),
        P("gx", "gy", None),
        P("gx", "gy", None),
        P(("gx", "gy"), None, None),
        P(("gx", "gy"), None),
        P("gx", "gy", None),
        P("gx", "gy", None),
    )
    return jax.shard_map(
        body,
        mesh=mesh,
        in_specs=placed,
        out_specs=(
            P("gx", "gy", None),
            P("gx", "gy", None),
            P("gx", "gy", None),
            P(None, "gx", "gy", None),
        ),
        check_vma=False,
    )
```

```python
import functools
import jax
import jax.numpy as jnp
from jax import lax
from jax.experimental import pallas as pl
from jax.experimental.pallas import tpu as pltpu
from jax.sharding import PartitionSpec as P

FSTEPS = 2
SSTEPS = 4
time_step = 0.1
diffusivity = 0.5
film_coef = 2.0
solid_step = 0.05
source_gain = 4.0
conduct_table = (0.4, 0.9, 1.5, 2.2)
modulus_table = (0.5, 1.0, 1.6, 2.4)
F32 = jnp.float32
BF16 = jnp.bfloat16
AXES = ("gx", "gy")
LANE = 128
PART = 16
OFF = 8


def params(mib):
    return pltpu.CompilerParams(vmem_limit_bytes=mib * 1024 * 1024)


def cost(flops, bytes_accessed):
    return pl.CostEstimate(flops=flops, bytes_accessed=bytes_accessed, transcendentals=0)


def halves(value):
    high = value.astype(BF16)
    low = (value - high.astype(F32)).astype(BF16)
    return high, low


def ones_where(test):
    return jnp.where(test, 1.0, 0.0).astype(BF16)


def neighbours(before, after, axis):
    size = lax.axis_size(axis)
    up = [(i, i + 1) for i in range(size - 1)]
    down = [(j, i) for i, j in up]
    return lax.ppermute(before, axis, up), lax.ppermute(after, axis, down)


def whole(shape):
    return pl.BlockSpec(shape, lambda i: (0,) * len(shape))


anywhere = pl.BlockSpec(memory_space=pl.ANY)
in_vmem = pl.BlockSpec(memory_space=pltpu.VMEM)
in_hbm = pl.BlockSpec(memory_space=pltpu.HBM)


def far(value):
    return pltpu.with_memory_space_constraint(value, pltpu.HBM)


def near(value):
    return pltpu.with_memory_space_constraint(value, pltpu.VMEM)


def rank_kernel(cap, owner_ref, slot_ref, dest_ref, where_ref, code_ref):
    rows = owner_ref.shape[1]
    ndev = code_ref.shape[0]
    tall = cap + 8
    tri = ones_where(
        lax.broadcasted_iota(jnp.int32, (LANE, LANE), 0)
        <= lax.broadcasted_iota(jnp.int32, (LANE, LANE), 1)
    )
    names = lax.broadcasted_iota(jnp.int32, (ndev, LANE), 0)
    steps = lax.broadcasted_iota(jnp.int32, (LANE, LANE), 0)
    carry = jnp.zeros((ndev, 1), F32)
    codes = jnp.zeros((2 * ndev, LANE), F32)
    for chunk in range(rows // LANE):
        cols = slice(chunk * LANE, (chunk + 1) * LANE)
        own = owner_ref[:, cols]
        hit = jnp.where(names == own, 1.0, 0.0)
        ranks = jnp.dot(hit.astype(BF16), tri, preferred_element_type=F32) + carry
        carry = ranks[:, LANE - 1:]
        place = jnp.sum(hit * ranks, axis=0, keepdims=True).astype(jnp.int32) - 1
        dest_ref[:, cols] = own * cap + place
        where_ref[:, cols] = own * tall + place
        code = slot_ref[:, cols] + 1
        pieces = jnp.concatenate(
            [hit * (code // 32).astype(F32), hit * (code % 32).astype(F32)], axis=0
        ).astype(BF16)
        codes = codes + lax.dot_general(
            pieces, ones_where(steps == place), (((1,), (1,)), ((), ())),
            preferred_element_type=F32,
        )
    code_ref[...] = codes[:ndev] * 32.0 + codes[ndev:]


def rank(owner, slot, ndev, cap):
    rows = owner.shape[1]
    line = jax.ShapeDtypeStruct((1, rows), jnp.int32)
    return pl.pallas_call(
        functools.partial(rank_kernel, cap),
        grid=(1,),
        in_specs=[whole((1, rows))] * 2,
        out_specs=[whole((1, rows))] * 2 + [whole((ndev, LANE))],
        out_shape=[line, line, jax.ShapeDtypeStruct((ndev, LANE), F32)],
        compiler_params=params(8),
        cost_estimate=cost(8 * ndev * LANE * rows, 20 * rows),
        name="rank",
    )(owner, slot)


GROUPS = 4


def pack_kernel(cap, where_ref, code_ref, temp_ref, old_ref, mask_ref, *refs):
    out_ref, flux_ref, rhs_ref, stage_ref, sems = refs[-5:]
    rows = where_ref.shape[1]
    ndev, tall, row_len = stage_ref.shape
    flux = mask_ref[...].astype(F32) * film_coef * (temp_ref[...] - old_ref[...])
    flux_ref[...] = flux
    high, low = halves(flux.reshape(rows, row_len))
    rhs_ref[:, :row_len] = high
    rhs_ref[:, row_len:] = low
    where = where_ref[...]
    group = ndev // GROUPS
    block = group * tall
    lines = lax.broadcasted_iota(jnp.int32, (block, rows), 0)
    copies = []
    for index in range(GROUPS):
        cut = slice(index * group, (index + 1) * group)
        pick = ones_where(lines == where - index * block)
        both = jnp.dot(pick, rhs_ref[...], preferred_element_type=F32)
        both = both[:, :row_len] + both[:, row_len:]
        stage_ref[cut] = both.reshape(group, tall, row_len)
        stage_ref[cut, cap, :] = code_ref[cut, :]
        copies.append(pltpu.make_async_copy(stage_ref.at[cut], out_ref.at[cut], sems.at[index]))
        copies[-1].start()
    for copy in copies:
        copy.wait()


def pack(where, code, temp, old, mask, cap, after):
    cx, cy, _ = temp.shape
    row_len = old.shape[2]
    rows = cx * cy
    ndev = code.shape[0]
    tall = cap + 8
    return pl.pallas_call(
        functools.partial(pack_kernel, cap),
        grid=(1,),
        in_specs=[whole((1, rows)), whole(code.shape)]
        + [whole((cx, cy, row_len))] * 3
        + [anywhere] * len(after),
        out_specs=[in_hbm, whole((cx, cy, row_len))],
        out_shape=[
            pltpu.HBM((ndev, tall, row_len), F32),
            jax.ShapeDtypeStruct((cx, cy, row_len), F32),
        ],
        scratch_shapes=[
            pltpu.VMEM((rows, 2 * row_len), BF16),
            pltpu.VMEM((ndev, tall, row_len), F32),
            pltpu.SemaphoreType.DMA((GROUPS,)),
        ],
        compiler_params=params(18),
        cost_estimate=cost(4 * ndev * tall * rows * row_len, 5 * rows * row_len * 4),
        name="pack",
    )(where, code, far(temp), far(old), far(mask), *after)


def heat_kernel(cap, thin, rows_ref, xfirst_ref, xlast_ref, ylo_ref, yhi_ref,
                yfirst_ref, ylast_ref, clo_ref, chi_ref,
                heat_ref, low_ref, high_ref, left_ref, right_ref, code_ref):
    ndev, tall, row_len = rows_ref.shape
    cx, depth = yfirst_ref.shape
    sx, sy, _ = heat_ref.shape
    slots = sx * sy
    left = yfirst_ref[...] + clo_ref[...] * ylo_ref[:cx, :]
    right = ylast_ref[...] + chi_ref[...] * yhi_ref[:cx, :]
    left_ref[...] = left
    right_ref[...] = right
    edge = thin * sy
    for ref, x in ((low_ref, 0), (high_ref, cx - 1)):
        for at, line in ((edge, left[x:x + 1]), (edge + depth // LANE, right[x:x + 1])):
            for i in range(depth // LANE):
                ref[at + i:at + i + 1, :] = line[:, i * LANE:(i + 1) * LANE]
    codes = rows_ref[:, cap, :].astype(jnp.int32) - 1
    code_ref[...] = codes
    group = ndev // GROUPS
    names = lax.broadcasted_iota(jnp.int32, (slots, tall), 0)
    total = jnp.zeros((slots, 2 * row_len), F32)
    for index in range(0, ndev, group):
        lines = rows_ref[index:index + group].reshape(group * tall, row_len)
        high, low = halves(lines)
        pick = jnp.concatenate(
            [
                jnp.where(names == codes[index + i:index + i + 1, :tall], 1.0, 0.0)
                for i in range(group)
            ],
            axis=1,
        ).astype(BF16)
        total = total + jnp.dot(
            pick, jnp.concatenate([high, low], axis=1), preferred_element_type=F32
        )
    heat = total[:, :row_len] + total[:, row_len:]
    heat_ref[...] = heat.reshape(sx, sy, row_len)
    low_ref[:edge, :] = heat[:edge]
    high_ref[:edge, :] = heat[slots - edge:]


def heat_sum(incoming, cap, block, thin, faces, edges):
    ndev, tall, row_len = incoming.shape
    sx, sy, _ = block
    line = edges[2].shape
    edge = (thin * sy + 2 * (line[1] // LANE), row_len)
    return pl.pallas_call(
        functools.partial(heat_kernel, cap, thin),
        grid=(1,),
        in_specs=[whole(incoming.shape)] + [anywhere] * 2 + [whole(x.shape) for x in edges],
        out_specs=[whole(block), whole(edge), whole(edge), whole(line), whole(line)]
        + [whole((ndev, row_len))],
        out_shape=[
            jax.ShapeDtypeStruct(block, F32),
            jax.ShapeDtypeStruct(edge, F32),
            jax.ShapeDtypeStruct(edge, F32),
            jax.ShapeDtypeStruct(line, F32),
            jax.ShapeDtypeStruct(line, F32),
            jax.ShapeDtypeStruct((ndev, row_len), jnp.int32),
        ],
        compiler_params=params(14),
        cost_estimate=cost(4 * ndev * tall * sx * sy * row_len, 4 * ndev * tall * row_len),
        name="heat_sum",
    )(incoming, *faces, *edges)


def put_rim(ref, base, slabs):
    across = ref.shape[1] // LANE
    for n, slab in enumerate(slabs):
        row = base + n // across * PART
        ref[row:row + PART, n % across * LANE:(n % across + 1) * LANE] = slab


def get_rim(ref, base, n):
    across = ref.shape[1] // LANE
    row = base + n // across * PART
    return ref[row:row + PART, n % across * LANE:(n % across + 1) * LANE]


def rim_rows(count, depth):
    across = depth // LANE
    return -(-count // across) * PART


def x_faces_kernel(rim, bottom_ref, top_ref, temp_ref, kind_ref, low_ref, high_ref):
    _, cy, _ = bottom_ref.shape
    sx, sy, _ = temp_ref.shape
    low_ref[:cy, :] = bottom_ref[0]
    high_ref[:cy, :] = top_ref[0]
    for ref, start in ((low_ref, 0), (high_ref, sx - rim)):
        slabs = [
            get(start + k, slice(h, h + PART))
            for get in (
                lambda x, cut: temp_ref[x, cut, :],
                lambda x, cut: kind_ref[x, cut, :].astype(F32) + 1.0,
            )
            for k in range(rim)
            for h in range(0, sy, PART)
        ]
        put_rim(ref, cy, slabs)


def x_faces(rim, fluid, temp, kind):
    cx, cy, depth = fluid.shape
    sx, sy, sz = temp.shape
    height = cy + rim_rows(2 * rim * (sy // PART), depth)
    plane = (1, cy, depth)
    return pl.pallas_call(
        functools.partial(x_faces_kernel, rim),
        grid=(1,),
        in_specs=[
            pl.BlockSpec(plane, lambda i: (0, 0, 0)),
            pl.BlockSpec(plane, lambda i: (cx - 1, 0, 0)),
            whole(temp.shape),
            whole(temp.shape),
        ],
        out_specs=[whole((height, depth))] * 2,
        out_shape=[jax.ShapeDtypeStruct((height, depth), F32)] * 2,
        compiler_params=params(16),
        cost_estimate=cost(1000, 4 * 4 * height * depth),
        name="x_faces",
    )(far(fluid), far(fluid), far(temp), far(kind))


def fill_x(rim, ref, which, own, lo_ref, hi_ref):
    sx, sy, _ = own.shape
    pieces = sy // PART
    base = lo_ref.shape[0] - rim_rows(2 * rim * pieces, lo_ref.shape[1])
    ref[rim:rim + sx, OFF:OFF + sy, :] = own
    for k in range(rim):
        for h in range(pieces):
            n = (which * rim + k) * pieces + h
            cut = slice(OFF + h * PART, OFF + (h + 1) * PART)
            ref[k, cut, :] = get_rim(lo_ref, base, n)
            ref[rim + sx + k, cut, :] = get_rim(hi_ref, base, n)


def y_faces_kernel(rim, near_ref, far_ref, temp_ref, kind_ref, lo_ref, hi_ref,
                   left_ref, right_ref, state_ref):
    cx, near_rows, _ = near_ref.shape
    sx, sy, _ = temp_ref.shape
    left_ref[:cx, :] = near_ref[:, 0, :]
    right_ref[:cx, :] = far_ref[:, near_rows - 1, :]
    slabs = ([], [])
    long = state_ref.shape[1]
    state_ref[...] = jnp.zeros_like(state_ref)
    for which, own in enumerate((temp_ref[...], kind_ref[...].astype(F32) + 1.0)):
        fill_x(rim, state_ref.at[which], which, own, lo_ref, hi_ref)
        for into, start in zip(slabs, (OFF, OFF + sy - rim)):
            for k in range(rim):
                for h in range(0, long, PART):
                    into.append(state_ref[which, h:h + PART, start + k, :])
    put_rim(left_ref, cx, slabs[0])
    put_rim(right_ref, cx, slabs[1])


def y_faces(rim, fluid, temp, kind, lo, hi):
    cx, cy, depth = fluid.shape
    sx, sy, sz = temp.shape
    long = -(-(sx + 2 * rim) // PART) * PART
    height = cx + rim_rows(2 * rim * (long // PART), depth)
    args = (far(temp), far(kind), lo, hi)
    edge = (cx, 8, depth)
    return pl.pallas_call(
        functools.partial(y_faces_kernel, rim),
        grid=(1,),
        in_specs=[
            pl.BlockSpec(edge, lambda i: (0, 0, 0)),
            pl.BlockSpec(edge, lambda i: (0, cy // 8 - 1, 0)),
        ]
        + [whole(x.shape) for x in args],
        out_specs=[whole((height, depth))] * 2 + [whole((2, long, sy + 2 * OFF, sz))],
        out_shape=[jax.ShapeDtypeStruct((height, depth), F32)] * 2
        + [pltpu.HBM((2, long, sy + 2 * OFF, sz), F32)],
        compiler_params=params(10),
        cost_estimate=cost(1000, 4 * 4 * height * depth),
        name="y_faces",
    )(far(fluid), far(fluid), *args)


def strips_kernel(thin, heat_ref, lo_ref, hi_ref, near_ref, away_ref,
                  left_ref, right_ref, work_ref):
    cx = near_ref.shape[0]
    sx, sy, sz = heat_ref.shape
    edge = thin * sy
    left_ref[:cx, :] = near_ref[...]
    right_ref[:cx, :] = away_ref[...]
    work_ref[...] = jnp.zeros_like(work_ref)
    work_ref[:thin] = lo_ref[:edge, :].reshape(thin, sy, sz)
    work_ref[thin:thin + sx] = heat_ref[...]
    work_ref[thin + sx:2 * thin + sx] = hi_ref[:edge, :].reshape(thin, sy, sz)
    long = work_ref.shape[0]
    for ref, start in ((left_ref, 0), (right_ref, sy - thin)):
        slabs = [
            work_ref[h:h + PART, start + k, :] for k in range(thin) for h in range(0, long, PART)
        ]
        put_rim(ref, cx, slabs)


def strips(thin, heat, lo, hi, left, right):
    cx, depth = left.shape
    sx, sy, sz = heat.shape
    long = -(-(sx + 2 * thin) // PART) * PART
    height = cx + rim_rows(thin * (long // PART), depth)
    return pl.pallas_call(
        functools.partial(strips_kernel, thin),
        in_specs=[in_vmem] * 5,
        out_specs=[in_vmem] * 2,
        out_shape=[jax.ShapeDtypeStruct((height, depth), F32)] * 2,
        scratch_shapes=[pltpu.VMEM((long, sy, sz), F32)],
        compiler_params=params(8),
        cost_estimate=cost(1000, 16 * height * depth),
        name="strips",
    )(heat, lo, hi, left, right)


def table(kind, values):
    out = jnp.zeros(kind.shape, F32)
    for index, value in enumerate(values):
        out = jnp.where(kind == index + 1.0, value, out)
    return out


def ready_kernel(rim, cap, state_ref, ylo_ref, yhi_ref, code_ref,
                 temp_ref, cond_ref, sigma_ref, pick_ref):
    _, long, height, sz = state_ref.shape
    ndev = code_ref.shape[0]
    slots = pick_ref.shape[1]
    sx = sigma_ref.shape[0] - 2
    sy = height - 2 * OFF
    pieces = long // PART
    turned = jnp.transpose(code_ref[...])
    names = lax.broadcasted_iota(jnp.int32, (cap, slots), 1)
    for source in range(0, ndev, 2):
        pick_ref[source * cap:(source + 2) * cap, :] = jnp.concatenate(
            [
                jnp.where(names == turned[:cap, one:one + 1], 1.0, 0.0)
                for one in (source, source + 1)
            ],
            axis=0,
        ).astype(BF16)
    base = ylo_ref.shape[0] - rim_rows(2 * rim * pieces, ylo_ref.shape[1])
    for which, ref in enumerate((temp_ref, cond_ref)):
        ref[...] = state_ref[which]
        for k in range(rim):
            for h in range(pieces):
                n = (which * rim + k) * pieces + h
                cut = slice(h * PART, (h + 1) * PART)
                ref[cut, OFF - rim + k, :] = get_rim(ylo_ref, base, n)
                ref[cut, OFF + sy + k, :] = get_rim(yhi_ref, base, n)
    kind = cond_ref[...]
    sigma_ref[...] = table(kind[rim - 1:rim + sx + 1], modulus_table)
    cond_ref[...] = solid_step * table(kind, conduct_table)


def ready(rim, cap, state, ylo, yhi, code, block):
    sx, sy, sz = block
    _, long, height, _ = state.shape
    ndev = code.shape[0]
    args = (far(state), ylo, yhi, code)
    return pl.pallas_call(
        functools.partial(ready_kernel, rim, cap),
        grid=(1,),
        in_specs=[whole(x.shape) for x in args],
        out_specs=[in_vmem] * 4,
        out_shape=[
            pltpu.VMEM((long, height, sz), F32),
            pltpu.VMEM((long, height, sz), F32),
            pltpu.VMEM((sx + 2, height, sz), F32),
            pltpu.VMEM((ndev * cap, sx * sy), BF16),
        ],
        compiler_params=params(14),
        cost_estimate=cost(4 * ndev * cap * sx * sy, 4 * ndev * cap * sx * sy),
        name="ready",
    )(*args)


def solid_kernel(rim, start_ref, cond_ref, modulus_ref, pick_ref,
                 heat_ref, hxlo_ref, hxhi_ref, hylo_ref, hyhi_ref,
                 next_ref, sigma_ref, reply_ref, even_ref, odd_ref, src_ref, rhs_ref,
                 stage_ref, sems):
    sx, sy, sz = heat_ref.shape
    wide = sx + 2 * rim
    thin = rim - 1
    edge = thin * sy
    src_ref[rim:rim + sx, OFF:OFF + sy, :] = heat_ref[...]
    src_ref[1:rim, OFF:OFF + sy, :] = hxlo_ref[:edge, :].reshape(thin, sy, sz)
    src_ref[rim + sx:wide - 1, OFF:OFF + sy, :] = hxhi_ref[:edge, :].reshape(thin, sy, sz)
    parts = -(-(sx + 2 * thin) // PART)
    base = hylo_ref.shape[0] - rim_rows(thin * parts, hylo_ref.shape[1])
    for k in range(thin):
        for h in range(parts):
            n = k * parts + h
            count = min(PART, sx + 2 * thin - h * PART)
            cut = slice(1 + h * PART, 1 + h * PART + count)
            src_ref[cut, OFF - thin + k, :] = get_rim(hylo_ref, base, n)[:count]
            src_ref[cut, OFF + sy + k, :] = get_rim(hyhi_ref, base, n)[:count]
    src_ref[...] = (solid_step * source_gain) * src_ref[...]
    height = start_ref.shape[1]
    first = lax.broadcasted_iota(jnp.int32, (height, sz), 1) == 0
    last = lax.broadcasted_iota(jnp.int32, (height, sz), 1) == sz - 1
    now = start_ref
    for turn in range(rim - 1):
        later = (odd_ref, even_ref)[turn % 2]
        for x in range(1 + turn, wide - 1 - turn):
            centre = now[x]
            beside = now[x - 1] + now[x + 1]
            beside += pltpu.roll(centre, 1, 0) + pltpu.roll(centre, height - 1, 0)
            beside += jnp.where(first, 0.0, pltpu.roll(centre, 1, 1))
            beside += jnp.where(last, 0.0, pltpu.roll(centre, sz - 1, 1))
            later[x] = centre + (cond_ref[x] * (beside - 6.0 * centre) + src_ref[x])
        now = later
    solid = now[rim:rim + sx, OFF:OFF + sy, :]
    next_ref[...] = solid
    sigma_ref[...] = modulus_ref[...] * now[rim - 1:rim + sx + 1]
    high, low = halves(solid.reshape(sx * sy, sz))
    rhs_ref[:, :sz] = high
    rhs_ref[:, sz:] = low
    block = pick_ref.shape[0] // GROUPS
    copies = []
    for index in range(GROUPS):
        cut = slice(index * block, (index + 1) * block)
        both = jnp.dot(pick_ref[cut, :], rhs_ref[...], preferred_element_type=F32)
        stage_ref[cut, :] = both[:, :sz] + both[:, sz:]
        copies.append(pltpu.make_async_copy(stage_ref.at[cut], reply_ref.at[cut], sems.at[index]))
        copies[-1].start()
    for copy in copies:
        copy.wait()


def solid_steps(rim, prepared, heat, heat_rim):
    sx, sy, sz = heat.shape
    long, height, _ = prepared[0].shape
    total = prepared[3].shape[0]
    return pl.pallas_call(
        functools.partial(solid_kernel, rim),
        in_specs=[in_vmem] * 9,
        out_specs=[in_vmem, in_vmem, in_hbm],
        out_shape=[
            jax.ShapeDtypeStruct((sx, sy, sz), F32),
            jax.ShapeDtypeStruct((sx + 2, height, sz), F32),
            pltpu.HBM((total, sz), F32),
        ],
        scratch_shapes=[pltpu.VMEM((long, height, sz), F32)] * 2
        + [
            pltpu.VMEM((sx + 2 * rim, height, sz), F32),
            pltpu.VMEM((sx * sy, 2 * sz), BF16),
            pltpu.VMEM((total, sz), F32),
            pltpu.SemaphoreType.DMA((GROUPS,)),
        ],
        compiler_params=params(14),
        cost_estimate=cost(4 * total * sx * sy * sz, 4 * total * sz),
        name="solid_steps",
    )(*[near(x) for x in prepared], heat, *heat_rim)


def stress_kernel(sigma_ref, out_ref, tick_ref):
    tick_ref[...] = jnp.zeros_like(tick_ref)
    _, sx, sy, sz = out_ref.shape
    height = sigma_ref.shape[1]
    first = lax.broadcasted_iota(jnp.int32, (height, sz), 1) == 0
    last = lax.broadcasted_iota(jnp.int32, (height, sz), 1) == sz - 1

    def plane(x, none):
        centre = sigma_ref[x + 1]
        out_ref[0, x] = 0.5 * (sigma_ref[x + 2] - sigma_ref[x])[OFF:OFF + sy]
        along = pltpu.roll(centre, height - 1, 0) - pltpu.roll(centre, 1, 0)
        out_ref[1, x] = 0.5 * along[OFF:OFF + sy]
        along = jnp.where(last, 0.0, pltpu.roll(centre, sz - 1, 1)) - jnp.where(
            first, 0.0, pltpu.roll(centre, 1, 1)
        )
        out_ref[2, x] = 0.5 * along[OFF:OFF + sy]
        return none

    lax.fori_loop(0, sx, plane, 0)


def stress(sigma, sx, sy):
    sz = sigma.shape[2]
    return pl.pallas_call(
        stress_kernel,
        grid=(1,),
        in_specs=[whole(sigma.shape)],
        out_specs=[whole((3, sx, sy, sz)), whole((8, LANE))],
        out_shape=[pltpu.HBM((3, sx, sy, sz), F32), jax.ShapeDtypeStruct((8, LANE), F32)],
        compiler_params=params(8),
        cost_estimate=cost(10 * sx * sy * sz, 16 * sx * sy * sz),
        name="stress",
    )(sigma)


def unpack_kernel(dest_ref, back_ref, *refs):
    out_ref = refs[-1]
    rows = out_ref.shape[0]

    def step(index, none):
        base = pl.multiple_of(index * 8, 8)
        lines = [back_ref[pl.ds(dest_ref[0, base + i], 1), :] for i in range(8)]
        for i, line in enumerate(lines):
            out_ref[pl.ds(base + i, 1), :] = line
        return none

    lax.fori_loop(0, rows // 8, step, 0, unroll=4)


def unpack(dest, back, after):
    rows = dest.shape[1]
    row_len = back.shape[1]
    return pl.pallas_call(
        unpack_kernel,
        grid=(1,),
        in_specs=[pl.BlockSpec(memory_space=pltpu.SMEM), whole(back.shape)]
        + [anywhere] * len(after),
        out_specs=whole((rows, row_len)),
        out_shape=jax.ShapeDtypeStruct((rows, row_len), F32),
        compiler_params=params(10),
        cost_estimate=cost(rows * 128, 8 * rows * row_len),
        name="unpack",
    )(dest, back, *after)


PLANES = 2
RING = 3 * PLANES


def fluid_kernel(opening, here_ref, xlo_ref, xhi_ref, speed_ref, flux_ref, *refs):
    index, count = pl.program_id(0), pl.num_programs(0)
    cx = (count - 1) * PLANES
    _, cy, depth = here_ref.shape
    row_len = flux_ref.shape[2]
    rows = slice(OFF, OFF + cy)
    if opening:
        out_ref, xfirst_ref, xlast_ref, yfirst_ref, ylast_ref, clo_ref, chi_ref, ring_ref = refs
    else:
        lo_ref, hi_ref, left_ref, right_ref, ylo_ref, yhi_ref = refs[:6]
        out_ref, tick_ref, ring_ref = refs[-3:]
        tick_ref[...] = jnp.zeros_like(tick_ref)

    def patch(slot, corner_ref):
        wide = depth // LANE
        base = corner_ref.shape[0] - 2 * wide
        for row, at in ((OFF, base), (OFF + cy - 1, base + wide)):
            for i in range(wide):
                ring_ref[slot, row:row + 1, i * LANE:(i + 1) * LANE] = (
                    corner_ref[at + i:at + i + 1, :]
                )

    @pl.when(index == 0)
    def _():
        ring_ref[RING - 1, rows, :] = xlo_ref[...]
        if opening:
            for slot in range(RING):
                ring_ref[slot, OFF - 8:OFF, :] = jnp.zeros((8, depth), F32)
                ring_ref[slot, OFF + cy:OFF + cy + 8, :] = jnp.zeros((8, depth), F32)
        else:
            patch(RING - 1, lo_ref)

    @pl.when(index < count - 1)
    def _():
        for p in range(PLANES):
            plane = index * PLANES + p
            slot = lax.rem(plane, RING)
            ring_ref[slot, rows, :] = here_ref[p]
            if not opening:
                one = pl.ds(plane, 1)
                ring_ref[slot, OFF:OFF + 1, :] = left_ref[one, :]
                ring_ref[slot, OFF + cy - 1:OFF + cy, :] = right_ref[one, :]
                ring_ref[slot, OFF - 1:OFF, :] = ylo_ref[one, :]
                ring_ref[slot, OFF + cy:OFF + cy + 1, :] = yhi_ref[one, :]

    @pl.when(index == count - 1)
    def _():
        ring_ref[lax.rem(cx, RING), rows, :] = xhi_ref[...]
        if not opening:
            patch(lax.rem(cx, RING), hi_ref)

    rate = time_step * diffusivity

    def push(total, centre, lower, upper, speed):
        scaled = time_step * speed
        total = total + (rate + jnp.maximum(scaled, 0.0)) * (lower - centre)
        return total + (rate - jnp.minimum(scaled, 0.0)) * (upper - centre)

    def advance(p, none):
        lanes = lax.broadcasted_iota(jnp.int32, (8, depth), 1)
        first, last = lanes == 0, lanes == depth - 1
        plane = (index - 1) * PLANES + p
        mid = lax.rem(plane, RING)
        old, new = lax.rem(plane + RING - 1, RING), lax.rem(plane + 1, RING)
        for tile in range(cy // 16):
            speeds = [
                speed_ref[k, p, tile * 16:tile * 16 + 16, :].astype(F32) for k in range(3)
            ]
            for part in range(2):
                y = tile * 16 + part * 8
                at = OFF + y
                u, v, w = [s[part * 8:part * 8 + 8] for s in speeds]
                centre = ring_ref[mid, at:at + 8, :]
                total = push(
                    centre, centre, ring_ref[old, at:at + 8, :], ring_ref[new, at:at + 8, :], u
                )
                total = push(
                    total, centre, ring_ref[mid, at - 1:at + 7, :],
                    ring_ref[mid, at + 1:at + 9, :], v,
                )
                lower = jnp.where(first, 0.0, pltpu.roll(centre, 1, 1))
                upper = jnp.where(last, 0.0, pltpu.roll(centre, depth - 1, 1))
                total = push(total, centre, lower, upper, w)
                out_ref[p, y:y + 8, row_len:] = total[:, row_len:]
                out_ref[p, y:y + 8, :row_len] = (
                    total[:, :row_len] - time_step * flux_ref[p, y:y + 8, :]
                )
        if opening:
            one = pl.ds(plane, 1)
            yfirst_ref[one, :] = out_ref[p, 0:1, :]
            ylast_ref[one, :] = out_ref[p, cy - 1:cy, :]
            edge = time_step * speed_ref[1, p, 0:16, :].astype(F32)
            clo_ref[one, :] = rate + jnp.maximum(edge[0:1], 0.0)
            edge = time_step * speed_ref[1, p, cy - 16:cy, :].astype(F32)
            chi_ref[one, :] = rate - jnp.minimum(edge[15:16], 0.0)
        return none

    @pl.when(index > 0)
    def _():
        lax.fori_loop(0, PLANES, advance, 0)

    if opening:

        @pl.when(index == 1)
        def _():
            xfirst_ref[...] = out_ref[0]

        @pl.when(index == count - 1)
        def _():
            xlast_ref[...] = out_ref[PLANES - 1]


def fluid_step(opening, temp, sides, velocity, flux, lines, after):
    cx, cy, depth = temp.shape
    row_len = flux.shape[2]
    plane = (PLANES, cy, depth)
    steps = cx // PLANES
    face = pl.BlockSpec((cy, depth), lambda i: (0, 0))
    line = pl.BlockSpec((cx, depth), lambda i: (0, 0))
    back = lambda i: (jnp.maximum(i - 1, 0), 0, 0)
    shape = jax.ShapeDtypeStruct
    outs = [pl.BlockSpec(plane, back)]
    outs += [face, face] + [line] * 4 if opening else [whole((8, LANE))]
    shapes = [pltpu.HBM(temp.shape, F32)]
    if opening:
        shapes += [shape((cy, depth), F32)] * 2 + [shape((cx, depth), F32)] * 4
    else:
        shapes += [shape((8, LANE), F32)]
    extra = [whole(x.shape) for x in lines[:2]] + [line] * len(lines[2:])
    return pl.pallas_call(
        functools.partial(fluid_kernel, opening),
        grid=(steps + 1,),
        in_specs=[
            pl.BlockSpec(plane, lambda i: (jnp.minimum(i, steps - 1), 0, 0)),
            face,
            face,
            pl.BlockSpec((3, PLANES, cy, depth), lambda i: (0, jnp.maximum(i - 1, 0), 0, 0)),
            pl.BlockSpec((PLANES, cy, row_len), back),
        ]
        + extra
        + [anywhere] * len(after),
        out_specs=outs,
        out_shape=shapes,
        scratch_shapes=[pltpu.VMEM((RING, cy + 2 * OFF, depth), F32)],
        compiler_params=params(16),
        cost_estimate=cost(40 * cx * cy * depth, 14 * cx * cy * depth),
        name="fluid_step",
    )(far(temp), *sides, far(velocity), flux, *lines, *after)


def body(temp_fluid, velocity, wall_old, wall_mask, owner_map, slot_map, temp_solid, material):
    cx, cy, depth = temp_fluid.shape
    row_len = wall_old.shape[2]
    sx, sy, sz = temp_solid.shape
    ndev = lax.axis_size("gx") * lax.axis_size("gy")
    rows = cx * cy
    cap = (3 * rows + ndev - 1) // ndev
    cap = -(-cap // 8) * 8
    total = ndev * cap
    rim = SSTEPS + 1

    first, last = x_faces(rim, temp_fluid, temp_solid, material)
    xlo, xhi = neighbours(last, first, "gx")
    dest, where, codes = rank(owner_map.reshape(1, rows), slot_map, ndev, cap)
    outgoing, flux = pack(where, codes, temp_fluid, wall_old, wall_mask, cap, (first, last))
    outgoing, xlo, xhi = lax.optimization_barrier((outgoing, xlo, xhi))
    incoming = lax.all_to_all(outgoing, AXES, split_axis=0, concat_axis=0, tiled=True)

    left, right, state = y_faces(rim, temp_fluid, temp_solid, material, xlo, xhi)
    ylo, yhi = neighbours(right, left, "gy")
    fluid, first, last, *edges = fluid_step(
        True, temp_fluid, (xlo, xhi), velocity, flux, (), ()
    )
    sides = neighbours(last, first, "gx")

    thin = rim - 1
    heat, first, last, left, right, code = heat_sum(
        incoming, cap, temp_solid.shape, thin, sides, (ylo, yhi, *edges)
    )
    hxlo, hxhi = neighbours(last, first, "gx")
    first, last = strips(thin, heat, hxlo, hxhi, left, right)
    hylo, hyhi = neighbours(last, first, "gy")
    prepared = ready(rim, cap, state, ylo, yhi, code, heat.shape)
    solid, sigma, replies = solid_steps(rim, prepared, heat, (hxlo, hxhi, hylo, hyhi))
    returned = lax.all_to_all(
        replies.reshape(ndev, cap, sz), AXES, split_axis=0, concat_axis=0, tiled=True
    )
    force, tick = stress(sigma, sx, sy)
    fluid, tick = fluid_step(
        False, fluid, sides, velocity, flux, (hxlo, hxhi, left, right, hylo, hyhi), (tick,)
    )
    wall_next = unpack(dest, returned.reshape(total, sz), (tick,))
    return fluid, wall_next.reshape(cx, cy, row_len), solid, force


def solution(mesh):
    placed = (
        P("gx", "gy", None),
        P(None, "gx", "gy", None),
        P("gx", "gy", None),
        P("gx", "gy", None),
        P(("gx", "gy"), None, None),
        P(("gx", "gy"), None),
        P("gx", "gy", None),
        P("gx", "gy", None),
    )
    return jax.shard_map(
        body,
        mesh=mesh,
        in_specs=placed,
        out_specs=(
            P("gx", "gy", None),
            P("gx", "gy", None),
            P("gx", "gy", None),
            P(None, "gx", "gy", None),
        ),
        check_vma=False,
    )
```

```python
import functools
import jax
import jax.numpy as jnp
from jax import lax
from jax.experimental import pallas as pl
from jax.experimental.pallas import tpu as pltpu
from jax.sharding import PartitionSpec as P

FSTEPS = 2
SSTEPS = 4
time_step = 0.1
diffusivity = 0.5
film_coef = 2.0
solid_step = 0.05
source_gain = 4.0
conduct_table = (0.4, 0.9, 1.5, 2.2)
modulus_table = (0.5, 1.0, 1.6, 2.4)
F32 = jnp.float32
BF16 = jnp.bfloat16
AXES = ("gx", "gy")
LANE = 128
PART = 8
OFF = 8


def params(mib):
    return pltpu.CompilerParams(vmem_limit_bytes=mib * 1024 * 1024)


def cost(flops, bytes_accessed):
    return pl.CostEstimate(flops=flops, bytes_accessed=bytes_accessed, transcendentals=0)


def halves(value):
    high = value.astype(BF16)
    low = (value - high.astype(F32)).astype(BF16)
    return high, low


def ones_where(test):
    return jnp.where(test, 1.0, 0.0).astype(BF16)


def neighbours(before, after, axis):
    size = lax.axis_size(axis)
    up = [(i, i + 1) for i in range(size - 1)]
    down = [(j, i) for i, j in up]
    return lax.ppermute(before, axis, up), lax.ppermute(after, axis, down)


def whole(shape):
    return pl.BlockSpec(shape, lambda i: (0,) * len(shape))


anywhere = pl.BlockSpec(memory_space=pl.ANY)
in_vmem = pl.BlockSpec(memory_space=pltpu.VMEM)
in_hbm = pl.BlockSpec(memory_space=pltpu.HBM)


def far(value):
    return pltpu.with_memory_space_constraint(value, pltpu.HBM)


def near(value):
    return pltpu.with_memory_space_constraint(value, pltpu.VMEM)


def rank_kernel(cap, owner_ref, slot_ref, dest_ref, where_ref, code_ref):
    rows = owner_ref.shape[1]
    ndev = code_ref.shape[0]
    tall = cap + 8
    tri = ones_where(
        lax.broadcasted_iota(jnp.int32, (LANE, LANE), 0)
        <= lax.broadcasted_iota(jnp.int32, (LANE, LANE), 1)
    )
    names = lax.broadcasted_iota(jnp.int32, (ndev, LANE), 0)
    steps = lax.broadcasted_iota(jnp.int32, (LANE, LANE), 0)
    carry = jnp.zeros((ndev, 1), F32)
    codes = jnp.zeros((2 * ndev, LANE), F32)
    for chunk in range(rows // LANE):
        cols = slice(chunk * LANE, (chunk + 1) * LANE)
        own = owner_ref[:, cols]
        hit = jnp.where(names == own, 1.0, 0.0)
        ranks = jnp.dot(hit.astype(BF16), tri, preferred_element_type=F32) + carry
        carry = ranks[:, LANE - 1:]
        place = jnp.sum(hit * ranks, axis=0, keepdims=True).astype(jnp.int32) - 1
        dest_ref[:, cols] = own * cap + place
        where_ref[:, cols] = own * tall + place
        code = slot_ref[:, cols] + 1
        pieces = jnp.concatenate(
            [hit * (code // 32).astype(F32), hit * (code % 32).astype(F32)], axis=0
        ).astype(BF16)
        codes = codes + lax.dot_general(
            pieces, ones_where(steps == place), (((1,), (1,)), ((), ())),
            preferred_element_type=F32,
        )
    code_ref[...] = codes[:ndev] * 32.0 + codes[ndev:]


def rank(owner, slot, ndev, cap):
    rows = owner.shape[1]
    line = jax.ShapeDtypeStruct((1, rows), jnp.int32)
    return pl.pallas_call(
        functools.partial(rank_kernel, cap),
        grid=(1,),
        in_specs=[whole((1, rows))] * 2,
        out_specs=[whole((1, rows))] * 2 + [whole((ndev, LANE))],
        out_shape=[line, line, jax.ShapeDtypeStruct((ndev, LANE), F32)],
        compiler_params=params(8),
        cost_estimate=cost(8 * ndev * LANE * rows, 20 * rows),
        name="rank",
    )(owner, slot)


GROUPS = 4


def pack_kernel(cap, where_ref, code_ref, temp_ref, old_ref, mask_ref, *refs):
    out_ref, flux_ref, rhs_ref, stage_ref, sems = refs[-5:]
    rows = where_ref.shape[1]
    ndev, tall, row_len = stage_ref.shape
    flux = mask_ref[...].astype(F32) * film_coef * (temp_ref[...] - old_ref[...])
    flux_ref[...] = flux
    high, low = halves(flux.reshape(rows, row_len))
    rhs_ref[:, :row_len] = high
    rhs_ref[:, row_len:] = low
    where = where_ref[...]
    group = ndev // GROUPS
    block = group * tall
    lines = lax.broadcasted_iota(jnp.int32, (block, rows), 0)
    copies = []
    for index in range(GROUPS):
        cut = slice(index * group, (index + 1) * group)
        pick = ones_where(lines == where - index * block)
        both = jnp.dot(pick, rhs_ref[...], preferred_element_type=F32)
        both = both[:, :row_len] + both[:, row_len:]
        stage_ref[cut] = both.reshape(group, tall, row_len)
        stage_ref[cut, cap, :] = code_ref[cut, :]
        copies.append(pltpu.make_async_copy(stage_ref.at[cut], out_ref.at[cut], sems.at[index]))
        copies[-1].start()
    for copy in copies:
        copy.wait()


def pack(where, code, temp, old, mask, cap, after):
    cx, cy, _ = temp.shape
    row_len = old.shape[2]
    rows = cx * cy
    ndev = code.shape[0]
    tall = cap + 8
    return pl.pallas_call(
        functools.partial(pack_kernel, cap),
        grid=(1,),
        in_specs=[whole((1, rows)), whole(code.shape)]
        + [whole((cx, cy, row_len))] * 3
        + [anywhere] * len(after),
        out_specs=[in_hbm, whole((cx, cy, row_len))],
        out_shape=[
            pltpu.HBM((ndev, tall, row_len), F32),
            jax.ShapeDtypeStruct((cx, cy, row_len), F32),
        ],
        scratch_shapes=[
            pltpu.VMEM((rows, 2 * row_len), BF16),
            pltpu.VMEM((ndev, tall, row_len), F32),
            pltpu.SemaphoreType.DMA((GROUPS,)),
        ],
        compiler_params=params(18),
        cost_estimate=cost(4 * ndev * tall * rows * row_len, 5 * rows * row_len * 4),
        name="pack",
    )(where, code, far(temp), far(old), far(mask), *after)


def heat_kernel(cap, thin, rows_ref, xfirst_ref, xlast_ref, ylo_ref, yhi_ref,
                yfirst_ref, ylast_ref, clo_ref, chi_ref,
                heat_ref, low_ref, high_ref, left_ref, right_ref, code_ref):
    ndev, tall, row_len = rows_ref.shape
    cx, depth = yfirst_ref.shape
    sx, sy, _ = heat_ref.shape
    slots = sx * sy
    left = yfirst_ref[...] + clo_ref[...] * ylo_ref[:cx, :]
    right = ylast_ref[...] + chi_ref[...] * yhi_ref[:cx, :]
    left_ref[...] = left
    right_ref[...] = right
    edge = thin * sy
    for ref, x in ((low_ref, 0), (high_ref, cx - 1)):
        for at, line in ((edge, left[x:x + 1]), (edge + depth // LANE, right[x:x + 1])):
            for i in range(depth // LANE):
                ref[at + i:at + i + 1, :] = line[:, i * LANE:(i + 1) * LANE]
    codes = rows_ref[:, cap, :].astype(jnp.int32) - 1
    code_ref[...] = codes
    group = ndev // GROUPS
    names = lax.broadcasted_iota(jnp.int32, (slots, tall), 0)
    total = jnp.zeros((slots, 2 * row_len), F32)
    for index in range(0, ndev, group):
        lines = rows_ref[index:index + group].reshape(group * tall, row_len)
        high, low = halves(lines)
        pick = jnp.concatenate(
            [
                jnp.where(names == codes[index + i:index + i + 1, :tall], 1.0, 0.0)
                for i in range(group)
            ],
            axis=1,
        ).astype(BF16)
        total = total + jnp.dot(
            pick, jnp.concatenate([high, low], axis=1), preferred_element_type=F32
        )
    heat = total[:, :row_len] + total[:, row_len:]
    heat_ref[...] = heat.reshape(sx, sy, row_len)
    low_ref[:edge, :] = heat[:edge]
    high_ref[:edge, :] = heat[slots - edge:]


def heat_sum(incoming, cap, block, thin, faces, edges):
    ndev, tall, row_len = incoming.shape
    sx, sy, _ = block
    line = edges[2].shape
    edge = (thin * sy + 2 * (line[1] // LANE), row_len)
    return pl.pallas_call(
        functools.partial(heat_kernel, cap, thin),
        grid=(1,),
        in_specs=[whole(incoming.shape)] + [anywhere] * 2 + [whole(x.shape) for x in edges],
        out_specs=[whole(block), whole(edge), whole(edge), whole(line), whole(line)]
        + [whole((ndev, row_len))],
        out_shape=[
            jax.ShapeDtypeStruct(block, F32),
            jax.ShapeDtypeStruct(edge, F32),
            jax.ShapeDtypeStruct(edge, F32),
            jax.ShapeDtypeStruct(line, F32),
            jax.ShapeDtypeStruct(line, F32),
            jax.ShapeDtypeStruct((ndev, row_len), jnp.int32),
        ],
        compiler_params=params(14),
        cost_estimate=cost(4 * ndev * tall * sx * sy * row_len, 4 * ndev * tall * row_len),
        name="heat_sum",
    )(incoming, *faces, *edges)


def put_rim(ref, base, slabs):
    across = ref.shape[1] // LANE
    for n, slab in enumerate(slabs):
        row = base + n // across * PART
        ref[row:row + PART, n % across * LANE:(n % across + 1) * LANE] = slab


def get_rim(ref, base, n):
    across = ref.shape[1] // LANE
    row = base + n // across * PART
    return ref[row:row + PART, n % across * LANE:(n % across + 1) * LANE]


def rim_rows(count, depth):
    across = depth // LANE
    return -(-count // across) * PART


def x_faces_kernel(rim, bottom_ref, top_ref, temp_ref, kind_ref, low_ref, high_ref):
    _, cy, _ = bottom_ref.shape
    sx, sy, _ = temp_ref.shape
    low_ref[:cy, :] = bottom_ref[0]
    high_ref[:cy, :] = top_ref[0]
    for ref, start in ((low_ref, 0), (high_ref, sx - rim)):
        slabs = [
            get(start + k, slice(h, h + PART))
            for get in (
                lambda x, cut: temp_ref[x, cut, :],
                lambda x, cut: kind_ref[x, cut, :].astype(F32) + 1.0,
            )
            for k in range(rim)
            for h in range(0, sy, PART)
        ]
        put_rim(ref, cy, slabs)


def x_faces(rim, fluid, temp, kind):
    cx, cy, depth = fluid.shape
    sx, sy, sz = temp.shape
    height = cy + rim_rows(2 * rim * (sy // PART), depth)
    plane = (1, cy, depth)
    return pl.pallas_call(
        functools.partial(x_faces_kernel, rim),
        grid=(1,),
        in_specs=[
            pl.BlockSpec(plane, lambda i: (0, 0, 0)),
            pl.BlockSpec(plane, lambda i: (cx - 1, 0, 0)),
            whole(temp.shape),
            whole(temp.shape),
        ],
        out_specs=[whole((height, depth))] * 2,
        out_shape=[jax.ShapeDtypeStruct((height, depth), F32)] * 2,
        compiler_params=params(16),
        cost_estimate=cost(1000, 4 * 4 * height * depth),
        name="x_faces",
    )(far(fluid), far(fluid), far(temp), far(kind))


def fill_x(rim, ref, which, own, lo_ref, hi_ref):
    sx, sy, _ = own.shape
    pieces = sy // PART
    base = lo_ref.shape[0] - rim_rows(2 * rim * pieces, lo_ref.shape[1])
    ref[rim:rim + sx, OFF:OFF + sy, :] = own
    for k in range(rim):
        for h in range(pieces):
            n = (which * rim + k) * pieces + h
            cut = slice(OFF + h * PART, OFF + (h + 1) * PART)
            ref[k, cut, :] = get_rim(lo_ref, base, n)
            ref[rim + sx + k, cut, :] = get_rim(hi_ref, base, n)


def y_faces_kernel(rim, near_ref, far_ref, temp_ref, kind_ref, lo_ref, hi_ref,
                   left_ref, right_ref, state_ref):
    cx, near_rows, _ = near_ref.shape
    sx, sy, _ = temp_ref.shape
    left_ref[:cx, :] = near_ref[:, 0, :]
    right_ref[:cx, :] = far_ref[:, near_rows - 1, :]
    slabs = ([], [])
    long = state_ref.shape[1]
    state_ref[...] = jnp.zeros_like(state_ref)
    for which, own in enumerate((temp_ref[...], kind_ref[...].astype(F32) + 1.0)):
        fill_x(rim, state_ref.at[which], which, own, lo_ref, hi_ref)
        for into, start in zip(slabs, (OFF, OFF + sy - rim)):
            for k in range(rim):
                for h in range(0, long, PART):
                    into.append(state_ref[which, h:h + PART, start + k, :])
    put_rim(left_ref, cx, slabs[0])
    put_rim(right_ref, cx, slabs[1])


def y_faces(rim, fluid, temp, kind, lo, hi):
    cx, cy, depth = fluid.shape
    sx, sy, sz = temp.shape
    long = -(-(sx + 2 * rim) // PART) * PART
    height = cx + rim_rows(2 * rim * (long // PART), depth)
    args = (far(temp), far(kind), lo, hi)
    edge = (cx, 8, depth)
    return pl.pallas_call(
        functools.partial(y_faces_kernel, rim),
        grid=(1,),
        in_specs=[
            pl.BlockSpec(edge, lambda i: (0, 0, 0)),
            pl.BlockSpec(edge, lambda i: (0, cy // 8 - 1, 0)),
        ]
        + [whole(x.shape) for x in args],
        out_specs=[whole((height, depth))] * 2 + [whole((2, long, sy + 2 * OFF, sz))],
        out_shape=[jax.ShapeDtypeStruct((height, depth), F32)] * 2
        + [pltpu.HBM((2, long, sy + 2 * OFF, sz), F32)],
        compiler_params=params(10),
        cost_estimate=cost(1000, 4 * 4 * height * depth),
        name="y_faces",
    )(far(fluid), far(fluid), *args)


def strips_kernel(thin, heat_ref, lo_ref, hi_ref, near_ref, away_ref,
                  left_ref, right_ref, work_ref):
    cx = near_ref.shape[0]
    sx, sy, sz = heat_ref.shape
    edge = thin * sy
    left_ref[:cx, :] = near_ref[...]
    right_ref[:cx, :] = away_ref[...]
    work_ref[...] = jnp.zeros_like(work_ref)
    work_ref[:thin] = lo_ref[:edge, :].reshape(thin, sy, sz)
    work_ref[thin:thin + sx] = heat_ref[...]
    work_ref[thin + sx:2 * thin + sx] = hi_ref[:edge, :].reshape(thin, sy, sz)
    long = work_ref.shape[0]
    for ref, start in ((left_ref, 0), (right_ref, sy - thin)):
        slabs = [
            work_ref[h:h + PART, start + k, :] for k in range(thin) for h in range(0, long, PART)
        ]
        put_rim(ref, cx, slabs)


def strips(thin, heat, lo, hi, left, right):
    cx, depth = left.shape
    sx, sy, sz = heat.shape
    long = -(-(sx + 2 * thin) // PART) * PART
    height = cx + rim_rows(thin * (long // PART), depth)
    return pl.pallas_call(
        functools.partial(strips_kernel, thin),
        in_specs=[in_vmem] * 5,
        out_specs=[in_vmem] * 2,
        out_shape=[jax.ShapeDtypeStruct((height, depth), F32)] * 2,
        scratch_shapes=[pltpu.VMEM((long, sy, sz), F32)],
        compiler_params=params(8),
        cost_estimate=cost(1000, 16 * height * depth),
        name="strips",
    )(heat, lo, hi, left, right)


def table(kind, values):
    out = jnp.zeros(kind.shape, F32)
    for index, value in enumerate(values):
        out = jnp.where(kind == index + 1.0, value, out)
    return out


def ready_kernel(rim, cap, state_ref, ylo_ref, yhi_ref, code_ref,
                 temp_ref, cond_ref, sigma_ref, pick_ref):
    _, long, height, sz = state_ref.shape
    ndev = code_ref.shape[0]
    slots = pick_ref.shape[1]
    sx = sigma_ref.shape[0] - 2
    sy = height - 2 * OFF
    pieces = long // PART
    turned = jnp.transpose(code_ref[...])
    names = lax.broadcasted_iota(jnp.int32, (cap, slots), 1)
    for source in range(0, ndev, 2):
        pick_ref[source * cap:(source + 2) * cap, :] = jnp.concatenate(
            [
                jnp.where(names == turned[:cap, one:one + 1], 1.0, 0.0)
                for one in (source, source + 1)
            ],
            axis=0,
        ).astype(BF16)
    base = ylo_ref.shape[0] - rim_rows(2 * rim * pieces, ylo_ref.shape[1])
    for which, ref in enumerate((temp_ref, cond_ref)):
        ref[...] = state_ref[which]
        for k in range(rim):
            for h in range(pieces):
                n = (which * rim + k) * pieces + h
                cut = slice(h * PART, (h + 1) * PART)
                ref[cut, OFF - rim + k, :] = get_rim(ylo_ref, base, n)
                ref[cut, OFF + sy + k, :] = get_rim(yhi_ref, base, n)
    kind = cond_ref[...]
    sigma_ref[...] = table(kind[rim - 1:rim + sx + 1], modulus_table)
    cond_ref[...] = solid_step * table(kind, conduct_table)


def ready(rim, cap, state, ylo, yhi, code, block):
    sx, sy, sz = block
    _, long, height, _ = state.shape
    ndev = code.shape[0]
    args = (far(state), ylo, yhi, code)
    return pl.pallas_call(
        functools.partial(ready_kernel, rim, cap),
        grid=(1,),
        in_specs=[whole(x.shape) for x in args],
        out_specs=[in_vmem] * 4,
        out_shape=[
            pltpu.VMEM((long, height, sz), F32),
            pltpu.VMEM((long, height, sz), F32),
            pltpu.VMEM((sx + 2, height, sz), F32),
            pltpu.VMEM((ndev * cap, sx * sy), BF16),
        ],
        compiler_params=params(14),
        cost_estimate=cost(4 * ndev * cap * sx * sy, 4 * ndev * cap * sx * sy),
        name="ready",
    )(*args)


def solid_kernel(rim, start_ref, cond_ref, modulus_ref, pick_ref,
                 heat_ref, hxlo_ref, hxhi_ref, hylo_ref, hyhi_ref,
                 next_ref, sigma_ref, reply_ref, even_ref, odd_ref, src_ref, rhs_ref,
                 stage_ref, sems):
    sx, sy, sz = heat_ref.shape
    wide = sx + 2 * rim
    thin = rim - 1
    edge = thin * sy
    src_ref[rim:rim + sx, OFF:OFF + sy, :] = heat_ref[...]
    src_ref[1:rim, OFF:OFF + sy, :] = hxlo_ref[:edge, :].reshape(thin, sy, sz)
    src_ref[rim + sx:wide - 1, OFF:OFF + sy, :] = hxhi_ref[:edge, :].reshape(thin, sy, sz)
    parts = -(-(sx + 2 * thin) // PART)
    base = hylo_ref.shape[0] - rim_rows(thin * parts, hylo_ref.shape[1])
    for k in range(thin):
        for h in range(parts):
            n = k * parts + h
            count = min(PART, sx + 2 * thin - h * PART)
            cut = slice(1 + h * PART, 1 + h * PART + count)
            src_ref[cut, OFF - thin + k, :] = get_rim(hylo_ref, base, n)[:count]
            src_ref[cut, OFF + sy + k, :] = get_rim(hyhi_ref, base, n)[:count]
    src_ref[...] = (solid_step * source_gain) * src_ref[...]
    height = start_ref.shape[1]
    first = lax.broadcasted_iota(jnp.int32, (height, sz), 1) == 0
    last = lax.broadcasted_iota(jnp.int32, (height, sz), 1) == sz - 1
    now = start_ref
    for turn in range(rim - 1):
        later = (odd_ref, even_ref)[turn % 2]
        for x in range(1 + turn, wide - 1 - turn):
            centre = now[x]
            beside = now[x - 1] + now[x + 1]
            beside += pltpu.roll(centre, 1, 0) + pltpu.roll(centre, height - 1, 0)
            beside += jnp.where(first, 0.0, pltpu.roll(centre, 1, 1))
            beside += jnp.where(last, 0.0, pltpu.roll(centre, sz - 1, 1))
            later[x] = centre + (cond_ref[x] * (beside - 6.0 * centre) + src_ref[x])
        now = later
    solid = now[rim:rim + sx, OFF:OFF + sy, :]
    next_ref[...] = solid
    sigma_ref[...] = modulus_ref[...] * now[rim - 1:rim + sx + 1]
    high, low = halves(solid.reshape(sx * sy, sz))
    rhs_ref[:, :sz] = high
    rhs_ref[:, sz:] = low
    block = pick_ref.shape[0] // GROUPS
    copies = []
    for index in range(GROUPS):
        cut = slice(index * block, (index + 1) * block)
        both = jnp.dot(pick_ref[cut, :], rhs_ref[...], preferred_element_type=F32)
        stage_ref[cut, :] = both[:, :sz] + both[:, sz:]
        copies.append(pltpu.make_async_copy(stage_ref.at[cut], reply_ref.at[cut], sems.at[index]))
        copies[-1].start()
    for copy in copies:
        copy.wait()


def solid_steps(rim, prepared, heat, heat_rim):
    sx, sy, sz = heat.shape
    long, height, _ = prepared[0].shape
    total = prepared[3].shape[0]
    return pl.pallas_call(
        functools.partial(solid_kernel, rim),
        in_specs=[in_vmem] * 9,
        out_specs=[in_vmem, in_vmem, in_hbm],
        out_shape=[
            jax.ShapeDtypeStruct((sx, sy, sz), F32),
            jax.ShapeDtypeStruct((sx + 2, height, sz), F32),
            pltpu.HBM((total, sz), F32),
        ],
        scratch_shapes=[pltpu.VMEM((long, height, sz), F32)] * 2
        + [
            pltpu.VMEM((sx + 2 * rim, height, sz), F32),
            pltpu.VMEM((sx * sy, 2 * sz), BF16),
            pltpu.VMEM((total, sz), F32),
            pltpu.SemaphoreType.DMA((GROUPS,)),
        ],
        compiler_params=params(14),
        cost_estimate=cost(4 * total * sx * sy * sz, 4 * total * sz),
        name="solid_steps",
    )(*[near(x) for x in prepared], heat, *heat_rim)


def stress_kernel(sigma_ref, out_ref, tick_ref):
    tick_ref[...] = jnp.zeros_like(tick_ref)
    _, sx, sy, sz = out_ref.shape
    height = sigma_ref.shape[1]
    first = lax.broadcasted_iota(jnp.int32, (height, sz), 1) == 0
    last = lax.broadcasted_iota(jnp.int32, (height, sz), 1) == sz - 1

    def plane(x, none):
        centre = sigma_ref[x + 1]
        out_ref[0, x] = 0.5 * (sigma_ref[x + 2] - sigma_ref[x])[OFF:OFF + sy]
        along = pltpu.roll(centre, height - 1, 0) - pltpu.roll(centre, 1, 0)
        out_ref[1, x] = 0.5 * along[OFF:OFF + sy]
        along = jnp.where(last, 0.0, pltpu.roll(centre, sz - 1, 1)) - jnp.where(
            first, 0.0, pltpu.roll(centre, 1, 1)
        )
        out_ref[2, x] = 0.5 * along[OFF:OFF + sy]
        return none

    lax.fori_loop(0, sx, plane, 0)


def stress(sigma, sx, sy):
    sz = sigma.shape[2]
    return pl.pallas_call(
        stress_kernel,
        grid=(1,),
        in_specs=[whole(sigma.shape)],
        out_specs=[whole((3, sx, sy, sz)), whole((8, LANE))],
        out_shape=[pltpu.HBM((3, sx, sy, sz), F32), jax.ShapeDtypeStruct((8, LANE), F32)],
        compiler_params=params(8),
        cost_estimate=cost(10 * sx * sy * sz, 16 * sx * sy * sz),
        name="stress",
    )(sigma)


def unpack_kernel(dest_ref, back_ref, *refs):
    out_ref = refs[-1]
    rows = out_ref.shape[0]

    def step(index, none):
        base = pl.multiple_of(index * 8, 8)
        lines = [back_ref[pl.ds(dest_ref[0, base + i], 1), :] for i in range(8)]
        for i, line in enumerate(lines):
            out_ref[pl.ds(base + i, 1), :] = line
        return none

    lax.fori_loop(0, rows // 8, step, 0, unroll=4)


def unpack(dest, back, after):
    rows = dest.shape[1]
    row_len = back.shape[1]
    return pl.pallas_call(
        unpack_kernel,
        grid=(1,),
        in_specs=[pl.BlockSpec(memory_space=pltpu.SMEM), whole(back.shape)]
        + [anywhere] * len(after),
        out_specs=whole((rows, row_len)),
        out_shape=jax.ShapeDtypeStruct((rows, row_len), F32),
        compiler_params=params(10),
        cost_estimate=cost(rows * 128, 8 * rows * row_len),
        name="unpack",
    )(dest, back, *after)


PLANES = 2
RING = 3 * PLANES


def fluid_kernel(opening, here_ref, xlo_ref, xhi_ref, speed_ref, flux_ref, *refs):
    index, count = pl.program_id(0), pl.num_programs(0)
    cx = (count - 1) * PLANES
    _, cy, depth = here_ref.shape
    row_len = flux_ref.shape[2]
    rows = slice(OFF, OFF + cy)
    if opening:
        out_ref, xfirst_ref, xlast_ref, yfirst_ref, ylast_ref, clo_ref, chi_ref, ring_ref = refs
    else:
        lo_ref, hi_ref, left_ref, right_ref, ylo_ref, yhi_ref = refs[:6]
        out_ref, tick_ref, ring_ref = refs[-3:]
        tick_ref[...] = jnp.zeros_like(tick_ref)

    def patch(slot, corner_ref):
        wide = depth // LANE
        base = corner_ref.shape[0] - 2 * wide
        for row, at in ((OFF, base), (OFF + cy - 1, base + wide)):
            for i in range(wide):
                ring_ref[slot, row:row + 1, i * LANE:(i + 1) * LANE] = (
                    corner_ref[at + i:at + i + 1, :]
                )

    @pl.when(index == 0)
    def _():
        ring_ref[RING - 1, rows, :] = xlo_ref[...]
        if opening:
            for slot in range(RING):
                ring_ref[slot, OFF - 8:OFF, :] = jnp.zeros((8, depth), F32)
                ring_ref[slot, OFF + cy:OFF + cy + 8, :] = jnp.zeros((8, depth), F32)
        else:
            patch(RING - 1, lo_ref)

    @pl.when(index < count - 1)
    def _():
        for p in range(PLANES):
            plane = index * PLANES + p
            slot = lax.rem(plane, RING)
            ring_ref[slot, rows, :] = here_ref[p]
            if not opening:
                one = pl.ds(plane, 1)
                ring_ref[slot, OFF:OFF + 1, :] = left_ref[one, :]
                ring_ref[slot, OFF + cy - 1:OFF + cy, :] = right_ref[one, :]
                ring_ref[slot, OFF - 1:OFF, :] = ylo_ref[one, :]
                ring_ref[slot, OFF + cy:OFF + cy + 1, :] = yhi_ref[one, :]

    @pl.when(index == count - 1)
    def _():
        ring_ref[lax.rem(cx, RING), rows, :] = xhi_ref[...]
        if not opening:
            patch(lax.rem(cx, RING), hi_ref)

    rate = time_step * diffusivity

    def push(total, centre, lower, upper, speed):
        scaled = time_step * speed
        total = total + (rate + jnp.maximum(scaled, 0.0)) * (lower - centre)
        return total + (rate - jnp.minimum(scaled, 0.0)) * (upper - centre)

    def advance(p, none):
        lanes = lax.broadcasted_iota(jnp.int32, (8, depth), 1)
        first, last = lanes == 0, lanes == depth - 1
        plane = (index - 1) * PLANES + p
        mid = lax.rem(plane, RING)
        old, new = lax.rem(plane + RING - 1, RING), lax.rem(plane + 1, RING)
        for tile in range(cy // 16):
            speeds = [
                speed_ref[k, p, tile * 16:tile * 16 + 16, :].astype(F32) for k in range(3)
            ]
            for part in range(2):
                y = tile * 16 + part * 8
                at = OFF + y
                u, v, w = [s[part * 8:part * 8 + 8] for s in speeds]
                centre = ring_ref[mid, at:at + 8, :]
                total = push(
                    centre, centre, ring_ref[old, at:at + 8, :], ring_ref[new, at:at + 8, :], u
                )
                total = push(
                    total, centre, ring_ref[mid, at - 1:at + 7, :],
                    ring_ref[mid, at + 1:at + 9, :], v,
                )
                lower = jnp.where(first, 0.0, pltpu.roll(centre, 1, 1))
                upper = jnp.where(last, 0.0, pltpu.roll(centre, depth - 1, 1))
                total = push(total, centre, lower, upper, w)
                out_ref[p, y:y + 8, row_len:] = total[:, row_len:]
                out_ref[p, y:y + 8, :row_len] = (
                    total[:, :row_len] - time_step * flux_ref[p, y:y + 8, :]
                )
        if opening:
            one = pl.ds(plane, 1)
            yfirst_ref[one, :] = out_ref[p, 0:1, :]
            ylast_ref[one, :] = out_ref[p, cy - 1:cy, :]
            edge = time_step * speed_ref[1, p, 0:16, :].astype(F32)
            clo_ref[one, :] = rate + jnp.maximum(edge[0:1], 0.0)
            edge = time_step * speed_ref[1, p, cy - 16:cy, :].astype(F32)
            chi_ref[one, :] = rate - jnp.minimum(edge[15:16], 0.0)
        return none

    @pl.when(index > 0)
    def _():
        lax.fori_loop(0, PLANES, advance, 0)

    if opening:

        @pl.when(index == 1)
        def _():
            xfirst_ref[...] = out_ref[0]

        @pl.when(index == count - 1)
        def _():
            xlast_ref[...] = out_ref[PLANES - 1]


def fluid_step(opening, temp, sides, velocity, flux, lines, after):
    cx, cy, depth = temp.shape
    row_len = flux.shape[2]
    plane = (PLANES, cy, depth)
    steps = cx // PLANES
    face = pl.BlockSpec((cy, depth), lambda i: (0, 0))
    line = pl.BlockSpec((cx, depth), lambda i: (0, 0))
    back = lambda i: (jnp.maximum(i - 1, 0), 0, 0)
    shape = jax.ShapeDtypeStruct
    outs = [pl.BlockSpec(plane, back)]
    outs += [face, face] + [line] * 4 if opening else [whole((8, LANE))]
    shapes = [pltpu.HBM(temp.shape, F32)]
    if opening:
        shapes += [shape((cy, depth), F32)] * 2 + [shape((cx, depth), F32)] * 4
    else:
        shapes += [shape((8, LANE), F32)]
    extra = [whole(x.shape) for x in lines[:2]] + [line] * len(lines[2:])
    return pl.pallas_call(
        functools.partial(fluid_kernel, opening),
        grid=(steps + 1,),
        in_specs=[
            pl.BlockSpec(plane, lambda i: (jnp.minimum(i, steps - 1), 0, 0)),
            face,
            face,
            pl.BlockSpec((3, PLANES, cy, depth), lambda i: (0, jnp.maximum(i - 1, 0), 0, 0)),
            pl.BlockSpec((PLANES, cy, row_len), back),
        ]
        + extra
        + [anywhere] * len(after),
        out_specs=outs,
        out_shape=shapes,
        scratch_shapes=[pltpu.VMEM((RING, cy + 2 * OFF, depth), F32)],
        compiler_params=params(16),
        cost_estimate=cost(40 * cx * cy * depth, 14 * cx * cy * depth),
        name="fluid_step",
    )(far(temp), *sides, far(velocity), flux, *lines, *after)


def body(temp_fluid, velocity, wall_old, wall_mask, owner_map, slot_map, temp_solid, material):
    cx, cy, depth = temp_fluid.shape
    row_len = wall_old.shape[2]
    sx, sy, sz = temp_solid.shape
    ndev = lax.axis_size("gx") * lax.axis_size("gy")
    rows = cx * cy
    cap = (3 * rows + ndev - 1) // ndev
    cap = -(-cap // 8) * 8
    total = ndev * cap
    rim = SSTEPS + 1

    first, last = x_faces(rim, temp_fluid, temp_solid, material)
    xlo, xhi = neighbours(last, first, "gx")
    dest, where, codes = rank(owner_map.reshape(1, rows), slot_map, ndev, cap)
    outgoing, flux = pack(where, codes, temp_fluid, wall_old, wall_mask, cap, (first, last))
    outgoing, xhi = lax.optimization_barrier((outgoing, xhi))
    incoming = lax.all_to_all(outgoing, AXES, split_axis=0, concat_axis=0, tiled=True)

    left, right, state = y_faces(rim, temp_fluid, temp_solid, material, xlo, xhi)
    ylo, yhi = neighbours(right, left, "gy")
    fluid, first, last, *edges = fluid_step(
        True, temp_fluid, (xlo, xhi), velocity, flux, (), ()
    )
    sides = neighbours(last, first, "gx")

    thin = rim - 1
    heat, first, last, left, right, code = heat_sum(
        incoming, cap, temp_solid.shape, thin, sides, (ylo, yhi, *edges)
    )
    hxlo, hxhi = neighbours(last, first, "gx")
    first, last = strips(thin, heat, hxlo, hxhi, left, right)
    hylo, hyhi = neighbours(last, first, "gy")
    prepared = ready(rim, cap, state, ylo, yhi, code, heat.shape)
    solid, sigma, replies = solid_steps(rim, prepared, heat, (hxlo, hxhi, hylo, hyhi))
    returned = lax.all_to_all(
        replies.reshape(ndev, cap, sz), AXES, split_axis=0, concat_axis=0, tiled=True
    )
    force, tick = stress(sigma, sx, sy)
    fluid, tick = fluid_step(
        False, fluid, sides, velocity, flux, (hxlo, hxhi, left, right, hylo, hyhi), (tick,)
    )
    wall_next = unpack(dest, returned.reshape(total, sz), (tick,))
    return fluid, wall_next.reshape(cx, cy, row_len), solid, force


def solution(mesh):
    placed = (
        P("gx", "gy", None),
        P(None, "gx", "gy", None),
        P("gx", "gy", None),
        P("gx", "gy", None),
        P(("gx", "gy"), None, None),
        P(("gx", "gy"), None),
        P("gx", "gy", None),
        P("gx", "gy", None),
    )
    return jax.shard_map(
        body,
        mesh=mesh,
        in_specs=placed,
        out_specs=(
            P("gx", "gy", None),
            P("gx", "gy", None),
            P("gx", "gy", None),
            P(None, "gx", "gy", None),
        ),
        check_vma=False,
    )
```

```python
import functools
import jax
import jax.numpy as jnp
from jax import lax
from jax.experimental import pallas as pl
from jax.experimental.pallas import tpu as pltpu
from jax.sharding import PartitionSpec as P

FSTEPS = 2
SSTEPS = 4
time_step = 0.1
diffusivity = 0.5
film_coef = 2.0
solid_step = 0.05
source_gain = 4.0
conduct_table = (0.4, 0.9, 1.5, 2.2)
modulus_table = (0.5, 1.0, 1.6, 2.4)
F32 = jnp.float32
BF16 = jnp.bfloat16
AXES = ("gx", "gy")
LANE = 128
PART = 8
OFF = 8


def params(mib):
    return pltpu.CompilerParams(vmem_limit_bytes=mib * 1024 * 1024)


def cost(flops, bytes_accessed):
    return pl.CostEstimate(flops=flops, bytes_accessed=bytes_accessed, transcendentals=0)


def halves(value):
    high = value.astype(BF16)
    low = (value - high.astype(F32)).astype(BF16)
    return high, low


def ones_where(test):
    return jnp.where(test, 1.0, 0.0).astype(BF16)


def neighbours(before, after, axis):
    size = lax.axis_size(axis)
    up = [(i, i + 1) for i in range(size - 1)]
    down = [(j, i) for i, j in up]
    return lax.ppermute(before, axis, up), lax.ppermute(after, axis, down)


def whole(shape):
    return pl.BlockSpec(shape, lambda i: (0,) * len(shape))


anywhere = pl.BlockSpec(memory_space=pl.ANY)
in_vmem = pl.BlockSpec(memory_space=pltpu.VMEM)
in_hbm = pl.BlockSpec(memory_space=pltpu.HBM)


def far(value):
    return pltpu.with_memory_space_constraint(value, pltpu.HBM)


def near(value):
    return pltpu.with_memory_space_constraint(value, pltpu.VMEM)


def rank_kernel(cap, owner_ref, slot_ref, dest_ref, where_ref, code_ref):
    rows = owner_ref.shape[1]
    ndev = code_ref.shape[0]
    tall = cap + 8
    tri = ones_where(
        lax.broadcasted_iota(jnp.int32, (LANE, LANE), 0)
        <= lax.broadcasted_iota(jnp.int32, (LANE, LANE), 1)
    )
    names = lax.broadcasted_iota(jnp.int32, (ndev, LANE), 0)
    steps = lax.broadcasted_iota(jnp.int32, (LANE, LANE), 0)
    carry = jnp.zeros((ndev, 1), F32)
    codes = jnp.zeros((2 * ndev, LANE), F32)
    for chunk in range(rows // LANE):
        cols = slice(chunk * LANE, (chunk + 1) * LANE)
        own = owner_ref[:, cols]
        hit = jnp.where(names == own, 1.0, 0.0)
        ranks = jnp.dot(hit.astype(BF16), tri, preferred_element_type=F32) + carry
        carry = ranks[:, LANE - 1:]
        place = jnp.sum(hit * ranks, axis=0, keepdims=True).astype(jnp.int32) - 1
        dest_ref[:, cols] = own * cap + place
        where_ref[:, cols] = own * tall + place
        code = slot_ref[:, cols] + 1
        pieces = jnp.concatenate(
            [hit * (code // 32).astype(F32), hit * (code % 32).astype(F32)], axis=0
        ).astype(BF16)
        codes = codes + lax.dot_general(
            pieces, ones_where(steps == place), (((1,), (1,)), ((), ())),
            preferred_element_type=F32,
        )
    code_ref[...] = codes[:ndev] * 32.0 + codes[ndev:]


def rank(owner, slot, ndev, cap):
    rows = owner.shape[1]
    line = jax.ShapeDtypeStruct((1, rows), jnp.int32)
    return pl.pallas_call(
        functools.partial(rank_kernel, cap),
        grid=(1,),
        in_specs=[whole((1, rows))] * 2,
        out_specs=[whole((1, rows))] * 2 + [whole((ndev, LANE))],
        out_shape=[line, line, jax.ShapeDtypeStruct((ndev, LANE), F32)],
        compiler_params=params(8),
        cost_estimate=cost(8 * ndev * LANE * rows, 20 * rows),
        name="rank",
    )(owner, slot)


GROUPS = 4


def pack_kernel(cap, where_ref, code_ref, temp_ref, old_ref, mask_ref, *refs):
    out_ref, flux_ref, rhs_ref, stage_ref, sems = refs[-5:]
    rows = where_ref.shape[1]
    ndev, tall, row_len = stage_ref.shape
    flux = mask_ref[...].astype(F32) * film_coef * (temp_ref[...] - old_ref[...])
    flux_ref[...] = flux
    high, low = halves(flux.reshape(rows, row_len))
    rhs_ref[:, :row_len] = high
    rhs_ref[:, row_len:] = low
    where = where_ref[...]
    group = ndev // GROUPS
    block = group * tall
    lines = lax.broadcasted_iota(jnp.int32, (block, rows), 0)
    copies = []
    for index in range(GROUPS):
        cut = slice(index * group, (index + 1) * group)
        pick = ones_where(lines == where - index * block)
        both = jnp.dot(pick, rhs_ref[...], preferred_element_type=F32)
        both = both[:, :row_len] + both[:, row_len:]
        stage_ref[cut] = both.reshape(group, tall, row_len)
        stage_ref[cut, cap, :] = code_ref[cut, :]
        copies.append(pltpu.make_async_copy(stage_ref.at[cut], out_ref.at[cut], sems.at[index]))
        copies[-1].start()
    for copy in copies:
        copy.wait()


def pack(where, code, temp, old, mask, cap, after):
    cx, cy, _ = temp.shape
    row_len = old.shape[2]
    rows = cx * cy
    ndev = code.shape[0]
    tall = cap + 8
    return pl.pallas_call(
        functools.partial(pack_kernel, cap),
        grid=(1,),
        in_specs=[whole((1, rows)), whole(code.shape)]
        + [whole((cx, cy, row_len))] * 3
        + [anywhere] * len(after),
        out_specs=[in_hbm, whole((cx, cy, row_len))],
        out_shape=[
            pltpu.HBM((ndev, tall, row_len), F32),
            jax.ShapeDtypeStruct((cx, cy, row_len), F32),
        ],
        scratch_shapes=[
            pltpu.VMEM((rows, 2 * row_len), BF16),
            pltpu.VMEM((ndev, tall, row_len), F32),
            pltpu.SemaphoreType.DMA((GROUPS,)),
        ],
        compiler_params=params(18),
        cost_estimate=cost(4 * ndev * tall * rows * row_len, 5 * rows * row_len * 4),
        name="pack",
    )(where, code, far(temp), far(old), far(mask), *after)


def heat_kernel(cap, thin, rows_ref, xfirst_ref, xlast_ref, ylo_ref, yhi_ref,
                yfirst_ref, ylast_ref, clo_ref, chi_ref,
                heat_ref, low_ref, high_ref, left_ref, right_ref, code_ref, total_ref):
    share, tall, row_len = rows_ref.shape
    cx, depth = yfirst_ref.shape
    sx, sy, _ = heat_ref.shape
    slots = sx * sy
    edge = thin * sy
    turn, turns = pl.program_id(0), pl.num_programs(0)

    @pl.when(turn == 0)
    def _():
        left = yfirst_ref[...] + clo_ref[...] * ylo_ref[:cx, :]
        right = ylast_ref[...] + chi_ref[...] * yhi_ref[:cx, :]
        left_ref[...] = left
        right_ref[...] = right
        for ref, x in ((low_ref, 0), (high_ref, cx - 1)):
            for at, line in ((edge, left[x:x + 1]), (edge + depth // LANE, right[x:x + 1])):
                for i in range(depth // LANE):
                    ref[at + i:at + i + 1, :] = line[:, i * LANE:(i + 1) * LANE]
        total_ref[...] = jnp.zeros_like(total_ref)

    codes = rows_ref[:, cap, :].astype(jnp.int32) - 1
    code_ref[pl.ds(pl.multiple_of(turn * share, 8), share), :] = codes
    group = share // 2
    names = lax.broadcasted_iota(jnp.int32, (slots, tall), 0)
    total = total_ref[...]
    for index in range(0, share, group):
        lines = rows_ref[index:index + group].reshape(group * tall, row_len)
        high, low = halves(lines)
        pick = jnp.concatenate(
            [
                jnp.where(names == codes[index + i:index + i + 1, :tall], 1.0, 0.0)
                for i in range(group)
            ],
            axis=1,
        ).astype(BF16)
        total = total + jnp.dot(
            pick, jnp.concatenate([high, low], axis=1), preferred_element_type=F32
        )
    total_ref[...] = total

    @pl.when(turn == turns - 1)
    def _():
        heat = total[:, :row_len] + total[:, row_len:]
        heat_ref[...] = heat.reshape(sx, sy, row_len)
        low_ref[:edge, :] = heat[:edge]
        high_ref[:edge, :] = heat[slots - edge:]


def heat_sum(incoming, cap, block, thin, faces, edges):
    ndev, tall, row_len = incoming.shape
    sx, sy, _ = block
    line = edges[2].shape
    edge = (thin * sy + 2 * (line[1] // LANE), row_len)
    return pl.pallas_call(
        functools.partial(heat_kernel, cap, thin),
        grid=(2,),
        in_specs=[pl.BlockSpec((ndev // 2, tall, row_len), lambda i: (i, 0, 0))]
        + [anywhere] * 2
        + [whole(x.shape) for x in edges],
        out_specs=[whole(block), whole(edge), whole(edge), whole(line), whole(line)]
        + [whole((ndev, row_len))],
        out_shape=[
            jax.ShapeDtypeStruct(block, F32),
            jax.ShapeDtypeStruct(edge, F32),
            jax.ShapeDtypeStruct(edge, F32),
            jax.ShapeDtypeStruct(line, F32),
            jax.ShapeDtypeStruct(line, F32),
            jax.ShapeDtypeStruct((ndev, row_len), jnp.int32),
        ],
        scratch_shapes=[pltpu.VMEM((sx * sy, 2 * row_len), F32)],
        compiler_params=params(14),
        cost_estimate=cost(4 * ndev * tall * sx * sy * row_len, 4 * ndev * tall * row_len),
        name="heat_sum",
    )(incoming, *faces, *edges)


def put_rim(ref, base, slabs):
    across = ref.shape[1] // LANE
    for n, slab in enumerate(slabs):
        row = base + n // across * PART
        ref[row:row + PART, n % across * LANE:(n % across + 1) * LANE] = slab


def get_rim(ref, base, n):
    across = ref.shape[1] // LANE
    row = base + n // across * PART
    return ref[row:row + PART, n % across * LANE:(n % across + 1) * LANE]


def rim_rows(count, depth):
    across = depth // LANE
    return -(-count // across) * PART


def x_faces_kernel(rim, bottom_ref, top_ref, temp_ref, kind_ref, low_ref, high_ref):
    _, cy, _ = bottom_ref.shape
    sx, sy, _ = temp_ref.shape
    low_ref[:cy, :] = bottom_ref[0]
    high_ref[:cy, :] = top_ref[0]
    for ref, start in ((low_ref, 0), (high_ref, sx - rim)):
        slabs = [
            get(start + k, slice(h, h + PART))
            for get in (
                lambda x, cut: temp_ref[x, cut, :],
                lambda x, cut: kind_ref[x, cut, :].astype(F32) + 1.0,
            )
            for k in range(rim)
            for h in range(0, sy, PART)
        ]
        put_rim(ref, cy, slabs)


def x_faces(rim, fluid, temp, kind):
    cx, cy, depth = fluid.shape
    sx, sy, sz = temp.shape
    height = cy + rim_rows(2 * rim * (sy // PART), depth)
    plane = (1, cy, depth)
    return pl.pallas_call(
        functools.partial(x_faces_kernel, rim),
        grid=(1,),
        in_specs=[
            pl.BlockSpec(plane, lambda i: (0, 0, 0)),
            pl.BlockSpec(plane, lambda i: (cx - 1, 0, 0)),
            whole(temp.shape),
            whole(temp.shape),
        ],
        out_specs=[whole((height, depth))] * 2,
        out_shape=[jax.ShapeDtypeStruct((height, depth), F32)] * 2,
        compiler_params=params(16),
        cost_estimate=cost(1000, 4 * 4 * height * depth),
        name="x_faces",
    )(far(fluid), far(fluid), far(temp), far(kind))


def fill_x(rim, ref, which, own, lo_ref, hi_ref):
    sx, sy, _ = own.shape
    pieces = sy // PART
    base = lo_ref.shape[0] - rim_rows(2 * rim * pieces, lo_ref.shape[1])
    ref[rim:rim + sx, OFF:OFF + sy, :] = own
    for k in range(rim):
        for h in range(pieces):
            n = (which * rim + k) * pieces + h
            cut = slice(OFF + h * PART, OFF + (h + 1) * PART)
            ref[k, cut, :] = get_rim(lo_ref, base, n)
            ref[rim + sx + k, cut, :] = get_rim(hi_ref, base, n)


def y_faces_kernel(rim, near_ref, far_ref, temp_ref, kind_ref, lo_ref, hi_ref,
                   left_ref, right_ref, state_ref):
    cx, near_rows, _ = near_ref.shape
    sx, sy, _ = temp_ref.shape
    left_ref[:cx, :] = near_ref[:, 0, :]
    right_ref[:cx, :] = far_ref[:, near_rows - 1, :]
    slabs = ([], [])
    long = state_ref.shape[1]
    state_ref[...] = jnp.zeros_like(state_ref)
    for which, own in enumerate((temp_ref[...], kind_ref[...].astype(F32) + 1.0)):
        fill_x(rim, state_ref.at[which], which, own, lo_ref, hi_ref)
        for into, start in zip(slabs, (OFF, OFF + sy - rim)):
            for k in range(rim):
                for h in range(0, long, PART):
                    into.append(state_ref[which, h:h + PART, start + k, :])
    put_rim(left_ref, cx, slabs[0])
    put_rim(right_ref, cx, slabs[1])


def y_faces(rim, fluid, temp, kind, lo, hi):
    cx, cy, depth = fluid.shape
    sx, sy, sz = temp.shape
    long = -(-(sx + 2 * rim) // PART) * PART
    height = cx + rim_rows(2 * rim * (long // PART), depth)
    args = (far(temp), far(kind), lo, hi)
    edge = (cx, 8, depth)
    return pl.pallas_call(
        functools.partial(y_faces_kernel, rim),
        grid=(1,),
        in_specs=[
            pl.BlockSpec(edge, lambda i: (0, 0, 0)),
            pl.BlockSpec(edge, lambda i: (0, cy // 8 - 1, 0)),
        ]
        + [whole(x.shape) for x in args],
        out_specs=[whole((height, depth))] * 2 + [whole((2, long, sy + 2 * OFF, sz))],
        out_shape=[jax.ShapeDtypeStruct((height, depth), F32)] * 2
        + [pltpu.HBM((2, long, sy + 2 * OFF, sz), F32)],
        compiler_params=params(10),
        cost_estimate=cost(1000, 4 * 4 * height * depth),
        name="y_faces",
    )(far(fluid), far(fluid), *args)


def strips_kernel(thin, heat_ref, lo_ref, hi_ref, near_ref, away_ref,
                  left_ref, right_ref, work_ref):
    cx = near_ref.shape[0]
    sx, sy, sz = heat_ref.shape
    edge = thin * sy
    left_ref[:cx, :] = near_ref[...]
    right_ref[:cx, :] = away_ref[...]
    work_ref[...] = jnp.zeros_like(work_ref)
    work_ref[:thin] = lo_ref[:edge, :].reshape(thin, sy, sz)
    work_ref[thin:thin + sx] = heat_ref[...]
    work_ref[thin + sx:2 * thin + sx] = hi_ref[:edge, :].reshape(thin, sy, sz)
    long = work_ref.shape[0]
    for ref, start in ((left_ref, 0), (right_ref, sy - thin)):
        slabs = [
            work_ref[h:h + PART, start + k, :] for k in range(thin) for h in range(0, long, PART)
        ]
        put_rim(ref, cx, slabs)


def strips(thin, heat, lo, hi, left, right):
    cx, depth = left.shape
    sx, sy, sz = heat.shape
    long = -(-(sx + 2 * thin) // PART) * PART
    height = cx + rim_rows(thin * (long // PART), depth)
    return pl.pallas_call(
        functools.partial(strips_kernel, thin),
        in_specs=[in_vmem] * 5,
        out_specs=[in_vmem] * 2,
        out_shape=[jax.ShapeDtypeStruct((height, depth), F32)] * 2,
        scratch_shapes=[pltpu.VMEM((long, sy, sz), F32)],
        compiler_params=params(8),
        cost_estimate=cost(1000, 16 * height * depth),
        name="strips",
    )(heat, lo, hi, left, right)


def table(kind, values):
    out = jnp.zeros(kind.shape, F32)
    for index, value in enumerate(values):
        out = jnp.where(kind == index + 1.0, value, out)
    return out


def ready_kernel(rim, cap, state_ref, ylo_ref, yhi_ref, code_ref,
                 temp_ref, cond_ref, sigma_ref, pick_ref):
    _, long, height, sz = state_ref.shape
    ndev = code_ref.shape[0]
    slots = pick_ref.shape[1]
    sx = sigma_ref.shape[0] - 2
    sy = height - 2 * OFF
    pieces = long // PART
    turned = jnp.transpose(code_ref[...])
    names = lax.broadcasted_iota(jnp.int32, (cap, slots), 1)
    for source in range(0, ndev, 2):
        pick_ref[source * cap:(source + 2) * cap, :] = jnp.concatenate(
            [
                jnp.where(names == turned[:cap, one:one + 1], 1.0, 0.0)
                for one in (source, source + 1)
            ],
            axis=0,
        ).astype(BF16)
    base = ylo_ref.shape[0] - rim_rows(2 * rim * pieces, ylo_ref.shape[1])
    for which, ref in enumerate((temp_ref, cond_ref)):
        ref[...] = state_ref[which]
        for k in range(rim):
            for h in range(pieces):
                n = (which * rim + k) * pieces + h
                cut = slice(h * PART, (h + 1) * PART)
                ref[cut, OFF - rim + k, :] = get_rim(ylo_ref, base, n)
                ref[cut, OFF + sy + k, :] = get_rim(yhi_ref, base, n)
    kind = cond_ref[...]
    sigma_ref[...] = table(kind[rim - 1:rim + sx + 1], modulus_table)
    cond_ref[...] = solid_step * table(kind, conduct_table)


def ready(rim, cap, state, ylo, yhi, code, block):
    sx, sy, sz = block
    _, long, height, _ = state.shape
    ndev = code.shape[0]
    args = (far(state), ylo, yhi, code)
    return pl.pallas_call(
        functools.partial(ready_kernel, rim, cap),
        grid=(1,),
        in_specs=[whole(x.shape) for x in args],
        out_specs=[in_vmem] * 4,
        out_shape=[
            pltpu.VMEM((long, height, sz), F32),
            pltpu.VMEM((long, height, sz), F32),
            pltpu.VMEM((sx + 2, height, sz), F32),
            pltpu.VMEM((ndev * cap, sx * sy), BF16),
        ],
        compiler_params=params(14),
        cost_estimate=cost(4 * ndev * cap * sx * sy, 4 * ndev * cap * sx * sy),
        name="ready",
    )(*args)


def solid_kernel(rim, start_ref, cond_ref, modulus_ref, pick_ref,
                 heat_ref, hxlo_ref, hxhi_ref, hylo_ref, hyhi_ref,
                 next_ref, sigma_ref, reply_ref, even_ref, odd_ref, src_ref, rhs_ref,
                 stage_ref, sems):
    sx, sy, sz = heat_ref.shape
    wide = sx + 2 * rim
    thin = rim - 1
    edge = thin * sy
    src_ref[rim:rim + sx, OFF:OFF + sy, :] = heat_ref[...]
    src_ref[1:rim, OFF:OFF + sy, :] = hxlo_ref[:edge, :].reshape(thin, sy, sz)
    src_ref[rim + sx:wide - 1, OFF:OFF + sy, :] = hxhi_ref[:edge, :].reshape(thin, sy, sz)
    parts = -(-(sx + 2 * thin) // PART)
    base = hylo_ref.shape[0] - rim_rows(thin * parts, hylo_ref.shape[1])
    for k in range(thin):
        for h in range(parts):
            n = k * parts + h
            count = min(PART, sx + 2 * thin - h * PART)
            cut = slice(1 + h * PART, 1 + h * PART + count)
            src_ref[cut, OFF - thin + k, :] = get_rim(hylo_ref, base, n)[:count]
            src_ref[cut, OFF + sy + k, :] = get_rim(hyhi_ref, base, n)[:count]
    src_ref[...] = (solid_step * source_gain) * src_ref[...]
    height = start_ref.shape[1]
    first = lax.broadcasted_iota(jnp.int32, (height, sz), 1) == 0
    last = lax.broadcasted_iota(jnp.int32, (height, sz), 1) == sz - 1
    now = start_ref
    for turn in range(rim - 1):
        later = (odd_ref, even_ref)[turn % 2]
        for x in range(1 + turn, wide - 1 - turn):
            centre = now[x]
            beside = now[x - 1] + now[x + 1]
            beside += pltpu.roll(centre, 1, 0) + pltpu.roll(centre, height - 1, 0)
            beside += jnp.where(first, 0.0, pltpu.roll(centre, 1, 1))
            beside += jnp.where(last, 0.0, pltpu.roll(centre, sz - 1, 1))
            later[x] = centre + (cond_ref[x] * (beside - 6.0 * centre) + src_ref[x])
        now = later
    solid = now[rim:rim + sx, OFF:OFF + sy, :]
    next_ref[...] = solid
    sigma_ref[...] = modulus_ref[...] * now[rim - 1:rim + sx + 1]
    high, low = halves(solid.reshape(sx * sy, sz))
    rhs_ref[:, :sz] = high
    rhs_ref[:, sz:] = low
    block = pick_ref.shape[0] // GROUPS
    copies = []
    for index in range(GROUPS):
        cut = slice(index * block, (index + 1) * block)
        both = jnp.dot(pick_ref[cut, :], rhs_ref[...], preferred_element_type=F32)
        stage_ref[cut, :] = both[:, :sz] + both[:, sz:]
        copies.append(pltpu.make_async_copy(stage_ref.at[cut], reply_ref.at[cut], sems.at[index]))
        copies[-1].start()
    for copy in copies:
        copy.wait()


def solid_steps(rim, prepared, heat, heat_rim):
    sx, sy, sz = heat.shape
    long, height, _ = prepared[0].shape
    total = prepared[3].shape[0]
    return pl.pallas_call(
        functools.partial(solid_kernel, rim),
        in_specs=[in_vmem] * 9,
        out_specs=[in_vmem, in_vmem, in_hbm],
        out_shape=[
            jax.ShapeDtypeStruct((sx, sy, sz), F32),
            jax.ShapeDtypeStruct((sx + 2, height, sz), F32),
            pltpu.HBM((total, sz), F32),
        ],
        scratch_shapes=[pltpu.VMEM((long, height, sz), F32)] * 2
        + [
            pltpu.VMEM((sx + 2 * rim, height, sz), F32),
            pltpu.VMEM((sx * sy, 2 * sz), BF16),
            pltpu.VMEM((total, sz), F32),
            pltpu.SemaphoreType.DMA((GROUPS,)),
        ],
        compiler_params=params(14),
        cost_estimate=cost(4 * total * sx * sy * sz, 4 * total * sz),
        name="solid_steps",
    )(*[near(x) for x in prepared], heat, *heat_rim)


def stress_kernel(sigma_ref, out_ref, tick_ref):
    tick_ref[...] = jnp.zeros_like(tick_ref)
    _, sx, sy, sz = out_ref.shape
    height = sigma_ref.shape[1]
    first = lax.broadcasted_iota(jnp.int32, (height, sz), 1) == 0
    last = lax.broadcasted_iota(jnp.int32, (height, sz), 1) == sz - 1

    def plane(x, none):
        centre = sigma_ref[x + 1]
        out_ref[0, x] = 0.5 * (sigma_ref[x + 2] - sigma_ref[x])[OFF:OFF + sy]
        along = pltpu.roll(centre, height - 1, 0) - pltpu.roll(centre, 1, 0)
        out_ref[1, x] = 0.5 * along[OFF:OFF + sy]
        along = jnp.where(last, 0.0, pltpu.roll(centre, sz - 1, 1)) - jnp.where(
            first, 0.0, pltpu.roll(centre, 1, 1)
        )
        out_ref[2, x] = 0.5 * along[OFF:OFF + sy]
        return none

    lax.fori_loop(0, sx, plane, 0)


def stress(sigma, sx, sy):
    sz = sigma.shape[2]
    return pl.pallas_call(
        stress_kernel,
        grid=(1,),
        in_specs=[whole(sigma.shape)],
        out_specs=[whole((3, sx, sy, sz)), whole((8, LANE))],
        out_shape=[pltpu.HBM((3, sx, sy, sz), F32), jax.ShapeDtypeStruct((8, LANE), F32)],
        compiler_params=params(8),
        cost_estimate=cost(10 * sx * sy * sz, 16 * sx * sy * sz),
        name="stress",
    )(sigma)


def unpack_kernel(dest_ref, back_ref, *refs):
    out_ref = refs[-1]
    rows = out_ref.shape[0]

    def step(index, none):
        base = pl.multiple_of(index * 8, 8)
        lines = [back_ref[pl.ds(dest_ref[0, base + i], 1), :] for i in range(8)]
        for i, line in enumerate(lines):
            out_ref[pl.ds(base + i, 1), :] = line
        return none

    lax.fori_loop(0, rows // 8, step, 0, unroll=4)


def unpack(dest, back, after):
    rows = dest.shape[1]
    row_len = back.shape[1]
    return pl.pallas_call(
        unpack_kernel,
        grid=(1,),
        in_specs=[pl.BlockSpec(memory_space=pltpu.SMEM), in_vmem]
        + [anywhere] * len(after),
        out_specs=whole((rows, row_len)),
        out_shape=jax.ShapeDtypeStruct((rows, row_len), F32),
        compiler_params=params(10),
        cost_estimate=cost(rows * 128, 8 * rows * row_len),
        name="unpack",
    )(dest, back, *after)


PLANES = 2
RING = 3 * PLANES


def fluid_kernel(opening, here_ref, xlo_ref, xhi_ref, speed_ref, flux_ref, *refs):
    index, count = pl.program_id(0), pl.num_programs(0)
    cx = (count - 1) * PLANES
    _, cy, depth = here_ref.shape
    row_len = flux_ref.shape[2]
    rows = slice(OFF, OFF + cy)
    if opening:
        out_ref, xfirst_ref, xlast_ref, yfirst_ref, ylast_ref, clo_ref, chi_ref, ring_ref = refs
    else:
        lo_ref, hi_ref, left_ref, right_ref, ylo_ref, yhi_ref = refs[:6]
        out_ref, tick_ref, ring_ref = refs[-3:]
        tick_ref[...] = jnp.zeros_like(tick_ref)

    def patch(slot, corner_ref):
        wide = depth // LANE
        base = corner_ref.shape[0] - 2 * wide
        for row, at in ((OFF, base), (OFF + cy - 1, base + wide)):
            for i in range(wide):
                ring_ref[slot, row:row + 1, i * LANE:(i + 1) * LANE] = (
                    corner_ref[at + i:at + i + 1, :]
                )

    @pl.when(index == 0)
    def _():
        ring_ref[RING - 1, rows, :] = xlo_ref[...]
        if opening:
            for slot in range(RING):
                ring_ref[slot, OFF - 8:OFF, :] = jnp.zeros((8, depth), F32)
                ring_ref[slot, OFF + cy:OFF + cy + 8, :] = jnp.zeros((8, depth), F32)
        else:
            patch(RING - 1, lo_ref)

    @pl.when(index < count - 1)
    def _():
        for p in range(PLANES):
            plane = index * PLANES + p
            slot = lax.rem(plane, RING)
            ring_ref[slot, rows, :] = here_ref[p]
            if not opening:
                one = pl.ds(plane, 1)
                ring_ref[slot, OFF:OFF + 1, :] = left_ref[one, :]
                ring_ref[slot, OFF + cy - 1:OFF + cy, :] = right_ref[one, :]
                ring_ref[slot, OFF - 1:OFF, :] = ylo_ref[one, :]
                ring_ref[slot, OFF + cy:OFF + cy + 1, :] = yhi_ref[one, :]

    @pl.when(index == count - 1)
    def _():
        ring_ref[lax.rem(cx, RING), rows, :] = xhi_ref[...]
        if not opening:
            patch(lax.rem(cx, RING), hi_ref)

    rate = time_step * diffusivity

    def push(total, centre, lower, upper, speed):
        scaled = time_step * speed
        total = total + (rate + jnp.maximum(scaled, 0.0)) * (lower - centre)
        return total + (rate - jnp.minimum(scaled, 0.0)) * (upper - centre)

    def advance(p, none):
        lanes = lax.broadcasted_iota(jnp.int32, (8, depth), 1)
        first, last = lanes == 0, lanes == depth - 1
        plane = (index - 1) * PLANES + p
        mid = lax.rem(plane, RING)
        old, new = lax.rem(plane + RING - 1, RING), lax.rem(plane + 1, RING)
        for tile in range(cy // 16):
            speeds = [
                speed_ref[k, p, tile * 16:tile * 16 + 16, :].astype(F32) for k in range(3)
            ]
            for part in range(2):
                y = tile * 16 + part * 8
                at = OFF + y
                u, v, w = [s[part * 8:part * 8 + 8] for s in speeds]
                centre = ring_ref[mid, at:at + 8, :]
                total = push(
                    centre, centre, ring_ref[old, at:at + 8, :], ring_ref[new, at:at + 8, :], u
                )
                total = push(
                    total, centre, ring_ref[mid, at - 1:at + 7, :],
                    ring_ref[mid, at + 1:at + 9, :], v,
                )
                lower = jnp.where(first, 0.0, pltpu.roll(centre, 1, 1))
                upper = jnp.where(last, 0.0, pltpu.roll(centre, depth - 1, 1))
                total = push(total, centre, lower, upper, w)
                out_ref[p, y:y + 8, row_len:] = total[:, row_len:]
                out_ref[p, y:y + 8, :row_len] = (
                    total[:, :row_len] - time_step * flux_ref[p, y:y + 8, :]
                )
        if opening:
            one = pl.ds(plane, 1)
            yfirst_ref[one, :] = out_ref[p, 0:1, :]
            ylast_ref[one, :] = out_ref[p, cy - 1:cy, :]
            edge = time_step * speed_ref[1, p, 0:16, :].astype(F32)
            clo_ref[one, :] = rate + jnp.maximum(edge[0:1], 0.0)
            edge = time_step * speed_ref[1, p, cy - 16:cy, :].astype(F32)
            chi_ref[one, :] = rate - jnp.minimum(edge[15:16], 0.0)
        return none

    @pl.when(index > 0)
    def _():
        lax.fori_loop(0, PLANES, advance, 0)

    if opening:

        @pl.when(index == 1)
        def _():
            xfirst_ref[...] = out_ref[0]

        @pl.when(index == count - 1)
        def _():
            xlast_ref[...] = out_ref[PLANES - 1]


def fluid_step(opening, temp, sides, velocity, flux, lines, after):
    cx, cy, depth = temp.shape
    row_len = flux.shape[2]
    plane = (PLANES, cy, depth)
    steps = cx // PLANES
    face = pl.BlockSpec((cy, depth), lambda i: (0, 0))
    line = pl.BlockSpec((cx, depth), lambda i: (0, 0))
    back = lambda i: (jnp.maximum(i - 1, 0), 0, 0)
    shape = jax.ShapeDtypeStruct
    outs = [pl.BlockSpec(plane, back)]
    outs += [face, face] + [line] * 4 if opening else [whole((8, LANE))]
    shapes = [pltpu.HBM(temp.shape, F32)]
    if opening:
        shapes += [shape((cy, depth), F32)] * 2 + [shape((cx, depth), F32)] * 4
    else:
        shapes += [shape((8, LANE), F32)]
    extra = [whole(x.shape) for x in lines[:2]] + [line] * len(lines[2:])
    return pl.pallas_call(
        functools.partial(fluid_kernel, opening),
        grid=(steps + 1,),
        in_specs=[
            pl.BlockSpec(plane, lambda i: (jnp.minimum(i, steps - 1), 0, 0)),
            face,
            face,
            pl.BlockSpec((3, PLANES, cy, depth), lambda i: (0, jnp.maximum(i - 1, 0), 0, 0)),
            pl.BlockSpec((PLANES, cy, row_len), back),
        ]
        + extra
        + [anywhere] * len(after),
        out_specs=outs,
        out_shape=shapes,
        scratch_shapes=[pltpu.VMEM((RING, cy + 2 * OFF, depth), F32)],
        compiler_params=params(16),
        cost_estimate=cost(40 * cx * cy * depth, 14 * cx * cy * depth),
        name="fluid_step",
    )(far(temp), *sides, far(velocity), flux, *lines, *after)


def body(temp_fluid, velocity, wall_old, wall_mask, owner_map, slot_map, temp_solid, material):
    cx, cy, depth = temp_fluid.shape
    row_len = wall_old.shape[2]
    sx, sy, sz = temp_solid.shape
    ndev = lax.axis_size("gx") * lax.axis_size("gy")
    rows = cx * cy
    cap = (3 * rows + ndev - 1) // ndev
    cap = -(-cap // 8) * 8
    total = ndev * cap
    rim = SSTEPS + 1

    first, last = x_faces(rim, temp_fluid, temp_solid, material)
    xlo, xhi = neighbours(last, first, "gx")
    dest, where, codes = rank(owner_map.reshape(1, rows), slot_map, ndev, cap)
    outgoing, flux = pack(where, codes, temp_fluid, wall_old, wall_mask, cap, (first, last))
    outgoing, xlo, xhi = lax.optimization_barrier((outgoing, xlo, xhi))
    incoming = lax.all_to_all(outgoing, AXES, split_axis=0, concat_axis=0, tiled=True)

    left, right, state = y_faces(rim, temp_fluid, temp_solid, material, xlo, xhi)
    ylo, yhi = neighbours(right, left, "gy")
    fluid, first, last, *edges = fluid_step(
        True, temp_fluid, (xlo, xhi), velocity, flux, (), ()
    )
    sides = neighbours(last, first, "gx")

    thin = rim - 1
    heat, first, last, left, right, code = heat_sum(
        incoming, cap, temp_solid.shape, thin, sides, (ylo, yhi, *edges)
    )
    hxlo, hxhi = neighbours(last, first, "gx")
    first, last = strips(thin, heat, hxlo, hxhi, left, right)
    hylo, hyhi = neighbours(last, first, "gy")
    prepared = ready(rim, cap, state, ylo, yhi, code, heat.shape)
    solid, sigma, replies = solid_steps(rim, prepared, heat, (hxlo, hxhi, hylo, hyhi))
    returned = lax.all_to_all(
        replies.reshape(ndev, cap, sz), AXES, split_axis=0, concat_axis=0, tiled=True
    )
    force, tick = stress(sigma, sx, sy)
    fluid, tick = fluid_step(
        False, fluid, sides, velocity, flux, (hxlo, hxhi, left, right, hylo, hyhi), (tick,)
    )
    wall_next = unpack(dest, returned.reshape(total, sz), (tick,))
    return fluid, wall_next.reshape(cx, cy, row_len), solid, force


def solution(mesh):
    placed = (
        P("gx", "gy", None),
        P(None, "gx", "gy", None),
        P("gx", "gy", None),
        P("gx", "gy", None),
        P(("gx", "gy"), None, None),
        P(("gx", "gy"), None),
        P("gx", "gy", None),
        P("gx", "gy", None),
    )
    return jax.shard_map(
        body,
        mesh=mesh,
        in_specs=placed,
        out_specs=(
            P("gx", "gy", None),
            P("gx", "gy", None),
            P("gx", "gy", None),
            P(None, "gx", "gy", None),
        ),
        check_vma=False,
    )
```

```python
import functools
import jax
import jax.numpy as jnp
from jax import lax
from jax.experimental import pallas as pl
from jax.experimental.pallas import tpu as pltpu
from jax.sharding import PartitionSpec as P

FSTEPS = 2
SSTEPS = 4
time_step = 0.1
diffusivity = 0.5
film_coef = 2.0
solid_step = 0.05
source_gain = 4.0
conduct_table = (0.4, 0.9, 1.5, 2.2)
modulus_table = (0.5, 1.0, 1.6, 2.4)
F32 = jnp.float32
BF16 = jnp.bfloat16
AXES = ("gx", "gy")
LANE = 128
PART = 8
OFF = 8


def params(mib):
    return pltpu.CompilerParams(vmem_limit_bytes=mib * 1024 * 1024)


def cost(flops, bytes_accessed):
    return pl.CostEstimate(flops=flops, bytes_accessed=bytes_accessed, transcendentals=0)


def halves(value):
    high = value.astype(BF16)
    low = (value - high.astype(F32)).astype(BF16)
    return high, low


def ones_where(test):
    return jnp.where(test, 1.0, 0.0).astype(BF16)


def neighbours(before, after, axis):
    size = lax.axis_size(axis)
    up = [(i, i + 1) for i in range(size - 1)]
    down = [(j, i) for i, j in up]
    return lax.ppermute(before, axis, up), lax.ppermute(after, axis, down)


def whole(shape):
    return pl.BlockSpec(shape, lambda i: (0,) * len(shape))


anywhere = pl.BlockSpec(memory_space=pl.ANY)
in_vmem = pl.BlockSpec(memory_space=pltpu.VMEM)
in_hbm = pl.BlockSpec(memory_space=pltpu.HBM)


def far(value):
    return pltpu.with_memory_space_constraint(value, pltpu.HBM)


def near(value):
    return pltpu.with_memory_space_constraint(value, pltpu.VMEM)


def rank_kernel(cap, owner_ref, slot_ref, dest_ref, where_ref, code_ref):
    rows = owner_ref.shape[1]
    ndev = code_ref.shape[0]
    tall = cap + 8
    tri = ones_where(
        lax.broadcasted_iota(jnp.int32, (LANE, LANE), 0)
        <= lax.broadcasted_iota(jnp.int32, (LANE, LANE), 1)
    )
    names = lax.broadcasted_iota(jnp.int32, (ndev, LANE), 0)
    steps = lax.broadcasted_iota(jnp.int32, (LANE, LANE), 0)
    carry = jnp.zeros((ndev, 1), F32)
    codes = jnp.zeros((2 * ndev, LANE), F32)
    for chunk in range(rows // LANE):
        cols = slice(chunk * LANE, (chunk + 1) * LANE)
        own = owner_ref[:, cols]
        hit = jnp.where(names == own, 1.0, 0.0)
        ranks = jnp.dot(hit.astype(BF16), tri, preferred_element_type=F32) + carry
        carry = ranks[:, LANE - 1:]
        place = jnp.sum(hit * ranks, axis=0, keepdims=True).astype(jnp.int32) - 1
        dest_ref[:, cols] = own * cap + place
        where_ref[:, cols] = own * tall + place
        code = slot_ref[:, cols] + 1
        pieces = jnp.concatenate(
            [hit * (code // 32).astype(F32), hit * (code % 32).astype(F32)], axis=0
        ).astype(BF16)
        codes = codes + lax.dot_general(
            pieces, ones_where(steps == place), (((1,), (1,)), ((), ())),
            preferred_element_type=F32,
        )
    code_ref[...] = codes[:ndev] * 32.0 + codes[ndev:]


def rank(owner, slot, ndev, cap):
    rows = owner.shape[1]
    line = jax.ShapeDtypeStruct((1, rows), jnp.int32)
    return pl.pallas_call(
        functools.partial(rank_kernel, cap),
        grid=(1,),
        in_specs=[whole((1, rows))] * 2,
        out_specs=[whole((1, rows))] * 2 + [whole((ndev, LANE))],
        out_shape=[line, line, jax.ShapeDtypeStruct((ndev, LANE), F32)],
        compiler_params=params(8),
        cost_estimate=cost(8 * ndev * LANE * rows, 20 * rows),
        name="rank",
    )(owner, slot)


GROUPS = 4


def pack_kernel(cap, where_ref, code_ref, temp_ref, old_ref, mask_ref, *refs):
    out_ref, flux_ref, rhs_ref, stage_ref, sems = refs[-5:]
    rows = where_ref.shape[1]
    ndev, tall, row_len = stage_ref.shape
    flux = mask_ref[...].astype(F32) * film_coef * (temp_ref[...] - old_ref[...])
    flux_ref[...] = flux
    high, low = halves(flux.reshape(rows, row_len))
    rhs_ref[:, :row_len] = high
    rhs_ref[:, row_len:] = low
    where = where_ref[...]
    group = ndev // GROUPS
    block = group * tall
    lines = lax.broadcasted_iota(jnp.int32, (block, rows), 0)
    copies = []
    for index in range(GROUPS):
        cut = slice(index * group, (index + 1) * group)
        pick = ones_where(lines == where - index * block)
        both = jnp.dot(pick, rhs_ref[...], preferred_element_type=F32)
        both = both[:, :row_len] + both[:, row_len:]
        stage_ref[cut] = both.reshape(group, tall, row_len)
        stage_ref[cut, cap, :] = code_ref[cut, :]
        copies.append(pltpu.make_async_copy(stage_ref.at[cut], out_ref.at[cut], sems.at[index]))
        copies[-1].start()
    for copy in copies:
        copy.wait()


def pack(where, code, temp, old, mask, cap, after):
    cx, cy, _ = temp.shape
    row_len = old.shape[2]
    rows = cx * cy
    ndev = code.shape[0]
    tall = cap + 8
    return pl.pallas_call(
        functools.partial(pack_kernel, cap),
        grid=(1,),
        in_specs=[whole((1, rows)), whole(code.shape)]
        + [whole((cx, cy, row_len))] * 3
        + [anywhere] * len(after),
        out_specs=[in_hbm, whole((cx, cy, row_len))],
        out_shape=[
            pltpu.HBM((ndev, tall, row_len), F32),
            jax.ShapeDtypeStruct((cx, cy, row_len), F32),
        ],
        scratch_shapes=[
            pltpu.VMEM((rows, 2 * row_len), BF16),
            pltpu.VMEM((ndev, tall, row_len), F32),
            pltpu.SemaphoreType.DMA((GROUPS,)),
        ],
        compiler_params=params(18),
        cost_estimate=cost(4 * ndev * tall * rows * row_len, 5 * rows * row_len * 4),
        name="pack",
    )(where, code, far(temp), far(old), far(mask), *after)


def heat_kernel(cap, thin, rows_ref, xfirst_ref, xlast_ref, ylo_ref, yhi_ref,
                yfirst_ref, ylast_ref, clo_ref, chi_ref,
                heat_ref, low_ref, high_ref, left_ref, right_ref, code_ref):
    ndev, tall, row_len = rows_ref.shape
    cx, depth = yfirst_ref.shape
    sx, sy, _ = heat_ref.shape
    slots = sx * sy
    left = yfirst_ref[...] + clo_ref[...] * ylo_ref[:cx, :]
    right = ylast_ref[...] + chi_ref[...] * yhi_ref[:cx, :]
    left_ref[...] = left
    right_ref[...] = right
    edge = thin * sy
    for ref, x in ((low_ref, 0), (high_ref, cx - 1)):
        for at, line in ((edge, left[x:x + 1]), (edge + depth // LANE, right[x:x + 1])):
            for i in range(depth // LANE):
                ref[at + i:at + i + 1, :] = line[:, i * LANE:(i + 1) * LANE]
    codes = rows_ref[:, cap, :].astype(jnp.int32) - 1
    code_ref[...] = codes
    group = ndev // GROUPS
    names = lax.broadcasted_iota(jnp.int32, (slots, tall), 0)
    total = jnp.zeros((slots, 2 * row_len), F32)
    for index in range(0, ndev, group):
        lines = rows_ref[index:index + group].reshape(group * tall, row_len)
        high, low = halves(lines)
        pick = jnp.concatenate(
            [
                jnp.where(names == codes[index + i:index + i + 1, :tall], 1.0, 0.0)
                for i in range(group)
            ],
            axis=1,
        ).astype(BF16)
        total = total + jnp.dot(
            pick, jnp.concatenate([high, low], axis=1), preferred_element_type=F32
        )
    heat = total[:, :row_len] + total[:, row_len:]
    heat_ref[...] = heat.reshape(sx, sy, row_len)
    low_ref[:edge, :] = heat[:edge]
    high_ref[:edge, :] = heat[slots - edge:]


def heat_sum(incoming, cap, block, thin, faces, edges):
    ndev, tall, row_len = incoming.shape
    sx, sy, _ = block
    line = edges[2].shape
    edge = (thin * sy + 2 * (line[1] // LANE), row_len)
    return pl.pallas_call(
        functools.partial(heat_kernel, cap, thin),
        grid=(1,),
        in_specs=[whole(incoming.shape)] + [anywhere] * 2 + [whole(x.shape) for x in edges],
        out_specs=[whole(block), whole(edge), whole(edge), whole(line), whole(line)]
        + [whole((ndev, row_len))],
        out_shape=[
            jax.ShapeDtypeStruct(block, F32),
            jax.ShapeDtypeStruct(edge, F32),
            jax.ShapeDtypeStruct(edge, F32),
            jax.ShapeDtypeStruct(line, F32),
            jax.ShapeDtypeStruct(line, F32),
            jax.ShapeDtypeStruct((ndev, row_len), jnp.int32),
        ],
        compiler_params=params(14),
        cost_estimate=cost(4 * ndev * tall * sx * sy * row_len, 4 * ndev * tall * row_len),
        name="heat_sum",
    )(incoming, *faces, *edges)


def put_rim(ref, base, slabs):
    across = ref.shape[1] // LANE
    for n, slab in enumerate(slabs):
        row = base + n // across * PART
        ref[row:row + PART, n % across * LANE:(n % across + 1) * LANE] = slab


def get_rim(ref, base, n):
    across = ref.shape[1] // LANE
    row = base + n // across * PART
    return ref[row:row + PART, n % across * LANE:(n % across + 1) * LANE]


def rim_rows(count, depth):
    across = depth // LANE
    return -(-count // across) * PART


def x_faces_kernel(rim, bottom_ref, top_ref, temp_ref, kind_ref, low_ref, high_ref):
    _, cy, _ = bottom_ref.shape
    sx, sy, _ = temp_ref.shape
    low_ref[:cy, :] = bottom_ref[0]
    high_ref[:cy, :] = top_ref[0]
    for ref, start in ((low_ref, 0), (high_ref, sx - rim)):
        slabs = [
            get(start + k, slice(h, h + PART))
            for get in (
                lambda x, cut: temp_ref[x, cut, :],
                lambda x, cut: kind_ref[x, cut, :].astype(F32) + 1.0,
            )
            for k in range(rim)
            for h in range(0, sy, PART)
        ]
        put_rim(ref, cy, slabs)


def x_faces(rim, fluid, temp, kind):
    cx, cy, depth = fluid.shape
    sx, sy, sz = temp.shape
    height = cy + rim_rows(2 * rim * (sy // PART), depth)
    plane = (1, cy, depth)
    return pl.pallas_call(
        functools.partial(x_faces_kernel, rim),
        grid=(1,),
        in_specs=[
            pl.BlockSpec(plane, lambda i: (0, 0, 0)),
            pl.BlockSpec(plane, lambda i: (cx - 1, 0, 0)),
            whole(temp.shape),
            whole(temp.shape),
        ],
        out_specs=[whole((height, depth))] * 2,
        out_shape=[jax.ShapeDtypeStruct((height, depth), F32)] * 2,
        compiler_params=params(16),
        cost_estimate=cost(1000, 4 * 4 * height * depth),
        name="x_faces",
    )(far(fluid), far(fluid), far(temp), far(kind))


def fill_x(rim, ref, which, own, lo_ref, hi_ref):
    sx, sy, _ = own.shape
    pieces = sy // PART
    base = lo_ref.shape[0] - rim_rows(2 * rim * pieces, lo_ref.shape[1])
    ref[rim:rim + sx, OFF:OFF + sy, :] = own
    for k in range(rim):
        for h in range(pieces):
            n = (which * rim + k) * pieces + h
            cut = slice(OFF + h * PART, OFF + (h + 1) * PART)
            ref[k, cut, :] = get_rim(lo_ref, base, n)
            ref[rim + sx + k, cut, :] = get_rim(hi_ref, base, n)


def y_faces_kernel(rim, near_ref, far_ref, temp_ref, kind_ref, lo_ref, hi_ref,
                   left_ref, right_ref, state_ref):
    cx, near_rows, _ = near_ref.shape
    sx, sy, _ = temp_ref.shape
    left_ref[:cx, :] = near_ref[:, 0, :]
    right_ref[:cx, :] = far_ref[:, near_rows - 1, :]
    slabs = ([], [])
    long = state_ref.shape[1]
    state_ref[...] = jnp.zeros_like(state_ref)
    for which, own in enumerate((temp_ref[...], kind_ref[...].astype(F32) + 1.0)):
        fill_x(rim, state_ref.at[which], which, own, lo_ref, hi_ref)
        for into, start in zip(slabs, (OFF, OFF + sy - rim)):
            for k in range(rim):
                for h in range(0, long, PART):
                    into.append(state_ref[which, h:h + PART, start + k, :])
    put_rim(left_ref, cx, slabs[0])
    put_rim(right_ref, cx, slabs[1])


def y_faces(rim, fluid, temp, kind, lo, hi):
    cx, cy, depth = fluid.shape
    sx, sy, sz = temp.shape
    long = -(-(sx + 2 * rim) // PART) * PART
    height = cx + rim_rows(2 * rim * (long // PART), depth)
    args = (far(temp), far(kind), lo, hi)
    edge = (cx, 8, depth)
    return pl.pallas_call(
        functools.partial(y_faces_kernel, rim),
        grid=(1,),
        in_specs=[
            pl.BlockSpec(edge, lambda i: (0, 0, 0)),
            pl.BlockSpec(edge, lambda i: (0, cy // 8 - 1, 0)),
        ]
        + [whole(x.shape) for x in args],
        out_specs=[whole((height, depth))] * 2 + [whole((2, long, sy + 2 * OFF, sz))],
        out_shape=[jax.ShapeDtypeStruct((height, depth), F32)] * 2
        + [pltpu.HBM((2, long, sy + 2 * OFF, sz), F32)],
        compiler_params=params(10),
        cost_estimate=cost(1000, 4 * 4 * height * depth),
        name="y_faces",
    )(far(fluid), far(fluid), *args)


def strips_kernel(thin, heat_ref, lo_ref, hi_ref, near_ref, away_ref,
                  left_ref, right_ref, work_ref):
    cx = near_ref.shape[0]
    sx, sy, sz = heat_ref.shape
    edge = thin * sy
    left_ref[:cx, :] = near_ref[...]
    right_ref[:cx, :] = away_ref[...]
    work_ref[...] = jnp.zeros_like(work_ref)
    work_ref[:thin] = lo_ref[:edge, :].reshape(thin, sy, sz)
    work_ref[thin:thin + sx] = heat_ref[...]
    work_ref[thin + sx:2 * thin + sx] = hi_ref[:edge, :].reshape(thin, sy, sz)
    long = work_ref.shape[0]
    for ref, start in ((left_ref, 0), (right_ref, sy - thin)):
        slabs = [
            work_ref[h:h + PART, start + k, :] for k in range(thin) for h in range(0, long, PART)
        ]
        put_rim(ref, cx, slabs)


def strips(thin, heat, lo, hi, left, right):
    cx, depth = left.shape
    sx, sy, sz = heat.shape
    long = -(-(sx + 2 * thin) // PART) * PART
    height = cx + rim_rows(thin * (long // PART), depth)
    return pl.pallas_call(
        functools.partial(strips_kernel, thin),
        in_specs=[in_vmem] * 5,
        out_specs=[in_vmem] * 2,
        out_shape=[jax.ShapeDtypeStruct((height, depth), F32)] * 2,
        scratch_shapes=[pltpu.VMEM((long, sy, sz), F32)],
        compiler_params=params(8),
        cost_estimate=cost(1000, 16 * height * depth),
        name="strips",
    )(heat, lo, hi, left, right)


def table(kind, values):
    out = jnp.zeros(kind.shape, F32)
    for index, value in enumerate(values):
        out = jnp.where(kind == index + 1.0, value, out)
    return out


def ready_kernel(rim, cap, state_ref, ylo_ref, yhi_ref, code_ref,
                 temp_ref, cond_ref, sigma_ref, pick_ref):
    _, long, height, sz = state_ref.shape
    ndev = code_ref.shape[0]
    slots = pick_ref.shape[1]
    sx = sigma_ref.shape[0] - 2
    sy = height - 2 * OFF
    pieces = long // PART
    turned = jnp.transpose(code_ref[...])
    names = lax.broadcasted_iota(jnp.int32, (cap, slots), 1)
    for source in range(0, ndev, 2):
        pick_ref[source * cap:(source + 2) * cap, :] = jnp.concatenate(
            [
                jnp.where(names == turned[:cap, one:one + 1], 1.0, 0.0)
                for one in (source, source + 1)
            ],
            axis=0,
        ).astype(BF16)
    base = ylo_ref.shape[0] - rim_rows(2 * rim * pieces, ylo_ref.shape[1])
    for which, ref in enumerate((temp_ref, cond_ref)):
        ref[...] = state_ref[which]
        for k in range(rim):
            for h in range(pieces):
                n = (which * rim + k) * pieces + h
                cut = slice(h * PART, (h + 1) * PART)
                ref[cut, OFF - rim + k, :] = get_rim(ylo_ref, base, n)
                ref[cut, OFF + sy + k, :] = get_rim(yhi_ref, base, n)
    kind = cond_ref[...]
    sigma_ref[...] = table(kind[rim - 1:rim + sx + 1], modulus_table)
    cond_ref[...] = solid_step * table(kind, conduct_table)


def ready(rim, cap, state, ylo, yhi, code, block):
    sx, sy, sz = block
    _, long, height, _ = state.shape
    ndev = code.shape[0]
    args = (far(state), ylo, yhi, code)
    return pl.pallas_call(
        functools.partial(ready_kernel, rim, cap),
        grid=(1,),
        in_specs=[whole(x.shape) for x in args],
        out_specs=[in_vmem] * 4,
        out_shape=[
            pltpu.VMEM((long, height, sz), F32),
            pltpu.VMEM((long, height, sz), F32),
            pltpu.VMEM((sx + 2, height, sz), F32),
            pltpu.VMEM((ndev * cap, sx * sy), BF16),
        ],
        compiler_params=params(14),
        cost_estimate=cost(4 * ndev * cap * sx * sy, 4 * ndev * cap * sx * sy),
        name="ready",
    )(*args)


def solid_kernel(rim, start_ref, cond_ref, modulus_ref, pick_ref,
                 heat_ref, hxlo_ref, hxhi_ref, hylo_ref, hyhi_ref,
                 next_ref, sigma_ref, reply_ref, even_ref, odd_ref, src_ref, rhs_ref,
                 stage_ref, leave, sems):
    sx, sy, sz = heat_ref.shape
    wide = sx + 2 * rim
    thin = rim - 1
    edge = thin * sy
    src_ref[rim:rim + sx, OFF:OFF + sy, :] = heat_ref[...]
    src_ref[1:rim, OFF:OFF + sy, :] = hxlo_ref[:edge, :].reshape(thin, sy, sz)
    src_ref[rim + sx:wide - 1, OFF:OFF + sy, :] = hxhi_ref[:edge, :].reshape(thin, sy, sz)
    parts = -(-(sx + 2 * thin) // PART)
    base = hylo_ref.shape[0] - rim_rows(thin * parts, hylo_ref.shape[1])
    for k in range(thin):
        for h in range(parts):
            n = k * parts + h
            count = min(PART, sx + 2 * thin - h * PART)
            cut = slice(1 + h * PART, 1 + h * PART + count)
            src_ref[cut, OFF - thin + k, :] = get_rim(hylo_ref, base, n)[:count]
            src_ref[cut, OFF + sy + k, :] = get_rim(hyhi_ref, base, n)[:count]
    src_ref[...] = (solid_step * source_gain) * src_ref[...]
    height = start_ref.shape[1]
    first = lax.broadcasted_iota(jnp.int32, (height, sz), 1) == 0
    last = lax.broadcasted_iota(jnp.int32, (height, sz), 1) == sz - 1
    now = start_ref
    for turn in range(rim - 1):
        later = (odd_ref, even_ref)[turn % 2]
        for x in range(1 + turn, wide - 1 - turn):
            centre = now[x]
            beside = now[x - 1] + now[x + 1]
            beside += pltpu.roll(centre, 1, 0) + pltpu.roll(centre, height - 1, 0)
            beside += jnp.where(first, 0.0, pltpu.roll(centre, 1, 1))
            beside += jnp.where(last, 0.0, pltpu.roll(centre, sz - 1, 1))
            later[x] = centre + (cond_ref[x] * (beside - 6.0 * centre) + src_ref[x])
        now = later
    solid = now[rim:rim + sx, OFF:OFF + sy, :]
    leaving = pltpu.make_async_copy(
        now.at[rim:rim + sx, OFF:OFF + sy, :], next_ref, leave
    )
    leaving.start()
    sigma_ref[...] = modulus_ref[...] * now[rim - 1:rim + sx + 1]
    high, low = halves(solid.reshape(sx * sy, sz))
    rhs_ref[:, :sz] = high
    rhs_ref[:, sz:] = low
    block = pick_ref.shape[0] // GROUPS
    copies = []
    for index in range(GROUPS):
        cut = slice(index * block, (index + 1) * block)
        both = jnp.dot(pick_ref[cut, :], rhs_ref[...], preferred_element_type=F32)
        stage_ref[cut, :] = both[:, :sz] + both[:, sz:]
        copies.append(pltpu.make_async_copy(stage_ref.at[cut], reply_ref.at[cut], sems.at[index]))
        copies[-1].start()
    leaving.wait()
    for copy in copies:
        copy.wait()


def solid_steps(rim, prepared, heat, heat_rim):
    sx, sy, sz = heat.shape
    long, height, _ = prepared[0].shape
    total = prepared[3].shape[0]
    return pl.pallas_call(
        functools.partial(solid_kernel, rim),
        in_specs=[in_vmem] * 9,
        out_specs=[in_hbm, in_vmem, in_hbm],
        out_shape=[
            pltpu.HBM((sx, sy, sz), F32),
            jax.ShapeDtypeStruct((sx + 2, height, sz), F32),
            pltpu.HBM((total, sz), F32),
        ],
        scratch_shapes=[pltpu.VMEM((long, height, sz), F32)] * 2
        + [
            pltpu.VMEM((sx + 2 * rim, height, sz), F32),
            pltpu.VMEM((sx * sy, 2 * sz), BF16),
            pltpu.VMEM((total, sz), F32),
            pltpu.SemaphoreType.DMA,
            pltpu.SemaphoreType.DMA((GROUPS,)),
        ],
        compiler_params=params(14),
        cost_estimate=cost(4 * total * sx * sy * sz, 4 * total * sz),
        name="solid_steps",
    )(*[near(x) for x in prepared], heat, *heat_rim)


def stress_kernel(sigma_ref, out_ref, tick_ref):
    tick_ref[...] = jnp.zeros_like(tick_ref)
    _, sx, sy, sz = out_ref.shape
    height = sigma_ref.shape[1]
    first = lax.broadcasted_iota(jnp.int32, (height, sz), 1) == 0
    last = lax.broadcasted_iota(jnp.int32, (height, sz), 1) == sz - 1

    def plane(x, none):
        centre = sigma_ref[x + 1]
        out_ref[0, x] = 0.5 * (sigma_ref[x + 2] - sigma_ref[x])[OFF:OFF + sy]
        along = pltpu.roll(centre, height - 1, 0) - pltpu.roll(centre, 1, 0)
        out_ref[1, x] = 0.5 * along[OFF:OFF + sy]
        along = jnp.where(last, 0.0, pltpu.roll(centre, sz - 1, 1)) - jnp.where(
            first, 0.0, pltpu.roll(centre, 1, 1)
        )
        out_ref[2, x] = 0.5 * along[OFF:OFF + sy]
        return none

    lax.fori_loop(0, sx, plane, 0)


def stress(sigma, sx, sy):
    sz = sigma.shape[2]
    return pl.pallas_call(
        stress_kernel,
        grid=(1,),
        in_specs=[whole(sigma.shape)],
        out_specs=[whole((3, sx, sy, sz)), whole((8, LANE))],
        out_shape=[pltpu.HBM((3, sx, sy, sz), F32), jax.ShapeDtypeStruct((8, LANE), F32)],
        compiler_params=params(8),
        cost_estimate=cost(10 * sx * sy * sz, 16 * sx * sy * sz),
        name="stress",
    )(sigma)


def unpack_kernel(dest_ref, back_ref, *refs):
    out_ref = refs[-1]
    rows = out_ref.shape[0]

    def step(index, none):
        base = pl.multiple_of(index * 8, 8)
        lines = [back_ref[pl.ds(dest_ref[0, base + i], 1), :] for i in range(8)]
        for i, line in enumerate(lines):
            out_ref[pl.ds(base + i, 1), :] = line
        return none

    lax.fori_loop(0, rows // 8, step, 0, unroll=4)


def unpack(dest, back, after):
    rows = dest.shape[1]
    row_len = back.shape[1]
    return pl.pallas_call(
        unpack_kernel,
        grid=(1,),
        in_specs=[pl.BlockSpec(memory_space=pltpu.SMEM), whole(back.shape)]
        + [anywhere] * len(after),
        out_specs=whole((rows, row_len)),
        out_shape=jax.ShapeDtypeStruct((rows, row_len), F32),
        compiler_params=params(10),
        cost_estimate=cost(rows * 128, 8 * rows * row_len),
        name="unpack",
    )(dest, back, *after)


PLANES = 2
RING = 3 * PLANES


def fluid_kernel(opening, here_ref, xlo_ref, xhi_ref, speed_ref, flux_ref, *refs):
    index, count = pl.program_id(0), pl.num_programs(0)
    cx = (count - 1) * PLANES
    _, cy, depth = here_ref.shape
    row_len = flux_ref.shape[2]
    rows = slice(OFF, OFF + cy)
    if opening:
        out_ref, xfirst_ref, xlast_ref, yfirst_ref, ylast_ref, clo_ref, chi_ref, ring_ref = refs
    else:
        lo_ref, hi_ref, left_ref, right_ref, ylo_ref, yhi_ref = refs[:6]
        out_ref, tick_ref, ring_ref = refs[-3:]
        tick_ref[...] = jnp.zeros_like(tick_ref)

    def patch(slot, corner_ref):
        wide = depth // LANE
        base = corner_ref.shape[0] - 2 * wide
        for row, at in ((OFF, base), (OFF + cy - 1, base + wide)):
            for i in range(wide):
                ring_ref[slot, row:row + 1, i * LANE:(i + 1) * LANE] = (
                    corner_ref[at + i:at + i + 1, :]
                )

    @pl.when(index == 0)
    def _():
        ring_ref[RING - 1, rows, :] = xlo_ref[...]
        if opening:
            for slot in range(RING):
                ring_ref[slot, OFF - 8:OFF, :] = jnp.zeros((8, depth), F32)
                ring_ref[slot, OFF + cy:OFF + cy + 8, :] = jnp.zeros((8, depth), F32)
        else:
            patch(RING - 1, lo_ref)

    @pl.when(index < count - 1)
    def _():
        for p in range(PLANES):
            plane = index * PLANES + p
            slot = lax.rem(plane, RING)
            ring_ref[slot, rows, :] = here_ref[p]
            if not opening:
                one = pl.ds(plane, 1)
                ring_ref[slot, OFF:OFF + 1, :] = left_ref[one, :]
                ring_ref[slot, OFF + cy - 1:OFF + cy, :] = right_ref[one, :]
                ring_ref[slot, OFF - 1:OFF, :] = ylo_ref[one, :]
                ring_ref[slot, OFF + cy:OFF + cy + 1, :] = yhi_ref[one, :]

    @pl.when(index == count - 1)
    def _():
        ring_ref[lax.rem(cx, RING), rows, :] = xhi_ref[...]
        if not opening:
            patch(lax.rem(cx, RING), hi_ref)

    rate = time_step * diffusivity

    def push(total, centre, lower, upper, speed):
        scaled = time_step * speed
        total = total + (rate + jnp.maximum(scaled, 0.0)) * (lower - centre)
        return total + (rate - jnp.minimum(scaled, 0.0)) * (upper - centre)

    def advance(p, none):
        lanes = lax.broadcasted_iota(jnp.int32, (8, depth), 1)
        first, last = lanes == 0, lanes == depth - 1
        plane = (index - 1) * PLANES + p
        mid = lax.rem(plane, RING)
        old, new = lax.rem(plane + RING - 1, RING), lax.rem(plane + 1, RING)
        for tile in range(cy // 16):
            speeds = [
                speed_ref[k, p, tile * 16:tile * 16 + 16, :].astype(F32) for k in range(3)
            ]
            for part in range(2):
                y = tile * 16 + part * 8
                at = OFF + y
                u, v, w = [s[part * 8:part * 8 + 8] for s in speeds]
                centre = ring_ref[mid, at:at + 8, :]
                total = push(
                    centre, centre, ring_ref[old, at:at + 8, :], ring_ref[new, at:at + 8, :], u
                )
                total = push(
                    total, centre, ring_ref[mid, at - 1:at + 7, :],
                    ring_ref[mid, at + 1:at + 9, :], v,
                )
                lower = jnp.where(first, 0.0, pltpu.roll(centre, 1, 1))
                upper = jnp.where(last, 0.0, pltpu.roll(centre, depth - 1, 1))
                total = push(total, centre, lower, upper, w)
                out_ref[p, y:y + 8, row_len:] = total[:, row_len:]
                out_ref[p, y:y + 8, :row_len] = (
                    total[:, :row_len] - time_step * flux_ref[p, y:y + 8, :]
                )
        if opening:
            one = pl.ds(plane, 1)
            yfirst_ref[one, :] = out_ref[p, 0:1, :]
            ylast_ref[one, :] = out_ref[p, cy - 1:cy, :]
            edge = time_step * speed_ref[1, p, 0:16, :].astype(F32)
            clo_ref[one, :] = rate + jnp.maximum(edge[0:1], 0.0)
            edge = time_step * speed_ref[1, p, cy - 16:cy, :].astype(F32)
            chi_ref[one, :] = rate - jnp.minimum(edge[15:16], 0.0)
        return none

    @pl.when(index > 0)
    def _():
        lax.fori_loop(0, PLANES, advance, 0)

    if opening:

        @pl.when(index == 1)
        def _():
            xfirst_ref[...] = out_ref[0]

        @pl.when(index == count - 1)
        def _():
            xlast_ref[...] = out_ref[PLANES - 1]


def fluid_step(opening, temp, sides, velocity, flux, lines, after):
    cx, cy, depth = temp.shape
    row_len = flux.shape[2]
    plane = (PLANES, cy, depth)
    steps = cx // PLANES
    face = pl.BlockSpec((cy, depth), lambda i: (0, 0))
    line = pl.BlockSpec((cx, depth), lambda i: (0, 0))
    back = lambda i: (jnp.maximum(i - 1, 0), 0, 0)
    shape = jax.ShapeDtypeStruct
    outs = [pl.BlockSpec(plane, back)]
    outs += [face, face] + [line] * 4 if opening else [whole((8, LANE))]
    shapes = [pltpu.HBM(temp.shape, F32)]
    if opening:
        shapes += [shape((cy, depth), F32)] * 2 + [shape((cx, depth), F32)] * 4
    else:
        shapes += [shape((8, LANE), F32)]
    extra = [whole(x.shape) for x in lines[:2]] + [line] * len(lines[2:])
    return pl.pallas_call(
        functools.partial(fluid_kernel, opening),
        grid=(steps + 1,),
        in_specs=[
            pl.BlockSpec(plane, lambda i: (jnp.minimum(i, steps - 1), 0, 0)),
            face,
            face,
            pl.BlockSpec((3, PLANES, cy, depth), lambda i: (0, jnp.maximum(i - 1, 0), 0, 0)),
            pl.BlockSpec((PLANES, cy, row_len), back),
        ]
        + extra
        + [anywhere] * len(after),
        out_specs=outs,
        out_shape=shapes,
        scratch_shapes=[pltpu.VMEM((RING, cy + 2 * OFF, depth), F32)],
        compiler_params=params(16),
        cost_estimate=cost(40 * cx * cy * depth, 14 * cx * cy * depth),
        name="fluid_step",
    )(far(temp), *sides, far(velocity), flux, *lines, *after)


def body(temp_fluid, velocity, wall_old, wall_mask, owner_map, slot_map, temp_solid, material):
    cx, cy, depth = temp_fluid.shape
    row_len = wall_old.shape[2]
    sx, sy, sz = temp_solid.shape
    ndev = lax.axis_size("gx") * lax.axis_size("gy")
    rows = cx * cy
    cap = (3 * rows + ndev - 1) // ndev
    cap = -(-cap // 8) * 8
    total = ndev * cap
    rim = SSTEPS + 1

    first, last = x_faces(rim, temp_fluid, temp_solid, material)
    xlo, xhi = neighbours(last, first, "gx")
    dest, where, codes = rank(owner_map.reshape(1, rows), slot_map, ndev, cap)
    outgoing, flux = pack(where, codes, temp_fluid, wall_old, wall_mask, cap, (first, last))
    outgoing, xlo, xhi = lax.optimization_barrier((outgoing, xlo, xhi))
    incoming = lax.all_to_all(outgoing, AXES, split_axis=0, concat_axis=0, tiled=True)

    left, right, state = y_faces(rim, temp_fluid, temp_solid, material, xlo, xhi)
    ylo, yhi = neighbours(right, left, "gy")
    fluid, first, last, *edges = fluid_step(
        True, temp_fluid, (xlo, xhi), velocity, flux, (), ()
    )
    sides = neighbours(last, first, "gx")

    thin = rim - 1
    heat, first, last, left, right, code = heat_sum(
        incoming, cap, temp_solid.shape, thin, sides, (ylo, yhi, *edges)
    )
    hxlo, hxhi = neighbours(last, first, "gx")
    first, last = strips(thin, heat, hxlo, hxhi, left, right)
    hylo, hyhi = neighbours(last, first, "gy")
    prepared = ready(rim, cap, state, ylo, yhi, code, heat.shape)
    solid, sigma, replies = solid_steps(rim, prepared, heat, (hxlo, hxhi, hylo, hyhi))
    returned = lax.all_to_all(
        replies.reshape(ndev, cap, sz), AXES, split_axis=0, concat_axis=0, tiled=True
    )
    force, tick = stress(sigma, sx, sy)
    fluid, tick = fluid_step(
        False, fluid, sides, velocity, flux, (hxlo, hxhi, left, right, hylo, hyhi), (tick,)
    )
    wall_next = unpack(dest, returned.reshape(total, sz), (tick,))
    return fluid, wall_next.reshape(cx, cy, row_len), solid, force


def solution(mesh):
    placed = (
        P("gx", "gy", None),
        P(None, "gx", "gy", None),
        P("gx", "gy", None),
        P("gx", "gy", None),
        P(("gx", "gy"), None, None),
        P(("gx", "gy"), None),
        P("gx", "gy", None),
        P("gx", "gy", None),
    )
    return jax.shard_map(
        body,
        mesh=mesh,
        in_specs=placed,
        out_specs=(
            P("gx", "gy", None),
            P("gx", "gy", None),
            P("gx", "gy", None),
            P(None, "gx", "gy", None),
        ),
        check_vma=False,
    )
```
